512 devices in a mesh: outer: 16 (over x_lo, z), inner: 32 (over x_hi, y, core).
Axes of the slice: x: 4 (x_hi: 2, x_lo: 2; x = x_hi * 2 + x_lo), y: 8, z: 8, core: 2. Of those that a mesh axis runs over, the one named last changes fastest.
Arguments:
- video: bfloat16 [1536, 32, 256], P(('outer', 'inner')), as said below
- gloss: bfloat16 [1536, 16, 256], P(('outer', 'inner'))
- frame_count: int32 [1536], P(('outer', 'inner')), may hold values from 1 to 32
- gloss_count: int32 [1536], P(('outer', 'inner')), may hold values from 1 to 16
Outputs:
- loss_mean: float32 [], replicated
- grad_video: float32 [1536, 32, 256], P(('outer', 'inner'))
- grad_gloss: float32 [1536, 16, 256], P(('outer', 'inner'))
The draws below stay inside these ranges and needn't reach their ends.
Inputs may be any that keep to these rules, and one draw needn't show every extreme that they name: `video`: embeddings of a clip's frames and of its text share a per-clip component; clips differ in it.
All inputs are finite; a program needn't handle non-finite values.
Results may differ from the reference program's by a relative error of at most 0.0045.
Values may be sent and summed in bfloat16 or wider, within the bound.
No kernel may reach another device: no remote copies, remote signals or barrier semaphores. Data moves between devices by JAX's collectives and lax.ppermute only.
A program may use at most 64 MiB of HBM per device.

```python
import math
import jax
import jax.numpy as jnp
from jax import lax

WIDTH = 256
FRAMES = 32
GLOSSES = 16
CLIPS = 1536


def clip_codes(key, floor_strength):
    theta = jax.random.uniform(jax.random.fold_in(key, 101), (CLIPS,), minval=-math.pi, maxval=math.pi)
    harmonic = jax.random.randint(jax.random.fold_in(key, 102), (WIDTH,), 1, 4).astype(jnp.float32)
    phase = jax.random.uniform(jax.random.fold_in(key, 103), (WIDTH,), minval=-math.pi, maxval=math.pi)
    position = jnp.arange(CLIPS, dtype=jnp.float32) / CLIPS
    strength = 1.6 * jnp.exp(position * math.log(floor_strength / 1.6))
    return strength[:, None] * math.sqrt(2.0) * jnp.cos(harmonic[None, :] * theta[:, None] + phase[None, :])


def draw_video(key, part):
    codes = clip_codes(key, 0.16)
    key = jax.random.fold_in(key, 1)
    noise = jax.random.normal(key, (CLIPS, FRAMES, WIDTH))
    scales = jnp.exp(jax.random.uniform(jax.random.fold_in(key, 7), (CLIPS, FRAMES, 1), minval=0.0, maxval=math.log(2.0)))
    return (0.005 * scales * (0.8 * codes[:, None, :] + 0.7 * noise)).astype(jnp.bfloat16)


def draw_gloss(key, part):
    codes = clip_codes(key, 0.16)
    key = jax.random.fold_in(key, 2)
    noise = jax.random.normal(key, (CLIPS, GLOSSES, WIDTH))
    scales = jnp.exp(jax.random.uniform(jax.random.fold_in(key, 9), (CLIPS, GLOSSES, 1), minval=0.0, maxval=math.log(2.0)))
    return (0.005 * scales * (0.8 * codes[:, None, :] + 0.7 * noise)).astype(jnp.bfloat16)


def set_ends(entries, stream_key, least, largest):
    longest = entries.shape.index(max(entries.shape))
    spots = []
    for shift in (0, 1):
        where = [jax.random.randint(jax.random.fold_in(stream_key, axis), (), 0, length) for axis, length in enumerate(entries.shape)]
        where[longest] = (where[longest] + shift) % entries.shape[longest]
        spots.append(tuple(where))
    return entries.at[spots[0]].set(least).at[spots[1]].set(largest)


def setup_inputs(seed: int = 0) -> dict:
    arg_keys = jax.random.split(jax.random.key(seed), 5)
    return {
        "video": draw_video(jax.random.fold_in(arg_keys[4], 71), 0),
        "gloss": draw_gloss(jax.random.fold_in(arg_keys[4], 71), 0),
        "frame_count": set_ends(jax.random.randint(arg_keys[2], (CLIPS,), 1, FRAMES + 1), jax.random.fold_in(arg_keys[2], 1), 1, FRAMES).astype(jnp.int32),
        "gloss_count": set_ends(jax.random.randint(arg_keys[3], (CLIPS,), 1, GLOSSES + 1), jax.random.fold_in(arg_keys[3], 1), 1, GLOSSES).astype(jnp.int32),
    }


SOFTMAX_TEMPER = 0.1
LOGIT_SCALE = 10.0
EPSILON = 1e-06

def unit_tokens(raw):
    values = raw.astype(jnp.float32)
    mean_sq = lax.optimization_barrier(jnp.mean(values * values, axis=-1, keepdims=True)) + EPSILON
    factor = lax.rsqrt(mean_sq) / math.sqrt(values.shape[-1])
    return ((values * factor).astype(jnp.bfloat16), values, factor)

def unit_grad(grad_unit, values, factor):
    features = values.shape[-1]
    mean_sq = lax.optimization_barrier(jnp.mean(values * values, axis=-1, keepdims=True)) + EPSILON
    inner_sum = lax.optimization_barrier(jnp.sum(grad_unit * values, axis=-1, keepdims=True))
    return factor * grad_unit - factor * values * inner_sum / (features * mean_sq)

def block_size(count, limit):
    best = 1
    for candidate in range(1, count + 1):
        if count % candidate == 0 and candidate <= limit:
            best = candidate
    return best

def block_parts(clip_units, video_clip_counts, text_units, gloss_text_counts):
    video_clip_total, frame_tokens, features = clip_units.shape
    gloss_text_total, gloss_tokens, _ = text_units.shape
    similarity_scores = lax.dot_general(clip_units.reshape(video_clip_total * frame_tokens, features), text_units.reshape(gloss_text_total * gloss_tokens, features), (((1,), (1,)), ((), ())), preferred_element_type=jnp.float32)
    softmax_weights = jnp.exp(similarity_scores.reshape(video_clip_total, frame_tokens, gloss_text_total, gloss_tokens) / SOFTMAX_TEMPER)
    video_frame_mask = (jnp.arange(frame_tokens, dtype=jnp.float32)[None, :] < video_clip_counts[:, None]).astype(jnp.float32)
    gloss_token_mask = (jnp.arange(gloss_tokens, dtype=jnp.float32)[None, :] < gloss_text_counts[:, None]).astype(jnp.float32)
    row_totals = lax.optimization_barrier(jnp.sum(softmax_weights * gloss_token_mask[None, None], axis=3))
    column_totals = lax.optimization_barrier(jnp.sum(softmax_weights * video_frame_mask[:, :, None, None], axis=1))
    video_direction = lax.optimization_barrier(jnp.sum(video_frame_mask[:, :, None] * SOFTMAX_TEMPER * jnp.log(row_totals / gloss_text_counts[None, None, :]), axis=1)) / video_clip_counts[:, None]
    text_direction = lax.optimization_barrier(jnp.sum(gloss_token_mask[None] * SOFTMAX_TEMPER * jnp.log(column_totals / video_clip_counts[:, None, None]), axis=2)) / gloss_text_counts[None, :]
    logits = LOGIT_SCALE * 0.5 * (video_direction + text_direction)
    return (logits, softmax_weights, row_totals, column_totals, video_frame_mask, gloss_token_mask)

def block_grads(clip_units, video_clip_counts, text_units, gloss_text_counts, pair_grad):
    video_clip_total, frame_tokens, features = clip_units.shape
    gloss_text_total, gloss_tokens, _ = text_units.shape
    logits, softmax_weights, row_totals, column_totals, video_frame_mask, gloss_token_mask = block_parts(clip_units, video_clip_counts, text_units, gloss_text_counts)
    valid = video_frame_mask[:, :, None, None] * gloss_token_mask[None, None]
    row_part = valid * softmax_weights / row_totals[..., None] / video_clip_counts[:, None, None, None]
    col_part = valid * softmax_weights / column_totals[:, None] / gloss_text_counts[None, None, :, None]
    score_grad = (0.5 * LOGIT_SCALE * pair_grad[:, None, :, None] * (row_part + col_part)).astype(jnp.bfloat16)
    score_grad = score_grad.reshape(video_clip_total * frame_tokens, gloss_text_total * gloss_tokens)
    clip_grad = jnp.dot(score_grad, text_units.reshape(gloss_text_total * gloss_tokens, features), preferred_element_type=jnp.float32)
    text_grad = lax.dot_general(score_grad, clip_units.reshape(video_clip_total * frame_tokens, features), (((0,), (0,)), ((), ())), preferred_element_type=jnp.float32)
    return (clip_grad, text_grad)

def reference(video, gloss, frame_count, gloss_count):
    clips_all, frame_tokens, features = video.shape
    gloss_tokens = gloss.shape[1]
    unit_v, video_f, video_fac = unit_tokens(video)
    unit_g, gloss_f, gloss_fac = unit_tokens(gloss)
    video_clip_counts = frame_count.astype(jnp.float32)
    gloss_text_counts = gloss_count.astype(jnp.float32)
    block = block_size(clips_all, max(1, 256 // frame_tokens))
    blocks = clips_all // block
    clip_blocks = unit_v.reshape(blocks, block, frame_tokens, features)
    count_blocks = video_clip_counts.reshape(blocks, block)
    logits = lax.map(lambda pieces: block_parts(pieces[0], pieces[1], unit_g, gloss_text_counts)[0], (clip_blocks, count_blocks)).reshape(clips_all, clips_all)
    exp_logits = jnp.exp(logits)
    row_all = lax.optimization_barrier(jnp.sum(exp_logits, axis=1))
    col_all = lax.optimization_barrier(jnp.sum(exp_logits, axis=0))
    loss_mean = 0.5 * jnp.sum(jnp.log(row_all) + jnp.log(col_all) - 2.0 * jnp.diagonal(logits)) / clips_all
    matched = jnp.eye(clips_all, dtype=jnp.float32)
    pair_grad = 0.5 * (exp_logits / row_all[:, None] + exp_logits / col_all[None, :]) - matched

    def backward_step(text_acc, pieces):
        clip_grad, text_grad = block_grads(pieces[0], pieces[1], unit_g, gloss_text_counts, pieces[2])
        return (text_acc + text_grad, clip_grad)
    text_sum, clip_grads = lax.scan(backward_step, jnp.zeros((clips_all * gloss_tokens, features), jnp.float32), (clip_blocks, count_blocks, pair_grad.reshape(blocks, block, clips_all)))
    grad_video = unit_grad(clip_grads.reshape(clips_all, frame_tokens, features), video_f, video_fac)
    grad_gloss = unit_grad(text_sum.reshape(clips_all, gloss_tokens, features), gloss_f, gloss_fac)
    return (loss_mean, grad_video, grad_gloss)
```

```python
import functools
import math

import jax
import jax.numpy as jnp
from jax import lax
from jax.experimental import pallas as pl
from jax.experimental.pallas import tpu as pltpu
from jax.sharding import PartitionSpec as P

F32 = jnp.float32
BF16 = jnp.bfloat16
EPSILON = 1e-06
EXP_SCALE = 10.0 * math.log2(math.e)
MARK = 2.0
MARK_LIMIT = 1.5
FAR = -1e30

NZ, NY, NX, NCORE = 8, 8, 4, 2
OWN = 3
FRAMES, GLOSSES, WIDTH = 32, 16, 256
CLIPS_DEV = NZ * NCORE * OWN
TEXTS_DEV = NY * NX * OWN
LANES = 128
VROWS = FRAMES * CLIPS_DEV
GROWS = GLOSSES * LANES
VOWN = FRAMES * OWN
GOWN = GLOSSES * OWN
EXTRA = 16
PAIRS = GLOSSES // 2

Z_GROUPS = [[h * NZ + i for i in range(NZ)] for h in range(2)]
Y_GROUPS = [[h * 16 + 2 * i + c for i in range(NY)] for h in range(2) for c in range(NCORE)]


def params(limit_mb=40):
    return pltpu.CompilerParams(vmem_limit_bytes=limit_mb * 1024 * 1024)


def cost(flops, nbytes, trans=0):
    return pl.CostEstimate(flops=int(flops), bytes_accessed=int(nbytes), transcendentals=int(trans))


def iota(shape, dim):
    return lax.broadcasted_iota(jnp.int32, shape, dim)


def nt(a, b, **kw):
    return lax.dot_general(a, b, (((1,), (1,)), ((), ())), preferred_element_type=F32, **kw)


def nn(a, b, **kw):
    return lax.dot_general(a, b, (((1,), (0,)), ((), ())), preferred_element_type=F32, **kw)


def tn(a, b, **kw):
    return lax.dot_general(a, b, (((0,), (0,)), ((), ())), preferred_element_type=F32, **kw)


def column_of(row, n):
    eye = iota((n, LANES), 0) == iota((n, LANES), 1)
    return jnp.sum(jnp.where(eye, jnp.broadcast_to(row[0:1], (n, LANES)), 0.0), axis=1, keepdims=True)


def pieces(value):
    lane = iota((EXTRA, WIDTH), 1)
    full = jnp.broadcast_to(value, (EXTRA, WIDTH))
    hi = full.astype(BF16).astype(F32)
    mid = (full - hi).astype(BF16).astype(F32)
    low = full - hi - mid
    return jnp.where(lane == 0, hi, jnp.where(lane == 1, mid, jnp.where(lane == 2, low, 0.0)))


def unpiece(block):
    mine = (iota((EXTRA, WIDTH), 0) == 0) & (iota((EXTRA, WIDTH), 1) < 3)
    return jnp.sum(jnp.where(mine, block, 0.0), keepdims=True).reshape(1, 1)


def put(ref, at, value):
    ref[0, at, :] = value[:, :LANES]
    ref[1, at, :] = value[:, LANES:]


def get(ref, at):
    return jnp.concatenate([ref[0, at, :], ref[1, at, :]], axis=1)


def two_halves(rows):
    return pltpu.VMEM((2, rows, LANES), F32)


def units_kernel(fc, gc, video, gloss, v_out, g_out, v_scr, g_scr):
    for count, raw, scr, tokens in ((fc, video, v_scr, FRAMES), (gc, gloss, g_scr, GLOSSES)):
        row, lane = iota((tokens, WIDTH), 0), iota((tokens, WIDTH), 1)
        for c in range(OWN):
            x = raw[c].astype(F32)
            mean_sq = jnp.mean(x * x, axis=-1, keepdims=True) + EPSILON
            unit = x * (lax.rsqrt(mean_sq) / math.sqrt(WIDTH))
            mark = jnp.where(lane == 0, MARK, 0.0)
            put(scr, pl.ds(c, tokens, stride=OWN), jnp.where(row < count[c], unit, mark))
    v = get(v_scr, pl.ds(0, VOWN)).astype(BF16)
    g = get(g_scr, pl.ds(0, GOWN)).astype(BF16)
    for i in range(NZ):
        v_out[i] = v
    for i in range(NY):
        g_out[i] = g


def diagonal_kernel(fc, gc, v_ref, g_ref, dv, dg, logit_sum):
    def pick(count, which):
        return jnp.where(which == 0, count[0], jnp.where(which == 1, count[1], count[2]))

    v, g = v_ref[0], g_ref[0]
    shape = (VOWN, GOWN)
    r, q = iota(shape, 0), iota(shape, 1)
    rc, qc = lax.rem(r, OWN), lax.rem(q, OWN)
    valid = (rc == qc) & (lax.div(r, OWN) < pick(fc, rc)) & (lax.div(q, OWN) < pick(gc, qc))
    e = jnp.where(valid, jnp.exp2(nt(v, g) * EXP_SCALE), 0.0)
    r1, q1 = iota((VOWN, 1), 0), iota((1, GOWN), 1)
    rc1, qc1 = lax.rem(r1, OWN), lax.rem(q1, OWN)
    frames_r, glosses_r = pick(fc, rc1), pick(gc, rc1)
    frames_q, glosses_q = pick(fc, qc1), pick(gc, qc1)
    row_ok = lax.div(r1, OWN) < frames_r
    col_ok = lax.div(q1, OWN) < glosses_q
    frames_r, glosses_r = frames_r.astype(F32), glosses_r.astype(F32)
    frames_q, glosses_q = frames_q.astype(F32), glosses_q.astype(F32)
    rows = jnp.where(row_ok, jnp.sum(e, axis=1, keepdims=True), 1.0)
    cols = jnp.where(col_ok, jnp.sum(e, axis=0, keepdims=True), 1.0)
    by_row = jnp.where(row_ok, jnp.log(rows / glosses_r) / frames_r, 0.0)
    by_col = jnp.where(col_ok, jnp.log(cols / frames_q) / glosses_q, 0.0)
    total = jnp.sum(by_row, axis=0, keepdims=True) + jnp.sum(by_col, axis=1, keepdims=True)
    logit_sum[...] = jnp.broadcast_to(0.5 * total, (8, LANES))
    weight = -5.0 * e * (1.0 / (rows * frames_r) + 1.0 / (cols * glosses_q))
    dv[...] = nn(weight, g.astype(F32), precision=lax.Precision.HIGHEST)
    dg[...] = tn(weight, v.astype(F32), precision=lax.Precision.HIGHEST)


def exp_scores(v, g):
    return jnp.exp2(nt(v, g) * EXP_SCALE)


def forward_kernel(
    v_mine, v_twin, g0, g1, g2, g3, diag,
    v_out, g_out, row_out, col_out, e_out, r_mine, r_twin, c_out,
    v_scr, g_scr, frame_mask, gloss_mask, rows, cols,
):
    for t, ref in enumerate((v_mine, v_twin)):
        put(v_scr.at[t], pl.ds(0, NZ * VOWN), ref[...].reshape(NZ * VOWN, WIDTH).astype(F32))
    for f in range(FRAMES):
        parts = [get(v_scr.at[t], pl.ds(f * OWN + c, NZ, stride=VOWN)) for t in range(NCORE) for c in range(OWN)]
        v_out[pl.ds(f * CLIPS_DEV, CLIPS_DEV), :] = jnp.concatenate(parts, axis=0).astype(BF16)
    for s, ref in enumerate((g0, g1, g2, g3)):
        put(g_scr.at[s], pl.ds(0, NY * GOWN), ref[...].reshape(NY * GOWN, WIDTH).astype(F32))
    pad = jnp.where(iota((LANES - TEXTS_DEV, WIDTH), 1) == 0, MARK, 0.0)
    for g in range(GLOSSES):
        parts = [get(g_scr.at[s], pl.ds(g * OWN + c, NY, stride=GOWN)) for s in range(NX) for c in range(OWN)]
        g_out[pl.ds(g * LANES, LANES), :] = jnp.concatenate(parts + [pad], axis=0).astype(BF16)

    first = jnp.where(iota((WIDTH, LANES), 0) == 0, 1.0, 0.0).astype(BF16)
    frame_mask[...] = jnp.where(nn(v_out[...], first) < MARK_LIMIT, 1.0, 0.0)
    first_row = jnp.where(iota((16, WIDTH), 1) == 0, 1.0, 0.0).astype(BF16)
    for g in range(GLOSSES):
        gloss_mask[g] = jnp.where(nt(first_row, g_out[pl.ds(g * LANES, LANES), :])[0:8] < MARK_LIMIT, 1.0, 0.0)
    frames = jnp.zeros((CLIPS_DEV, LANES), F32)
    for f in range(FRAMES):
        frames = frames + frame_mask[pl.ds(f * CLIPS_DEV, CLIPS_DEV), :]
    glosses = gloss_mask[0]
    for g in range(1, GLOSSES):
        glosses = glosses + gloss_mask[g]
    glosses = jnp.maximum(glosses, 1.0)[0:1]

    rows[...] = jnp.zeros_like(rows)

    def two_glosses(p, _):
        e = exp_scores(v_out[...], g_out[pl.ds(pl.multiple_of(p * WIDTH, WIDTH), WIDTH), :])
        m0, m1 = gloss_mask[2 * p][0:1], gloss_mask[2 * p + 1][0:1]
        col0 = jnp.zeros((CLIPS_DEV, LANES), F32)
        col1 = jnp.zeros((CLIPS_DEV, LANES), F32)
        for f in range(FRAMES):
            at = pl.ds(f * CLIPS_DEV, CLIPS_DEV)
            block = e[f * CLIPS_DEV : (f + 1) * CLIPS_DEV]
            e0, e1 = block[:, :LANES], block[:, LANES:]
            mask = frame_mask[at, :]
            rows[at, :] = rows[at, :] + (e0 * m0 + e1 * m1)
            col0 = col0 + e0 * mask
            col1 = col1 + e1 * mask
        cols[2 * p] = col0
        cols[2 * p + 1] = col1
        return 0

    lax.fori_loop(0, PAIRS, two_glosses, 0)

    lane = iota((CLIPS_DEV, LANES), 1)
    real = lane < TEXTS_DEV
    video_part = jnp.zeros((CLIPS_DEV, LANES), F32)
    for f in range(FRAMES):
        at = pl.ds(f * CLIPS_DEV, CLIPS_DEV)
        mask = frame_mask[at, :]
        total = jnp.where(real, rows[at, :], 1.0)
        video_part = video_part + mask * jnp.log(total / glosses)
        row_out[at, :] = jnp.where(mask > 0.0, 1.0 / (total * frames), FAR)
    gloss_part = jnp.zeros((CLIPS_DEV, LANES), F32)
    for g in range(GLOSSES):
        mask = gloss_mask[g][0:1]
        total = cols[g]
        gloss_part = gloss_part + mask * jnp.log(total / frames)
        col_out[g] = jnp.where(mask > 0.0, 1.0 / (total * glosses), FAR)
    logits = 0.5 * (video_part / frames + gloss_part / glosses)
    e_pair = jnp.where(real, jnp.exp(logits), 0.0)
    e_out[...] = e_pair

    sums = jnp.sum(e_pair, axis=1, keepdims=True)
    clip = iota((CLIPS_DEV, LANES), 0)
    half = CLIPS_DEV // 2
    swapped = jnp.where(clip < half, clip + half, clip - half)
    spread = jnp.broadcast_to(sums, (CLIPS_DEV, LANES))
    row_mine = jnp.sum(jnp.where(lane == clip, spread, 0.0), axis=0, keepdims=True)
    row_twin = jnp.sum(jnp.where(lane == swapped, spread, 0.0), axis=0, keepdims=True)
    at_diag = iota((8, LANES), 1) == CLIPS_DEV
    r_mine[...] = jnp.where(at_diag, diag[...], jnp.broadcast_to(row_mine, (8, LANES)))
    r_twin[...] = jnp.where(at_diag, diag[...], jnp.broadcast_to(row_twin, (8, LANES)))
    c_row = jnp.broadcast_to(jnp.sum(e_pair, axis=0, keepdims=True), (8, LANES))
    for i in range(NY):
        c_out[i] = c_row


def weights_kernel(v_ref, g_ref, row_ref, col_ref, e_ref, p_out, av_out, ag_out):
    p = pl.program_id(0)
    e = exp_scores(v_ref[...], g_ref[...])
    scale = 2.5 * e_ref[...]
    col0, col1 = col_ref[0], col_ref[1]
    for f in range(FRAMES):
        at = pl.ds(f * CLIPS_DEV, CLIPS_DEV)
        block = e[f * CLIPS_DEV : (f + 1) * CLIPS_DEV]
        row = row_ref[at, :]
        w0 = scale * block[:, :LANES] * jnp.maximum(row + col0, 0.0)
        w1 = scale * block[:, LANES:] * jnp.maximum(row + col1, 0.0)
        p_out[0, at, :] = jnp.concatenate([w0, w1], axis=1).astype(BF16)
    weights = p_out[0]
    part = nn(weights, g_ref[...])

    @pl.when(p == 0)
    def _():
        av_out[...] = part

    @pl.when(p > 0)
    def _():
        av_out[...] = av_out[...] + part

    ag_out[...] = tn(weights, v_ref[...])


def text_sums(q0, q1, q2, q3):
    lane = iota((8, LANES), 1)
    slot = OWN * NY
    total = q0[...]
    for s, q in enumerate((q1, q2, q3), start=1):
        part = q[...]
        ahead = pltpu.roll(part, slot * s, 1)
        behind = pltpu.roll(part, (slot * s - TEXTS_DEV) % LANES, 1)
        total = total + jnp.where(lane < slot * s, behind, ahead)
    return jnp.where(lane < TEXTS_DEV, total, 0.0)


def by_text_kernel(q0, q1, q2, q3, p_ref, g_ref, out):
    step = pl.program_id(0)
    c_row = text_sums(q0, q1, q2, q3)
    inverse = jnp.where(c_row > 0.0, 1.0 / c_row, 0.0)
    col = jnp.broadcast_to(column_of(inverse, LANES), (LANES, WIDTH))
    scaled = g_ref[...].astype(F32) * jnp.concatenate([col, col], axis=0)
    hi = scaled.astype(BF16)
    low = (scaled - hi.astype(F32)).astype(BF16)
    part = nn(p_ref[0], hi) + nn(p_ref[0], low)

    @pl.when(step == 0)
    def _():
        out[...] = part

    @pl.when(step > 0)
    def _():
        out[...] = out[...] + part


def clip_sums(z_ref):
    total = z_ref[0]
    for i in range(1, NZ):
        total = total + z_ref[i]
    return total


def video_partial_kernel(z_ref, q0, q1, q2, q3, av_ref, bv_ref, mine, twin):
    r_row = clip_sums(z_ref)
    inverse = jnp.broadcast_to(1.0 / column_of(r_row, CLIPS_DEV), (CLIPS_DEV, WIDTH))
    half = CLIPS_DEV // 2
    for pair in range(FRAMES // 2):
        blocks = []
        for f in (2 * pair, 2 * pair + 1):
            at = pl.ds(f * CLIPS_DEV, CLIPS_DEV)
            block = av_ref[at, :] * inverse + bv_ref[at, :]
            mine[pl.ds(f * half, half), :] = block[:half]
            blocks.append(block[half:])
        twin[pl.ds(pair * CLIPS_DEV, CLIPS_DEV), :] = jnp.concatenate(blocks, axis=0).astype(BF16)
    c_row = text_sums(q0, q1, q2, q3)[0:1]
    logs = jnp.where(iota((1, LANES), 1) < TEXTS_DEV, jnp.log(jnp.where(c_row > 0.0, c_row, 1.0)), 0.0)
    total = pieces(jnp.sum(logs, axis=1, keepdims=True))
    mine[pl.ds(FRAMES * half, EXTRA), :] = total
    twin[pl.ds(FRAMES * half, EXTRA), :] = total.astype(BF16)


def gloss_partial_kernel(z_ref, q0, q1, q2, q3, p_ref, v_ref, ag_ref, s0, s1, s2, s3, v_hi, v_low):
    step = pl.program_id(0)
    r_row = clip_sums(z_ref)
    slot = OWN * NY

    @pl.when(step == 0)
    def _():
        inverse = jnp.broadcast_to(1.0 / column_of(r_row, CLIPS_DEV), (CLIPS_DEV, WIDTH))
        for f in range(FRAMES):
            at = pl.ds(f * CLIPS_DEV, CLIPS_DEV)
            scaled = v_ref[at, :].astype(F32) * inverse
            hi = scaled.astype(BF16)
            v_hi[at, :] = hi
            v_low[at, :] = (scaled - hi.astype(F32)).astype(BF16)
        lane = iota((1, LANES), 1)
        r_real = jnp.where(lane < CLIPS_DEV, r_row[0:1], 1.0)
        logs = jnp.where(lane < CLIPS_DEV, jnp.log(r_real), 0.0)
        logs = logs - jnp.where(lane == CLIPS_DEV, 2.0 * r_row[0:1], 0.0)
        total = pieces(jnp.sum(logs, axis=1, keepdims=True))
        at = pl.ds(GLOSSES * slot, EXTRA)
        s0[at, :] = total
        for out in (s1, s2, s3):
            out[at, :] = total.astype(BF16)

    c_row = text_sums(q0, q1, q2, q3)
    inverse = jnp.where(c_row > 0.0, 1.0 / c_row, 0.0)
    col = jnp.broadcast_to(column_of(inverse, LANES), (LANES, WIDTH))
    part = tn(p_ref[0], v_hi[...]) + tn(p_ref[0], v_low[...])
    part = part + ag_ref[...] * jnp.concatenate([col, col], axis=0)
    at = pl.ds(pl.multiple_of(step * 2 * slot, 2 * slot), 2 * slot)
    for s, out in enumerate((s0, s1, s2, s3)):
        both = [part[g * LANES + s * slot : g * LANES + (s + 1) * slot] for g in range(2)]
        out[at, :] = jnp.concatenate(both, axis=0).astype(out.dtype)


def spread_kernel(rows, peers, *refs):
    mine, others, out, scr = refs[0], refs[1:-2], refs[-2], refs[-1]
    height = rows + EXTRA

    def block(at, n):
        total = mine[pl.ds(at, n), :]
        for other in others:
            total = total + other[pl.ds(at, n), :].astype(F32)
        return total

    step = 2 * peers
    for i in range(rows // 2):
        two = block(i * step, step)
        for k in range(2):
            put(scr, pl.ds(2 * i + k, peers, stride=height), two[k * peers : (k + 1) * peers])
    tail = mine[pl.ds(rows * peers, EXTRA), :]
    value = unpiece(tail)
    for other in others:
        value = value + unpiece(other[pl.ds(rows * peers, EXTRA), :].astype(F32))
    extra = pieces(value)
    for i in range(peers):
        put(scr, pl.ds(i * height + rows, EXTRA), extra)
    out[...] = get(scr, pl.ds(0, peers * height)).astype(BF16).reshape(peers, height, WIDTH)


def token_grads(total, scr, raw, out, tokens):
    put(scr, pl.ds(0, OWN * tokens), total)
    for c in range(OWN):
        x = raw[c].astype(F32)
        d = get(scr, pl.ds(c, tokens, stride=OWN))
        mean_sq = jnp.mean(x * x, axis=-1, keepdims=True) + EPSILON
        factor = lax.rsqrt(mean_sq) / math.sqrt(WIDTH)
        inner = jnp.sum(d * x, axis=-1, keepdims=True)
        out[c] = factor * d - factor * x * (inner / (WIDTH * mean_sq))


def summed(ref, rows):
    total = ref[0].astype(F32)
    for i in range(1, ref.shape[0]):
        total = total + ref[i].astype(F32)
    return total[:rows], unpiece(total[rows:])


def video_grad_kernel(got, diag, video, out, logs, scr):
    total, value = summed(got, VOWN)
    token_grads(total + diag[...], scr, video, out, FRAMES)
    logs[...] = jnp.broadcast_to(value, (8, LANES))


def gloss_grad_kernel(clips, got, diag, gloss, logs, out, loss, scr):
    total, value = summed(got, GOWN)
    token_grads(total + diag[...], scr, gloss, out, GLOSSES)
    loss[...] = (value + logs[0:1, 0:1]) * (0.5 / clips)


def shape(*dims, dtype=F32):
    return jax.ShapeDtypeStruct(dims, dtype)


def on_device(clips, video, gloss, frame_count, gloss_count):
    vmem, smem = pl.BlockSpec(memory_space=pltpu.VMEM), pl.BlockSpec(memory_space=pltpu.SMEM)
    core_pairs = [(i, i ^ 1) for i in range(NX // 2 * NY * NCORE)]

    def x_shift(s):
        pairs = []
        for x in range(NX):
            for z in range(NZ):
                for rest in range(NY * NCORE):
                    flat = [((a % 2) * NZ + z) * 32 + (a // 2) * 16 + rest for a in (x, (x + s) % NX)]
                    pairs.append((flat[0], flat[1]))
        return sorted(pairs)

    def to_core(a):
        return lax.ppermute(a, "inner", core_pairs)

    def to_x(a, s):
        return lax.ppermute(a, ("outer", "inner"), x_shift(s % NX))

    def over_y(a):
        return lax.all_to_all(a, "inner", 0, 0, axis_index_groups=Y_GROUPS, tiled=True)

    def over_z(a):
        return lax.all_to_all(a, "outer", 0, 0, axis_index_groups=Z_GROUPS, tiled=True)

    with jax.named_scope("unit_tokens"):
        v_own, g_own = pl.pallas_call(
            units_kernel,
            in_specs=[smem, smem, vmem, vmem],
            out_shape=(shape(NZ, VOWN, WIDTH, dtype=BF16), shape(NY, GOWN, WIDTH, dtype=BF16)),
            scratch_shapes=[two_halves(VOWN), two_halves(GOWN)],
            compiler_params=params(),
            cost_estimate=cost(2e5, 7e5),
        )(frame_count, gloss_count, video, gloss)

    with jax.named_scope("gather"):
        g_mine = over_y(g_own)
        g_parts = [g_mine] + [to_x(g_mine, s) for s in range(1, NX)]
        v_mine = over_z(v_own)
        v_twin = to_core(v_mine)

    def first(rows):
        return pl.BlockSpec((1, rows, WIDTH), lambda i: (0, 0, 0))

    def whole(*dims):
        return pl.BlockSpec(dims, lambda i: (0,) * len(dims))

    with jax.named_scope("diagonal"):
        dv_diag, dg_diag, logit_sum = pl.pallas_call(
            diagonal_kernel,
            grid=(1,),
            in_specs=[smem, smem, first(VOWN), first(GOWN)],
            out_specs=(whole(VOWN, WIDTH), whole(GOWN, WIDTH), whole(8, LANES)),
            out_shape=(shape(VOWN, WIDTH), shape(GOWN, WIDTH), shape(8, LANES)),
            compiler_params=params(),
            cost_estimate=cost(2e7, 3e5),
        )(frame_count, gloss_count, v_own, g_own)

    with jax.named_scope("forward"):
        v_all, g_all, row_inv, col_inv, e_pair, r_mine, r_twin, c_part = pl.pallas_call(
            forward_kernel,
            in_specs=[vmem] * 7,
            out_shape=(
                shape(VROWS, WIDTH, dtype=BF16),
                shape(GROWS, WIDTH, dtype=BF16),
                shape(VROWS, LANES),
                shape(GLOSSES, CLIPS_DEV, LANES),
                shape(CLIPS_DEV, LANES),
                shape(8, LANES),
                shape(8, LANES),
                shape(NY, 8, LANES),
            ),
            scratch_shapes=[
                pltpu.VMEM((NCORE, 2, NZ * VOWN, LANES), F32),
                pltpu.VMEM((NX, 2, NY * GOWN, LANES), F32),
                pltpu.VMEM((VROWS, LANES), F32),
                pltpu.VMEM((GLOSSES, 8, LANES), F32),
                pltpu.VMEM((VROWS, LANES), F32),
                pltpu.VMEM((GLOSSES, CLIPS_DEV, LANES), F32),
            ],
            compiler_params=params(),
            cost_estimate=cost(2 * VROWS * GROWS * WIDTH, 8e6, VROWS * GROWS),
        )(v_mine, v_twin, *g_parts, logit_sum)

    with jax.named_scope("batch_sums"):
        c_mine = jnp.sum(over_y(c_part), axis=0)
        c_parts = [c_mine] + [to_x(c_mine, s) for s in range(1, NX)]
        r_pair = r_mine + to_core(r_twin)
        r_got = over_z(jnp.broadcast_to(r_pair[None], (NZ, 8, LANES)))

    def halves(rows):
        return pl.BlockSpec((rows, WIDTH), lambda i: (i, 0))

    p_spec = pl.BlockSpec((1, VROWS, WIDTH), lambda i: (i, 0, 0))
    with jax.named_scope("weights"):
        weights, av, ag = pl.pallas_call(
            weights_kernel,
            grid=(PAIRS,),
            in_specs=[
                whole(VROWS, WIDTH),
                halves(2 * LANES),
                whole(VROWS, LANES),
                pl.BlockSpec((2, CLIPS_DEV, LANES), lambda i: (i, 0, 0)),
                whole(CLIPS_DEV, LANES),
            ],
            out_specs=(p_spec, whole(VROWS, WIDTH), halves(2 * LANES)),
            out_shape=(shape(PAIRS, VROWS, WIDTH, dtype=BF16), shape(VROWS, WIDTH), shape(GROWS, WIDTH)),
            compiler_params=params(),
            cost_estimate=cost(6 * VROWS * GROWS * WIDTH, 16e6, VROWS * GROWS),
        )(v_all, g_all, row_inv, col_inv, e_pair)

    part_spec = whole(8, LANES)
    with jax.named_scope("by_text"):
        bv = pl.pallas_call(
            by_text_kernel,
            grid=(PAIRS,),
            in_specs=[part_spec] * 4 + [p_spec, halves(2 * LANES)],
            out_specs=whole(VROWS, WIDTH),
            out_shape=shape(VROWS, WIDTH),
            compiler_params=params(),
            cost_estimate=cost(4 * VROWS * GROWS * WIDTH, 9e6),
        )(*c_parts, weights, g_all)

    with jax.named_scope("video_partial"):
        v_rows = FRAMES * CLIPS_DEV // 2 + EXTRA
        dv_mine, dv_twin = pl.pallas_call(
            video_partial_kernel,
            in_specs=[vmem] * 7,
            out_shape=(shape(v_rows, WIDTH), shape(v_rows, WIDTH, dtype=BF16)),
            compiler_params=params(),
            cost_estimate=cost(2e6, 5e6),
        )(r_got, *c_parts, av, bv)
    with jax.named_scope("video_to_owner"):
        dv_got = to_core(dv_twin)
        dv_send = pl.pallas_call(
            functools.partial(spread_kernel, VOWN, NZ),
            in_specs=[vmem] * 2,
            out_shape=shape(NZ, VOWN + EXTRA, WIDTH, dtype=BF16),
            scratch_shapes=[two_halves(NZ * (VOWN + EXTRA))],
            compiler_params=params(),
            cost_estimate=cost(1e6, 2e6),
        )(dv_mine, dv_got)
        dv_parts = over_z(dv_send)

    with jax.named_scope("gloss_partial"):
        g_rows = GLOSSES * OWN * NY + EXTRA
        dg_slots = pl.pallas_call(
            gloss_partial_kernel,
            grid=(PAIRS,),
            in_specs=[whole(NZ, 8, LANES)] + [part_spec] * 4 + [p_spec, whole(VROWS, WIDTH), halves(2 * LANES)],
            out_specs=(whole(g_rows, WIDTH),) * NX,
            out_shape=(shape(g_rows, WIDTH),) + (shape(g_rows, WIDTH, dtype=BF16),) * (NX - 1),
            scratch_shapes=[pltpu.VMEM((VROWS, WIDTH), BF16), pltpu.VMEM((VROWS, WIDTH), BF16)],
            compiler_params=params(),
            cost_estimate=cost(4 * VROWS * GROWS * WIDTH, 9e6),
        )(r_got, *c_parts, weights, v_all, ag)
    with jax.named_scope("gloss_to_owner"):
        dg_got = [to_x(dg_slots[s], -s) for s in range(1, NX)]
        dg_send = pl.pallas_call(
            functools.partial(spread_kernel, GOWN, NY),
            in_specs=[vmem] * NX,
            out_shape=shape(NY, GOWN + EXTRA, WIDTH, dtype=BF16),
            scratch_shapes=[two_halves(NY * (GOWN + EXTRA))],
            compiler_params=params(),
            cost_estimate=cost(1e6, 2e6),
        )(dg_slots[0], *dg_got)
        dg_parts = over_y(dg_send)

    with jax.named_scope("video_grad"):
        grad_video, logs = pl.pallas_call(
            video_grad_kernel,
            in_specs=[vmem] * 3,
            out_shape=(shape(OWN, FRAMES, WIDTH), shape(8, LANES)),
            scratch_shapes=[two_halves(VOWN)],
            compiler_params=params(),
            cost_estimate=cost(1e6, 1e6),
        )(dv_parts, dv_diag, video)
    with jax.named_scope("gloss_grad"):
        grad_gloss, loss = pl.pallas_call(
            functools.partial(gloss_grad_kernel, clips),
            in_specs=[vmem] * 4,
            out_shape=(shape(OWN, GLOSSES, WIDTH), shape(1, 1)),
            scratch_shapes=[two_halves(GOWN)],
            compiler_params=params(),
            cost_estimate=cost(1e6, 1e6),
        )(dg_parts, dg_diag, gloss, logs)
    return loss.reshape(()), grad_video, grad_gloss


def solution(mesh):
    clips = OWN * mesh.shape["outer"] * mesh.shape["inner"]
    over_all = ("outer", "inner")
    tokens, counts = P(over_all, None, None), P(over_all)
    return jax.shard_map(
        functools.partial(on_device, clips),
        mesh=mesh,
        in_specs=(tokens, tokens, counts, counts),
        out_specs=(P(), tokens, tokens),
        check_vma=False,
    )
```

```python
import functools
import math

import jax
import jax.numpy as jnp
from jax import lax
from jax.experimental import pallas as pl
from jax.experimental.pallas import tpu as pltpu
from jax.sharding import PartitionSpec as P

F32 = jnp.float32
BF16 = jnp.bfloat16
EPSILON = 1e-06
EXP_SCALE = 10.0 * math.log2(math.e)
MARK = 2.0
MARK_LIMIT = 1.5
FAR = -1e30

NZ, NY, NX, NCORE = 8, 8, 4, 2
OWN = 3
FRAMES, GLOSSES, WIDTH = 32, 16, 256
CLIPS_DEV = NZ * NCORE * OWN
TEXTS_DEV = NY * NX * OWN
LANES = 128
VROWS = FRAMES * CLIPS_DEV
GROWS = GLOSSES * LANES
VOWN = FRAMES * OWN
GOWN = GLOSSES * OWN
SLOT = OWN * NY
EXTRA = 16
PAIRS = GLOSSES // 2

Z_GROUPS = [[h * NZ + i for i in range(NZ)] for h in range(2)]
Y_GROUPS = [[h * 16 + 2 * i + c for i in range(NY)] for h in range(2) for c in range(NCORE)]


def flat(x, z, y, core):
    return ((x % 2) * NZ + z) * 32 + (x // 2) * 16 + 2 * y + core


XY_GROUPS = [[flat(x, z, y, c) for x in range(NX) for y in range(NY)] for z in range(NZ) for c in range(NCORE)]
ZC_GROUPS = [[flat(x, z, y, c) for c in range(NCORE) for z in range(NZ)] for x in range(NX) for y in range(NY)]


def params(limit_mb=16):
    return pltpu.CompilerParams(vmem_limit_bytes=limit_mb * 1024 * 1024)


def cost(flops, nbytes, trans=0):
    return pl.CostEstimate(flops=int(flops), bytes_accessed=int(nbytes), transcendentals=int(trans))


def iota(shape, dim):
    return lax.broadcasted_iota(jnp.int32, shape, dim)


def nt(a, b, **kw):
    return lax.dot_general(a, b, (((1,), (1,)), ((), ())), preferred_element_type=F32, **kw)


def nn(a, b, **kw):
    return lax.dot_general(a, b, (((1,), (0,)), ((), ())), preferred_element_type=F32, **kw)


def tn(a, b, **kw):
    return lax.dot_general(a, b, (((0,), (0,)), ((), ())), preferred_element_type=F32, **kw)


def column_of(row, n):
    eye = iota((n, LANES), 0) == iota((n, LANES), 1)
    return jnp.sum(jnp.where(eye, jnp.broadcast_to(row[0:1], (n, LANES)), 0.0), axis=1, keepdims=True)


def pieces(value):
    lane = iota((EXTRA, WIDTH), 1)
    full = jnp.broadcast_to(value, (EXTRA, WIDTH))
    hi = full.astype(BF16).astype(F32)
    mid = (full - hi).astype(BF16).astype(F32)
    low = full - hi - mid
    return jnp.where(lane == 0, hi, jnp.where(lane == 1, mid, jnp.where(lane == 2, low, 0.0)))


def unpiece(block):
    mine = (iota((EXTRA, WIDTH), 0) == 0) & (iota((EXTRA, WIDTH), 1) < 3)
    return jnp.sum(jnp.where(mine, block, 0.0), keepdims=True).reshape(1, 1)


def put(ref, at, value):
    ref[0, at, :] = value[:, :LANES]
    ref[1, at, :] = value[:, LANES:]


def get(ref, at):
    return jnp.concatenate([ref[0, at, :], ref[1, at, :]], axis=1)


def two_halves(rows):
    return pltpu.VMEM((2, rows, LANES), F32)


def units_kernel(fc_in, gc_in, video_in, gloss_in, v_out, g_out, count_out, fc, gc, video, gloss, v_scr, g_scr, sems):
    pairs = ((fc_in, fc), (gc_in, gc), (video_in, video), (gloss_in, gloss))
    copies = [pltpu.make_async_copy(a, b, sems.at[i]) for i, (a, b) in enumerate(pairs)]
    for copy in copies:
        copy.start()
    for copy in copies:
        copy.wait()
    row = iota((8, LANES), 0)
    counts = jnp.zeros((8, LANES), jnp.int32)
    for c in range(OWN):
        counts = jnp.where(row == c, fc[c], jnp.where(row == OWN + c, gc[c], counts))
    count_out[...] = counts
    for count, raw, scr, tokens in ((fc, video, v_scr, FRAMES), (gc, gloss, g_scr, GLOSSES)):
        row, lane = iota((tokens, WIDTH), 0), iota((tokens, WIDTH), 1)
        for c in range(OWN):
            x = raw[c].astype(F32)
            mean_sq = jnp.mean(x * x, axis=-1, keepdims=True) + EPSILON
            unit = x * (lax.rsqrt(mean_sq) / math.sqrt(WIDTH))
            mark = jnp.where(lane == 0, MARK, 0.0)
            put(scr, pl.ds(c, tokens, stride=OWN), jnp.where(row < count[c], unit, mark))
    v = get(v_scr, pl.ds(0, VOWN)).astype(BF16)
    g = get(g_scr, pl.ds(0, GOWN)).astype(BF16)
    for i in range(NZ):
        v_out[i] = v
    for i in range(NY):
        g_out[i] = g


def diagonal_kernel(count_ref, v_ref, g_ref, dv, dg, logit_sum):
    def pick(count, which):
        return jnp.where(which == 0, count[0], jnp.where(which == 1, count[1], count[2]))

    fc = [count_ref[c : c + 1, 0:1] for c in range(OWN)]
    gc = [count_ref[OWN + c : OWN + c + 1, 0:1] for c in range(OWN)]
    v, g = v_ref[0], g_ref[0]
    shape = (VOWN, GOWN)
    r, q = iota(shape, 0), iota(shape, 1)
    rc, qc = lax.rem(r, OWN), lax.rem(q, OWN)
    valid = (rc == qc) & (lax.div(r, OWN) < pick(fc, rc)) & (lax.div(q, OWN) < pick(gc, qc))
    e = jnp.where(valid, jnp.exp2(nt(v, g) * EXP_SCALE), 0.0)
    r1, q1 = iota((VOWN, 1), 0), iota((1, GOWN), 1)
    rc1, qc1 = lax.rem(r1, OWN), lax.rem(q1, OWN)
    frames_r, glosses_r = pick(fc, rc1), pick(gc, rc1)
    frames_q, glosses_q = pick(fc, qc1), pick(gc, qc1)
    row_ok = lax.div(r1, OWN) < frames_r
    col_ok = lax.div(q1, OWN) < glosses_q
    frames_r, glosses_r = frames_r.astype(F32), glosses_r.astype(F32)
    frames_q, glosses_q = frames_q.astype(F32), glosses_q.astype(F32)
    rows = jnp.where(row_ok, jnp.sum(e, axis=1, keepdims=True), 1.0)
    cols = jnp.where(col_ok, jnp.sum(e, axis=0, keepdims=True), 1.0)
    by_row = jnp.where(row_ok, jnp.log(rows / glosses_r) / frames_r, 0.0)
    by_col = jnp.where(col_ok, jnp.log(cols / frames_q) / glosses_q, 0.0)
    total = jnp.sum(by_row, axis=0, keepdims=True) + jnp.sum(by_col, axis=1, keepdims=True)
    logit_sum[...] = jnp.broadcast_to(0.5 * total, (8, LANES))
    weight = -5.0 * e * (1.0 / (rows * frames_r) + 1.0 / (cols * glosses_q))
    dv[...] = nn(weight, g.astype(F32), precision=lax.Precision.HIGHEST)
    dg[...] = tn(weight, v.astype(F32), precision=lax.Precision.HIGHEST)


def exp_scores(v, g):
    return jnp.exp2(nt(v, g) * EXP_SCALE)


def forward_kernel(
    v_mine, v_twin, g0, g1, g2, g3, diag,
    v_out, g_out, row_out, col_out, e_out, r_out, c_out,
    v_scr, g_scr, frame_mask, gloss_mask, rows, cols,
):
    for t, ref in enumerate((v_mine, v_twin)):
        put(v_scr.at[t], pl.ds(0, NZ * VOWN), ref[...].reshape(NZ * VOWN, WIDTH).astype(F32))
    for f in range(FRAMES):
        parts = [get(v_scr.at[t], pl.ds(f * OWN + c, NZ, stride=VOWN)) for t in range(NCORE) for c in range(OWN)]
        v_out[pl.ds(f * CLIPS_DEV, CLIPS_DEV), :] = jnp.concatenate(parts, axis=0).astype(BF16)
    for s, ref in enumerate((g0, g1, g2, g3)):
        put(g_scr.at[s], pl.ds(0, NY * GOWN), ref[...].reshape(NY * GOWN, WIDTH).astype(F32))
    pad = jnp.where(iota((LANES - TEXTS_DEV, WIDTH), 1) == 0, MARK, 0.0)
    for g in range(GLOSSES):
        parts = [get(g_scr.at[s], pl.ds(g * OWN + c, NY, stride=GOWN)) for s in range(NX) for c in range(OWN)]
        g_out[pl.ds(g * LANES, LANES), :] = jnp.concatenate(parts + [pad], axis=0).astype(BF16)

    first = jnp.where(iota((WIDTH, LANES), 0) == 0, 1.0, 0.0).astype(BF16)
    frame_mask[...] = jnp.where(nn(v_out[...], first) < MARK_LIMIT, 1.0, 0.0)
    first_row = jnp.where(iota((16, WIDTH), 1) == 0, 1.0, 0.0).astype(BF16)
    for g in range(GLOSSES):
        gloss_mask[g] = jnp.where(nt(first_row, g_out[pl.ds(g * LANES, LANES), :])[0:8] < MARK_LIMIT, 1.0, 0.0)
    frames = jnp.zeros((CLIPS_DEV, LANES), F32)
    for f in range(FRAMES):
        frames = frames + frame_mask[pl.ds(f * CLIPS_DEV, CLIPS_DEV), :]
    glosses = gloss_mask[0]
    for g in range(1, GLOSSES):
        glosses = glosses + gloss_mask[g]
    glosses = jnp.maximum(glosses, 1.0)[0:1]

    rows[...] = jnp.zeros_like(rows)

    def two_glosses(p, _):
        e = exp_scores(v_out[...], g_out[pl.ds(pl.multiple_of(p * WIDTH, WIDTH), WIDTH), :])
        m0, m1 = gloss_mask[2 * p][0:1], gloss_mask[2 * p + 1][0:1]
        col0 = jnp.zeros((CLIPS_DEV, LANES), F32)
        col1 = jnp.zeros((CLIPS_DEV, LANES), F32)
        for f in range(FRAMES):
            at = pl.ds(f * CLIPS_DEV, CLIPS_DEV)
            block = e[f * CLIPS_DEV : (f + 1) * CLIPS_DEV]
            e0, e1 = block[:, :LANES], block[:, LANES:]
            mask = frame_mask[at, :]
            rows[at, :] = rows[at, :] + (e0 * m0 + e1 * m1)
            col0 = col0 + e0 * mask
            col1 = col1 + e1 * mask
        cols[2 * p] = col0
        cols[2 * p + 1] = col1
        return 0

    lax.fori_loop(0, PAIRS, two_glosses, 0)

    lane = iota((CLIPS_DEV, LANES), 1)
    real = lane < TEXTS_DEV
    video_part = jnp.zeros((CLIPS_DEV, LANES), F32)
    for f in range(FRAMES):
        at = pl.ds(f * CLIPS_DEV, CLIPS_DEV)
        mask = frame_mask[at, :]
        total = jnp.where(real, rows[at, :], 1.0)
        video_part = video_part + mask * jnp.log(total / glosses)
        row_out[at, :] = jnp.where(mask > 0.0, 1.0 / (total * frames), FAR)
    gloss_part = jnp.zeros((CLIPS_DEV, LANES), F32)
    for g in range(GLOSSES):
        mask = gloss_mask[g][0:1]
        total = cols[g]
        gloss_part = gloss_part + mask * jnp.log(total / frames)
        col_out[g] = jnp.where(mask > 0.0, 1.0 / (total * glosses), FAR)
    logits = 0.5 * (video_part / frames + gloss_part / glosses)
    e_pair = jnp.where(real, jnp.exp(logits), 0.0)
    e_out[...] = e_pair

    sums = jnp.sum(e_pair, axis=1, keepdims=True)
    clip = iota((CLIPS_DEV, LANES), 0)
    half = CLIPS_DEV // 2
    swapped = jnp.where(clip < half, clip + half, clip - half)
    spread = jnp.broadcast_to(sums, (CLIPS_DEV, LANES))
    row_mine = jnp.sum(jnp.where(lane == clip, spread, 0.0), axis=0, keepdims=True)
    row_twin = jnp.sum(jnp.where(lane == swapped, spread, 0.0), axis=0, keepdims=True)
    row8, lane8 = iota((8, LANES), 0), iota((8, LANES), 1)
    r_rows = jnp.where(row8 == 1, row_twin, row_mine)
    r_rows = jnp.where(lane8 == CLIPS_DEV, diag[...], r_rows)
    for i in range(NZ * NCORE):
        r_out[i] = r_rows
    c_row = jnp.broadcast_to(jnp.sum(e_pair, axis=0, keepdims=True), (8, LANES))
    c_rows = c_row
    for s in range(1, NX):
        ahead = pltpu.roll(c_row, SLOT * s, 1)
        behind = pltpu.roll(c_row, (SLOT * s - TEXTS_DEV) % LANES, 1)
        c_rows = jnp.where(row8 == s, jnp.where(lane8 < SLOT * s, behind, ahead), c_rows)
    for i in range(NX * NY):
        c_out[i] = c_rows


def weights_kernel(v_ref, g_ref, row_ref, col_ref, e_ref, p_out, av_out, ag_out):
    p = pl.program_id(0)
    e = exp_scores(v_ref[...], g_ref[...])
    scale = 2.5 * e_ref[...]
    col0, col1 = col_ref[0], col_ref[1]
    for f in range(FRAMES):
        at = pl.ds(f * CLIPS_DEV, CLIPS_DEV)
        block = e[f * CLIPS_DEV : (f + 1) * CLIPS_DEV]
        row = row_ref[at, :]
        w0 = scale * block[:, :LANES] * jnp.maximum(row + col0, 0.0)
        w1 = scale * block[:, LANES:] * jnp.maximum(row + col1, 0.0)
        p_out[0, at, :] = jnp.concatenate([w0, w1], axis=1).astype(BF16)
    weights = p_out[0]
    part = nn(weights, g_ref[...])

    @pl.when(p == 0)
    def _():
        av_out[...] = part

    @pl.when(p > 0)
    def _():
        av_out[...] = av_out[...] + part

    ag_out[...] = tn(weights, v_ref[...])


def text_sums(got):
    x = 2 * lax.div(lax.axis_index("inner"), 16) + lax.div(lax.axis_index("outer"), NZ)
    total = jnp.zeros((1, LANES), F32)
    for s in range(NX):
        base = lax.rem(x - s + NX, NX) * NY
        part = got[base]
        for i in range(1, NY):
            part = part + got[base + i]
        total = total + part[s : s + 1]
    return jnp.where(iota((1, LANES), 1) < TEXTS_DEV, total, 0.0)


def by_text_kernel(got, p_ref, g_ref, out, c_out):
    step = pl.program_id(0)

    @pl.when(step == 0)
    def _():
        c_out[...] = jnp.broadcast_to(text_sums(got), (8, LANES))

    c_row = c_out[...]
    inverse = jnp.where(c_row > 0.0, 1.0 / c_row, 0.0)
    col = jnp.broadcast_to(column_of(inverse, LANES), (LANES, WIDTH))
    scaled = g_ref[...].astype(F32) * jnp.concatenate([col, col], axis=0)
    hi = scaled.astype(BF16)
    low = (scaled - hi.astype(F32)).astype(BF16)
    part = nn(p_ref[0], hi) + nn(p_ref[0], low)

    @pl.when(step == 0)
    def _():
        out[...] = part

    @pl.when(step > 0)
    def _():
        out[...] = out[...] + part


def clip_sums(got):
    core = lax.rem(lax.axis_index("inner"), NCORE)
    total = jnp.zeros((1, LANES), F32)
    for t in range(NCORE):
        base = lax.rem(core + t, NCORE) * NZ
        part = got[base]
        for i in range(1, NZ):
            part = part + got[base + i]
        total = total + part[t : t + 1]
    return jnp.broadcast_to(total, (8, LANES))


def video_partial_kernel(z_ref, c_ref, av_ref, bv_ref, mine, twin):
    r_row = clip_sums(z_ref)
    inverse = jnp.broadcast_to(1.0 / column_of(r_row, CLIPS_DEV), (CLIPS_DEV, WIDTH))
    half = CLIPS_DEV // 2
    for pair in range(FRAMES // 2):
        blocks = []
        for f in (2 * pair, 2 * pair + 1):
            at = pl.ds(f * CLIPS_DEV, CLIPS_DEV)
            block = av_ref[at, :] * inverse + bv_ref[at, :]
            mine[pl.ds(f * half, half), :] = block[:half]
            blocks.append(block[half:])
        twin[pl.ds(pair * CLIPS_DEV, CLIPS_DEV), :] = jnp.concatenate(blocks, axis=0).astype(BF16)
    c_row = c_ref[0:1]
    logs = jnp.where(iota((1, LANES), 1) < TEXTS_DEV, jnp.log(jnp.where(c_row > 0.0, c_row, 1.0)), 0.0)
    total = pieces(jnp.sum(logs, axis=1, keepdims=True))
    mine[pl.ds(FRAMES * half, EXTRA), :] = total
    twin[pl.ds(FRAMES * half, EXTRA), :] = total.astype(BF16)


def gloss_partial_kernel(z_ref, c_ref, p_ref, v_ref, ag_ref, s0, s1, s2, s3, v_hi, v_low):
    step = pl.program_id(0)
    slot = SLOT

    @pl.when(step == 0)
    def _():
        r_row = clip_sums(z_ref)
        inverse = jnp.broadcast_to(1.0 / column_of(r_row, CLIPS_DEV), (CLIPS_DEV, WIDTH))
        for f in range(FRAMES):
            at = pl.ds(f * CLIPS_DEV, CLIPS_DEV)
            scaled = v_ref[at, :].astype(F32) * inverse
            hi = scaled.astype(BF16)
            v_hi[at, :] = hi
            v_low[at, :] = (scaled - hi.astype(F32)).astype(BF16)
        lane = iota((1, LANES), 1)
        r_real = jnp.where(lane < CLIPS_DEV, r_row[0:1], 1.0)
        logs = jnp.where(lane < CLIPS_DEV, jnp.log(r_real), 0.0)
        logs = logs - jnp.where(lane == CLIPS_DEV, 2.0 * r_row[0:1], 0.0)
        total = pieces(jnp.sum(logs, axis=1, keepdims=True))
        at = pl.ds(GLOSSES * slot, EXTRA)
        s0[at, :] = total
        for out in (s1, s2, s3):
            out[at, :] = total.astype(BF16)

    c_row = c_ref[...]
    inverse = jnp.where(c_row > 0.0, 1.0 / c_row, 0.0)
    col = jnp.broadcast_to(column_of(inverse, LANES), (LANES, WIDTH))
    part = tn(p_ref[0], v_hi[...]) + tn(p_ref[0], v_low[...])
    part = part + ag_ref[...] * jnp.concatenate([col, col], axis=0)
    at = pl.ds(pl.multiple_of(step * 2 * slot, 2 * slot), 2 * slot)
    for s, out in enumerate((s0, s1, s2, s3)):
        both = [part[g * LANES + s * slot : g * LANES + (s + 1) * slot] for g in range(2)]
        out[at, :] = jnp.concatenate(both, axis=0).astype(out.dtype)


def spread_kernel(rows, peers, *refs):
    mine, others, out, scr = refs[0], refs[1:-2], refs[-2], refs[-1]
    height = rows + EXTRA

    def block(at, n):
        total = mine[pl.ds(at, n), :]
        for other in others:
            total = total + other[pl.ds(at, n), :].astype(F32)
        return total

    step = 2 * peers
    for i in range(rows // 2):
        two = block(i * step, step)
        for k in range(2):
            put(scr, pl.ds(2 * i + k, peers, stride=height), two[k * peers : (k + 1) * peers])
    tail = mine[pl.ds(rows * peers, EXTRA), :]
    value = unpiece(tail)
    for other in others:
        value = value + unpiece(other[pl.ds(rows * peers, EXTRA), :].astype(F32))
    extra = pieces(value)
    for i in range(peers):
        put(scr, pl.ds(i * height + rows, EXTRA), extra)
    out[...] = get(scr, pl.ds(0, peers * height)).astype(BF16).reshape(peers, height, WIDTH)


def token_grads(total, scr, raw, out, tokens):
    put(scr, pl.ds(0, OWN * tokens), total)
    for c in range(OWN):
        x = raw[c].astype(F32)
        d = get(scr, pl.ds(c, tokens, stride=OWN))
        mean_sq = jnp.mean(x * x, axis=-1, keepdims=True) + EPSILON
        factor = lax.rsqrt(mean_sq) / math.sqrt(WIDTH)
        inner = jnp.sum(d * x, axis=-1, keepdims=True)
        out[c] = factor * d - factor * x * (inner / (WIDTH * mean_sq))


def summed(ref, rows):
    total = ref[0].astype(F32)
    for i in range(1, ref.shape[0]):
        total = total + ref[i].astype(F32)
    return total[:rows], unpiece(total[rows:])


def video_grad_kernel(got, diag, video, out, logs, scr):
    total, value = summed(got, VOWN)
    token_grads(total + diag[...], scr, video, out, FRAMES)
    logs[...] = jnp.broadcast_to(value, (8, LANES))


def gloss_grad_kernel(clips, got, diag, gloss, logs, out, loss, scr):
    total, value = summed(got, GOWN)
    token_grads(total + diag[...], scr, gloss, out, GLOSSES)
    loss[...] = (value + logs[0:1, 0:1]) * (0.5 / clips)


def shape(*dims, dtype=F32):
    return jax.ShapeDtypeStruct(dims, dtype)


def on_device(clips, video, gloss, frame_count, gloss_count):
    vmem = pl.BlockSpec(memory_space=pltpu.VMEM)
    core_pairs = [(i, i ^ 1) for i in range(NX // 2 * NY * NCORE)]

    def x_shift(s):
        pairs = []
        for x in range(NX):
            for z in range(NZ):
                for rest in range(NY * NCORE):
                    pairs.append((flat(x, z, 0, rest), flat((x + s) % NX, z, 0, rest)))
        return sorted(pairs)

    def to_core(a):
        return lax.ppermute(a, "inner", core_pairs)

    def to_x(a, s):
        return lax.ppermute(a, ("outer", "inner"), x_shift(s % NX))

    def over_y(a):
        return lax.all_to_all(a, "inner", 0, 0, axis_index_groups=Y_GROUPS, tiled=True)

    def over_z(a):
        return lax.all_to_all(a, "outer", 0, 0, axis_index_groups=Z_GROUPS, tiled=True)

    def over_groups(a, groups):
        return lax.all_to_all(a, ("outer", "inner"), 0, 0, axis_index_groups=groups, tiled=True)

    with jax.named_scope("unit_tokens"):
        v_own, g_own, counts = pl.pallas_call(
            units_kernel,
            in_specs=[pl.BlockSpec(memory_space=pltpu.HBM)] * 4,
            out_shape=(
                shape(NZ, VOWN, WIDTH, dtype=BF16),
                shape(NY, GOWN, WIDTH, dtype=BF16),
                shape(8, LANES, dtype=jnp.int32),
            ),
            scratch_shapes=[
                pltpu.SMEM((OWN,), jnp.int32),
                pltpu.SMEM((OWN,), jnp.int32),
                pltpu.VMEM((OWN, FRAMES, WIDTH), BF16),
                pltpu.VMEM((OWN, GLOSSES, WIDTH), BF16),
                two_halves(VOWN),
                two_halves(GOWN),
                pltpu.SemaphoreType.DMA((4,)),
            ],
            compiler_params=params(),
            cost_estimate=cost(2e5, 7e5),
        )(frame_count, gloss_count, video, gloss)

    with jax.named_scope("gather"):
        g_mine, v_ready = lax.optimization_barrier((over_y(g_own), v_own))
        g_parts = [g_mine] + [to_x(g_mine, s) for s in range(1, NX)]
        v_mine = over_z(v_ready)
        v_twin = to_core(v_mine)

    def first(rows):
        return pl.BlockSpec((1, rows, WIDTH), lambda i: (0, 0, 0))

    def whole(*dims):
        return pl.BlockSpec(dims, lambda i: (0,) * len(dims))

    with jax.named_scope("diagonal"):
        dv_diag, dg_diag, logit_sum = pl.pallas_call(
            diagonal_kernel,
            grid=(1,),
            in_specs=[whole(8, LANES), first(VOWN), first(GOWN)],
            out_specs=(whole(VOWN, WIDTH), whole(GOWN, WIDTH), whole(8, LANES)),
            out_shape=(shape(VOWN, WIDTH), shape(GOWN, WIDTH), shape(8, LANES)),
            compiler_params=params(),
            cost_estimate=cost(2e7, 3e5),
        )(counts, v_own, g_own)

    with jax.named_scope("forward"):
        v_all, g_all, row_inv, col_inv, e_pair, r_part, c_part = pl.pallas_call(
            forward_kernel,
            in_specs=[vmem] * 7,
            out_shape=(
                shape(VROWS, WIDTH, dtype=BF16),
                shape(GROWS, WIDTH, dtype=BF16),
                shape(VROWS, LANES),
                shape(GLOSSES, CLIPS_DEV, LANES),
                shape(CLIPS_DEV, LANES),
                shape(NZ * NCORE, 8, LANES),
                shape(NX * NY, 8, LANES),
            ),
            scratch_shapes=[
                pltpu.VMEM((NCORE, 2, NZ * VOWN, LANES), F32),
                pltpu.VMEM((NX, 2, NY * GOWN, LANES), F32),
                pltpu.VMEM((VROWS, LANES), F32),
                pltpu.VMEM((GLOSSES, 8, LANES), F32),
                pltpu.VMEM((VROWS, LANES), F32),
                pltpu.VMEM((GLOSSES, CLIPS_DEV, LANES), F32),
            ],
            compiler_params=params(),
            cost_estimate=cost(2 * VROWS * GROWS * WIDTH, 8e6, VROWS * GROWS),
        )(v_mine, v_twin, *g_parts, logit_sum)

    with jax.named_scope("batch_sums"):
        c_got, r_ready = lax.optimization_barrier((over_groups(c_part, XY_GROUPS), r_part))
        r_got = over_groups(r_ready, ZC_GROUPS)

    def halves(rows):
        return pl.BlockSpec((rows, WIDTH), lambda i: (i, 0))

    p_spec = pl.BlockSpec((1, VROWS, WIDTH), lambda i: (i, 0, 0))
    with jax.named_scope("weights"):
        weights, av, ag = pl.pallas_call(
            weights_kernel,
            grid=(PAIRS,),
            in_specs=[
                whole(VROWS, WIDTH),
                halves(2 * LANES),
                whole(VROWS, LANES),
                pl.BlockSpec((2, CLIPS_DEV, LANES), lambda i: (i, 0, 0)),
                whole(CLIPS_DEV, LANES),
            ],
            out_specs=(p_spec, whole(VROWS, WIDTH), halves(2 * LANES)),
            out_shape=(shape(PAIRS, VROWS, WIDTH, dtype=BF16), shape(VROWS, WIDTH), shape(GROWS, WIDTH)),
            compiler_params=params(),
            cost_estimate=cost(6 * VROWS * GROWS * WIDTH, 16e6, VROWS * GROWS),
        )(v_all, g_all, row_inv, col_inv, e_pair)

    with jax.named_scope("by_text"):
        bv, c_sums = pl.pallas_call(
            by_text_kernel,
            grid=(PAIRS,),
            in_specs=[whole(NX * NY, 8, LANES), p_spec, halves(2 * LANES)],
            out_specs=(whole(VROWS, WIDTH), whole(8, LANES)),
            out_shape=(shape(VROWS, WIDTH), shape(8, LANES)),
            compiler_params=params(),
            cost_estimate=cost(4 * VROWS * GROWS * WIDTH, 9e6),
        )(c_got, weights, g_all)

    with jax.named_scope("video_partial"):
        v_rows = FRAMES * CLIPS_DEV // 2 + EXTRA
        dv_mine, dv_twin = pl.pallas_call(
            video_partial_kernel,
            in_specs=[vmem] * 4,
            out_shape=(shape(v_rows, WIDTH), shape(v_rows, WIDTH, dtype=BF16)),
            compiler_params=params(),
            cost_estimate=cost(2e6, 5e6),
        )(r_got, c_sums, av, bv)
    with jax.named_scope("video_to_owner"):
        dv_got = to_core(dv_twin)
        dv_send = pl.pallas_call(
            functools.partial(spread_kernel, VOWN, NZ),
            in_specs=[vmem] * 2,
            out_shape=shape(NZ, VOWN + EXTRA, WIDTH, dtype=BF16),
            scratch_shapes=[two_halves(NZ * (VOWN + EXTRA))],
            compiler_params=params(),
            cost_estimate=cost(1e6, 2e6),
        )(dv_mine, dv_got)
        dv_parts = over_z(dv_send)

    with jax.named_scope("gloss_partial"):
        g_rows = GLOSSES * SLOT + EXTRA
        dg_slots = pl.pallas_call(
            gloss_partial_kernel,
            grid=(PAIRS,),
            in_specs=[whole(NZ * NCORE, 8, LANES), whole(8, LANES), p_spec, whole(VROWS, WIDTH), halves(2 * LANES)],
            out_specs=(whole(g_rows, WIDTH),) * NX,
            out_shape=(shape(g_rows, WIDTH),) + (shape(g_rows, WIDTH, dtype=BF16),) * (NX - 1),
            scratch_shapes=[pltpu.VMEM((VROWS, WIDTH), BF16), pltpu.VMEM((VROWS, WIDTH), BF16)],
            compiler_params=params(),
            cost_estimate=cost(4 * VROWS * GROWS * WIDTH, 9e6),
        )(r_got, c_sums, weights, v_all, ag)
    with jax.named_scope("gloss_to_owner"):
        dg_got = [to_x(dg_slots[s], -s) for s in range(1, NX)]
        dg_send = pl.pallas_call(
            functools.partial(spread_kernel, GOWN, NY),
            in_specs=[vmem] * NX,
            out_shape=shape(NY, GOWN + EXTRA, WIDTH, dtype=BF16),
            scratch_shapes=[two_halves(NY * (GOWN + EXTRA))],
            compiler_params=params(),
            cost_estimate=cost(1e6, 2e6),
        )(dg_slots[0], *dg_got)
        dg_parts = over_y(dg_send)

    with jax.named_scope("video_grad"):
        grad_video, logs = pl.pallas_call(
            video_grad_kernel,
            in_specs=[vmem] * 3,
            out_shape=(shape(OWN, FRAMES, WIDTH), shape(8, LANES)),
            scratch_shapes=[two_halves(VOWN)],
            compiler_params=params(),
            cost_estimate=cost(1e6, 1e6),
        )(dv_parts, dv_diag, video)
    with jax.named_scope("gloss_grad"):
        grad_gloss, loss = pl.pallas_call(
            functools.partial(gloss_grad_kernel, clips),
            in_specs=[vmem] * 4,
            out_shape=(shape(OWN, GLOSSES, WIDTH), shape(1, 1)),
            scratch_shapes=[two_halves(GOWN)],
            compiler_params=params(),
            cost_estimate=cost(1e6, 1e6),
        )(dg_parts, dg_diag, gloss, logs)
    return loss.reshape(()), grad_video, grad_gloss


def solution(mesh):
    clips = OWN * mesh.shape["outer"] * mesh.shape["inner"]
    over_all = ("outer", "inner")
    tokens, counts = P(over_all, None, None), P(over_all)
    return jax.shard_map(
        functools.partial(on_device, clips),
        mesh=mesh,
        in_specs=(tokens, tokens, counts, counts),
        out_specs=(P(), tokens, tokens),
        check_vma=False,
    )
```

```python
import functools
import math

import jax
import jax.numpy as jnp
from jax import lax
from jax.experimental import pallas as pl
from jax.experimental.pallas import tpu as pltpu
from jax.sharding import PartitionSpec as P

F32 = jnp.float32
BF16 = jnp.bfloat16
EPSILON = 1e-06
EXP_SCALE = 10.0 * math.log2(math.e)
MARK = 2.0
MARK_LIMIT = 1.5
FAR = -1e30

NZ, NY, NX, NCORE = 8, 8, 4, 2
OWN = 3
FRAMES, GLOSSES, WIDTH = 32, 16, 256
CLIPS_DEV = NZ * NCORE * OWN
TEXTS_DEV = NY * NX * OWN
LANES = 128
VROWS = FRAMES * CLIPS_DEV
GROWS = GLOSSES * LANES
VOWN = FRAMES * OWN
GOWN = GLOSSES * OWN
EXTRA = 16
PAIRS = GLOSSES // 2
QUADS = GLOSSES // 4
NXY, NZC = NX * NY, NZ * NCORE
CHUNK = VOWN + EXTRA


def flat(x, z, y, core):
    return ((x % 2) * NZ + z) * 32 + (x // 2) * 16 + 2 * y + core


Z_GROUPS = [[flat(x, z, y, c) for z in range(NZ)] for x in range(NX) for y in range(NY) for c in range(NCORE)]
CORE_GROUPS = [[flat(x, z, y, c) for c in range(NCORE)] for x in range(NX) for y in range(NY) for z in range(NZ)]
XY_GROUPS = [[flat(x, z, y, c) for x in range(NX) for y in range(NY)] for z in range(NZ) for c in range(NCORE)]
ZC_GROUPS = [[flat(x, z, y, c) for c in range(NCORE) for z in range(NZ)] for x in range(NX) for y in range(NY)]


def params(limit_mb=16):
    return pltpu.CompilerParams(vmem_limit_bytes=limit_mb * 1024 * 1024)


def cost(flops, nbytes, trans=0):
    return pl.CostEstimate(flops=int(flops), bytes_accessed=int(nbytes), transcendentals=int(trans))


def iota(shape, dim):
    return lax.broadcasted_iota(jnp.int32, shape, dim)


def nt(a, b, **kw):
    return lax.dot_general(a, b, (((1,), (1,)), ((), ())), preferred_element_type=F32, **kw)


def nn(a, b, **kw):
    return lax.dot_general(a, b, (((1,), (0,)), ((), ())), preferred_element_type=F32, **kw)


def tn(a, b, **kw):
    return lax.dot_general(a, b, (((0,), (0,)), ((), ())), preferred_element_type=F32, **kw)


def column_of(row, n):
    eye = iota((n, LANES), 0) == iota((n, LANES), 1)
    return jnp.sum(jnp.where(eye, jnp.broadcast_to(row[0:1], (n, LANES)), 0.0), axis=1, keepdims=True)


def pieces(value):
    lane = iota((EXTRA, WIDTH), 1)
    full = jnp.broadcast_to(value, (EXTRA, WIDTH))
    hi = full.astype(BF16).astype(F32)
    mid = (full - hi).astype(BF16).astype(F32)
    low = (full - hi - mid).astype(BF16).astype(F32)
    return jnp.where(lane == 0, hi, jnp.where(lane == 1, mid, jnp.where(lane == 2, low, 0.0)))


def unpiece(block):
    mine = (iota((EXTRA, WIDTH), 0) == 0) & (iota((EXTRA, WIDTH), 1) < 3)
    return jnp.sum(jnp.where(mine, block, 0.0), keepdims=True).reshape(1, 1)


def put(ref, at, value):
    ref[0, at, :] = value[:, :LANES]
    ref[1, at, :] = value[:, LANES:]


def get(ref, at):
    return jnp.concatenate([ref[0, at, :], ref[1, at, :]], axis=1)


def two_halves(rows):
    return pltpu.VMEM((2, rows, LANES), F32)


def units_kernel(fc_in, gc_in, video_in, gloss_in, v_out, g_out, count_out, fc, gc, video, gloss, v_scr, g_scr, sems):
    pairs = ((fc_in, fc), (gc_in, gc), (video_in, video), (gloss_in, gloss))
    copies = [pltpu.make_async_copy(a, b, sems.at[i]) for i, (a, b) in enumerate(pairs)]
    for copy in copies:
        copy.start()
    for copy in copies:
        copy.wait()
    row = iota((8, LANES), 0)
    counts = jnp.zeros((8, LANES), jnp.int32)
    for c in range(OWN):
        counts = jnp.where(row == c, fc[c], jnp.where(row == OWN + c, gc[c], counts))
    count_out[...] = counts
    for count, raw, scr, tokens in ((fc, video, v_scr, FRAMES), (gc, gloss, g_scr, GLOSSES)):
        row, lane = iota((tokens, WIDTH), 0), iota((tokens, WIDTH), 1)
        for c in range(OWN):
            x = raw[c].astype(F32)
            mean_sq = jnp.mean(x * x, axis=-1, keepdims=True) + EPSILON
            unit = x * (lax.rsqrt(mean_sq) / math.sqrt(WIDTH))
            mark = jnp.where(lane == 0, MARK, 0.0)
            put(scr, pl.ds(c, tokens, stride=OWN), jnp.where(row < count[c], unit, mark))
    v = get(v_scr, pl.ds(0, VOWN)).astype(BF16)
    g = get(g_scr, pl.ds(0, GOWN)).astype(BF16)
    v_out[...] = v
    for i in range(NXY):
        g_out[i] = g


def diagonal_kernel(count_ref, v_ref, g_ref, dv, dg, logit_sum):
    def pick(count, which):
        return jnp.where(which == 0, count[0], jnp.where(which == 1, count[1], count[2]))

    fc = [count_ref[c : c + 1, 0:1] for c in range(OWN)]
    gc = [count_ref[OWN + c : OWN + c + 1, 0:1] for c in range(OWN)]
    v, g = v_ref[...], g_ref[0]
    shape = (VOWN, GOWN)
    r, q = iota(shape, 0), iota(shape, 1)
    rc, qc = lax.rem(r, OWN), lax.rem(q, OWN)
    valid = (rc == qc) & (lax.div(r, OWN) < pick(fc, rc)) & (lax.div(q, OWN) < pick(gc, qc))
    e = jnp.where(valid, jnp.exp2(nt(v, g) * EXP_SCALE), 0.0)
    r1, q1 = iota((VOWN, 1), 0), iota((1, GOWN), 1)
    rc1, qc1 = lax.rem(r1, OWN), lax.rem(q1, OWN)
    frames_r, glosses_r = pick(fc, rc1), pick(gc, rc1)
    frames_q, glosses_q = pick(fc, qc1), pick(gc, qc1)
    row_ok = lax.div(r1, OWN) < frames_r
    col_ok = lax.div(q1, OWN) < glosses_q
    frames_r, glosses_r = frames_r.astype(F32), glosses_r.astype(F32)
    frames_q, glosses_q = frames_q.astype(F32), glosses_q.astype(F32)
    rows = jnp.where(row_ok, jnp.sum(e, axis=1, keepdims=True), 1.0)
    cols = jnp.where(col_ok, jnp.sum(e, axis=0, keepdims=True), 1.0)
    by_row = jnp.where(row_ok, jnp.log(rows / glosses_r) / frames_r, 0.0)
    by_col = jnp.where(col_ok, jnp.log(cols / frames_q) / glosses_q, 0.0)
    total = jnp.sum(by_row, axis=0, keepdims=True) + jnp.sum(by_col, axis=1, keepdims=True)
    logit_sum[...] = jnp.broadcast_to(0.5 * total, (8, LANES))
    weight = -5.0 * e * (1.0 / (rows * frames_r) + 1.0 / (cols * glosses_q))
    dv[...] = nn(weight, g.astype(F32), precision=lax.Precision.HIGHEST)
    dg[...] = tn(weight, v.astype(F32), precision=lax.Precision.HIGHEST)


def exp_scores(v, g):
    return jnp.exp2(nt(v, g) * EXP_SCALE)


def forward_kernel(
    v_got, g_got, diag,
    v_out, g_out, row_out, col_out, e_out, r_out, c_out,
    v_scr, g_scr, frame_mask, gloss_mask, rows, cols,
):
    put(v_scr, pl.ds(0, VROWS), v_got[...].astype(F32))
    for f in range(FRAMES):
        parts = [
            get(v_scr, pl.ds(k * NZ * VOWN + f * OWN + c, NZ, stride=VOWN)) for k in range(NCORE) for c in range(OWN)
        ]
        v_out[pl.ds(f * CLIPS_DEV, CLIPS_DEV), :] = jnp.concatenate(parts, axis=0).astype(BF16)
    put(g_scr, pl.ds(0, NXY * GOWN), g_got[...].reshape(NXY * GOWN, WIDTH).astype(F32))
    pad = jnp.where(iota((LANES - TEXTS_DEV, WIDTH), 1) == 0, MARK, 0.0)
    for g in range(GLOSSES):
        parts = [get(g_scr, pl.ds(x * NY * GOWN + g * OWN + c, NY, stride=GOWN)) for x in range(NX) for c in range(OWN)]
        g_out[pl.ds(g * LANES, LANES), :] = jnp.concatenate(parts + [pad], axis=0).astype(BF16)

    first = jnp.where(iota((WIDTH, LANES), 0) == 0, 1.0, 0.0).astype(BF16)
    frame_mask[...] = jnp.where(nn(v_out[...], first) < MARK_LIMIT, 1.0, 0.0)
    first_row = jnp.where(iota((16, WIDTH), 1) == 0, 1.0, 0.0).astype(BF16)
    for g in range(GLOSSES):
        gloss_mask[g] = jnp.where(nt(first_row, g_out[pl.ds(g * LANES, LANES), :])[0:8] < MARK_LIMIT, 1.0, 0.0)
    frames = jnp.zeros((CLIPS_DEV, LANES), F32)
    for f in range(FRAMES):
        frames = frames + frame_mask[pl.ds(f * CLIPS_DEV, CLIPS_DEV), :]
    glosses = gloss_mask[0]
    for g in range(1, GLOSSES):
        glosses = glosses + gloss_mask[g]
    glosses = jnp.maximum(glosses, 1.0)[0:1]

    rows[...] = jnp.zeros_like(rows)

    def two_glosses(p, _):
        e = exp_scores(v_out[...], g_out[pl.ds(pl.multiple_of(p * WIDTH, WIDTH), WIDTH), :])
        m0, m1 = gloss_mask[2 * p][0:1], gloss_mask[2 * p + 1][0:1]
        col0 = jnp.zeros((CLIPS_DEV, LANES), F32)
        col1 = jnp.zeros((CLIPS_DEV, LANES), F32)
        for f in range(FRAMES):
            at = pl.ds(f * CLIPS_DEV, CLIPS_DEV)
            block = e[f * CLIPS_DEV : (f + 1) * CLIPS_DEV]
            e0, e1 = block[:, :LANES], block[:, LANES:]
            mask = frame_mask[at, :]
            rows[at, :] = rows[at, :] + (e0 * m0 + e1 * m1)
            col0 = col0 + e0 * mask
            col1 = col1 + e1 * mask
        cols[2 * p] = col0
        cols[2 * p + 1] = col1
        return 0

    lax.fori_loop(0, PAIRS, two_glosses, 0)

    lane = iota((CLIPS_DEV, LANES), 1)
    real = lane < TEXTS_DEV
    video_part = jnp.zeros((CLIPS_DEV, LANES), F32)
    for f in range(FRAMES):
        at = pl.ds(f * CLIPS_DEV, CLIPS_DEV)
        mask = frame_mask[at, :]
        total = jnp.where(real, rows[at, :], 1.0)
        video_part = video_part + mask * jnp.log(total / glosses)
        row_out[at, :] = jnp.where(mask > 0.0, 1.0 / (total * frames), FAR)
    gloss_part = jnp.zeros((CLIPS_DEV, LANES), F32)
    for g in range(GLOSSES):
        mask = gloss_mask[g][0:1]
        total = cols[g]
        gloss_part = gloss_part + mask * jnp.log(total / frames)
        col_out[g] = jnp.where(mask > 0.0, 1.0 / (total * glosses), FAR)
    logits = 0.5 * (video_part / frames + gloss_part / glosses)
    e_pair = jnp.where(real, jnp.exp(logits), 0.0)
    e_out[...] = e_pair

    sums = jnp.sum(e_pair, axis=1, keepdims=True)
    across = lane == iota((CLIPS_DEV, LANES), 0)
    r_row = jnp.sum(jnp.where(across, jnp.broadcast_to(sums, (CLIPS_DEV, LANES)), 0.0), axis=0, keepdims=True)
    r_rows = jnp.where(iota((8, LANES), 1) == CLIPS_DEV, diag[...], r_row)
    for i in range(NZC):
        r_out[i] = r_rows
    c_out[...] = jnp.broadcast_to(jnp.sum(e_pair, axis=0, keepdims=True), (8, LANES))


def weights_kernel(v_ref, g_ref, row_ref, col_ref, e_ref, p_out, av_out, ag_out):
    p = pl.program_id(0)
    e = exp_scores(v_ref[...], g_ref[...])
    scale = 2.5 * e_ref[...]
    col0, col1 = col_ref[0], col_ref[1]
    for f in range(FRAMES):
        at = pl.ds(f * CLIPS_DEV, CLIPS_DEV)
        block = e[f * CLIPS_DEV : (f + 1) * CLIPS_DEV]
        row = row_ref[at, :]
        w0 = scale * block[:, :LANES] * jnp.maximum(row + col0, 0.0)
        w1 = scale * block[:, LANES:] * jnp.maximum(row + col1, 0.0)
        p_out[0, at, :] = jnp.concatenate([w0, w1], axis=1).astype(BF16)
    weights = p_out[0]
    part = nn(weights, g_ref[...])

    @pl.when(p == 0)
    def _():
        av_out[...] = part

    @pl.when(p > 0)
    def _():
        av_out[...] = av_out[...] + part

    ag_out[...] = tn(weights, v_ref[...])


def added(got):
    total = got[0]
    for i in range(1, got.shape[0]):
        total = total + got[i]
    return total


def row_sums_kernel(r_got, c_part, c_out, r_out):
    r_rows = added(r_got)
    r_out[...] = r_rows
    lane = iota((1, LANES), 1)
    logs = jnp.where(lane < CLIPS_DEV, jnp.log(jnp.where(lane < CLIPS_DEV, r_rows[0:1], 1.0)), 0.0)
    logs = logs - jnp.where(lane == CLIPS_DEV, 2.0 * r_rows[0:1], 0.0)
    total = jnp.sum(logs, axis=1, keepdims=True)
    message = jnp.where(iota((8, LANES), 1) == TEXTS_DEV, total, c_part[...])
    for i in range(NXY):
        c_out[i] = message


def inverse_texts(c_rows):
    real = iota((8, LANES), 1) < TEXTS_DEV
    inverse = jnp.where(real, 1.0 / jnp.where(real, c_rows, 1.0), 0.0)
    return jnp.broadcast_to(column_of(inverse, LANES), (LANES, WIDTH))


def by_clip_kernel(r_ref, p_ref, v_ref, out, v_hi, v_low):
    @pl.when(pl.program_id(0) == 0)
    def _():
        inverse = jnp.broadcast_to(1.0 / column_of(r_ref[...], CLIPS_DEV), (CLIPS_DEV, WIDTH))
        for f in range(FRAMES):
            at = pl.ds(f * CLIPS_DEV, CLIPS_DEV)
            scaled = v_ref[at, :].astype(F32) * inverse
            hi = scaled.astype(BF16)
            v_hi[at, :] = hi
            v_low[at, :] = (scaled - hi.astype(F32)).astype(BF16)

    out[...] = tn(p_ref[0], v_hi[...]) + tn(p_ref[0], v_low[...])


def gloss_send_kernel(c_got, ag_ref, bg_ref, out, c_out, scr):
    step = pl.program_id(0)

    @pl.when(step == 0)
    def _():
        c_out[...] = added(c_got)

    col = inverse_texts(c_out[...])
    for k in range(GLOSSES // QUADS):
        at = pl.ds(k * LANES, LANES)
        block = ag_ref[at, :] * col + bg_ref[at, :]
        row = (step * (GLOSSES // QUADS) + k) * OWN
        for x in range(NX):
            for c in range(OWN):
                first = (x * OWN + c) * NY
                put(scr, pl.ds(x * NY * GOWN + row + c, NY, stride=GOWN), block[first : first + NY])

    @pl.when(step == QUADS - 1)
    def _():
        out[...] = get(scr, pl.ds(0, NXY * GOWN)).astype(BF16).reshape(NXY, GOWN, WIDTH)


def clip_send_kernel(c_got, r_ref, p_ref, g_ref, av_ref, mine, twin, c_rows, total):
    step = pl.program_id(0)

    @pl.when(step == 0)
    def _():
        c_rows[...] = added(c_got)

    col = inverse_texts(c_rows[...])
    scaled = g_ref[...].astype(F32) * jnp.concatenate([col] * (GLOSSES // QUADS), axis=0)
    part = nn(p_ref[0], scaled.astype(BF16))

    @pl.when(step == 0)
    def _():
        total[...] = part

    @pl.when((step > 0) & (step < QUADS - 1))
    def _():
        total[...] = total[...] + part

    @pl.when(step == QUADS - 1)
    def _():
        core = lax.rem(lax.axis_index("inner"), NCORE)
        inverse = jnp.broadcast_to(1.0 / column_of(r_ref[...], CLIPS_DEV), (CLIPS_DEV, WIDTH))
        half = CLIPS_DEV // 2
        for pair in range(FRAMES // 2):
            others = []
            for f in (2 * pair, 2 * pair + 1):
                at = pl.ds(f * CLIPS_DEV, CLIPS_DEV)
                new = part[f * CLIPS_DEV : (f + 1) * CLIPS_DEV]
                block = av_ref[at, :] * inverse + (total[at, :] + new)
                low, high = block[:half], block[half:]
                mine[pl.ds(f * half, half), :] = jnp.where(core == 0, low, high)
                others.append(jnp.where(core == 0, high, low))
            twin[pl.ds(pair * CLIPS_DEV, CLIPS_DEV), :] = jnp.concatenate(others, axis=0).astype(BF16)
        real = iota((1, LANES), 1) < TEXTS_DEV
        logs = jnp.where(real, jnp.log(jnp.where(real, c_rows[0:1], 1.0)), 0.0)
        extra = pieces(jnp.sum(logs, axis=1, keepdims=True))
        mine[pl.ds(FRAMES * half, EXTRA), :] = extra
        twin[pl.ds(FRAMES * half, EXTRA), :] = extra.astype(BF16)


def z_bits():
    z = lax.rem(lax.axis_index("outer"), NZ)
    return lax.rem(z, 2), lax.rem(lax.div(z, 2), 2), lax.div(z, 4)


def clip_rows_kernel(mine, got, keep, send, scr):
    step = 2 * NZ
    for i in range(VOWN // 2):
        at = pl.ds(i * step, step)
        two = mine[at, :] + got[at, :].astype(F32)
        for k in range(2):
            put(scr, pl.ds(2 * i + k, NZ, stride=CHUNK), two[k * NZ : (k + 1) * NZ])
    at = pl.ds(VOWN * NZ, EXTRA)
    extra = pieces(unpiece(mine[at, :]) + unpiece(got[at, :].astype(F32)))
    for i in range(NZ):
        put(scr, pl.ds(i * CHUNK + VOWN, EXTRA), extra)
    bit = z_bits()[0]
    for i in range(NZ // 2):
        at = pl.ds(i * CHUNK, CHUNK)
        keep[at, :] = get(scr, pl.ds(pl.multiple_of((2 * i + bit) * CHUNK, CHUNK), CHUNK))
        send[at, :] = get(scr, pl.ds(pl.multiple_of((2 * i + 1 - bit) * CHUNK, CHUNK), CHUNK)).astype(BF16)


def joined(mine, got, owner):
    start = owner * CHUNK if isinstance(owner, int) else pl.multiple_of(owner * CHUNK, CHUNK)
    at = pl.ds(start, VOWN)
    tail = pl.ds(start + VOWN, EXTRA)
    extra = pieces(unpiece(mine[tail, :]) + unpiece(got[tail, :].astype(F32)))
    return mine[at, :] + got[at, :].astype(F32), extra


def halve_kernel(which, mine, got, keep, send):
    bit = z_bits()[which]
    for i in range(NZ // 2 ** (which + 1)):
        for out, chosen in ((keep, bit), (send, 1 - bit)):
            rows, extra = joined(mine, got, 2 * i + chosen)
            out[pl.ds(i * CHUNK, VOWN), :] = rows.astype(out.dtype)
            out[pl.ds(i * CHUNK + VOWN, EXTRA), :] = extra.astype(out.dtype)


def token_grads(total, scr, raw, out, tokens):
    put(scr, pl.ds(0, OWN * tokens), total)
    for c in range(OWN):
        x = raw[c].astype(F32)
        d = get(scr, pl.ds(c, tokens, stride=OWN))
        mean_sq = jnp.mean(x * x, axis=-1, keepdims=True) + EPSILON
        factor = lax.rsqrt(mean_sq) / math.sqrt(WIDTH)
        inner = jnp.sum(d * x, axis=-1, keepdims=True)
        out[c] = factor * d - factor * x * (inner / (WIDTH * mean_sq))


def video_grad_kernel(clips, mine, got, c_rows, diag, video, out, loss, scr):
    total, extra = joined(mine, got, 0)
    token_grads(total + diag[...], scr, video, out, FRAMES)
    row_part = c_rows[0:1, TEXTS_DEV : TEXTS_DEV + 1]
    loss[...] = (unpiece(extra) + row_part) * (0.5 / clips)


def gloss_grad_kernel(got, diag, gloss, out, scr):
    total = got[0].astype(F32)
    for i in range(1, NXY):
        total = total + got[i].astype(F32)
    token_grads(total + diag[...], scr, gloss, out, GLOSSES)


def shape(*dims, dtype=F32):
    return jax.ShapeDtypeStruct(dims, dtype)


def on_device(clips, video, gloss, frame_count, gloss_count):
    vmem = pl.BlockSpec(memory_space=pltpu.VMEM)
    over_all = ("outer", "inner")

    def to_core(a):
        return lax.ppermute(a, "inner", [(i, i ^ 1) for i in range(lax.axis_size("inner"))])

    def to_z(a, mask):
        return lax.ppermute(a, "outer", [(i, i ^ mask) for i in range(lax.axis_size("outer"))])

    def exchanged(a, groups):
        return lax.all_to_all(a, over_all, 0, 0, axis_index_groups=groups, tiled=True)

    def gathered(a, groups):
        return lax.all_gather(a, over_all, axis=0, axis_index_groups=groups, tiled=True)

    def in_hbm(*arrays):
        return [pltpu.with_memory_space_constraint(a, pltpu.HBM) for a in arrays]

    with jax.named_scope("unit_tokens"):
        v_own, g_own, counts = pl.pallas_call(
            units_kernel,
            in_specs=[pl.BlockSpec(memory_space=pltpu.HBM)] * 4,
            out_shape=(
                shape(VOWN, WIDTH, dtype=BF16),
                shape(NXY, GOWN, WIDTH, dtype=BF16),
                shape(8, LANES, dtype=jnp.int32),
            ),
            scratch_shapes=[
                pltpu.SMEM((OWN,), jnp.int32),
                pltpu.SMEM((OWN,), jnp.int32),
                pltpu.VMEM((OWN, FRAMES, WIDTH), BF16),
                pltpu.VMEM((OWN, GLOSSES, WIDTH), BF16),
                two_halves(VOWN),
                two_halves(GOWN),
                pltpu.SemaphoreType.DMA((4,)),
            ],
            compiler_params=params(),
            cost_estimate=cost(2e5, 7e5),
        )(*in_hbm(frame_count, gloss_count, video, gloss))

    with jax.named_scope("gather"):
        g_got = exchanged(g_own, XY_GROUPS)
        v_got = gathered(gathered(v_own, Z_GROUPS), CORE_GROUPS)

    def first(rows):
        return pl.BlockSpec((1, rows, WIDTH), lambda i: (0, 0, 0))

    def whole(*dims):
        return pl.BlockSpec(dims, lambda i: (0,) * len(dims))

    with jax.named_scope("diagonal"):
        dv_diag, dg_diag, logit_sum = pl.pallas_call(
            diagonal_kernel,
            grid=(1,),
            in_specs=[whole(8, LANES), whole(VOWN, WIDTH), first(GOWN)],
            out_specs=(whole(VOWN, WIDTH), whole(GOWN, WIDTH), whole(8, LANES)),
            out_shape=(shape(VOWN, WIDTH), shape(GOWN, WIDTH), shape(8, LANES)),
            compiler_params=params(),
            cost_estimate=cost(2e7, 3e5),
        )(counts, v_own, g_own)

    with jax.named_scope("forward"):
        v_all, g_all, row_inv, col_inv, e_pair, r_part, c_part = pl.pallas_call(
            forward_kernel,
            in_specs=[vmem] * 3,
            out_shape=(
                shape(VROWS, WIDTH, dtype=BF16),
                shape(GROWS, WIDTH, dtype=BF16),
                shape(VROWS, LANES),
                shape(GLOSSES, CLIPS_DEV, LANES),
                shape(CLIPS_DEV, LANES),
                shape(NZC, 8, LANES),
                shape(8, LANES),
            ),
            scratch_shapes=[
                two_halves(VROWS),
                two_halves(NXY * GOWN),
                pltpu.VMEM((VROWS, LANES), F32),
                pltpu.VMEM((GLOSSES, 8, LANES), F32),
                pltpu.VMEM((VROWS, LANES), F32),
                pltpu.VMEM((GLOSSES, CLIPS_DEV, LANES), F32),
            ],
            compiler_params=params(),
            cost_estimate=cost(2 * VROWS * GROWS * WIDTH, 8e6, VROWS * GROWS),
        )(v_got, g_got, logit_sum)

    with jax.named_scope("row_sums"):
        c_send, r_rows = pl.pallas_call(
            row_sums_kernel,
            in_specs=[vmem] * 2,
            out_shape=(shape(NXY, 8, LANES), shape(8, LANES)),
            compiler_params=params(),
            cost_estimate=cost(1e5, 3e5),
        )(exchanged(r_part, ZC_GROUPS), c_part)
    with jax.named_scope("column_sums"):
        c_got = exchanged(c_send, XY_GROUPS)

    def halves(rows):
        return pl.BlockSpec((rows, WIDTH), lambda i: (i, 0))

    p_spec = pl.BlockSpec((1, VROWS, 2 * WIDTH), lambda i: (i, 0, 0))
    with jax.named_scope("weights"):
        weights, av, ag = pl.pallas_call(
            weights_kernel,
            grid=(PAIRS,),
            in_specs=[
                whole(VROWS, WIDTH),
                halves(2 * LANES),
                whole(VROWS, LANES),
                pl.BlockSpec((2, CLIPS_DEV, LANES), lambda i: (i, 0, 0)),
                whole(CLIPS_DEV, LANES),
            ],
            out_specs=(
                pl.BlockSpec((1, VROWS, WIDTH), lambda i: (i // 2, 0, i % 2)),
                whole(VROWS, WIDTH),
                halves(2 * LANES),
            ),
            out_shape=(shape(QUADS, VROWS, 2 * WIDTH, dtype=BF16), shape(VROWS, WIDTH), shape(GROWS, WIDTH)),
            compiler_params=params(),
            cost_estimate=cost(6 * VROWS * GROWS * WIDTH, 16e6, VROWS * GROWS),
        )(*in_hbm(v_all, g_all, row_inv, col_inv), e_pair)

    with jax.named_scope("by_clip"):
        bg = pl.pallas_call(
            by_clip_kernel,
            grid=(QUADS,),
            in_specs=[whole(8, LANES), p_spec, whole(VROWS, WIDTH)],
            out_specs=halves(4 * LANES),
            out_shape=shape(GROWS, WIDTH),
            scratch_shapes=[pltpu.VMEM((VROWS, WIDTH), BF16), pltpu.VMEM((VROWS, WIDTH), BF16)],
            compiler_params=params(),
            cost_estimate=cost(4 * VROWS * GROWS * WIDTH, 9e6),
        )(r_rows, *in_hbm(weights, v_all))

    with jax.named_scope("gloss_send"):
        dg_send, c_rows = pl.pallas_call(
            gloss_send_kernel,
            grid=(QUADS,),
            in_specs=[whole(NXY, 8, LANES), halves(4 * LANES), halves(4 * LANES)],
            out_specs=(whole(NXY, GOWN, WIDTH), whole(8, LANES)),
            out_shape=(shape(NXY, GOWN, WIDTH, dtype=BF16), shape(8, LANES)),
            scratch_shapes=[two_halves(NXY * GOWN)],
            compiler_params=params(),
            cost_estimate=cost(2e6, 5e6),
        )(c_got, *in_hbm(ag, bg))
        dg_got = exchanged(dg_send, XY_GROUPS)

    with jax.named_scope("clip_send"):
        v_rows = FRAMES * CLIPS_DEV // 2 + EXTRA
        mine, twin = pl.pallas_call(
            clip_send_kernel,
            grid=(QUADS,),
            in_specs=[whole(NXY, 8, LANES), whole(8, LANES), p_spec, halves(4 * LANES), whole(VROWS, WIDTH)],
            out_specs=(whole(v_rows, WIDTH), whole(v_rows, WIDTH)),
            out_shape=(shape(v_rows, WIDTH), shape(v_rows, WIDTH, dtype=BF16)),
            scratch_shapes=[pltpu.VMEM((8, LANES), F32), pltpu.VMEM((VROWS, WIDTH), F32)],
            compiler_params=params(),
            cost_estimate=cost(2 * VROWS * GROWS * WIDTH, 1e7),
        )(c_got, r_rows, *in_hbm(weights, g_all), av)

    def kept_and_sent(owners):
        return (shape(owners * CHUNK, WIDTH), shape(owners * CHUNK, WIDTH, dtype=BF16))

    with jax.named_scope("clips_by_core"):
        mine, sent = pl.pallas_call(
            clip_rows_kernel,
            in_specs=[vmem] * 2,
            out_shape=kept_and_sent(NZ // 2),
            scratch_shapes=[two_halves(NZ * CHUNK)],
            compiler_params=params(),
            cost_estimate=cost(1e6, 2e6),
        )(mine, to_core(twin))
    for which, scope in ((1, "clips_by_z1"), (2, "clips_by_z2")):
        with jax.named_scope(scope):
            mine, sent = pl.pallas_call(
                functools.partial(halve_kernel, which),
                in_specs=[vmem] * 2,
                out_shape=kept_and_sent(NZ // 2 ** (which + 1)),
                compiler_params=params(),
                cost_estimate=cost(1e6, 1e6),
            )(mine, to_z(sent, 2 ** (which - 1)))

    with jax.named_scope("video_grad"):
        grad_video, loss = pl.pallas_call(
            functools.partial(video_grad_kernel, clips),
            in_specs=[vmem] * 5,
            out_shape=(shape(OWN, FRAMES, WIDTH), shape(1, 1)),
            scratch_shapes=[two_halves(VOWN)],
            compiler_params=params(),
            cost_estimate=cost(1e6, 1e6),
        )(mine, to_z(sent, NZ // 2), c_rows, dv_diag, video)
    with jax.named_scope("gloss_grad"):
        grad_gloss = pl.pallas_call(
            gloss_grad_kernel,
            in_specs=[vmem] * 3,
            out_shape=shape(OWN, GLOSSES, WIDTH),
            scratch_shapes=[two_halves(GOWN)],
            compiler_params=params(),
            cost_estimate=cost(1e6, 1e6),
        )(dg_got, dg_diag, gloss)
    return loss.reshape(()), grad_video, grad_gloss


def solution(mesh):
    clips = OWN * mesh.shape["outer"] * mesh.shape["inner"]
    over_all = ("outer", "inner")
    tokens, counts = P(over_all, None, None), P(over_all)
    return jax.shard_map(
        functools.partial(on_device, clips),
        mesh=mesh,
        in_specs=(tokens, tokens, counts, counts),
        out_specs=(P(), tokens, tokens),
        check_vma=False,
    )
```

```python
import functools
import math

import jax
import jax.numpy as jnp
from jax import lax
from jax.experimental import pallas as pl
from jax.experimental.pallas import tpu as pltpu
from jax.sharding import PartitionSpec as P

F32 = jnp.float32
BF16 = jnp.bfloat16
EPSILON = 1e-06
EXP_SCALE = 10.0 * math.log2(math.e)
MARK = 2.0
MARK_LIMIT = 1.5
FAR = -1e30

NZ, NY, NX, NCORE = 8, 8, 4, 2
OWN = 3
FRAMES, GLOSSES, WIDTH = 32, 16, 256
CLIPS_DEV = NZ * NCORE * OWN
TEXTS_DEV = NY * NX * OWN
LANES = 128
VROWS = FRAMES * CLIPS_DEV
GROWS = GLOSSES * LANES
VOWN = FRAMES * OWN
GOWN = GLOSSES * OWN
EXTRA = 16
PAIRS = GLOSSES // 2
QUADS = GLOSSES // 4
NXY, NZC = NX * NY, NZ * NCORE
CHUNK = VOWN + EXTRA


def flat(x, z, y, core):
    return ((x % 2) * NZ + z) * 32 + (x // 2) * 16 + 2 * y + core


def z_pairs(mask):
    return [
        [flat(x, z, y, c), flat(x, z ^ mask, y, c)]
        for x in range(NX)
        for y in range(NY)
        for c in range(NCORE)
        for z in range(NZ)
        if not z & mask
    ]


CORE_GROUPS = [[flat(x, z, y, c) for c in range(NCORE)] for x in range(NX) for y in range(NY) for z in range(NZ)]
XY_GROUPS = [[flat(x, z, y, c) for x in range(NX) for y in range(NY)] for z in range(NZ) for c in range(NCORE)]
ZC_GROUPS = [[flat(x, z, y, c) for c in range(NCORE) for z in range(NZ)] for x in range(NX) for y in range(NY)]


def params(limit_mb=16):
    return pltpu.CompilerParams(vmem_limit_bytes=limit_mb * 1024 * 1024)


def cost(flops, nbytes, trans=0):
    return pl.CostEstimate(flops=int(flops), bytes_accessed=int(nbytes), transcendentals=int(trans))


def iota(shape, dim):
    return lax.broadcasted_iota(jnp.int32, shape, dim)


def nt(a, b, **kw):
    return lax.dot_general(a, b, (((1,), (1,)), ((), ())), preferred_element_type=F32, **kw)


def nn(a, b, **kw):
    return lax.dot_general(a, b, (((1,), (0,)), ((), ())), preferred_element_type=F32, **kw)


def tn(a, b, **kw):
    return lax.dot_general(a, b, (((0,), (0,)), ((), ())), preferred_element_type=F32, **kw)


def column_of(row, n):
    eye = iota((n, LANES), 0) == iota((n, LANES), 1)
    return jnp.sum(jnp.where(eye, jnp.broadcast_to(row[0:1], (n, LANES)), 0.0), axis=1, keepdims=True)


def pieces(value):
    lane = iota((EXTRA, WIDTH), 1)
    full = jnp.broadcast_to(value, (EXTRA, WIDTH))
    hi = full.astype(BF16).astype(F32)
    mid = (full - hi).astype(BF16).astype(F32)
    low = (full - hi - mid).astype(BF16).astype(F32)
    return jnp.where(lane == 0, hi, jnp.where(lane == 1, mid, jnp.where(lane == 2, low, 0.0)))


def unpiece(block):
    mine = (iota((EXTRA, WIDTH), 0) == 0) & (iota((EXTRA, WIDTH), 1) < 3)
    return jnp.sum(jnp.where(mine, block, 0.0), keepdims=True).reshape(1, 1)


def put(ref, at, value):
    ref[0, at, :] = value[:, :LANES]
    ref[1, at, :] = value[:, LANES:]


def get(ref, at):
    return jnp.concatenate([ref[0, at, :], ref[1, at, :]], axis=1)


def two_halves(rows):
    return pltpu.VMEM((2, rows, LANES), F32)


def units_kernel(fc_in, gc_in, video_in, gloss_in, v_out, g_out, count_out, fc, gc, video, gloss, v_scr, g_scr, sems):
    pairs = ((fc_in, fc), (gc_in, gc), (video_in, video), (gloss_in, gloss))
    copies = [pltpu.make_async_copy(a, b, sems.at[i]) for i, (a, b) in enumerate(pairs)]
    for copy in copies:
        copy.start()
    for copy in copies:
        copy.wait()
    row = iota((8, LANES), 0)
    counts = jnp.zeros((8, LANES), jnp.int32)
    for c in range(OWN):
        counts = jnp.where(row == c, fc[c], jnp.where(row == OWN + c, gc[c], counts))
    count_out[...] = counts
    for count, raw, scr, tokens in ((fc, video, v_scr, FRAMES), (gc, gloss, g_scr, GLOSSES)):
        row, lane = iota((tokens, WIDTH), 0), iota((tokens, WIDTH), 1)
        for c in range(OWN):
            x = raw[c].astype(F32)
            mean_sq = jnp.mean(x * x, axis=-1, keepdims=True) + EPSILON
            unit = x * (lax.rsqrt(mean_sq) / math.sqrt(WIDTH))
            mark = jnp.where(lane == 0, MARK, 0.0)
            put(scr, pl.ds(c, tokens, stride=OWN), jnp.where(row < count[c], unit, mark))
    v = get(v_scr, pl.ds(0, VOWN)).astype(BF16)
    g = get(g_scr, pl.ds(0, GOWN)).astype(BF16)
    v_out[...] = v
    for i in range(NXY):
        g_out[i] = g


def diagonal_kernel(count_ref, v_ref, g_ref, dv, dg, logit_sum):
    def pick(count, which):
        return jnp.where(which == 0, count[0], jnp.where(which == 1, count[1], count[2]))

    fc = [count_ref[c : c + 1, 0:1] for c in range(OWN)]
    gc = [count_ref[OWN + c : OWN + c + 1, 0:1] for c in range(OWN)]
    v, g = v_ref[...], g_ref[0]
    shape = (VOWN, GOWN)
    r, q = iota(shape, 0), iota(shape, 1)
    rc, qc = lax.rem(r, OWN), lax.rem(q, OWN)
    valid = (rc == qc) & (lax.div(r, OWN) < pick(fc, rc)) & (lax.div(q, OWN) < pick(gc, qc))
    e = jnp.where(valid, jnp.exp2(nt(v, g) * EXP_SCALE), 0.0)
    r1, q1 = iota((VOWN, 1), 0), iota((1, GOWN), 1)
    rc1, qc1 = lax.rem(r1, OWN), lax.rem(q1, OWN)
    frames_r, glosses_r = pick(fc, rc1), pick(gc, rc1)
    frames_q, glosses_q = pick(fc, qc1), pick(gc, qc1)
    row_ok = lax.div(r1, OWN) < frames_r
    col_ok = lax.div(q1, OWN) < glosses_q
    frames_r, glosses_r = frames_r.astype(F32), glosses_r.astype(F32)
    frames_q, glosses_q = frames_q.astype(F32), glosses_q.astype(F32)
    rows = jnp.where(row_ok, jnp.sum(e, axis=1, keepdims=True), 1.0)
    cols = jnp.where(col_ok, jnp.sum(e, axis=0, keepdims=True), 1.0)
    by_row = jnp.where(row_ok, jnp.log(rows / glosses_r) / frames_r, 0.0)
    by_col = jnp.where(col_ok, jnp.log(cols / frames_q) / glosses_q, 0.0)
    total = jnp.sum(by_row, axis=0, keepdims=True) + jnp.sum(by_col, axis=1, keepdims=True)
    logit_sum[...] = jnp.broadcast_to(0.5 * total, (8, LANES))
    weight = -5.0 * e * (1.0 / (rows * frames_r) + 1.0 / (cols * glosses_q))
    dv[...] = nn(weight, g.astype(F32), precision=lax.Precision.HIGHEST)
    dg[...] = tn(weight, v.astype(F32), precision=lax.Precision.HIGHEST)


def exp_scores(v, g):
    return jnp.exp2(nt(v, g) * EXP_SCALE)


def forward_kernel(
    v_got, g_got, diag,
    v_hbm, g_hbm, row_hbm, col_hbm, e_out, r_out, c_out,
    v_out, g_out, row_out, col_out, v_scr, g_scr, frame_mask, gloss_mask, rows, cols, sems,
):
    results = ((v_out, v_hbm), (g_out, g_hbm), (row_out, row_hbm), (col_out, col_hbm))
    copies = [pltpu.make_async_copy(a, b, sems.at[i]) for i, (a, b) in enumerate(results)]
    put(v_scr, pl.ds(0, VROWS), v_got[...].astype(F32))
    for f in range(FRAMES):
        parts = [
            get(v_scr, pl.ds(k * NZ * VOWN + f * OWN + c, NZ, stride=VOWN)) for k in range(NCORE) for c in range(OWN)
        ]
        v_out[pl.ds(f * CLIPS_DEV, CLIPS_DEV), :] = jnp.concatenate(parts, axis=0).astype(BF16)
    copies[0].start()
    put(g_scr, pl.ds(0, NXY * GOWN), g_got[...].reshape(NXY * GOWN, WIDTH).astype(F32))
    pad = jnp.where(iota((LANES - TEXTS_DEV, WIDTH), 1) == 0, MARK, 0.0)
    for g in range(GLOSSES):
        parts = [get(g_scr, pl.ds(x * NY * GOWN + g * OWN + c, NY, stride=GOWN)) for x in range(NX) for c in range(OWN)]
        g_out[pl.ds(g * LANES, LANES), :] = jnp.concatenate(parts + [pad], axis=0).astype(BF16)

    copies[1].start()

    first = jnp.where(iota((WIDTH, LANES), 0) == 0, 1.0, 0.0).astype(BF16)
    frame_mask[...] = jnp.where(nn(v_out[...], first) < MARK_LIMIT, 1.0, 0.0)
    first_row = jnp.where(iota((16, WIDTH), 1) == 0, 1.0, 0.0).astype(BF16)
    for g in range(GLOSSES):
        gloss_mask[g] = jnp.where(nt(first_row, g_out[pl.ds(g * LANES, LANES), :])[0:8] < MARK_LIMIT, 1.0, 0.0)
    frames = jnp.zeros((CLIPS_DEV, LANES), F32)
    for f in range(FRAMES):
        frames = frames + frame_mask[pl.ds(f * CLIPS_DEV, CLIPS_DEV), :]
    glosses = gloss_mask[0]
    for g in range(1, GLOSSES):
        glosses = glosses + gloss_mask[g]
    glosses = jnp.maximum(glosses, 1.0)[0:1]

    rows[...] = jnp.zeros_like(rows)

    def two_glosses(p, _):
        e = exp_scores(v_out[...], g_out[pl.ds(pl.multiple_of(p * WIDTH, WIDTH), WIDTH), :])
        m0, m1 = gloss_mask[2 * p][0:1], gloss_mask[2 * p + 1][0:1]
        col0 = jnp.zeros((CLIPS_DEV, LANES), F32)
        col1 = jnp.zeros((CLIPS_DEV, LANES), F32)
        for f in range(FRAMES):
            at = pl.ds(f * CLIPS_DEV, CLIPS_DEV)
            block = e[f * CLIPS_DEV : (f + 1) * CLIPS_DEV]
            e0, e1 = block[:, :LANES], block[:, LANES:]
            mask = frame_mask[at, :]
            rows[at, :] = rows[at, :] + (e0 * m0 + e1 * m1)
            col0 = col0 + e0 * mask
            col1 = col1 + e1 * mask
        cols[2 * p] = col0
        cols[2 * p + 1] = col1
        return 0

    lax.fori_loop(0, PAIRS, two_glosses, 0)

    lane = iota((CLIPS_DEV, LANES), 1)
    real = lane < TEXTS_DEV
    video_part = jnp.zeros((CLIPS_DEV, LANES), F32)
    for f in range(FRAMES):
        at = pl.ds(f * CLIPS_DEV, CLIPS_DEV)
        mask = frame_mask[at, :]
        total = jnp.where(real, rows[at, :], 1.0)
        video_part = video_part + mask * jnp.log(total / glosses)
        row_out[at, :] = jnp.where(mask > 0.0, 1.0 / (total * frames), FAR)
    copies[2].start()
    gloss_part = jnp.zeros((CLIPS_DEV, LANES), F32)
    for g in range(GLOSSES):
        mask = gloss_mask[g][0:1]
        total = cols[g]
        gloss_part = gloss_part + mask * jnp.log(total / frames)
        col_out[g] = jnp.where(mask > 0.0, 1.0 / (total * glosses), FAR)
    copies[3].start()
    logits = 0.5 * (video_part / frames + gloss_part / glosses)
    e_pair = jnp.where(real, jnp.exp(logits), 0.0)
    e_out[...] = e_pair

    sums = jnp.sum(e_pair, axis=1, keepdims=True)
    across = lane == iota((CLIPS_DEV, LANES), 0)
    r_row = jnp.sum(jnp.where(across, jnp.broadcast_to(sums, (CLIPS_DEV, LANES)), 0.0), axis=0, keepdims=True)
    r_rows = jnp.where(iota((8, LANES), 1) == CLIPS_DEV, diag[...], r_row)
    for i in range(NZC):
        r_out[i] = r_rows
    c_out[...] = jnp.broadcast_to(jnp.sum(e_pair, axis=0, keepdims=True), (8, LANES))
    for copy in copies:
        copy.wait()


def weights_kernel(v_ref, g_ref, row_ref, col_ref, e_ref, p_out, av_out):
    p = pl.program_id(0)
    e = exp_scores(v_ref[...], g_ref[...])
    scale = 2.5 * e_ref[...]
    col0, col1 = col_ref[0], col_ref[1]
    for f in range(FRAMES):
        at = pl.ds(f * CLIPS_DEV, CLIPS_DEV)
        block = e[f * CLIPS_DEV : (f + 1) * CLIPS_DEV]
        row = row_ref[at, :]
        w0 = scale * block[:, :LANES] * jnp.maximum(row + col0, 0.0)
        w1 = scale * block[:, LANES:] * jnp.maximum(row + col1, 0.0)
        p_out[0, at, :] = jnp.concatenate([w0, w1], axis=1).astype(BF16)
    weights = p_out[0]
    part = nn(weights, g_ref[...])

    @pl.when(p == 0)
    def _():
        av_out[...] = part

    @pl.when(p > 0)
    def _():
        av_out[...] = av_out[...] + part


def added(got):
    total = got[0]
    for i in range(1, got.shape[0]):
        total = total + got[i]
    return total


def row_sums_kernel(r_got, c_part, c_out, r_out):
    r_rows = added(r_got)
    r_out[...] = r_rows
    lane = iota((1, LANES), 1)
    logs = jnp.where(lane < CLIPS_DEV, jnp.log(jnp.where(lane < CLIPS_DEV, r_rows[0:1], 1.0)), 0.0)
    logs = logs - jnp.where(lane == CLIPS_DEV, 2.0 * r_rows[0:1], 0.0)
    total = jnp.sum(logs, axis=1, keepdims=True)
    message = jnp.where(iota((8, LANES), 1) == TEXTS_DEV, total, c_part[...])
    for i in range(NXY):
        c_out[i] = message


def inverse_texts(c_rows):
    real = iota((8, LANES), 1) < TEXTS_DEV
    inverse = jnp.where(real, 1.0 / jnp.where(real, c_rows, 1.0), 0.0)
    return jnp.broadcast_to(column_of(inverse, LANES), (LANES, WIDTH))


def by_clip_kernel(r_ref, p_ref, v_ref, out, both):
    @pl.when(pl.program_id(0) == 0)
    def _():
        inverse = jnp.broadcast_to(1.0 / column_of(r_ref[...], CLIPS_DEV), (CLIPS_DEV, WIDTH))
        for f in range(FRAMES):
            at = pl.ds(f * CLIPS_DEV, CLIPS_DEV)
            v = v_ref[at, :]
            both[at, :WIDTH] = v
            both[at, WIDTH:] = (v.astype(F32) * inverse).astype(BF16)

    out[...] = tn(p_ref[0], both[...])


def gloss_send_kernel(c_got, by_clip, out, c_out, scr):
    step = pl.program_id(0)

    @pl.when(step == 0)
    def _():
        c_out[...] = added(c_got)

    col = inverse_texts(c_out[...])
    for k in range(GLOSSES // QUADS):
        at = pl.ds(k * LANES, LANES)
        block = by_clip[at, :WIDTH] * col + by_clip[at, WIDTH:]
        row = (step * (GLOSSES // QUADS) + k) * OWN
        for x in range(NX):
            for c in range(OWN):
                first = (x * OWN + c) * NY
                put(scr, pl.ds(x * NY * GOWN + row + c, NY, stride=GOWN), block[first : first + NY])

    @pl.when(step == QUADS - 1)
    def _():
        out[...] = get(scr, pl.ds(0, NXY * GOWN)).astype(BF16).reshape(NXY, GOWN, WIDTH)


def clip_send_kernel(c_got, r_ref, p_ref, g_ref, av_ref, mine, twin, c_rows, total):
    step = pl.program_id(0)

    @pl.when(step == 0)
    def _():
        c_rows[...] = added(c_got)

    col = inverse_texts(c_rows[...])
    scaled = g_ref[...].astype(F32) * jnp.concatenate([col] * (GLOSSES // QUADS), axis=0)
    part = nn(p_ref[0], scaled.astype(BF16))

    @pl.when(step == 0)
    def _():
        total[...] = part

    @pl.when((step > 0) & (step < QUADS - 1))
    def _():
        total[...] = total[...] + part

    @pl.when(step == QUADS - 1)
    def _():
        core = lax.rem(lax.axis_index("inner"), NCORE)
        inverse = jnp.broadcast_to(1.0 / column_of(r_ref[...], CLIPS_DEV), (CLIPS_DEV, WIDTH))
        half = CLIPS_DEV // 2
        for pair in range(FRAMES // 2):
            others = []
            for f in (2 * pair, 2 * pair + 1):
                at = pl.ds(f * CLIPS_DEV, CLIPS_DEV)
                new = part[f * CLIPS_DEV : (f + 1) * CLIPS_DEV]
                block = av_ref[at, :] * inverse + (total[at, :] + new)
                low, high = block[:half], block[half:]
                mine[pl.ds(f * half, half), :] = jnp.where(core == 0, low, high)
                others.append(jnp.where(core == 0, high, low))
            twin[pl.ds(pair * CLIPS_DEV, CLIPS_DEV), :] = jnp.concatenate(others, axis=0).astype(BF16)
        real = iota((1, LANES), 1) < TEXTS_DEV
        logs = jnp.where(real, jnp.log(jnp.where(real, c_rows[0:1], 1.0)), 0.0)
        extra = pieces(jnp.sum(logs, axis=1, keepdims=True))
        mine[pl.ds(FRAMES * half, EXTRA), :] = extra
        twin[pl.ds(FRAMES * half, EXTRA), :] = extra.astype(BF16)


def z_bits():
    z = lax.rem(lax.axis_index("outer"), NZ)
    return lax.rem(z, 2), lax.rem(lax.div(z, 2), 2), lax.div(z, 4)


def clip_rows_kernel(mine, got, keep, send, scr):
    step = 2 * NZ
    for i in range(VOWN // 2):
        at = pl.ds(i * step, step)
        two = mine[at, :] + got[at, :].astype(F32)
        for k in range(2):
            put(scr, pl.ds(2 * i + k, NZ, stride=CHUNK), two[k * NZ : (k + 1) * NZ])
    at = pl.ds(VOWN * NZ, EXTRA)
    extra = pieces(unpiece(mine[at, :]) + unpiece(got[at, :].astype(F32)))
    for i in range(NZ):
        put(scr, pl.ds(i * CHUNK + VOWN, EXTRA), extra)
    bit = z_bits()[0]
    for i in range(NZ // 2):
        at = pl.ds(i * CHUNK, CHUNK)
        keep[at, :] = get(scr, pl.ds(pl.multiple_of((NZ // 2 * bit + i) * CHUNK, CHUNK), CHUNK))
        send[at, :] = get(scr, pl.ds(pl.multiple_of((NZ // 2 * (1 - bit) + i) * CHUNK, CHUNK), CHUNK)).astype(BF16)


def joined(mine, got, owner):
    start = owner * CHUNK if isinstance(owner, int) else pl.multiple_of(owner * CHUNK, CHUNK)
    at = pl.ds(start, VOWN)
    tail = pl.ds(start + VOWN, EXTRA)
    extra = pieces(unpiece(mine[tail, :]) + unpiece(got[tail, :].astype(F32)))
    return mine[at, :] + got[at, :].astype(F32), extra


def halve_kernel(which, mine, got, keep, send):
    bit = z_bits()[which]
    owners = NZ // 2 ** (which + 1)
    for i in range(owners):
        for out, chosen in ((keep, bit), (send, 1 - bit)):
            rows, extra = joined(mine, got, owners * chosen + i)
            out[pl.ds(i * CHUNK, VOWN), :] = rows.astype(out.dtype)
            out[pl.ds(i * CHUNK + VOWN, EXTRA), :] = extra.astype(out.dtype)


def token_grads(total, scr, raw, out, tokens):
    put(scr, pl.ds(0, OWN * tokens), total)
    for c in range(OWN):
        x = raw[c].astype(F32)
        d = get(scr, pl.ds(c, tokens, stride=OWN))
        mean_sq = jnp.mean(x * x, axis=-1, keepdims=True) + EPSILON
        factor = lax.rsqrt(mean_sq) / math.sqrt(WIDTH)
        inner = jnp.sum(d * x, axis=-1, keepdims=True)
        out[c] = factor * d - factor * x * (inner / (WIDTH * mean_sq))


def video_grad_kernel(clips, mine, got, c_rows, diag, video, out, loss, scr):
    total, extra = joined(mine, got, 0)
    token_grads(total + diag[...], scr, video, out, FRAMES)
    row_part = c_rows[0:1, TEXTS_DEV : TEXTS_DEV + 1]
    loss[...] = (unpiece(extra) + row_part) * (0.5 / clips)


def gloss_grad_kernel(got, diag, gloss, out, scr):
    total = got[0].astype(F32)
    for i in range(1, NXY):
        total = total + got[i].astype(F32)
    token_grads(total + diag[...], scr, gloss, out, GLOSSES)


def shape(*dims, dtype=F32):
    return jax.ShapeDtypeStruct(dims, dtype)


def on_device(clips, video, gloss, frame_count, gloss_count):
    vmem = pl.BlockSpec(memory_space=pltpu.VMEM)
    over_all = ("outer", "inner")

    def to_core(a):
        return lax.ppermute(a, "inner", [(i, i ^ 1) for i in range(lax.axis_size("inner"))])

    def to_z(a, mask):
        return lax.ppermute(a, "outer", [(i, i ^ mask) for i in range(lax.axis_size("outer"))])

    def exchanged(a, groups):
        return lax.all_to_all(a, over_all, 0, 0, axis_index_groups=groups, tiled=True)

    def gathered(a, groups):
        return lax.all_gather(a, over_all, axis=0, axis_index_groups=groups, tiled=True)

    def in_hbm(*arrays):
        return [pltpu.with_memory_space_constraint(a, pltpu.HBM) for a in arrays]

    with jax.named_scope("unit_tokens"):
        v_own, g_own, counts = pl.pallas_call(
            units_kernel,
            in_specs=[pl.BlockSpec(memory_space=pltpu.HBM)] * 4,
            out_shape=(
                shape(VOWN, WIDTH, dtype=BF16),
                shape(NXY, GOWN, WIDTH, dtype=BF16),
                shape(8, LANES, dtype=jnp.int32),
            ),
            scratch_shapes=[
                pltpu.SMEM((OWN,), jnp.int32),
                pltpu.SMEM((OWN,), jnp.int32),
                pltpu.VMEM((OWN, FRAMES, WIDTH), BF16),
                pltpu.VMEM((OWN, GLOSSES, WIDTH), BF16),
                two_halves(VOWN),
                two_halves(GOWN),
                pltpu.SemaphoreType.DMA((4,)),
            ],
            compiler_params=params(),
            cost_estimate=cost(2e5, 7e5),
        )(*in_hbm(frame_count, gloss_count, video, gloss))

    with jax.named_scope("gather"):
        g_got = exchanged(g_own, XY_GROUPS)
        v_got = v_own
        for mask in (4, 2, 1):
            v_got = gathered(v_got, z_pairs(mask))
        v_got = gathered(v_got, CORE_GROUPS)

    def first(rows):
        return pl.BlockSpec((1, rows, WIDTH), lambda i: (0, 0, 0))

    def whole(*dims):
        return pl.BlockSpec(dims, lambda i: (0,) * len(dims))

    with jax.named_scope("diagonal"):
        dv_diag, dg_diag, logit_sum = pl.pallas_call(
            diagonal_kernel,
            grid=(1,),
            in_specs=[whole(8, LANES), whole(VOWN, WIDTH), first(GOWN)],
            out_specs=(whole(VOWN, WIDTH), whole(GOWN, WIDTH), whole(8, LANES)),
            out_shape=(shape(VOWN, WIDTH), shape(GOWN, WIDTH), shape(8, LANES)),
            compiler_params=params(),
            cost_estimate=cost(2e7, 3e5),
        )(counts, v_own, g_own)

    with jax.named_scope("forward"):
        v_all, g_all, row_inv, col_inv, e_pair, r_part, c_part = pl.pallas_call(
            forward_kernel,
            in_specs=[vmem] * 3,
            out_specs=[pl.BlockSpec(memory_space=pltpu.HBM)] * 4 + [vmem] * 3,
            out_shape=(
                pltpu.HBM((VROWS, WIDTH), BF16),
                pltpu.HBM((GROWS, WIDTH), BF16),
                pltpu.HBM((VROWS, LANES), F32),
                pltpu.HBM((GLOSSES, CLIPS_DEV, LANES), F32),
                shape(CLIPS_DEV, LANES),
                shape(NZC, 8, LANES),
                shape(8, LANES),
            ),
            scratch_shapes=[
                pltpu.VMEM((VROWS, WIDTH), BF16),
                pltpu.VMEM((GROWS, WIDTH), BF16),
                pltpu.VMEM((VROWS, LANES), F32),
                pltpu.VMEM((GLOSSES, CLIPS_DEV, LANES), F32),
                two_halves(VROWS),
                two_halves(NXY * GOWN),
                pltpu.VMEM((VROWS, LANES), F32),
                pltpu.VMEM((GLOSSES, 8, LANES), F32),
                pltpu.VMEM((VROWS, LANES), F32),
                pltpu.VMEM((GLOSSES, CLIPS_DEV, LANES), F32),
                pltpu.SemaphoreType.DMA((4,)),
            ],
            compiler_params=params(),
            cost_estimate=cost(2 * VROWS * GROWS * WIDTH, 8e6, VROWS * GROWS),
        )(v_got, g_got, logit_sum)

    with jax.named_scope("row_sums"):
        c_send, r_rows = pl.pallas_call(
            row_sums_kernel,
            in_specs=[vmem] * 2,
            out_shape=(shape(NXY, 8, LANES), shape(8, LANES)),
            compiler_params=params(),
            cost_estimate=cost(1e5, 3e5),
        )(exchanged(r_part, ZC_GROUPS), c_part)
    with jax.named_scope("column_sums"):
        c_got = exchanged(c_send, XY_GROUPS)

    def halves(rows):
        return pl.BlockSpec((rows, WIDTH), lambda i: (i, 0))

    p_spec = pl.BlockSpec((1, VROWS, 2 * WIDTH), lambda i: (i, 0, 0))
    with jax.named_scope("weights"):
        weights, av = pl.pallas_call(
            weights_kernel,
            grid=(PAIRS,),
            in_specs=[
                whole(VROWS, WIDTH),
                halves(2 * LANES),
                whole(VROWS, LANES),
                pl.BlockSpec((2, CLIPS_DEV, LANES), lambda i: (i, 0, 0)),
                whole(CLIPS_DEV, LANES),
            ],
            out_specs=(
                pl.BlockSpec((1, VROWS, WIDTH), lambda i: (i // 2, 0, i % 2)),
                whole(VROWS, WIDTH),
            ),
            out_shape=(pltpu.HBM((QUADS, VROWS, 2 * WIDTH), BF16), shape(VROWS, WIDTH)),
            compiler_params=params(),
            cost_estimate=cost(4 * VROWS * GROWS * WIDTH, 12e6, VROWS * GROWS),
        )(*in_hbm(v_all, g_all, row_inv, col_inv), e_pair)

    with jax.named_scope("by_clip"):
        by_clip = pl.pallas_call(
            by_clip_kernel,
            grid=(QUADS,),
            in_specs=[whole(8, LANES), p_spec, whole(VROWS, WIDTH)],
            out_specs=pl.BlockSpec((4 * LANES, 2 * WIDTH), lambda i: (i, 0)),
            out_shape=pltpu.HBM((GROWS, 2 * WIDTH), F32),
            scratch_shapes=[pltpu.VMEM((VROWS, 2 * WIDTH), BF16)],
            compiler_params=params(),
            cost_estimate=cost(4 * VROWS * GROWS * WIDTH, 9e6),
        )(r_rows, *in_hbm(weights, v_all))

    with jax.named_scope("clip_send"):
        v_rows = FRAMES * CLIPS_DEV // 2 + EXTRA
        mine, twin = pl.pallas_call(
            clip_send_kernel,
            grid=(QUADS,),
            in_specs=[whole(NXY, 8, LANES), whole(8, LANES), p_spec, halves(4 * LANES), whole(VROWS, WIDTH)],
            out_specs=(whole(v_rows, WIDTH), whole(v_rows, WIDTH)),
            out_shape=(shape(v_rows, WIDTH), shape(v_rows, WIDTH, dtype=BF16)),
            scratch_shapes=[pltpu.VMEM((8, LANES), F32), pltpu.VMEM((VROWS, WIDTH), F32)],
            compiler_params=params(),
            cost_estimate=cost(2 * VROWS * GROWS * WIDTH, 1e7),
        )(c_got, r_rows, *in_hbm(weights, g_all), av)

    with jax.named_scope("gloss_send"):
        twin, c_ready = lax.optimization_barrier((twin, c_got))
        dg_send, c_rows = pl.pallas_call(
            gloss_send_kernel,
            grid=(QUADS,),
            in_specs=[whole(NXY, 8, LANES), pl.BlockSpec((4 * LANES, 2 * WIDTH), lambda i: (i, 0))],
            out_specs=(whole(NXY, GOWN, WIDTH), whole(8, LANES)),
            out_shape=(shape(NXY, GOWN, WIDTH, dtype=BF16), shape(8, LANES)),
            scratch_shapes=[two_halves(NXY * GOWN)],
            compiler_params=params(),
            cost_estimate=cost(2e6, 5e6),
        )(c_ready, *in_hbm(by_clip))
        dg_got = exchanged(dg_send, XY_GROUPS)

    def kept_and_sent(owners):
        return (shape(owners * CHUNK, WIDTH), shape(owners * CHUNK, WIDTH, dtype=BF16))

    with jax.named_scope("clips_by_core"):
        mine, sent = pl.pallas_call(
            clip_rows_kernel,
            in_specs=[vmem] * 2,
            out_shape=kept_and_sent(NZ // 2),
            scratch_shapes=[two_halves(NZ * CHUNK)],
            compiler_params=params(),
            cost_estimate=cost(1e6, 2e6),
        )(mine, to_core(twin))
    for which, scope in ((1, "clips_by_z1"), (2, "clips_by_z2")):
        with jax.named_scope(scope):
            mine, sent = pl.pallas_call(
                functools.partial(halve_kernel, which),
                in_specs=[vmem] * 2,
                out_shape=kept_and_sent(NZ // 2 ** (which + 1)),
                compiler_params=params(),
                cost_estimate=cost(1e6, 1e6),
            )(mine, to_z(sent, 2 ** (which - 1)))

    with jax.named_scope("video_grad"):
        grad_video, loss = pl.pallas_call(
            functools.partial(video_grad_kernel, clips),
            in_specs=[vmem] * 5,
            out_shape=(shape(OWN, FRAMES, WIDTH), shape(1, 1)),
            scratch_shapes=[two_halves(VOWN)],
            compiler_params=params(),
            cost_estimate=cost(1e6, 1e6),
        )(mine, to_z(sent, NZ // 2), c_rows, dv_diag, video)
    with jax.named_scope("gloss_grad"):
        grad_gloss = pl.pallas_call(
            gloss_grad_kernel,
            in_specs=[vmem] * 3,
            out_shape=shape(OWN, GLOSSES, WIDTH),
            scratch_shapes=[two_halves(GOWN)],
            compiler_params=params(),
            cost_estimate=cost(1e6, 1e6),
        )(dg_got, dg_diag, gloss)
    return loss.reshape(()), grad_video, grad_gloss


def solution(mesh):
    clips = OWN * mesh.shape["outer"] * mesh.shape["inner"]
    over_all = ("outer", "inner")
    tokens, counts = P(over_all, None, None), P(over_all)
    return jax.shard_map(
        functools.partial(on_device, clips),
        mesh=mesh,
        in_specs=(tokens, tokens, counts, counts),
        out_specs=(P(), tokens, tokens),
        check_vma=False,
    )
```

```python
import functools
import math

import jax
import jax.numpy as jnp
from jax import lax
from jax.experimental import pallas as pl
from jax.experimental.pallas import tpu as pltpu
from jax.sharding import PartitionSpec as P

F32 = jnp.float32
BF16 = jnp.bfloat16
EPSILON = 1e-06
EXP_SCALE = 10.0 * math.log2(math.e)
MARK = 2.0
MARK_LIMIT = 1.5
FAR = -1e30

NZ, NY, NX, NCORE = 8, 8, 4, 2
OWN = 3
FRAMES, GLOSSES, WIDTH = 32, 16, 256
CLIPS_DEV = NZ * NCORE * OWN
TEXTS_DEV = NY * NX * OWN
LANES = 128
VROWS = FRAMES * CLIPS_DEV
GROWS = GLOSSES * LANES
VOWN = FRAMES * OWN
GOWN = GLOSSES * OWN
EXTRA = 16
PAIRS = GLOSSES // 2
QUADS = GLOSSES // 4
NXY, NZC = NX * NY, NZ * NCORE

def flat(x, z, y, core):
    return ((x % 2) * NZ + z) * 32 + (x // 2) * 16 + 2 * y + core


def z_pairs(mask):
    return [
        [flat(x, z, y, c), flat(x, z ^ mask, y, c)]
        for x in range(NX)
        for y in range(NY)
        for c in range(NCORE)
        for z in range(NZ)
        if not z & mask
    ]


CORE_GROUPS = [[flat(x, z, y, c) for c in range(NCORE)] for x in range(NX) for y in range(NY) for z in range(NZ)]
XY_GROUPS = [[flat(x, z, y, c) for x in range(NX) for y in range(NY)] for z in range(NZ) for c in range(NCORE)]
ZC_GROUPS = [[flat(x, z, y, c) for c in range(NCORE) for z in range(NZ)] for x in range(NX) for y in range(NY)]


def params(limit_mb=16):
    return pltpu.CompilerParams(vmem_limit_bytes=limit_mb * 1024 * 1024)


def cost(flops, nbytes, trans=0):
    return pl.CostEstimate(flops=int(flops), bytes_accessed=int(nbytes), transcendentals=int(trans))


def iota(shape, dim):
    return lax.broadcasted_iota(jnp.int32, shape, dim)


def nt(a, b, **kw):
    return lax.dot_general(a, b, (((1,), (1,)), ((), ())), preferred_element_type=F32, **kw)


def nn(a, b, **kw):
    return lax.dot_general(a, b, (((1,), (0,)), ((), ())), preferred_element_type=F32, **kw)


def tn(a, b, **kw):
    return lax.dot_general(a, b, (((0,), (0,)), ((), ())), preferred_element_type=F32, **kw)


def column_of(row, n):
    eye = iota((n, LANES), 0) == iota((n, LANES), 1)
    return jnp.sum(jnp.where(eye, jnp.broadcast_to(row, (n, LANES)), 0.0), axis=1, keepdims=True)


def pieces(value):
    lane = iota((EXTRA, WIDTH), 1)
    full = jnp.broadcast_to(value, (EXTRA, WIDTH))
    hi = full.astype(BF16).astype(F32)
    mid = (full - hi).astype(BF16).astype(F32)
    low = (full - hi - mid).astype(BF16).astype(F32)
    return jnp.where(lane == 0, hi, jnp.where(lane == 1, mid, jnp.where(lane == 2, low, 0.0)))


def unpiece(block):
    mine = (iota((EXTRA, WIDTH), 0) == 0) & (iota((EXTRA, WIDTH), 1) < 3)
    return jnp.sum(jnp.where(mine, block, 0.0), keepdims=True).reshape(1, 1)


def put(ref, at, value):
    ref[0, at, :] = value[:, :LANES]
    ref[1, at, :] = value[:, LANES:]


def get(ref, at):
    return jnp.concatenate([ref[0, at, :], ref[1, at, :]], axis=1)


def two_halves(rows):
    return pltpu.VMEM((2, rows, LANES), F32)


def units_kernel(fc_in, gc_in, video_in, gloss_in, v_out, g_out, count_out, fc, gc, video, gloss, v_scr, g_scr, sems):
    pairs = ((fc_in, fc), (gc_in, gc), (video_in, video), (gloss_in, gloss))
    copies = [pltpu.make_async_copy(a, b, sems.at[i]) for i, (a, b) in enumerate(pairs)]
    for copy in copies:
        copy.start()
    for copy in copies:
        copy.wait()
    row = iota((8, LANES), 0)
    counts = jnp.zeros((8, LANES), jnp.int32)
    for c in range(OWN):
        counts = jnp.where(row == c, fc[c], jnp.where(row == OWN + c, gc[c], counts))
    count_out[...] = counts
    for count, raw, scr, tokens in ((fc, video, v_scr, FRAMES), (gc, gloss, g_scr, GLOSSES)):
        row, lane = iota((tokens, WIDTH), 0), iota((tokens, WIDTH), 1)
        for c in range(OWN):
            x = raw[c].astype(F32)
            mean_sq = jnp.mean(x * x, axis=-1, keepdims=True) + EPSILON
            unit = x * (lax.rsqrt(mean_sq) / math.sqrt(WIDTH))
            mark = jnp.where(lane == 0, MARK, 0.0)
            put(scr, pl.ds(c, tokens, stride=OWN), jnp.where(row < count[c], unit, mark))
    v = get(v_scr, pl.ds(0, VOWN)).astype(BF16)
    g = get(g_scr, pl.ds(0, GOWN)).astype(BF16)
    v_out[...] = v
    for i in range(NXY):
        g_out[i] = g


def diagonal_kernel(count_ref, v_ref, g_ref, dv, dg, logit_sum):
    def pick(count, which):
        return jnp.where(which == 0, count[0], jnp.where(which == 1, count[1], count[2]))

    fc = [count_ref[c : c + 1, 0:1] for c in range(OWN)]
    gc = [count_ref[OWN + c : OWN + c + 1, 0:1] for c in range(OWN)]
    v, g = v_ref[...], g_ref[0]
    shape = (VOWN, GOWN)
    r, q = iota(shape, 0), iota(shape, 1)
    rc, qc = lax.rem(r, OWN), lax.rem(q, OWN)
    valid = (rc == qc) & (lax.div(r, OWN) < pick(fc, rc)) & (lax.div(q, OWN) < pick(gc, qc))
    e = jnp.where(valid, jnp.exp2(nt(v, g) * EXP_SCALE), 0.0)
    r1, q1 = iota((VOWN, 1), 0), iota((1, GOWN), 1)
    rc1, qc1 = lax.rem(r1, OWN), lax.rem(q1, OWN)
    frames_r, glosses_r = pick(fc, rc1), pick(gc, rc1)
    frames_q, glosses_q = pick(fc, qc1), pick(gc, qc1)
    row_ok = lax.div(r1, OWN) < frames_r
    col_ok = lax.div(q1, OWN) < glosses_q
    frames_r, glosses_r = frames_r.astype(F32), glosses_r.astype(F32)
    frames_q, glosses_q = frames_q.astype(F32), glosses_q.astype(F32)
    rows = jnp.where(row_ok, jnp.sum(e, axis=1, keepdims=True), 1.0)
    cols = jnp.where(col_ok, jnp.sum(e, axis=0, keepdims=True), 1.0)
    by_row = jnp.where(row_ok, jnp.log(rows / glosses_r) / frames_r, 0.0)
    by_col = jnp.where(col_ok, jnp.log(cols / frames_q) / glosses_q, 0.0)
    total = jnp.sum(by_row, axis=0, keepdims=True) + jnp.sum(by_col, axis=1, keepdims=True)
    logit_sum[...] = jnp.broadcast_to(0.5 * total, (1, LANES))
    weight = -5.0 * e * (1.0 / (rows * frames_r) + 1.0 / (cols * glosses_q))
    dv[...] = nn(weight, g.astype(F32), precision=lax.Precision.HIGHEST)
    dg[...] = tn(weight, v.astype(F32), precision=lax.Precision.HIGHEST)


def exp_scores(v, g):
    return jnp.exp2(nt(v, g) * EXP_SCALE)


def forward_kernel(
    v_got, g_got, diag,
    v_hbm, g_hbm, row_hbm, col_hbm, e_out, r_out, c_out,
    v_out, g_out, row_out, col_out, v_scr, g_scr, frame_mask, gloss_mask, rows, cols, sems,
):
    results = ((v_out, v_hbm), (g_out, g_hbm), (row_out, row_hbm), (col_out, col_hbm))
    copies = [pltpu.make_async_copy(a, b, sems.at[i]) for i, (a, b) in enumerate(results)]
    put(v_scr, pl.ds(0, VROWS), v_got[...].astype(F32))
    for f in range(FRAMES):
        parts = [
            get(v_scr, pl.ds(k * NZ * VOWN + f * OWN + c, NZ, stride=VOWN)) for k in range(NCORE) for c in range(OWN)
        ]
        v_out[pl.ds(f * CLIPS_DEV, CLIPS_DEV), :] = jnp.concatenate(parts, axis=0).astype(BF16)
    copies[0].start()
    put(g_scr, pl.ds(0, NXY * GOWN), g_got[...].reshape(NXY * GOWN, WIDTH).astype(F32))
    pad = jnp.where(iota((LANES - TEXTS_DEV, WIDTH), 1) == 0, MARK, 0.0)
    for g in range(GLOSSES):
        parts = [get(g_scr, pl.ds(x * NY * GOWN + g * OWN + c, NY, stride=GOWN)) for x in range(NX) for c in range(OWN)]
        g_out[pl.ds(g * LANES, LANES), :] = jnp.concatenate(parts + [pad], axis=0).astype(BF16)

    copies[1].start()

    first = jnp.where(iota((WIDTH, LANES), 0) == 0, 1.0, 0.0).astype(BF16)
    frame_mask[...] = jnp.where(nn(v_out[...], first) < MARK_LIMIT, 1.0, 0.0)
    first_row = jnp.where(iota((16, WIDTH), 1) == 0, 1.0, 0.0).astype(BF16)
    for g in range(GLOSSES):
        gloss_mask[g] = jnp.where(nt(first_row, g_out[pl.ds(g * LANES, LANES), :])[0:8] < MARK_LIMIT, 1.0, 0.0)
    frames = jnp.zeros((CLIPS_DEV, LANES), F32)
    for f in range(FRAMES):
        frames = frames + frame_mask[pl.ds(f * CLIPS_DEV, CLIPS_DEV), :]
    glosses = gloss_mask[0]
    for g in range(1, GLOSSES):
        glosses = glosses + gloss_mask[g]
    glosses = jnp.maximum(glosses, 1.0)[0:1]

    rows[...] = jnp.zeros_like(rows)

    def two_glosses(p, _):
        e = exp_scores(v_out[...], g_out[pl.ds(pl.multiple_of(p * WIDTH, WIDTH), WIDTH), :])
        m0, m1 = gloss_mask[2 * p][0:1], gloss_mask[2 * p + 1][0:1]
        col0 = jnp.zeros((CLIPS_DEV, LANES), F32)
        col1 = jnp.zeros((CLIPS_DEV, LANES), F32)
        for f in range(FRAMES):
            at = pl.ds(f * CLIPS_DEV, CLIPS_DEV)
            block = e[f * CLIPS_DEV : (f + 1) * CLIPS_DEV]
            e0, e1 = block[:, :LANES], block[:, LANES:]
            mask = frame_mask[at, :]
            rows[at, :] = rows[at, :] + (e0 * m0 + e1 * m1)
            col0 = col0 + e0 * mask
            col1 = col1 + e1 * mask
        cols[2 * p] = col0
        cols[2 * p + 1] = col1
        return 0

    lax.fori_loop(0, PAIRS, two_glosses, 0)

    lane = iota((CLIPS_DEV, LANES), 1)
    real = lane < TEXTS_DEV
    video_part = jnp.zeros((CLIPS_DEV, LANES), F32)
    for f in range(FRAMES):
        at = pl.ds(f * CLIPS_DEV, CLIPS_DEV)
        mask = frame_mask[at, :]
        total = jnp.where(real, rows[at, :], 1.0)
        video_part = video_part + mask * jnp.log(total / glosses)
        row_out[at, :] = jnp.where(mask > 0.0, 1.0 / (total * frames), FAR)
    copies[2].start()
    gloss_part = jnp.zeros((CLIPS_DEV, LANES), F32)
    for g in range(GLOSSES):
        mask = gloss_mask[g][0:1]
        total = cols[g]
        gloss_part = gloss_part + mask * jnp.log(total / frames)
        col_out[g] = jnp.where(mask > 0.0, 1.0 / (total * glosses), FAR)
    copies[3].start()
    logits = 0.5 * (video_part / frames + gloss_part / glosses)
    e_pair = jnp.where(real, jnp.exp(logits), 0.0)
    e_out[...] = e_pair

    sums = jnp.sum(e_pair, axis=1, keepdims=True)
    across = lane == iota((CLIPS_DEV, LANES), 0)
    r_row = jnp.sum(jnp.where(across, jnp.broadcast_to(sums, (CLIPS_DEV, LANES)), 0.0), axis=0, keepdims=True)
    r_row = jnp.where(iota((1, LANES), 1) == CLIPS_DEV, diag[...], r_row)
    for i in range(NZC):
        r_out[i] = r_row
    c_out[...] = jnp.sum(e_pair, axis=0, keepdims=True)
    for copy in copies:
        copy.wait()


def weights_kernel(v_ref, g_ref, row_ref, col_ref, e_ref, p_out):
    e = exp_scores(v_ref[...], g_ref[...])
    scale = 2.5 * e_ref[...]
    col0, col1 = col_ref[0], col_ref[1]
    for f in range(FRAMES):
        at = pl.ds(f * CLIPS_DEV, CLIPS_DEV)
        block = e[f * CLIPS_DEV : (f + 1) * CLIPS_DEV]
        row = row_ref[at, :]
        w0 = scale * block[:, :LANES] * jnp.maximum(row + col0, 0.0)
        w1 = scale * block[:, LANES:] * jnp.maximum(row + col1, 0.0)
        p_out[0, at, :] = jnp.concatenate([w0, w1], axis=1).astype(BF16)

def added(got):
    total = got[0]
    for i in range(1, got.shape[0]):
        total = total + got[i]
    return total


def row_sums_kernel(r_got, c_part, c_out, r_out):
    r_row = added(r_got)
    r_out[...] = r_row
    lane = iota((1, LANES), 1)
    logs = jnp.where(lane < CLIPS_DEV, jnp.log(jnp.where(lane < CLIPS_DEV, r_row, 1.0)), 0.0)
    logs = logs - jnp.where(lane == CLIPS_DEV, 2.0 * r_row, 0.0)
    total = jnp.sum(logs, axis=1, keepdims=True)
    message = jnp.where(lane == TEXTS_DEV, total, c_part[...])
    for i in range(NXY):
        c_out[i] = message


def inverse_texts(c_row):
    real = iota((1, LANES), 1) < TEXTS_DEV
    inverse = jnp.where(real, 1.0 / jnp.where(real, c_row, 1.0), 0.0)
    return jnp.broadcast_to(column_of(inverse, LANES), (LANES, WIDTH))


def by_clip_kernel(r_ref, p_ref, v_ref, g_ref, out, av_out, both):
    step = pl.program_id(0)

    @pl.when(step == 0)
    def _():
        inverse = jnp.broadcast_to(1.0 / column_of(r_ref[...], CLIPS_DEV), (CLIPS_DEV, WIDTH))
        for f in range(FRAMES):
            at = pl.ds(f * CLIPS_DEV, CLIPS_DEV)
            v = v_ref[at, :]
            both[at, :WIDTH] = v
            both[at, WIDTH:] = (v.astype(F32) * inverse).astype(BF16)

    out[...] = tn(p_ref[0], both[...])
    part = nn(p_ref[0], g_ref[...])

    @pl.when(step == 0)
    def _():
        av_out[...] = part

    @pl.when(step > 0)
    def _():
        av_out[...] = av_out[...] + part


def gloss_send_kernel(c_got, by_clip, out, c_out, scr):
    step = pl.program_id(0)

    @pl.when(step == 0)
    def _():
        c_out[...] = added(c_got)

    col = inverse_texts(c_out[...])
    for k in range(GLOSSES // QUADS):
        at = pl.ds(k * LANES, LANES)
        block = by_clip[at, :WIDTH] * col + by_clip[at, WIDTH:]
        row = (step * (GLOSSES // QUADS) + k) * OWN
        for x in range(NX):
            for c in range(OWN):
                first = (x * OWN + c) * NY
                put(scr, pl.ds(x * NY * GOWN + row + c, NY, stride=GOWN), block[first : first + NY])

    @pl.when(step == QUADS - 1)
    def _():
        out[...] = get(scr, pl.ds(0, NXY * GOWN)).astype(BF16).reshape(NXY, GOWN, WIDTH)


def clip_send_kernel(c_got, r_ref, p_ref, g_ref, av_ref, mine, twin, c_row, total):
    step = pl.program_id(0)

    @pl.when(step == 0)
    def _():
        c_row[...] = added(c_got)

    col = inverse_texts(c_row[...])
    scaled = g_ref[...].astype(F32) * jnp.concatenate([col] * (GLOSSES // QUADS), axis=0)
    part = nn(p_ref[0], scaled.astype(BF16))

    @pl.when(step == 0)
    def _():
        total[...] = part

    @pl.when((step > 0) & (step < QUADS - 1))
    def _():
        total[...] = total[...] + part

    @pl.when(step == QUADS - 1)
    def _():
        core = lax.rem(lax.axis_index("inner"), NCORE)
        inverse = jnp.broadcast_to(1.0 / column_of(r_ref[...], CLIPS_DEV), (CLIPS_DEV, WIDTH))
        half = CLIPS_DEV // 2
        for pair in range(FRAMES // 2):
            others = []
            for f in (2 * pair, 2 * pair + 1):
                at = pl.ds(f * CLIPS_DEV, CLIPS_DEV)
                new = part[f * CLIPS_DEV : (f + 1) * CLIPS_DEV]
                block = av_ref[at, :] * inverse + (total[at, :] + new)
                low, high = block[:half], block[half:]
                mine[pl.ds(f * half, half), :] = jnp.where(core == 0, low, high)
                others.append(jnp.where(core == 0, high, low))
            twin[pl.ds(pair * CLIPS_DEV, CLIPS_DEV), :] = jnp.concatenate(others, axis=0).astype(BF16)
        real = iota((1, LANES), 1) < TEXTS_DEV
        logs = jnp.where(real, jnp.log(jnp.where(real, c_row[...], 1.0)), 0.0)
        extra = pieces(jnp.sum(logs, axis=1, keepdims=True))
        mine[pl.ds(FRAMES * half, EXTRA), :] = extra
        twin[pl.ds(FRAMES * half, EXTRA), :] = extra.astype(BF16)


def z_bits():
    z = lax.rem(lax.axis_index("outer"), NZ)
    return lax.rem(z, 2), lax.rem(lax.div(z, 2), 2), lax.div(z, 4)


def clip_rows_kernel(mine, got, keep, send, scr):
    step = 2 * NZ
    for i in range(VOWN // 2):
        at = pl.ds(i * step, step)
        two = mine[at, :] + got[at, :].astype(F32)
        for k in range(2):
            put(scr, pl.ds(2 * i + k, NZ, stride=VOWN), two[k * NZ : (k + 1) * NZ])
    bit = z_bits()[0]
    owners = NZ // 2
    for i in range(owners):
        at = pl.ds(i * VOWN, VOWN)
        keep[at, :] = get(scr, pl.ds(pl.multiple_of((owners * bit + i) * VOWN, VOWN), VOWN))
        send[at, :] = get(scr, pl.ds(pl.multiple_of((owners * (1 - bit) + i) * VOWN, VOWN), VOWN)).astype(BF16)
    extra = loss_rows(mine, got, NZ)
    keep[pl.ds(owners * VOWN, EXTRA), :] = extra
    send[pl.ds(owners * VOWN, EXTRA), :] = extra.astype(BF16)


def loss_rows(mine, got, owners):
    tail = pl.ds(owners * VOWN, EXTRA)
    return pieces(unpiece(mine[tail, :]) + unpiece(got[tail, :].astype(F32)))


def halve_kernel(which, mine, got, keep, send):
    bit = z_bits()[which]
    owners = NZ // 2 ** (which + 1)
    extra = loss_rows(mine, got, 2 * owners)
    for out, chosen in ((keep, bit), (send, 1 - bit)):
        half = pl.ds(pl.multiple_of(chosen * owners * VOWN, VOWN), owners * VOWN)
        out[pl.ds(0, owners * VOWN), :] = (mine[half, :] + got[half, :].astype(F32)).astype(out.dtype)
        out[pl.ds(owners * VOWN, EXTRA), :] = extra.astype(out.dtype)


def token_grads(total, scr, raw, out, tokens):
    put(scr, pl.ds(0, OWN * tokens), total)
    for c in range(OWN):
        x = raw[c].astype(F32)
        d = get(scr, pl.ds(c, tokens, stride=OWN))
        mean_sq = jnp.mean(x * x, axis=-1, keepdims=True) + EPSILON
        factor = lax.rsqrt(mean_sq) / math.sqrt(WIDTH)
        inner = jnp.sum(d * x, axis=-1, keepdims=True)
        out[c] = factor * d - factor * x * (inner / (WIDTH * mean_sq))


def video_grad_kernel(clips, mine, got, c_row, diag, video, out, loss, scr):
    at = pl.ds(0, VOWN)
    total = mine[at, :] + got[at, :].astype(F32)
    token_grads(total + diag[...], scr, video, out, FRAMES)
    row_part = c_row[:, TEXTS_DEV : TEXTS_DEV + 1]
    loss[...] = (unpiece(loss_rows(mine, got, 1)) + row_part) * (0.5 / clips)


def gloss_grad_kernel(got, diag, gloss, out, scr):
    total = got[0].astype(F32)
    for i in range(1, NXY):
        total = total + got[i].astype(F32)
    token_grads(total + diag[...], scr, gloss, out, GLOSSES)


def shape(*dims, dtype=F32):
    return jax.ShapeDtypeStruct(dims, dtype)


def on_device(clips, video, gloss, frame_count, gloss_count):
    vmem = pl.BlockSpec(memory_space=pltpu.VMEM)
    over_all = ("outer", "inner")

    def to_core(a):
        return lax.ppermute(a, "inner", [(i, i ^ 1) for i in range(lax.axis_size("inner"))])

    def to_z(a, mask):
        return lax.ppermute(a, "outer", [(i, i ^ mask) for i in range(lax.axis_size("outer"))])

    def exchanged(a, groups):
        return lax.all_to_all(a, over_all, 0, 0, axis_index_groups=groups, tiled=True)

    def gathered(a, groups):
        return lax.all_gather(a, over_all, axis=0, axis_index_groups=groups, tiled=True)

    def in_hbm(*arrays):
        return [pltpu.with_memory_space_constraint(a, pltpu.HBM) for a in arrays]

    with jax.named_scope("unit_tokens"):
        v_own, g_own, counts = pl.pallas_call(
            units_kernel,
            in_specs=[pl.BlockSpec(memory_space=pltpu.HBM)] * 4,
            out_shape=(
                shape(VOWN, WIDTH, dtype=BF16),
                shape(NXY, GOWN, WIDTH, dtype=BF16),
                shape(8, LANES, dtype=jnp.int32),
            ),
            scratch_shapes=[
                pltpu.SMEM((OWN,), jnp.int32),
                pltpu.SMEM((OWN,), jnp.int32),
                pltpu.VMEM((OWN, FRAMES, WIDTH), BF16),
                pltpu.VMEM((OWN, GLOSSES, WIDTH), BF16),
                two_halves(VOWN),
                two_halves(GOWN),
                pltpu.SemaphoreType.DMA((4,)),
            ],
            compiler_params=params(),
            cost_estimate=cost(2e5, 7e5),
        )(*in_hbm(frame_count, gloss_count, video, gloss))

    with jax.named_scope("gather"):
        g_got = exchanged(g_own, XY_GROUPS)
        v_got = v_own
        for mask in (4, 2, 1):
            v_got = gathered(v_got, z_pairs(mask))
        v_got = gathered(v_got, CORE_GROUPS)

    def first(rows):
        return pl.BlockSpec((1, rows, WIDTH), lambda i: (0, 0, 0))

    def whole(*dims):
        return pl.BlockSpec(dims, lambda i: (0,) * len(dims))

    with jax.named_scope("diagonal"):
        dv_diag, dg_diag, logit_sum = pl.pallas_call(
            diagonal_kernel,
            grid=(1,),
            in_specs=[whole(8, LANES), whole(VOWN, WIDTH), first(GOWN)],
            out_specs=(whole(VOWN, WIDTH), whole(GOWN, WIDTH), whole(1, LANES)),
            out_shape=(shape(VOWN, WIDTH), shape(GOWN, WIDTH), shape(1, LANES)),
            compiler_params=params(),
            cost_estimate=cost(2e7, 3e5),
        )(counts, v_own, g_own)

    with jax.named_scope("forward"):
        v_all, g_all, row_inv, col_inv, e_pair, r_part, c_part = pl.pallas_call(
            forward_kernel,
            in_specs=[vmem] * 3,
            out_specs=[pl.BlockSpec(memory_space=pltpu.HBM)] * 4 + [vmem] * 3,
            out_shape=(
                pltpu.HBM((VROWS, WIDTH), BF16),
                pltpu.HBM((GROWS, WIDTH), BF16),
                pltpu.HBM((VROWS, LANES), F32),
                pltpu.HBM((GLOSSES, CLIPS_DEV, LANES), F32),
                shape(CLIPS_DEV, LANES),
                shape(NZC, 1, LANES),
                shape(1, LANES),
            ),
            scratch_shapes=[
                pltpu.VMEM((VROWS, WIDTH), BF16),
                pltpu.VMEM((GROWS, WIDTH), BF16),
                pltpu.VMEM((VROWS, LANES), F32),
                pltpu.VMEM((GLOSSES, CLIPS_DEV, LANES), F32),
                two_halves(VROWS),
                two_halves(NXY * GOWN),
                pltpu.VMEM((VROWS, LANES), F32),
                pltpu.VMEM((GLOSSES, 8, LANES), F32),
                pltpu.VMEM((VROWS, LANES), F32),
                pltpu.VMEM((GLOSSES, CLIPS_DEV, LANES), F32),
                pltpu.SemaphoreType.DMA((4,)),
            ],
            compiler_params=params(),
            cost_estimate=cost(2 * VROWS * GROWS * WIDTH, 8e6, VROWS * GROWS),
        )(v_got, g_got, logit_sum)

    with jax.named_scope("row_sums"):
        c_send, r_row = pl.pallas_call(
            row_sums_kernel,
            in_specs=[vmem] * 2,
            out_shape=(shape(NXY, 1, LANES), shape(1, LANES)),
            compiler_params=params(),
            cost_estimate=cost(1e5, 3e5),
        )(exchanged(r_part, ZC_GROUPS), c_part)
    with jax.named_scope("column_sums"):
        c_got = exchanged(c_send, XY_GROUPS)

    def halves(rows):
        return pl.BlockSpec((rows, WIDTH), lambda i: (i, 0))

    p_spec = pl.BlockSpec((1, VROWS, 2 * WIDTH), lambda i: (i, 0, 0))
    with jax.named_scope("weights"):
        weights = pl.pallas_call(
            weights_kernel,
            grid=(PAIRS,),
            in_specs=[
                whole(VROWS, WIDTH),
                halves(2 * LANES),
                whole(VROWS, LANES),
                pl.BlockSpec((2, CLIPS_DEV, LANES), lambda i: (i, 0, 0)),
                whole(CLIPS_DEV, LANES),
            ],
            out_specs=pl.BlockSpec((1, VROWS, WIDTH), lambda i: (i // 2, 0, i % 2)),
            out_shape=pltpu.HBM((QUADS, VROWS, 2 * WIDTH), BF16),
            compiler_params=params(),
            cost_estimate=cost(2 * VROWS * GROWS * WIDTH, 12e6, VROWS * GROWS),
        )(*in_hbm(v_all, g_all, row_inv, col_inv), e_pair)

    with jax.named_scope("by_clip"):
        by_clip, av = pl.pallas_call(
            by_clip_kernel,
            grid=(QUADS,),
            in_specs=[whole(1, LANES), p_spec, whole(VROWS, WIDTH), halves(4 * LANES)],
            out_specs=(pl.BlockSpec((4 * LANES, 2 * WIDTH), lambda i: (i, 0)), whole(VROWS, WIDTH)),
            out_shape=(pltpu.HBM((GROWS, 2 * WIDTH), F32), shape(VROWS, WIDTH)),
            scratch_shapes=[pltpu.VMEM((VROWS, 2 * WIDTH), BF16)],
            compiler_params=params(),
            cost_estimate=cost(6 * VROWS * GROWS * WIDTH, 14e6),
        )(r_row, *in_hbm(weights, v_all, g_all))

    with jax.named_scope("clip_send"):
        v_rows = FRAMES * CLIPS_DEV // 2 + EXTRA
        mine, twin = pl.pallas_call(
            clip_send_kernel,
            grid=(QUADS,),
            in_specs=[whole(NXY, 1, LANES), whole(1, LANES), p_spec, halves(4 * LANES), whole(VROWS, WIDTH)],
            out_specs=(whole(v_rows, WIDTH), whole(v_rows, WIDTH)),
            out_shape=(shape(v_rows, WIDTH), shape(v_rows, WIDTH, dtype=BF16)),
            scratch_shapes=[pltpu.VMEM((1, LANES), F32), pltpu.VMEM((VROWS, WIDTH), F32)],
            compiler_params=params(),
            cost_estimate=cost(2 * VROWS * GROWS * WIDTH, 1e7),
        )(c_got, r_row, *in_hbm(weights, g_all), av)

    def kept_and_sent(owners):
        rows = owners * VOWN + EXTRA
        return (shape(rows, WIDTH), shape(rows, WIDTH, dtype=BF16))

    with jax.named_scope("clips_by_core"):
        mine, sent = pl.pallas_call(
            clip_rows_kernel,
            in_specs=[vmem] * 2,
            out_shape=kept_and_sent(NZ // 2),
            scratch_shapes=[two_halves(NZ * VOWN)],
            compiler_params=params(),
            cost_estimate=cost(1e6, 2e6),
        )(mine, to_core(twin))
    with jax.named_scope("gloss_send"):
        sent, c_ready = lax.optimization_barrier((sent, c_got))
        dg_send, c_row = pl.pallas_call(
            gloss_send_kernel,
            grid=(QUADS,),
            in_specs=[whole(NXY, 1, LANES), pl.BlockSpec((4 * LANES, 2 * WIDTH), lambda i: (i, 0))],
            out_specs=(whole(NXY, GOWN, WIDTH), whole(1, LANES)),
            out_shape=(shape(NXY, GOWN, WIDTH, dtype=BF16), shape(1, LANES)),
            scratch_shapes=[two_halves(NXY * GOWN)],
            compiler_params=params(),
            cost_estimate=cost(2e6, 5e6),
        )(c_ready, *in_hbm(by_clip))
        dg_got = exchanged(dg_send, XY_GROUPS)

    for which, scope in ((1, "clips_by_z1"), (2, "clips_by_z2")):
        with jax.named_scope(scope):
            mine, sent = pl.pallas_call(
                functools.partial(halve_kernel, which),
                in_specs=[vmem] * 2,
                out_shape=kept_and_sent(NZ // 2 ** (which + 1)),
                compiler_params=params(),
                cost_estimate=cost(1e6, 1e6),
            )(mine, to_z(sent, 2 ** (which - 1)))

    with jax.named_scope("video_grad"):
        grad_video, loss = pl.pallas_call(
            functools.partial(video_grad_kernel, clips),
            in_specs=[vmem] * 5,
            out_shape=(shape(OWN, FRAMES, WIDTH), shape(1, 1)),
            scratch_shapes=[two_halves(VOWN)],
            compiler_params=params(),
            cost_estimate=cost(1e6, 1e6),
        )(mine, to_z(sent, NZ // 2), c_row, dv_diag, video)
    with jax.named_scope("gloss_grad"):
        grad_gloss = pl.pallas_call(
            gloss_grad_kernel,
            in_specs=[vmem] * 3,
            out_shape=shape(OWN, GLOSSES, WIDTH),
            scratch_shapes=[two_halves(GOWN)],
            compiler_params=params(),
            cost_estimate=cost(1e6, 1e6),
        )(dg_got, dg_diag, gloss)
    return loss.reshape(()), grad_video, grad_gloss


def solution(mesh):
    clips = OWN * mesh.shape["outer"] * mesh.shape["inner"]
    over_all = ("outer", "inner")
    tokens, counts = P(over_all, None, None), P(over_all)
    return jax.shard_map(
        functools.partial(on_device, clips),
        mesh=mesh,
        in_specs=(tokens, tokens, counts, counts),
        out_specs=(P(), tokens, tokens),
        check_vma=False,
    )
```

```python
import functools
import math

import jax
import jax.numpy as jnp
from jax import lax
from jax.experimental import pallas as pl
from jax.experimental.pallas import tpu as pltpu
from jax.sharding import PartitionSpec as P

F32 = jnp.float32
BF16 = jnp.bfloat16
EPSILON = 1e-06
EXP_SCALE = 10.0 * math.log2(math.e)
MARK = 2.0
MARK_LIMIT = 1.5
FAR = -1e30

NZ, NY, NX, NCORE = 8, 8, 4, 2
OWN = 3
FRAMES, GLOSSES, WIDTH = 32, 16, 256
CLIPS_DEV = NZ * NCORE * OWN
TEXTS_DEV = NY * NX * OWN
LANES = 128
VROWS = FRAMES * CLIPS_DEV
GROWS = GLOSSES * LANES
VOWN = FRAMES * OWN
GOWN = GLOSSES * OWN
EXTRA = 16
PAIRS = GLOSSES // 2
QUADS = GLOSSES // 4
NXY, NZC = NX * NY, NZ * NCORE

def flat(x, z, y, core):
    return ((x % 2) * NZ + z) * 32 + (x // 2) * 16 + 2 * y + core


def z_groups(masks):
    return [
        [flat(x, z ^ mask, y, c) for mask in masks]
        for x in range(NX)
        for y in range(NY)
        for c in range(NCORE)
        for z in range(NZ)
        if not z & masks[-1] and not z & masks[len(masks) // 2]
    ]


Z_QUADS, Z_PAIRS = z_groups((0, 2, 4, 6)), z_groups((0, 1))
CORE_GROUPS = [[flat(x, z, y, c) for c in range(NCORE)] for x in range(NX) for y in range(NY) for z in range(NZ)]
XY_GROUPS = [[flat(x, z, y, c) for x in range(NX) for y in range(NY)] for z in range(NZ) for c in range(NCORE)]
ZC_GROUPS = [[flat(x, z, y, c) for c in range(NCORE) for z in range(NZ)] for x in range(NX) for y in range(NY)]


def params(limit_mb=16):
    return pltpu.CompilerParams(vmem_limit_bytes=limit_mb * 1024 * 1024)


def cost(flops, nbytes, trans=0):
    return pl.CostEstimate(flops=int(flops), bytes_accessed=int(nbytes), transcendentals=int(trans))


def iota(shape, dim):
    return lax.broadcasted_iota(jnp.int32, shape, dim)


def nt(a, b, **kw):
    return lax.dot_general(a, b, (((1,), (1,)), ((), ())), preferred_element_type=F32, **kw)


def nn(a, b, **kw):
    return lax.dot_general(a, b, (((1,), (0,)), ((), ())), preferred_element_type=F32, **kw)


def tn(a, b, **kw):
    return lax.dot_general(a, b, (((0,), (0,)), ((), ())), preferred_element_type=F32, **kw)


def column_of(row, n):
    eye = iota((n, LANES), 0) == iota((n, LANES), 1)
    return jnp.sum(jnp.where(eye, jnp.broadcast_to(row, (n, LANES)), 0.0), axis=1, keepdims=True)


def pieces(value):
    lane = iota((EXTRA, WIDTH), 1)
    full = jnp.broadcast_to(value, (EXTRA, WIDTH))
    hi = full.astype(BF16).astype(F32)
    mid = (full - hi).astype(BF16).astype(F32)
    low = (full - hi - mid).astype(BF16).astype(F32)
    return jnp.where(lane == 0, hi, jnp.where(lane == 1, mid, jnp.where(lane == 2, low, 0.0)))


def unpiece(block):
    mine = (iota((EXTRA, WIDTH), 0) == 0) & (iota((EXTRA, WIDTH), 1) < 3)
    return jnp.sum(jnp.where(mine, block, 0.0), keepdims=True).reshape(1, 1)


def put(ref, at, value):
    ref[0, at, :] = value[:, :LANES]
    ref[1, at, :] = value[:, LANES:]


def get(ref, at):
    return jnp.concatenate([ref[0, at, :], ref[1, at, :]], axis=1)


def two_halves(rows):
    return pltpu.VMEM((2, rows, LANES), F32)


def units_kernel(fc_in, gc_in, video_in, gloss_in, v_out, g_out, count_out, fc, gc, video, gloss, v_scr, g_scr, sems):
    pairs = ((fc_in, fc), (gc_in, gc), (video_in, video), (gloss_in, gloss))
    copies = [pltpu.make_async_copy(a, b, sems.at[i]) for i, (a, b) in enumerate(pairs)]
    for copy in copies:
        copy.start()
    for copy in copies:
        copy.wait()
    row = iota((8, LANES), 0)
    counts = jnp.zeros((8, LANES), jnp.int32)
    for c in range(OWN):
        counts = jnp.where(row == c, fc[c], jnp.where(row == OWN + c, gc[c], counts))
    count_out[...] = counts
    for count, raw, scr, tokens in ((fc, video, v_scr, FRAMES), (gc, gloss, g_scr, GLOSSES)):
        row, lane = iota((tokens, WIDTH), 0), iota((tokens, WIDTH), 1)
        for c in range(OWN):
            x = raw[c].astype(F32)
            mean_sq = jnp.mean(x * x, axis=-1, keepdims=True) + EPSILON
            unit = x * (lax.rsqrt(mean_sq) / math.sqrt(WIDTH))
            mark = jnp.where(lane == 0, MARK, 0.0)
            put(scr, pl.ds(c, tokens, stride=OWN), jnp.where(row < count[c], unit, mark))
    v = get(v_scr, pl.ds(0, VOWN)).astype(BF16)
    g = get(g_scr, pl.ds(0, GOWN)).astype(BF16)
    v_out[...] = v
    for i in range(NXY):
        g_out[i] = g


def diagonal_kernel(count_ref, v_ref, g_ref, dv, dg, logit_sum):
    def pick(count, which):
        return jnp.where(which == 0, count[0], jnp.where(which == 1, count[1], count[2]))

    fc = [count_ref[c : c + 1, 0:1] for c in range(OWN)]
    gc = [count_ref[OWN + c : OWN + c + 1, 0:1] for c in range(OWN)]
    v, g = v_ref[...], g_ref[0]
    shape = (VOWN, GOWN)
    r, q = iota(shape, 0), iota(shape, 1)
    rc, qc = lax.rem(r, OWN), lax.rem(q, OWN)
    valid = (rc == qc) & (lax.div(r, OWN) < pick(fc, rc)) & (lax.div(q, OWN) < pick(gc, qc))
    e = jnp.where(valid, jnp.exp2(nt(v, g) * EXP_SCALE), 0.0)
    r1, q1 = iota((VOWN, 1), 0), iota((1, GOWN), 1)
    rc1, qc1 = lax.rem(r1, OWN), lax.rem(q1, OWN)
    frames_r, glosses_r = pick(fc, rc1), pick(gc, rc1)
    frames_q, glosses_q = pick(fc, qc1), pick(gc, qc1)
    row_ok = lax.div(r1, OWN) < frames_r
    col_ok = lax.div(q1, OWN) < glosses_q
    frames_r, glosses_r = frames_r.astype(F32), glosses_r.astype(F32)
    frames_q, glosses_q = frames_q.astype(F32), glosses_q.astype(F32)
    rows = jnp.where(row_ok, jnp.sum(e, axis=1, keepdims=True), 1.0)
    cols = jnp.where(col_ok, jnp.sum(e, axis=0, keepdims=True), 1.0)
    by_row = jnp.where(row_ok, jnp.log(rows / glosses_r) / frames_r, 0.0)
    by_col = jnp.where(col_ok, jnp.log(cols / frames_q) / glosses_q, 0.0)
    total = jnp.sum(by_row, axis=0, keepdims=True) + jnp.sum(by_col, axis=1, keepdims=True)
    logit_sum[...] = jnp.broadcast_to(0.5 * total, (1, LANES))
    weight = -5.0 * e * (1.0 / (rows * frames_r) + 1.0 / (cols * glosses_q))
    dv[...] = nn(weight, g.astype(F32), precision=lax.Precision.HIGHEST)
    dg[...] = tn(weight, v.astype(F32), precision=lax.Precision.HIGHEST)


def exp_scores(v, g):
    return jnp.exp2(nt(v, g) * EXP_SCALE)


def forward_kernel(
    v_got, g_got, diag,
    v_hbm, g_hbm, row_hbm, col_hbm, e_out, r_out, c_out,
    v_out, g_out, row_out, col_out, v_scr, g_scr, frame_mask, gloss_mask, rows, cols, sems,
):
    results = ((v_out, v_hbm), (g_out, g_hbm), (row_out, row_hbm), (col_out, col_hbm))
    copies = [pltpu.make_async_copy(a, b, sems.at[i]) for i, (a, b) in enumerate(results)]
    put(v_scr, pl.ds(0, VROWS), v_got[...].astype(F32))
    for f in range(FRAMES):
        parts = [
            get(v_scr, pl.ds(k * NZ * VOWN + f * OWN + c, NZ, stride=VOWN)) for k in range(NCORE) for c in range(OWN)
        ]
        v_out[pl.ds(f * CLIPS_DEV, CLIPS_DEV), :] = jnp.concatenate(parts, axis=0).astype(BF16)
    copies[0].start()
    put(g_scr, pl.ds(0, NXY * GOWN), g_got[...].reshape(NXY * GOWN, WIDTH).astype(F32))
    pad = jnp.where(iota((LANES - TEXTS_DEV, WIDTH), 1) == 0, MARK, 0.0)
    for g in range(GLOSSES):
        parts = [get(g_scr, pl.ds(x * NY * GOWN + g * OWN + c, NY, stride=GOWN)) for x in range(NX) for c in range(OWN)]
        g_out[pl.ds(g * LANES, LANES), :] = jnp.concatenate(parts + [pad], axis=0).astype(BF16)

    copies[1].start()

    first = jnp.where(iota((WIDTH, LANES), 0) == 0, 1.0, 0.0).astype(BF16)
    frame_mask[...] = jnp.where(nn(v_out[...], first) < MARK_LIMIT, 1.0, 0.0)
    first_row = jnp.where(iota((16, WIDTH), 1) == 0, 1.0, 0.0).astype(BF16)
    for g in range(GLOSSES):
        gloss_mask[g] = jnp.where(nt(first_row, g_out[pl.ds(g * LANES, LANES), :])[0:8] < MARK_LIMIT, 1.0, 0.0)
    frames = jnp.zeros((CLIPS_DEV, LANES), F32)
    for f in range(FRAMES):
        frames = frames + frame_mask[pl.ds(f * CLIPS_DEV, CLIPS_DEV), :]
    glosses = gloss_mask[0]
    for g in range(1, GLOSSES):
        glosses = glosses + gloss_mask[g]
    glosses = jnp.maximum(glosses, 1.0)[0:1]

    rows[...] = jnp.zeros_like(rows)

    def two_glosses(p, _):
        e = exp_scores(v_out[...], g_out[pl.ds(pl.multiple_of(p * WIDTH, WIDTH), WIDTH), :])
        m0, m1 = gloss_mask[2 * p][0:1], gloss_mask[2 * p + 1][0:1]
        col0 = jnp.zeros((CLIPS_DEV, LANES), F32)
        col1 = jnp.zeros((CLIPS_DEV, LANES), F32)
        for f in range(FRAMES):
            at = pl.ds(f * CLIPS_DEV, CLIPS_DEV)
            block = e[f * CLIPS_DEV : (f + 1) * CLIPS_DEV]
            e0, e1 = block[:, :LANES], block[:, LANES:]
            mask = frame_mask[at, :]
            rows[at, :] = rows[at, :] + (e0 * m0 + e1 * m1)
            col0 = col0 + e0 * mask
            col1 = col1 + e1 * mask
        cols[2 * p] = col0
        cols[2 * p + 1] = col1
        return 0

    lax.fori_loop(0, PAIRS, two_glosses, 0)

    lane = iota((CLIPS_DEV, LANES), 1)
    real = lane < TEXTS_DEV
    video_part = jnp.zeros((CLIPS_DEV, LANES), F32)
    for f in range(FRAMES):
        at = pl.ds(f * CLIPS_DEV, CLIPS_DEV)
        mask = frame_mask[at, :]
        total = jnp.where(real, rows[at, :], 1.0)
        video_part = video_part + mask * jnp.log(total / glosses)
        row_out[at, :] = jnp.where(mask > 0.0, 1.0 / (total * frames), FAR)
    copies[2].start()
    gloss_part = jnp.zeros((CLIPS_DEV, LANES), F32)
    for g in range(GLOSSES):
        mask = gloss_mask[g][0:1]
        total = cols[g]
        gloss_part = gloss_part + mask * jnp.log(total / frames)
        col_out[g] = jnp.where(mask > 0.0, 1.0 / (total * glosses), FAR)
    copies[3].start()
    logits = 0.5 * (video_part / frames + gloss_part / glosses)
    e_pair = jnp.where(real, jnp.exp(logits), 0.0)
    e_out[...] = e_pair

    sums = jnp.sum(e_pair, axis=1, keepdims=True)
    across = lane == iota((CLIPS_DEV, LANES), 0)
    r_row = jnp.sum(jnp.where(across, jnp.broadcast_to(sums, (CLIPS_DEV, LANES)), 0.0), axis=0, keepdims=True)
    r_row = jnp.where(iota((1, LANES), 1) == CLIPS_DEV, diag[...], r_row)
    for i in range(NZC):
        r_out[i] = r_row
    c_out[...] = jnp.sum(e_pair, axis=0, keepdims=True)
    for copy in copies:
        copy.wait()


def weights_kernel(v_ref, g_ref, row_ref, col_ref, e_ref, p_out):
    e = exp_scores(v_ref[...], g_ref[...])
    scale = 2.5 * e_ref[...]
    col0, col1 = col_ref[0], col_ref[1]
    for f in range(FRAMES):
        at = pl.ds(f * CLIPS_DEV, CLIPS_DEV)
        block = e[f * CLIPS_DEV : (f + 1) * CLIPS_DEV]
        row = row_ref[at, :]
        w0 = scale * block[:, :LANES] * jnp.maximum(row + col0, 0.0)
        w1 = scale * block[:, LANES:] * jnp.maximum(row + col1, 0.0)
        p_out[0, at, :] = jnp.concatenate([w0, w1], axis=1).astype(BF16)

def added(got):
    total = got[0]
    for i in range(1, got.shape[0]):
        total = total + got[i]
    return total


def row_sums_kernel(r_got, c_part, c_out, r_out):
    r_row = added(r_got)
    r_out[...] = r_row
    lane = iota((1, LANES), 1)
    logs = jnp.where(lane < CLIPS_DEV, jnp.log(jnp.where(lane < CLIPS_DEV, r_row, 1.0)), 0.0)
    logs = logs - jnp.where(lane == CLIPS_DEV, 2.0 * r_row, 0.0)
    total = jnp.sum(logs, axis=1, keepdims=True)
    message = jnp.where(lane == TEXTS_DEV, total, c_part[...])
    for i in range(NXY):
        c_out[i] = message


def inverse_texts(c_row):
    real = iota((1, LANES), 1) < TEXTS_DEV
    inverse = jnp.where(real, 1.0 / jnp.where(real, c_row, 1.0), 0.0)
    return jnp.broadcast_to(column_of(inverse, LANES), (LANES, WIDTH))


def by_clip_kernel(r_ref, p_ref, v_ref, g_ref, out, av_out, both):
    step = pl.program_id(0)

    @pl.when(step == 0)
    def _():
        inverse = jnp.broadcast_to(1.0 / column_of(r_ref[...], CLIPS_DEV), (CLIPS_DEV, WIDTH))
        for f in range(FRAMES):
            at = pl.ds(f * CLIPS_DEV, CLIPS_DEV)
            v = v_ref[at, :]
            both[at, :WIDTH] = v
            both[at, WIDTH:] = (v.astype(F32) * inverse).astype(BF16)

    out[...] = tn(p_ref[0], both[...])
    part = nn(p_ref[0], g_ref[...])

    @pl.when(step == 0)
    def _():
        av_out[...] = part

    @pl.when(step > 0)
    def _():
        av_out[...] = av_out[...] + part


def gloss_send_kernel(c_got, by_clip, out, c_out, scr):
    step = pl.program_id(0)

    @pl.when(step == 0)
    def _():
        c_out[...] = added(c_got)

    col = inverse_texts(c_out[...])
    for k in range(GLOSSES // QUADS):
        at = pl.ds(k * LANES, LANES)
        block = by_clip[at, :WIDTH] * col + by_clip[at, WIDTH:]
        row = (step * (GLOSSES // QUADS) + k) * OWN
        for x in range(NX):
            for c in range(OWN):
                first = (x * OWN + c) * NY
                put(scr, pl.ds(x * NY * GOWN + row + c, NY, stride=GOWN), block[first : first + NY])

    @pl.when(step == QUADS - 1)
    def _():
        out[...] = get(scr, pl.ds(0, NXY * GOWN)).astype(BF16).reshape(NXY, GOWN, WIDTH)


def clip_send_kernel(c_got, r_ref, p_ref, g_ref, av_ref, mine, twin, c_row, total):
    step = pl.program_id(0)

    @pl.when(step == 0)
    def _():
        c_row[...] = added(c_got)

    col = inverse_texts(c_row[...])
    scaled = g_ref[...].astype(F32) * jnp.concatenate([col] * (GLOSSES // QUADS), axis=0)
    part = nn(p_ref[0], scaled.astype(BF16))

    @pl.when(step == 0)
    def _():
        total[...] = part

    @pl.when((step > 0) & (step < QUADS - 1))
    def _():
        total[...] = total[...] + part

    @pl.when(step == QUADS - 1)
    def _():
        core = lax.rem(lax.axis_index("inner"), NCORE)
        inverse = jnp.broadcast_to(1.0 / column_of(r_ref[...], CLIPS_DEV), (CLIPS_DEV, WIDTH))
        half = CLIPS_DEV // 2
        for pair in range(FRAMES // 2):
            others = []
            for f in (2 * pair, 2 * pair + 1):
                at = pl.ds(f * CLIPS_DEV, CLIPS_DEV)
                new = part[f * CLIPS_DEV : (f + 1) * CLIPS_DEV]
                block = av_ref[at, :] * inverse + (total[at, :] + new)
                low, high = block[:half], block[half:]
                mine[pl.ds(f * half, half), :] = jnp.where(core == 0, low, high)
                others.append(jnp.where(core == 0, high, low))
            twin[pl.ds(pair * CLIPS_DEV, CLIPS_DEV), :] = jnp.concatenate(others, axis=0).astype(BF16)
        real = iota((1, LANES), 1) < TEXTS_DEV
        logs = jnp.where(real, jnp.log(jnp.where(real, c_row[...], 1.0)), 0.0)
        extra = pieces(jnp.sum(logs, axis=1, keepdims=True))
        mine[pl.ds(FRAMES * half, EXTRA), :] = extra
        twin[pl.ds(FRAMES * half, EXTRA), :] = extra.astype(BF16)


def own_z():
    return lax.rem(lax.axis_index("outer"), NZ)


def clip_rows_kernel(mine, got, keep, send, scr):
    step = 2 * NZ
    for i in range(VOWN // 2):
        at = pl.ds(i * step, step)
        two = mine[at, :] + got[at, :].astype(F32)
        for k in range(2):
            put(scr, pl.ds(2 * i + k, NZ, stride=VOWN), two[k * NZ : (k + 1) * NZ])
    bit = lax.rem(own_z(), 2)
    owners = NZ // 2
    for i in range(owners):
        at = pl.ds(i * VOWN, VOWN)
        keep[at, :] = get(scr, pl.ds(pl.multiple_of((owners * bit + i) * VOWN, VOWN), VOWN))
        send[at, :] = get(scr, pl.ds(pl.multiple_of((owners * (1 - bit) + i) * VOWN, VOWN), VOWN)).astype(BF16)
    extra = loss_rows(mine, got, NZ)
    keep[pl.ds(owners * VOWN, EXTRA), :] = extra
    send[pl.ds(owners * VOWN, EXTRA), :] = extra.astype(BF16)


def loss_rows(mine, got, owners):
    tail = pl.ds(owners * VOWN, EXTRA)
    return pieces(unpiece(mine[tail, :]) + unpiece(got[tail, :].astype(F32)))


def quarter_kernel(mine, got, keep, *sends):
    own = lax.div(own_z(), 2)
    extra = loss_rows(mine, got, NZ // 2)
    for out, owner in zip((keep, *sends), (own, own ^ 1, own ^ 2, own ^ 3), strict=True):
        at = pl.ds(pl.multiple_of(owner * VOWN, VOWN), VOWN)
        out[pl.ds(0, VOWN), :] = (mine[at, :] + got[at, :].astype(F32)).astype(out.dtype)
        out[pl.ds(VOWN, EXTRA), :] = extra.astype(out.dtype)


def token_grads(total, scr, raw, out, tokens):
    put(scr, pl.ds(0, OWN * tokens), total)
    for c in range(OWN):
        x = raw[c].astype(F32)
        d = get(scr, pl.ds(c, tokens, stride=OWN))
        mean_sq = jnp.mean(x * x, axis=-1, keepdims=True) + EPSILON
        factor = lax.rsqrt(mean_sq) / math.sqrt(WIDTH)
        inner = jnp.sum(d * x, axis=-1, keepdims=True)
        out[c] = factor * d - factor * x * (inner / (WIDTH * mean_sq))


def video_grad_kernel(clips, mine, got1, got2, got3, c_row, diag, video, out, loss, scr):
    at = pl.ds(0, VOWN)
    total = mine[at, :]
    for got in (got1, got2, got3):
        total = total + got[at, :].astype(F32)
    token_grads(total + diag[...], scr, video, out, FRAMES)
    row_part = c_row[:, TEXTS_DEV : TEXTS_DEV + 1]
    tail = pl.ds(VOWN, EXTRA)
    near = unpiece(mine[tail, :]) + unpiece(got1[tail, :].astype(F32))
    far = unpiece(got2[tail, :].astype(F32)) + unpiece(got3[tail, :].astype(F32))
    loss[...] = (near + far + row_part) * (0.5 / clips)


def gloss_grad_kernel(got, diag, gloss, out, scr):
    total = got[0].astype(F32)
    for i in range(1, NXY):
        total = total + got[i].astype(F32)
    token_grads(total + diag[...], scr, gloss, out, GLOSSES)


def shape(*dims, dtype=F32):
    return jax.ShapeDtypeStruct(dims, dtype)


def on_device(clips, video, gloss, frame_count, gloss_count):
    vmem = pl.BlockSpec(memory_space=pltpu.VMEM)
    over_all = ("outer", "inner")

    def to_core(a):
        return lax.ppermute(a, "inner", [(i, i ^ 1) for i in range(lax.axis_size("inner"))])

    def to_z(a, mask):
        return lax.ppermute(a, "outer", [(i, i ^ mask) for i in range(lax.axis_size("outer"))])

    def exchanged(a, groups):
        return lax.all_to_all(a, over_all, 0, 0, axis_index_groups=groups, tiled=True)

    def gathered(a, groups):
        return lax.all_gather(a, over_all, axis=0, axis_index_groups=groups, tiled=True)

    def in_hbm(*arrays):
        return [pltpu.with_memory_space_constraint(a, pltpu.HBM) for a in arrays]

    with jax.named_scope("unit_tokens"):
        v_own, g_own, counts = pl.pallas_call(
            units_kernel,
            in_specs=[pl.BlockSpec(memory_space=pltpu.HBM)] * 4,
            out_shape=(
                shape(VOWN, WIDTH, dtype=BF16),
                shape(NXY, GOWN, WIDTH, dtype=BF16),
                shape(8, LANES, dtype=jnp.int32),
            ),
            scratch_shapes=[
                pltpu.SMEM((OWN,), jnp.int32),
                pltpu.SMEM((OWN,), jnp.int32),
                pltpu.VMEM((OWN, FRAMES, WIDTH), BF16),
                pltpu.VMEM((OWN, GLOSSES, WIDTH), BF16),
                two_halves(VOWN),
                two_halves(GOWN),
                pltpu.SemaphoreType.DMA((4,)),
            ],
            compiler_params=params(),
            cost_estimate=cost(2e5, 7e5),
        )(*in_hbm(frame_count, gloss_count, video, gloss))

    with jax.named_scope("gather"):
        g_got = exchanged(g_own, XY_GROUPS)
        v_got = gathered(gathered(v_own, Z_QUADS), Z_PAIRS)
        v_got = gathered(v_got, CORE_GROUPS)

    def first(rows):
        return pl.BlockSpec((1, rows, WIDTH), lambda i: (0, 0, 0))

    def whole(*dims):
        return pl.BlockSpec(dims, lambda i: (0,) * len(dims))

    with jax.named_scope("diagonal"):
        dv_diag, dg_diag, logit_sum = pl.pallas_call(
            diagonal_kernel,
            grid=(1,),
            in_specs=[whole(8, LANES), whole(VOWN, WIDTH), first(GOWN)],
            out_specs=(whole(VOWN, WIDTH), whole(GOWN, WIDTH), whole(1, LANES)),
            out_shape=(shape(VOWN, WIDTH), shape(GOWN, WIDTH), shape(1, LANES)),
            compiler_params=params(),
            cost_estimate=cost(2e7, 3e5),
        )(counts, v_own, g_own)

    with jax.named_scope("forward"):
        v_all, g_all, row_inv, col_inv, e_pair, r_part, c_part = pl.pallas_call(
            forward_kernel,
            in_specs=[vmem] * 3,
            out_specs=[pl.BlockSpec(memory_space=pltpu.HBM)] * 4 + [vmem] * 3,
            out_shape=(
                pltpu.HBM((VROWS, WIDTH), BF16),
                pltpu.HBM((GROWS, WIDTH), BF16),
                pltpu.HBM((VROWS, LANES), F32),
                pltpu.HBM((GLOSSES, CLIPS_DEV, LANES), F32),
                shape(CLIPS_DEV, LANES),
                shape(NZC, 1, LANES),
                shape(1, LANES),
            ),
            scratch_shapes=[
                pltpu.VMEM((VROWS, WIDTH), BF16),
                pltpu.VMEM((GROWS, WIDTH), BF16),
                pltpu.VMEM((VROWS, LANES), F32),
                pltpu.VMEM((GLOSSES, CLIPS_DEV, LANES), F32),
                two_halves(VROWS),
                two_halves(NXY * GOWN),
                pltpu.VMEM((VROWS, LANES), F32),
                pltpu.VMEM((GLOSSES, 8, LANES), F32),
                pltpu.VMEM((VROWS, LANES), F32),
                pltpu.VMEM((GLOSSES, CLIPS_DEV, LANES), F32),
                pltpu.SemaphoreType.DMA((4,)),
            ],
            compiler_params=params(),
            cost_estimate=cost(2 * VROWS * GROWS * WIDTH, 8e6, VROWS * GROWS),
        )(v_got, g_got, logit_sum)

    with jax.named_scope("row_sums"):
        c_send, r_row = pl.pallas_call(
            row_sums_kernel,
            in_specs=[vmem] * 2,
            out_shape=(shape(NXY, 1, LANES), shape(1, LANES)),
            compiler_params=params(),
            cost_estimate=cost(1e5, 3e5),
        )(exchanged(r_part, ZC_GROUPS), c_part)
    with jax.named_scope("column_sums"):
        c_got = exchanged(c_send, XY_GROUPS)

    def halves(rows):
        return pl.BlockSpec((rows, WIDTH), lambda i: (i, 0))

    p_spec = pl.BlockSpec((1, VROWS, 2 * WIDTH), lambda i: (i, 0, 0))
    with jax.named_scope("weights"):
        weights = pl.pallas_call(
            weights_kernel,
            grid=(PAIRS,),
            in_specs=[
                whole(VROWS, WIDTH),
                halves(2 * LANES),
                whole(VROWS, LANES),
                pl.BlockSpec((2, CLIPS_DEV, LANES), lambda i: (i, 0, 0)),
                whole(CLIPS_DEV, LANES),
            ],
            out_specs=pl.BlockSpec((1, VROWS, WIDTH), lambda i: (i // 2, 0, i % 2)),
            out_shape=pltpu.HBM((QUADS, VROWS, 2 * WIDTH), BF16),
            compiler_params=params(),
            cost_estimate=cost(2 * VROWS * GROWS * WIDTH, 12e6, VROWS * GROWS),
        )(*in_hbm(v_all, g_all, row_inv, col_inv), e_pair)

    with jax.named_scope("by_clip"):
        by_clip, av = pl.pallas_call(
            by_clip_kernel,
            grid=(QUADS,),
            in_specs=[whole(1, LANES), p_spec, whole(VROWS, WIDTH), halves(4 * LANES)],
            out_specs=(pl.BlockSpec((4 * LANES, 2 * WIDTH), lambda i: (i, 0)), whole(VROWS, WIDTH)),
            out_shape=(pltpu.HBM((GROWS, 2 * WIDTH), F32), shape(VROWS, WIDTH)),
            scratch_shapes=[pltpu.VMEM((VROWS, 2 * WIDTH), BF16)],
            compiler_params=params(),
            cost_estimate=cost(6 * VROWS * GROWS * WIDTH, 14e6),
        )(r_row, *in_hbm(weights, v_all, g_all))

    with jax.named_scope("clip_send"):
        v_rows = FRAMES * CLIPS_DEV // 2 + EXTRA
        mine, twin = pl.pallas_call(
            clip_send_kernel,
            grid=(QUADS,),
            in_specs=[whole(NXY, 1, LANES), whole(1, LANES), p_spec, halves(4 * LANES), whole(VROWS, WIDTH)],
            out_specs=(whole(v_rows, WIDTH), whole(v_rows, WIDTH)),
            out_shape=(shape(v_rows, WIDTH), shape(v_rows, WIDTH, dtype=BF16)),
            scratch_shapes=[pltpu.VMEM((1, LANES), F32), pltpu.VMEM((VROWS, WIDTH), F32)],
            compiler_params=params(),
            cost_estimate=cost(2 * VROWS * GROWS * WIDTH, 1e7),
        )(c_got, r_row, *in_hbm(weights, g_all), av)

    with jax.named_scope("gloss_send"):
        twin, c_ready = lax.optimization_barrier((twin, c_got))
        dg_send, c_row = pl.pallas_call(
            gloss_send_kernel,
            grid=(QUADS,),
            in_specs=[whole(NXY, 1, LANES), pl.BlockSpec((4 * LANES, 2 * WIDTH), lambda i: (i, 0))],
            out_specs=(whole(NXY, GOWN, WIDTH), whole(1, LANES)),
            out_shape=(shape(NXY, GOWN, WIDTH, dtype=BF16), shape(1, LANES)),
            scratch_shapes=[two_halves(NXY * GOWN)],
            compiler_params=params(),
            cost_estimate=cost(2e6, 5e6),
        )(c_ready, *in_hbm(by_clip))
        dg_got = exchanged(dg_send, XY_GROUPS)

    def kept_and_sent(owners):
        rows = owners * VOWN + EXTRA
        return (shape(rows, WIDTH), shape(rows, WIDTH, dtype=BF16))

    with jax.named_scope("clips_by_core"):
        mine, sent = pl.pallas_call(
            clip_rows_kernel,
            in_specs=[vmem] * 2,
            out_shape=kept_and_sent(NZ // 2),
            scratch_shapes=[two_halves(NZ * VOWN)],
            compiler_params=params(),
            cost_estimate=cost(1e6, 2e6),
        )(mine, to_core(twin))
    with jax.named_scope("clips_by_z"):
        mine, *sent = pl.pallas_call(
            quarter_kernel,
            in_specs=[vmem] * 2,
            out_shape=kept_and_sent(1) + kept_and_sent(1)[1:] * 2,
            compiler_params=params(),
            cost_estimate=cost(1e6, 1e6),
        )(mine, to_z(sent, 1))

    with jax.named_scope("video_grad"):
        grad_video, loss = pl.pallas_call(
            functools.partial(video_grad_kernel, clips),
            in_specs=[vmem] * 7,
            out_shape=(shape(OWN, FRAMES, WIDTH), shape(1, 1)),
            scratch_shapes=[two_halves(VOWN)],
            compiler_params=params(),
            cost_estimate=cost(1e6, 1e6),
        )(mine, *[to_z(a, 2 * m) for m, a in enumerate(sent, start=1)], c_row, dv_diag, video)
    with jax.named_scope("gloss_grad"):
        grad_gloss = pl.pallas_call(
            gloss_grad_kernel,
            in_specs=[vmem] * 3,
            out_shape=shape(OWN, GLOSSES, WIDTH),
            scratch_shapes=[two_halves(GOWN)],
            compiler_params=params(),
            cost_estimate=cost(1e6, 1e6),
        )(dg_got, dg_diag, gloss)
    return loss.reshape(()), grad_video, grad_gloss


def solution(mesh):
    clips = OWN * mesh.shape["outer"] * mesh.shape["inner"]
    over_all = ("outer", "inner")
    tokens, counts = P(over_all, None, None), P(over_all)
    return jax.shard_map(
        functools.partial(on_device, clips),
        mesh=mesh,
        in_specs=(tokens, tokens, counts, counts),
        out_specs=(P(), tokens, tokens),
        check_vma=False,
    )
```

```python
import functools
import math

import jax
import jax.numpy as jnp
from jax import lax
from jax.experimental import pallas as pl
from jax.experimental.pallas import tpu as pltpu
from jax.sharding import PartitionSpec as P

F32 = jnp.float32
BF16 = jnp.bfloat16
EPSILON = 1e-06
EXP_SCALE = 10.0 * math.log2(math.e)
MARK = 2.0
MARK_LIMIT = 1.5
FAR = -1e30

NZ, NY, NX, NCORE = 8, 8, 4, 2
OWN = 3
FRAMES, GLOSSES, WIDTH = 32, 16, 256
CLIPS_DEV = NZ * NCORE * OWN
TEXTS_DEV = NY * NX * OWN
LANES = 128
VROWS = FRAMES * CLIPS_DEV
GROWS = GLOSSES * LANES
VOWN = FRAMES * OWN
GOWN = GLOSSES * OWN
EXTRA = 16
PAIRS = GLOSSES // 2
QUADS = GLOSSES // 4
NXY, NZC = NX * NY, NZ * NCORE

def flat(x, z, y, core):
    return ((x % 2) * NZ + z) * 32 + (x // 2) * 16 + 2 * y + core


def z_groups(masks):
    return [
        [flat(x, z ^ mask, y, c) for mask in masks]
        for x in range(NX)
        for y in range(NY)
        for c in range(NCORE)
        for z in range(NZ)
        if not z & masks[-1] and not z & masks[len(masks) // 2]
    ]


Z_QUADS, Z_PAIRS = z_groups((0, 2, 4, 6)), z_groups((0, 1))
CORE_GROUPS = [[flat(x, z, y, c) for c in range(NCORE)] for x in range(NX) for y in range(NY) for z in range(NZ)]
XY_GROUPS = [[flat(x, z, y, c) for x in range(NX) for y in range(NY)] for z in range(NZ) for c in range(NCORE)]
ZC_GROUPS = [[flat(x, z, y, c) for c in range(NCORE) for z in range(NZ)] for x in range(NX) for y in range(NY)]


def params(limit_mb=20):
    return pltpu.CompilerParams(vmem_limit_bytes=limit_mb * 1024 * 1024)


def cost(flops, nbytes, trans=0):
    return pl.CostEstimate(flops=int(flops), bytes_accessed=int(nbytes), transcendentals=int(trans))


def iota(shape, dim):
    return lax.broadcasted_iota(jnp.int32, shape, dim)


def nt(a, b, **kw):
    return lax.dot_general(a, b, (((1,), (1,)), ((), ())), preferred_element_type=F32, **kw)


def nn(a, b, **kw):
    return lax.dot_general(a, b, (((1,), (0,)), ((), ())), preferred_element_type=F32, **kw)


def tn(a, b, **kw):
    return lax.dot_general(a, b, (((0,), (0,)), ((), ())), preferred_element_type=F32, **kw)


def column_of(row, n):
    eye = iota((n, LANES), 0) == iota((n, LANES), 1)
    return jnp.sum(jnp.where(eye, jnp.broadcast_to(row, (n, LANES)), 0.0), axis=1, keepdims=True)


def pieces(value):
    lane = iota((EXTRA, WIDTH), 1)
    full = jnp.broadcast_to(value, (EXTRA, WIDTH))
    hi = full.astype(BF16).astype(F32)
    mid = (full - hi).astype(BF16).astype(F32)
    low = (full - hi - mid).astype(BF16).astype(F32)
    return jnp.where(lane == 0, hi, jnp.where(lane == 1, mid, jnp.where(lane == 2, low, 0.0)))


def unpiece(block):
    mine = (iota((EXTRA, WIDTH), 0) == 0) & (iota((EXTRA, WIDTH), 1) < 3)
    return jnp.sum(jnp.where(mine, block, 0.0), keepdims=True).reshape(1, 1)


def put(ref, at, value):
    ref[0, at, :] = value[:, :LANES]
    ref[1, at, :] = value[:, LANES:]


def get(ref, at):
    return jnp.concatenate([ref[0, at, :], ref[1, at, :]], axis=1)


def two_halves(rows):
    return pltpu.VMEM((2, rows, LANES), F32)


def units_kernel(fc_in, gc_in, video_in, gloss_in, v_out, g_out, g_one, count_out, fc, gc, video, gloss, v_scr, g_scr, sems):
    pairs = ((fc_in, fc), (gc_in, gc), (video_in, video), (gloss_in, gloss))
    copies = [pltpu.make_async_copy(a, b, sems.at[i]) for i, (a, b) in enumerate(pairs)]
    for copy in copies:
        copy.start()
    for copy in copies:
        copy.wait()
    row = iota((8, LANES), 0)
    counts = jnp.zeros((8, LANES), jnp.int32)
    for c in range(OWN):
        counts = jnp.where(row == c, fc[c], jnp.where(row == OWN + c, gc[c], counts))
    count_out[...] = counts
    for count, raw, scr, tokens in ((fc, video, v_scr, FRAMES), (gc, gloss, g_scr, GLOSSES)):
        row, lane = iota((tokens, WIDTH), 0), iota((tokens, WIDTH), 1)
        for c in range(OWN):
            x = raw[c].astype(F32)
            mean_sq = jnp.mean(x * x, axis=-1, keepdims=True) + EPSILON
            unit = x * (lax.rsqrt(mean_sq) / math.sqrt(WIDTH))
            mark = jnp.where(lane == 0, MARK, 0.0)
            put(scr, pl.ds(c, tokens, stride=OWN), jnp.where(row < count[c], unit, mark))
    v = get(v_scr, pl.ds(0, VOWN)).astype(BF16)
    g = get(g_scr, pl.ds(0, GOWN)).astype(BF16)
    v_out[...] = v
    g_one[...] = g
    for i in range(NXY):
        g_out[i] = g


def diagonal_kernel(count_ref, v_ref, g_ref, dv, dg):
    def pick(count, which):
        return jnp.where(which == 0, count[0], jnp.where(which == 1, count[1], count[2]))

    fc = [count_ref[c : c + 1, 0:1] for c in range(OWN)]
    gc = [count_ref[OWN + c : OWN + c + 1, 0:1] for c in range(OWN)]
    v, g = v_ref[...], g_ref[...]
    shape = (VOWN, GOWN)
    r, q = iota(shape, 0), iota(shape, 1)
    rc, qc = lax.rem(r, OWN), lax.rem(q, OWN)
    valid = (rc == qc) & (lax.div(r, OWN) < pick(fc, rc)) & (lax.div(q, OWN) < pick(gc, qc))
    e = jnp.where(valid, jnp.exp2(nt(v, g) * EXP_SCALE), 0.0)
    r1, q1 = iota((VOWN, 1), 0), iota((1, GOWN), 1)
    rc1, qc1 = lax.rem(r1, OWN), lax.rem(q1, OWN)
    frames_r, glosses_q = pick(fc, rc1), pick(gc, qc1)
    row_ok = lax.div(r1, OWN) < frames_r
    col_ok = lax.div(q1, OWN) < glosses_q
    frames_r, glosses_q = frames_r.astype(F32), glosses_q.astype(F32)
    rows = jnp.where(row_ok, jnp.sum(e, axis=1, keepdims=True), 1.0)
    cols = jnp.where(col_ok, jnp.sum(e, axis=0, keepdims=True), 1.0)
    weight = -5.0 * e * (1.0 / (rows * frames_r) + 1.0 / (cols * glosses_q))
    dv[...] = nn(weight, g.astype(F32), precision=lax.Precision.HIGHEST)
    dg[...] = tn(weight, v.astype(F32), precision=lax.Precision.HIGHEST)


def exp_scores(v, g):
    return jnp.exp2(nt(v, g) * EXP_SCALE)


def forward_kernel(
    v_got, g_got,
    v_hbm, g_hbm, row_out, col_out, e_out, r_out, c_out,
    v_out, g_out, v_scr, g_scr, frame_mask, gloss_mask, rows, cols, sems,
):
    results = ((v_out, v_hbm), (g_out, g_hbm))
    copies = [pltpu.make_async_copy(a, b, sems.at[i]) for i, (a, b) in enumerate(results)]
    put(v_scr, pl.ds(0, VROWS), v_got[...].astype(F32))
    for f in range(FRAMES):
        parts = [
            get(v_scr, pl.ds(k * NZ * VOWN + f * OWN + c, NZ, stride=VOWN)) for k in range(NCORE) for c in range(OWN)
        ]
        v_out[pl.ds(f * CLIPS_DEV, CLIPS_DEV), :] = jnp.concatenate(parts, axis=0).astype(BF16)
    copies[0].start()
    put(g_scr, pl.ds(0, NXY * GOWN), g_got[...].reshape(NXY * GOWN, WIDTH).astype(F32))
    pad = jnp.where(iota((LANES - TEXTS_DEV, WIDTH), 1) == 0, MARK, 0.0)
    for g in range(GLOSSES):
        parts = [get(g_scr, pl.ds(x * NY * GOWN + g * OWN + c, NY, stride=GOWN)) for x in range(NX) for c in range(OWN)]
        g_out[pl.ds(g * LANES, LANES), :] = jnp.concatenate(parts + [pad], axis=0).astype(BF16)

    copies[1].start()

    first = jnp.where(iota((WIDTH, LANES), 0) == 0, 1.0, 0.0).astype(BF16)
    frame_mask[...] = jnp.where(nn(v_out[...], first) < MARK_LIMIT, 1.0, 0.0)
    first_row = jnp.where(iota((16, WIDTH), 1) == 0, 1.0, 0.0).astype(BF16)
    for g in range(GLOSSES):
        gloss_mask[g] = jnp.where(nt(first_row, g_out[pl.ds(g * LANES, LANES), :])[0:8] < MARK_LIMIT, 1.0, 0.0)
    frames = jnp.zeros((CLIPS_DEV, LANES), F32)
    for f in range(FRAMES):
        frames = frames + frame_mask[pl.ds(f * CLIPS_DEV, CLIPS_DEV), :]
    glosses = gloss_mask[0]
    for g in range(1, GLOSSES):
        glosses = glosses + gloss_mask[g]
    glosses = jnp.maximum(glosses, 1.0)[0:1]

    rows[...] = jnp.zeros_like(rows)

    def two_glosses(p, _):
        e = exp_scores(v_out[...], g_out[pl.ds(pl.multiple_of(p * WIDTH, WIDTH), WIDTH), :])
        m0, m1 = gloss_mask[2 * p][0:1], gloss_mask[2 * p + 1][0:1]
        col0 = jnp.zeros((CLIPS_DEV, LANES), F32)
        col1 = jnp.zeros((CLIPS_DEV, LANES), F32)
        for f in range(FRAMES):
            at = pl.ds(f * CLIPS_DEV, CLIPS_DEV)
            block = e[f * CLIPS_DEV : (f + 1) * CLIPS_DEV]
            e0, e1 = block[:, :LANES], block[:, LANES:]
            mask = frame_mask[at, :]
            rows[at, :] = rows[at, :] + (e0 * m0 + e1 * m1)
            col0 = col0 + e0 * mask
            col1 = col1 + e1 * mask
        cols[2 * p] = col0
        cols[2 * p + 1] = col1
        return 0

    lax.fori_loop(0, PAIRS, two_glosses, 0, unroll=2)

    lane = iota((CLIPS_DEV, LANES), 1)
    real = lane < TEXTS_DEV
    video_part = jnp.zeros((CLIPS_DEV, LANES), F32)
    for f in range(FRAMES):
        at = pl.ds(f * CLIPS_DEV, CLIPS_DEV)
        mask = frame_mask[at, :]
        total = jnp.where(real, rows[at, :], 1.0)
        video_part = video_part + mask * jnp.log(total / glosses)
        row_out[at, :] = jnp.where(mask > 0.0, 1.0 / (total * frames), FAR)
    gloss_part = jnp.zeros((CLIPS_DEV, LANES), F32)
    for g in range(GLOSSES):
        mask = gloss_mask[g][0:1]
        total = cols[g]
        gloss_part = gloss_part + mask * jnp.log(total / frames)
        col_out[g] = jnp.where(mask > 0.0, 1.0 / (total * glosses), FAR)
    logits = 0.5 * (video_part / frames + gloss_part / glosses)
    e_pair = jnp.where(real, jnp.exp(logits), 0.0)
    e_out[...] = e_pair

    sums = jnp.sum(e_pair, axis=1, keepdims=True)
    across = lane == iota((CLIPS_DEV, LANES), 0)
    r_row = jnp.sum(jnp.where(across, jnp.broadcast_to(sums, (CLIPS_DEV, LANES)), 0.0), axis=0, keepdims=True)
    inner, outer = lax.axis_index("inner"), lax.axis_index("outer")
    z, core = lax.rem(outer, NZ), lax.rem(inner, NCORE)
    x, y = 2 * lax.div(inner, 16) + lax.div(outer, NZ), lax.rem(lax.div(inner, NCORE), NY)
    clip0 = core * OWN * NZ + lax.rem(z, 2) * (NZ // 2) + lax.div(z, 2)
    text0 = x * OWN * NY + y
    own = jnp.zeros((CLIPS_DEV, LANES), jnp.bool_)
    for c in range(OWN):
        own = own | ((iota((CLIPS_DEV, LANES), 0) == clip0 + c * NZ) & (lane == text0 + c * NY))
    diag = jnp.sum(jnp.where(own, logits, 0.0), keepdims=True).reshape(1, 1)
    r_row = jnp.where(iota((1, LANES), 1) == CLIPS_DEV, diag, r_row)
    for i in range(NZC):
        r_out[i] = r_row
    c_out[...] = jnp.sum(e_pair, axis=0, keepdims=True)
    for copy in copies:
        copy.wait()


def weights_kernel(v_ref, g_ref, row_ref, col_ref, e_ref, p_out):
    e = exp_scores(v_ref[...], g_ref[...])
    scale = 2.5 * e_ref[...]
    col0, col1 = col_ref[0], col_ref[1]
    for f in range(FRAMES):
        at = pl.ds(f * CLIPS_DEV, CLIPS_DEV)
        block = e[f * CLIPS_DEV : (f + 1) * CLIPS_DEV]
        row = row_ref[at, :]
        w0 = scale * block[:, :LANES] * jnp.maximum(row + col0, 0.0)
        w1 = scale * block[:, LANES:] * jnp.maximum(row + col1, 0.0)
        p_out[0, at, :] = jnp.concatenate([w0, w1], axis=1).astype(BF16)

def added(got):
    total = got[0]
    for i in range(1, got.shape[0]):
        total = total + got[i]
    return total


def row_sums_kernel(r_got, c_part, c_out, r_out):
    r_row = added(r_got)
    r_out[...] = r_row
    lane = iota((1, LANES), 1)
    logs = jnp.where(lane < CLIPS_DEV, jnp.log(jnp.where(lane < CLIPS_DEV, r_row, 1.0)), 0.0)
    logs = logs - jnp.where(lane == CLIPS_DEV, 2.0 * r_row, 0.0)
    total = jnp.sum(logs, axis=1, keepdims=True)
    message = jnp.where(lane == TEXTS_DEV, total, c_part[...])
    for i in range(NXY):
        c_out[i] = message


def inverse_texts(c_row):
    real = iota((1, LANES), 1) < TEXTS_DEV
    inverse = jnp.where(real, 1.0 / jnp.where(real, c_row, 1.0), 0.0)
    return jnp.broadcast_to(column_of(inverse, LANES), (LANES, WIDTH))


def by_clip_kernel(r_ref, p_ref, v_ref, g_ref, out, av_out, both):
    step = pl.program_id(0)

    @pl.when(step == 0)
    def _():
        inverse = jnp.broadcast_to(1.0 / column_of(r_ref[...], CLIPS_DEV), (CLIPS_DEV, WIDTH))
        for f in range(FRAMES):
            at = pl.ds(f * CLIPS_DEV, CLIPS_DEV)
            v = v_ref[at, :]
            both[at, :WIDTH] = v
            both[at, WIDTH:] = (v.astype(F32) * inverse).astype(BF16)

    out[...] = tn(p_ref[0], both[...]).reshape(GLOSSES // QUADS, LANES, 2 * WIDTH)
    part = nn(p_ref[0], g_ref[...])

    @pl.when(step == 0)
    def _():
        av_out[...] = part

    @pl.when(step > 0)
    def _():
        av_out[...] = av_out[...] + part


def started(copies):
    for copy in copies:
        copy.start()
    return copies


def gloss_send_kernel(c_got, by_clip, out, c_out, held, scr, sems):
    many = GLOSSES // QUADS
    copies = started(
        [
            pltpu.make_async_copy(by_clip.at[pl.ds(q * many, many), pl.ds(0, TEXTS_DEV)], held.at[q], sems.at[q])
            for q in range(QUADS)
        ]
    )
    c_out[...] = added(c_got)
    col = inverse_texts(c_out[...])[:TEXTS_DEV]
    for q, copy in enumerate(copies):
        copy.wait()
        for k in range(many):
            block = held[q, k, :, :WIDTH] * col + held[q, k, :, WIDTH:]
            row = (q * many + k) * OWN
            for x in range(NX):
                for c in range(OWN):
                    first = (x * OWN + c) * NY
                    put(scr, pl.ds(x * NY * GOWN + row + c, NY, stride=GOWN), block[first : first + NY])
    out[...] = get(scr, pl.ds(0, NXY * GOWN)).astype(BF16).reshape(NXY, GOWN, WIDTH)


def clip_send_kernel(c_got, r_ref, p_hbm, g_hbm, av_ref, mine, twin, held, g_held, total, sems):
    g_copy = pltpu.make_async_copy(g_hbm, g_held, sems.at[QUADS])
    copies = [pltpu.make_async_copy(p_hbm.at[q], held.at[q], sems.at[q]) for q in range(QUADS)]
    started([g_copy, *copies])
    c_row = added(c_got)
    col = inverse_texts(c_row)
    cols = jnp.concatenate([col] * (GLOSSES // QUADS), axis=0)
    core = lax.rem(lax.axis_index("inner"), NCORE)
    inverse = jnp.broadcast_to(1.0 / column_of(r_ref[...], CLIPS_DEV), (CLIPS_DEV, WIDTH))
    half = CLIPS_DEV // 2
    g_copy.wait()
    for q, copy in enumerate(copies):
        scaled = (g_held[pl.ds(q * 4 * LANES, 4 * LANES), :].astype(F32) * cols).astype(BF16)
        copy.wait()
        part = nn(held[q], scaled)
        if q == 0:
            total[...] = part
        elif q < QUADS - 1:
            total[...] = total[...] + part
    for pair in range(FRAMES // 2):
        others = []
        for f in (2 * pair, 2 * pair + 1):
            at = pl.ds(f * CLIPS_DEV, CLIPS_DEV)
            new = part[f * CLIPS_DEV : (f + 1) * CLIPS_DEV]
            block = av_ref[at, :] * inverse + (total[at, :] + new)
            low, high = block[:half], block[half:]
            mine[pl.ds(f * half, half), :] = jnp.where(core == 0, low, high)
            others.append(jnp.where(core == 0, high, low))
        twin[pl.ds(pair * CLIPS_DEV, CLIPS_DEV), :] = jnp.concatenate(others, axis=0).astype(BF16)
    real = iota((1, LANES), 1) < TEXTS_DEV
    logs = jnp.where(real, jnp.log(jnp.where(real, c_row, 1.0)), 0.0)
    extra = pieces(jnp.sum(logs, axis=1, keepdims=True))
    mine[pl.ds(FRAMES * half, EXTRA), :] = extra
    twin[pl.ds(FRAMES * half, EXTRA), :] = extra.astype(BF16)


def own_z():
    return lax.rem(lax.axis_index("outer"), NZ)


def clip_rows_kernel(mine, got, keep, send, scr):
    step = 2 * NZ
    for i in range(VOWN // 2):
        at = pl.ds(i * step, step)
        two = mine[at, :] + got[at, :].astype(F32)
        for k in range(2):
            put(scr, pl.ds(2 * i + k, NZ, stride=VOWN), two[k * NZ : (k + 1) * NZ])
    bit = lax.rem(own_z(), 2)
    owners = NZ // 2
    for i in range(owners):
        at = pl.ds(i * VOWN, VOWN)
        keep[at, :] = get(scr, pl.ds(pl.multiple_of((owners * bit + i) * VOWN, VOWN), VOWN))
        send[at, :] = get(scr, pl.ds(pl.multiple_of((owners * (1 - bit) + i) * VOWN, VOWN), VOWN)).astype(BF16)
    extra = loss_rows(mine, got, NZ)
    keep[pl.ds(owners * VOWN, EXTRA), :] = extra
    send[pl.ds(owners * VOWN, EXTRA), :] = extra.astype(BF16)


def loss_rows(mine, got, owners):
    tail = pl.ds(owners * VOWN, EXTRA)
    return pieces(unpiece(mine[tail, :]) + unpiece(got[tail, :].astype(F32)))


def quarter_kernel(mine, got, keep, *sends):
    own = lax.div(own_z(), 2)
    extra = loss_rows(mine, got, NZ // 2)
    for out, owner in zip((keep, *sends), (own, own ^ 1, own ^ 2, own ^ 3), strict=True):
        at = pl.ds(pl.multiple_of(owner * VOWN, VOWN), VOWN)
        out[pl.ds(0, VOWN), :] = (mine[at, :] + got[at, :].astype(F32)).astype(out.dtype)
        out[pl.ds(VOWN, EXTRA), :] = extra.astype(out.dtype)


def token_grads(total, scr, raw, out, tokens):
    put(scr, pl.ds(0, OWN * tokens), total)
    for c in range(OWN):
        x = raw[c].astype(F32)
        d = get(scr, pl.ds(c, tokens, stride=OWN))
        mean_sq = jnp.mean(x * x, axis=-1, keepdims=True) + EPSILON
        factor = lax.rsqrt(mean_sq) / math.sqrt(WIDTH)
        inner = jnp.sum(d * x, axis=-1, keepdims=True)
        out[c] = factor * d - factor * x * (inner / (WIDTH * mean_sq))


def video_grad_kernel(clips, mine, got1, got2, got3, c_row, diag, video, out, loss, scr):
    at = pl.ds(0, VOWN)
    total = mine[at, :]
    for got in (got1, got2, got3):
        total = total + got[at, :].astype(F32)
    token_grads(total + diag[...], scr, video, out, FRAMES)
    row_part = c_row[:, TEXTS_DEV : TEXTS_DEV + 1]
    tail = pl.ds(VOWN, EXTRA)
    near = unpiece(mine[tail, :]) + unpiece(got1[tail, :].astype(F32))
    far = unpiece(got2[tail, :].astype(F32)) + unpiece(got3[tail, :].astype(F32))
    loss[...] = (near + far + row_part) * (0.5 / clips)


def gloss_grad_kernel(got, diag, gloss, out, scr):
    total = got[0].astype(F32)
    for i in range(1, NXY):
        total = total + got[i].astype(F32)
    token_grads(total + diag[...], scr, gloss, out, GLOSSES)


def shape(*dims, dtype=F32):
    return jax.ShapeDtypeStruct(dims, dtype)


def on_device(clips, video, gloss, frame_count, gloss_count):
    vmem, hbm = pl.BlockSpec(memory_space=pltpu.VMEM), pl.BlockSpec(memory_space=pltpu.HBM)
    over_all = ("outer", "inner")

    def to_core(a):
        return lax.ppermute(a, "inner", [(i, i ^ 1) for i in range(lax.axis_size("inner"))])

    def to_z(a, mask):
        return lax.ppermute(a, "outer", [(i, i ^ mask) for i in range(lax.axis_size("outer"))])

    def exchanged(a, groups):
        return lax.all_to_all(a, over_all, 0, 0, axis_index_groups=groups, tiled=True)

    def gathered(a, groups):
        return lax.all_gather(a, over_all, axis=0, axis_index_groups=groups, tiled=True)

    def in_hbm(*arrays):
        return [pltpu.with_memory_space_constraint(a, pltpu.HBM) for a in arrays]

    with jax.named_scope("unit_tokens"):
        v_own, g_send, g_own, counts = pl.pallas_call(
            units_kernel,
            in_specs=[hbm] * 4,
            out_shape=(
                shape(VOWN, WIDTH, dtype=BF16),
                shape(NXY, GOWN, WIDTH, dtype=BF16),
                shape(GOWN, WIDTH, dtype=BF16),
                shape(8, LANES, dtype=jnp.int32),
            ),
            scratch_shapes=[
                pltpu.SMEM((OWN,), jnp.int32),
                pltpu.SMEM((OWN,), jnp.int32),
                pltpu.VMEM((OWN, FRAMES, WIDTH), BF16),
                pltpu.VMEM((OWN, GLOSSES, WIDTH), BF16),
                two_halves(VOWN),
                two_halves(GOWN),
                pltpu.SemaphoreType.DMA((4,)),
            ],
            compiler_params=params(),
            cost_estimate=cost(2e5, 7e5),
        )(*in_hbm(frame_count, gloss_count, video, gloss))

    with jax.named_scope("gather"):
        g_got = exchanged(g_send, XY_GROUPS)
        v_got = gathered(gathered(v_own, Z_QUADS), Z_PAIRS)
        v_got = gathered(v_got, CORE_GROUPS)

    def whole(*dims):
        return pl.BlockSpec(dims, lambda i: (0,) * len(dims))

    with jax.named_scope("forward"):
        v_all, g_all, row_inv, col_inv, e_pair, r_part, c_part = pl.pallas_call(
            forward_kernel,
            in_specs=[vmem] * 2,
            out_specs=[hbm] * 2 + [vmem] * 5,
            out_shape=(
                pltpu.HBM((VROWS, WIDTH), BF16),
                pltpu.HBM((GROWS, WIDTH), BF16),
                shape(VROWS, LANES),
                shape(GLOSSES, CLIPS_DEV, LANES),
                shape(CLIPS_DEV, LANES),
                shape(NZC, 1, LANES),
                shape(1, LANES),
            ),
            scratch_shapes=[
                pltpu.VMEM((VROWS, WIDTH), BF16),
                pltpu.VMEM((GROWS, WIDTH), BF16),
                two_halves(VROWS),
                two_halves(NXY * GOWN),
                pltpu.VMEM((VROWS, LANES), F32),
                pltpu.VMEM((GLOSSES, 8, LANES), F32),
                pltpu.VMEM((VROWS, LANES), F32),
                pltpu.VMEM((GLOSSES, CLIPS_DEV, LANES), F32),
                pltpu.SemaphoreType.DMA((2,)),
            ],
            compiler_params=params(),
            cost_estimate=cost(2 * VROWS * GROWS * WIDTH, 8e6, VROWS * GROWS),
        )(v_got, g_got)

    with jax.named_scope("row_sums"):
        c_send, r_row = pl.pallas_call(
            row_sums_kernel,
            in_specs=[vmem] * 2,
            out_shape=(shape(NXY, 1, LANES), shape(1, LANES)),
            compiler_params=params(),
            cost_estimate=cost(1e5, 3e5),
        )(exchanged(r_part, ZC_GROUPS), c_part)
    with jax.named_scope("column_sums"):
        c_got = exchanged(c_send, XY_GROUPS)

    def halves(rows):
        return pl.BlockSpec((rows, WIDTH), lambda i: (i, 0))

    p_spec = pl.BlockSpec((1, VROWS, 2 * WIDTH), lambda i: (i, 0, 0))
    with jax.named_scope("weights"):
        weights = pl.pallas_call(
            weights_kernel,
            grid=(PAIRS,),
            in_specs=[
                whole(VROWS, WIDTH),
                halves(2 * LANES),
                whole(VROWS, LANES),
                pl.BlockSpec((2, CLIPS_DEV, LANES), lambda i: (i, 0, 0)),
                whole(CLIPS_DEV, LANES),
            ],
            out_specs=pl.BlockSpec((1, VROWS, WIDTH), lambda i: (i // 2, 0, i % 2)),
            out_shape=pltpu.HBM((QUADS, VROWS, 2 * WIDTH), BF16),
            compiler_params=params(),
            cost_estimate=cost(2 * VROWS * GROWS * WIDTH, 12e6, VROWS * GROWS),
        )(*in_hbm(v_all, g_all), row_inv, col_inv, e_pair)

    with jax.named_scope("by_clip"):
        by_clip, av = pl.pallas_call(
            by_clip_kernel,
            grid=(QUADS,),
            in_specs=[whole(1, LANES), p_spec, whole(VROWS, WIDTH), halves(4 * LANES)],
            out_specs=(pl.BlockSpec((GLOSSES // QUADS, LANES, 2 * WIDTH), lambda i: (i, 0, 0)), whole(VROWS, WIDTH)),
            out_shape=(pltpu.HBM((GLOSSES, LANES, 2 * WIDTH), F32), shape(VROWS, WIDTH)),
            scratch_shapes=[pltpu.VMEM((VROWS, 2 * WIDTH), BF16)],
            compiler_params=params(),
            cost_estimate=cost(6 * VROWS * GROWS * WIDTH, 14e6),
        )(r_row, *in_hbm(weights, v_all, g_all))

    with jax.named_scope("clip_send"):
        v_rows = FRAMES * CLIPS_DEV // 2 + EXTRA
        mine, twin = pl.pallas_call(
            clip_send_kernel,
            in_specs=[vmem, vmem, hbm, hbm, vmem],
            out_shape=(shape(v_rows, WIDTH), shape(v_rows, WIDTH, dtype=BF16)),
            scratch_shapes=[
                pltpu.VMEM((QUADS, VROWS, 2 * WIDTH), BF16),
                pltpu.VMEM((GROWS, WIDTH), BF16),
                pltpu.VMEM((VROWS, WIDTH), F32),
                pltpu.SemaphoreType.DMA((QUADS + 1,)),
            ],
            compiler_params=params(),
            cost_estimate=cost(2 * VROWS * GROWS * WIDTH, 1e7),
        )(c_got, r_row, *in_hbm(weights, g_all), av)

    with jax.named_scope("gloss_send"):
        twin, c_ready = lax.optimization_barrier((twin, c_got))
        dg_send, c_row = pl.pallas_call(
            gloss_send_kernel,
            in_specs=[vmem, hbm],
            out_shape=(shape(NXY, GOWN, WIDTH, dtype=BF16), shape(1, LANES)),
            scratch_shapes=[
                pltpu.VMEM((QUADS, GLOSSES // QUADS, TEXTS_DEV, 2 * WIDTH), F32),
                two_halves(NXY * GOWN),
                pltpu.SemaphoreType.DMA((QUADS,)),
            ],
            compiler_params=params(),
            cost_estimate=cost(2e6, 5e6),
        )(c_ready, *in_hbm(by_clip))
        dg_got = exchanged(dg_send, XY_GROUPS)

    def kept_and_sent(owners):
        rows = owners * VOWN + EXTRA
        return (shape(rows, WIDTH), shape(rows, WIDTH, dtype=BF16))

    with jax.named_scope("clips_by_core"):
        mine, sent = pl.pallas_call(
            clip_rows_kernel,
            in_specs=[vmem] * 2,
            out_shape=kept_and_sent(NZ // 2),
            scratch_shapes=[two_halves(NZ * VOWN)],
            compiler_params=params(),
            cost_estimate=cost(1e6, 2e6),
        )(mine, to_core(twin))
    with jax.named_scope("clips_by_z"):
        mine, *sent = pl.pallas_call(
            quarter_kernel,
            in_specs=[vmem] * 2,
            out_shape=kept_and_sent(1) + kept_and_sent(1)[1:] * 2,
            compiler_params=params(),
            cost_estimate=cost(3e10, 1e6),
        )(mine, to_z(sent, 1))

    with jax.named_scope("diagonal"):
        mine, v_own, g_own, counts = lax.optimization_barrier((mine, v_own, g_own, counts))
        dv_diag, dg_diag = pl.pallas_call(
            diagonal_kernel,
            in_specs=[vmem] * 3,
            out_shape=(shape(VOWN, WIDTH), shape(GOWN, WIDTH)),
            compiler_params=params(),
            cost_estimate=cost(2e7, 3e5),
        )(counts, v_own, g_own)

    with jax.named_scope("video_grad"):
        grad_video, loss = pl.pallas_call(
            functools.partial(video_grad_kernel, clips),
            in_specs=[vmem] * 7,
            out_shape=(shape(OWN, FRAMES, WIDTH), shape(1, 1)),
            scratch_shapes=[two_halves(VOWN)],
            compiler_params=params(),
            cost_estimate=cost(1e6, 1e6),
        )(mine, *[to_z(a, 2 * m) for m, a in enumerate(sent, start=1)], c_row, dv_diag, video)
    with jax.named_scope("gloss_grad"):
        grad_gloss = pl.pallas_call(
            gloss_grad_kernel,
            in_specs=[vmem] * 3,
            out_shape=shape(OWN, GLOSSES, WIDTH),
            scratch_shapes=[two_halves(GOWN)],
            compiler_params=params(),
            cost_estimate=cost(1e6, 1e6),
        )(dg_got, dg_diag, gloss)
    return loss.reshape(()), grad_video, grad_gloss


def solution(mesh):
    clips = OWN * mesh.shape["outer"] * mesh.shape["inner"]
    over_all = ("outer", "inner")
    tokens, counts = P(over_all, None, None), P(over_all)
    return jax.shard_map(
        functools.partial(on_device, clips),
        mesh=mesh,
        in_specs=(tokens, tokens, counts, counts),
        out_specs=(P(), tokens, tokens),
        check_vma=False,
    )
```

```python
import functools
import math

import jax
import jax.numpy as jnp
from jax import lax
from jax.experimental import pallas as pl
from jax.experimental.pallas import tpu as pltpu
from jax.sharding import PartitionSpec as P

F32 = jnp.float32
BF16 = jnp.bfloat16
EPSILON = 1e-06
EXP_SCALE = 10.0 * math.log2(math.e)
MARK = 2.0
MARK_LIMIT = 1.5
FAR = -1e30

NZ, NY, NX, NCORE = 8, 8, 4, 2
OWN = 3
FRAMES, GLOSSES, WIDTH = 32, 16, 256
CLIPS_DEV = NZ * NCORE * OWN
TEXTS_DEV = NY * NX * OWN
LANES = 128
VROWS = FRAMES * CLIPS_DEV
GROWS = GLOSSES * TEXTS_DEV
VOWN = FRAMES * OWN
GOWN = GLOSSES * OWN
EXTRA = 16
QUADS = GLOSSES // 4
TILES = GROWS // LANES
HALF = GROWS // 2
NXY, NZC = NX * NY, NZ * NCORE

def flat(x, z, y, core):
    return ((x % 2) * NZ + z) * 32 + (x // 2) * 16 + 2 * y + core


def z_groups(masks):
    return [
        [flat(x, z ^ mask, y, c) for mask in masks]
        for x in range(NX)
        for y in range(NY)
        for c in range(NCORE)
        for z in range(NZ)
        if not z & masks[-1] and not z & masks[len(masks) // 2]
    ]


Z_QUADS, Z_PAIRS = z_groups((0, 2, 4, 6)), z_groups((0, 1))
CORE_GROUPS = [[flat(x, z, y, c) for c in range(NCORE)] for x in range(NX) for y in range(NY) for z in range(NZ)]
XY_GROUPS = [[flat(x, z, y, c) for x in range(NX) for y in range(NY)] for z in range(NZ) for c in range(NCORE)]
ZC_GROUPS = [[flat(x, z, y, c) for c in range(NCORE) for z in range(NZ)] for x in range(NX) for y in range(NY)]


def params(limit_mb=32):
    return pltpu.CompilerParams(vmem_limit_bytes=limit_mb * 1024 * 1024)


def cost(flops, nbytes, trans=0):
    return pl.CostEstimate(flops=int(flops), bytes_accessed=int(nbytes), transcendentals=int(trans))


def iota(shape, dim):
    return lax.broadcasted_iota(jnp.int32, shape, dim)


def nt(a, b, **kw):
    return lax.dot_general(a, b, (((1,), (1,)), ((), ())), preferred_element_type=F32, **kw)


def nn(a, b, **kw):
    return lax.dot_general(a, b, (((1,), (0,)), ((), ())), preferred_element_type=F32, **kw)


def tn(a, b, **kw):
    return lax.dot_general(a, b, (((0,), (0,)), ((), ())), preferred_element_type=F32, **kw)


def column_of(row, n):
    eye = iota((n, LANES), 0) == iota((n, LANES), 1)
    return jnp.sum(jnp.where(eye, jnp.broadcast_to(row, (n, LANES)), 0.0), axis=1, keepdims=True)


def packed(x):
    lane = iota(x.shape, 1)
    a, b, c = (pltpu.roll(x, shift, 1) for shift in (96, 64, 32))
    return jnp.where(lane < 96, x, a), jnp.where(lane < 64, a, b), jnp.where(lane < 32, b, c)


def unpacked_sum(t0, t1, t2):
    lane = iota(t0.shape, 1)
    second = pltpu.roll(jnp.where(lane >= 96, t0, t1), 32, 1)
    third = pltpu.roll(jnp.where(lane >= 64, t1, t2), 64, 1)
    return (t0 + second) + (third + pltpu.roll(t2, 96, 1))


def pieces(value):
    lane = iota((EXTRA, WIDTH), 1)
    full = jnp.broadcast_to(value, (EXTRA, WIDTH))
    hi = full.astype(BF16).astype(F32)
    mid = (full - hi).astype(BF16).astype(F32)
    low = (full - hi - mid).astype(BF16).astype(F32)
    return jnp.where(lane == 0, hi, jnp.where(lane == 1, mid, jnp.where(lane == 2, low, 0.0)))


def unpiece(block):
    mine = (iota((EXTRA, WIDTH), 0) == 0) & (iota((EXTRA, WIDTH), 1) < 3)
    return jnp.sum(jnp.where(mine, block, 0.0), keepdims=True).reshape(1, 1)


def put(ref, at, value):
    ref[0, at, :] = value[:, :LANES]
    ref[1, at, :] = value[:, LANES:]


def get(ref, at):
    return jnp.concatenate([ref[0, at, :], ref[1, at, :]], axis=1)


def two_halves(rows):
    return pltpu.VMEM((2, rows, LANES), F32)


def units_kernel(fc_in, gc_in, video_in, gloss_in, v_out, g_out, g_one, count_out, fc, gc, video, gloss, v_scr, g_scr, sems):
    pairs = ((fc_in, fc), (gc_in, gc), (video_in, video), (gloss_in, gloss))
    copies = [pltpu.make_async_copy(a, b, sems.at[i]) for i, (a, b) in enumerate(pairs)]
    for copy in copies:
        copy.start()
    for copy in copies:
        copy.wait()
    row = iota((8, LANES), 0)
    counts = jnp.zeros((8, LANES), jnp.int32)
    for c in range(OWN):
        counts = jnp.where(row == c, fc[c], jnp.where(row == OWN + c, gc[c], counts))
    count_out[...] = counts
    for count, raw, scr, tokens in ((fc, video, v_scr, FRAMES), (gc, gloss, g_scr, GLOSSES)):
        row, lane = iota((tokens, WIDTH), 0), iota((tokens, WIDTH), 1)
        for c in range(OWN):
            x = raw[c].astype(F32)
            mean_sq = jnp.mean(x * x, axis=-1, keepdims=True) + EPSILON
            unit = x * (lax.rsqrt(mean_sq) / math.sqrt(WIDTH))
            mark = jnp.where(lane == 0, MARK, 0.0)
            put(scr, pl.ds(c, tokens, stride=OWN), jnp.where(row < count[c], unit, mark))
    v = get(v_scr, pl.ds(0, VOWN)).astype(BF16)
    g = get(g_scr, pl.ds(0, GOWN)).astype(BF16)
    v_out[...] = v
    g_one[...] = g
    for i in range(NXY):
        g_out[i] = g


def diagonal_kernel(count_ref, v_ref, g_ref, dv, dg):
    def pick(count, which):
        return jnp.where(which == 0, count[0], jnp.where(which == 1, count[1], count[2]))

    fc = [count_ref[c : c + 1, 0:1] for c in range(OWN)]
    gc = [count_ref[OWN + c : OWN + c + 1, 0:1] for c in range(OWN)]
    v, g = v_ref[...], g_ref[...]
    shape = (VOWN, GOWN)
    r, q = iota(shape, 0), iota(shape, 1)
    rc, qc = lax.rem(r, OWN), lax.rem(q, OWN)
    valid = (rc == qc) & (lax.div(r, OWN) < pick(fc, rc)) & (lax.div(q, OWN) < pick(gc, qc))
    e = jnp.where(valid, jnp.exp2(nt(v, g) * EXP_SCALE), 0.0)
    r1, q1 = iota((VOWN, 1), 0), iota((1, GOWN), 1)
    rc1, qc1 = lax.rem(r1, OWN), lax.rem(q1, OWN)
    frames_r, glosses_q = pick(fc, rc1), pick(gc, qc1)
    row_ok = lax.div(r1, OWN) < frames_r
    col_ok = lax.div(q1, OWN) < glosses_q
    frames_r, glosses_q = frames_r.astype(F32), glosses_q.astype(F32)
    rows = jnp.where(row_ok, jnp.sum(e, axis=1, keepdims=True), 1.0)
    cols = jnp.where(col_ok, jnp.sum(e, axis=0, keepdims=True), 1.0)
    weight = -5.0 * e * (1.0 / (rows * frames_r) + 1.0 / (cols * glosses_q))
    dv[...] = nn(weight, g.astype(F32), precision=lax.Precision.HIGHEST)
    dg[...] = tn(weight, v.astype(F32), precision=lax.Precision.HIGHEST)


def exp_scores(v, g):
    return jnp.exp2(nt(v, g) * EXP_SCALE)


def forward_kernel(
    v_got, g_got,
    v_hbm, g_hbm, row_out, col_out, e_out, r_out, c_out,
    v_out, g_out, v_scr, g_scr, frame_mask, gloss_mask, rows, cols, sems,
):
    results = ((v_out, v_hbm), (g_out, g_hbm))
    copies = [pltpu.make_async_copy(a, b, sems.at[i]) for i, (a, b) in enumerate(results)]
    put(v_scr, pl.ds(0, VROWS), v_got[...].astype(F32))
    for f in range(FRAMES):
        parts = [
            get(v_scr, pl.ds(k * NZ * VOWN + f * OWN + c, NZ, stride=VOWN)) for k in range(NCORE) for c in range(OWN)
        ]
        v_out[pl.ds(f * CLIPS_DEV, CLIPS_DEV), :] = jnp.concatenate(parts, axis=0).astype(BF16)
    copies[0].start()
    put(g_scr, pl.ds(0, NXY * GOWN), g_got[...].reshape(NXY * GOWN, WIDTH).astype(F32))
    for g in range(GLOSSES):
        parts = [get(g_scr, pl.ds(x * NY * GOWN + g * OWN + c, NY, stride=GOWN)) for x in range(NX) for c in range(OWN)]
        g_out[pl.ds(g * TEXTS_DEV, TEXTS_DEV), :] = jnp.concatenate(parts, axis=0).astype(BF16)
    copies[1].start()

    first = jnp.where(iota((WIDTH, LANES), 0) == 0, 1.0, 0.0).astype(BF16)
    frame_mask[...] = jnp.where(nn(v_out[...], first) < MARK_LIMIT, 1.0, 0.0)
    first_row = jnp.where(iota((16, WIDTH), 1) == 0, 1.0, 0.0).astype(BF16)
    for t in range(TILES):
        found = nt(first_row, g_out[pl.ds(t * LANES, LANES), :])[0:1]
        gloss_mask[t] = jnp.where(found < MARK_LIMIT, 1.0, 0.0)
    frames = jnp.zeros((CLIPS_DEV, LANES), F32)
    for f in range(FRAMES):
        frames = frames + frame_mask[pl.ds(f * CLIPS_DEV, CLIPS_DEV), :]
    by_tile = []
    for t in range(3):
        by_tile.append(gloss_mask[t] + gloss_mask[t + 3] + gloss_mask[t + 6] + gloss_mask[t + 9])
    lane = iota((CLIPS_DEV, LANES), 1)
    real = lane < TEXTS_DEV
    counts = unpacked_sum(*[jnp.broadcast_to(t, (8, LANES)) for t in by_tile])
    glosses = jnp.where(real[0:8], counts, 1.0)
    packed_glosses = [t[0:1] for t in packed(glosses)]
    glosses = glosses[0:1]

    for half in range(2):
        e = exp_scores(v_out[...], g_out[pl.ds(half * HALF, HALF), :])
        tiles = range(half * TILES // 2, (half + 1) * TILES // 2)
        masks = [gloss_mask[t] for t in tiles]
        sums = [jnp.zeros((CLIPS_DEV, LANES), F32) for _ in tiles]
        for f in range(FRAMES):
            at = pl.ds(f * CLIPS_DEV, CLIPS_DEV)
            mask = frame_mask[at, :]
            block = e[f * CLIPS_DEV : (f + 1) * CLIPS_DEV]
            parts = [block[:, k * LANES : (k + 1) * LANES] for k in range(TILES // 2)]
            sums = [total + part * mask for total, part in zip(sums, parts, strict=True)]
            for k in range(3):
                part = parts[k] * masks[k] + parts[k + 3] * masks[k + 3]
                rows[at, pl.ds(k * LANES, LANES)] = part if half == 0 else rows[at, pl.ds(k * LANES, LANES)] + part
        for k, t in enumerate(tiles):
            cols[t] = sums[k]

    video_part = jnp.zeros((CLIPS_DEV, LANES), F32)
    for f in range(FRAMES):
        at = pl.ds(f * CLIPS_DEV, CLIPS_DEV)
        mask = frame_mask[at, :]
        total = unpacked_sum(*[rows[at, pl.ds(k * LANES, LANES)] for k in range(3)])
        total = jnp.where(real, total, 1.0)
        video_part = video_part + mask * jnp.log(total)
        row_out[at, :] = jnp.where(mask > 0.0, 1.0 / (total * frames), FAR)
    video_part = video_part / frames - jnp.log(glosses)
    gloss_parts = [jnp.zeros((CLIPS_DEV, LANES), F32)] * 3
    for t in range(TILES):
        mask = gloss_mask[t]
        total = cols[t]
        gloss_parts[t % 3] = gloss_parts[t % 3] + mask * jnp.log(total)
        col_out[t] = jnp.where(mask > 0.0, 1.0 / (total * packed_glosses[t % 3]), FAR)
    gloss_part = unpacked_sum(*gloss_parts) / glosses - jnp.log(frames)
    logits = 0.5 * (video_part + gloss_part)
    e_pair = jnp.where(real, jnp.exp(logits), 0.0)
    e_out[...] = e_pair

    sums = jnp.sum(e_pair, axis=1, keepdims=True)
    across = lane == iota((CLIPS_DEV, LANES), 0)
    r_row = jnp.sum(jnp.where(across, jnp.broadcast_to(sums, (CLIPS_DEV, LANES)), 0.0), axis=0, keepdims=True)
    inner, outer = lax.axis_index("inner"), lax.axis_index("outer")
    z, core = lax.rem(outer, NZ), lax.rem(inner, NCORE)
    x, y = 2 * lax.div(inner, 16) + lax.div(outer, NZ), lax.rem(lax.div(inner, NCORE), NY)
    clip0 = core * OWN * NZ + lax.rem(z, 2) * (NZ // 2) + lax.div(z, 2)
    text0 = x * OWN * NY + y
    own = jnp.zeros((CLIPS_DEV, LANES), jnp.bool_)
    for c in range(OWN):
        own = own | ((iota((CLIPS_DEV, LANES), 0) == clip0 + c * NZ) & (lane == text0 + c * NY))
    diag = jnp.sum(jnp.where(own, logits, 0.0), keepdims=True).reshape(1, 1)
    r_row = jnp.where(iota((1, LANES), 1) == CLIPS_DEV, diag, r_row)
    for i in range(NZC):
        r_out[i] = r_row
    c_out[...] = jnp.sum(e_pair, axis=0, keepdims=True)
    for copy in copies:
        copy.wait()


def started(copies):
    for copy in copies:
        copy.start()
    return copies


def halves_of(p):
    return [(r, h, p.at[h, pl.ds(r * VROWS // 2, VROWS // 2)]) for r in range(2) for h in range(2)]


def weights_kernel(v_hbm, g_hbm, row_ref, col_ref, e_ref, p_hbm, v, g, p, sems):
    loads = started([pltpu.make_async_copy(a, b, sems.at[i]) for i, (a, b) in enumerate(((v_hbm, v), (g_hbm, g)))])
    scales = packed(2.5 * e_ref[...])
    for load in loads:
        load.wait()
    stores = []
    for (r, h, out), (_, _, here) in zip(halves_of(p_hbm), halves_of(p), strict=True):
        e = exp_scores(v[pl.ds(r * VROWS // 2, VROWS // 2), :], g[pl.ds(h * HALF, HALF), :])
        for f in range(FRAMES // 2):
            row = packed(row_ref[pl.ds((r * FRAMES // 2 + f) * CLIPS_DEV, CLIPS_DEV), :])
            block = e[f * CLIPS_DEV : (f + 1) * CLIPS_DEV]
            parts = []
            for k in range(TILES // 2):
                share = jnp.maximum(row[k % 3] + col_ref[h * TILES // 2 + k], 0.0)
                parts.append(scales[k % 3] * block[:, k * LANES : (k + 1) * LANES] * share)
            here[pl.ds(f * CLIPS_DEV, CLIPS_DEV), :] = jnp.concatenate(parts, axis=1).astype(BF16)
        stores += started([pltpu.make_async_copy(here, out, sems.at[2 + 2 * r + h])])
    for store in stores:
        store.wait()


def added(got):
    total = got[0]
    for i in range(1, got.shape[0]):
        total = total + got[i]
    return total


def row_sums_kernel(r_got, c_part, c_out, r_out):
    r_row = added(r_got)
    r_out[...] = r_row
    lane = iota((1, LANES), 1)
    logs = jnp.where(lane < CLIPS_DEV, jnp.log(jnp.where(lane < CLIPS_DEV, r_row, 1.0)), 0.0)
    logs = logs - jnp.where(lane == CLIPS_DEV, 2.0 * r_row, 0.0)
    total = jnp.sum(logs, axis=1, keepdims=True)
    message = jnp.where(lane == TEXTS_DEV, total, c_part[...])
    for i in range(NXY):
        c_out[i] = message


def inverse_texts(c_row):
    return jnp.broadcast_to(1.0 / column_of(c_row, TEXTS_DEV), (TEXTS_DEV, WIDTH))


def by_clip_kernel(r_ref, p_ref, v_ref, g_ref, out, av_out, both):
    step = pl.program_id(0)

    @pl.when(step == 0)
    def _():
        inverse = jnp.broadcast_to(1.0 / column_of(r_ref[...], CLIPS_DEV), (CLIPS_DEV, WIDTH))
        for f in range(FRAMES):
            at = pl.ds(f * CLIPS_DEV, CLIPS_DEV)
            v = v_ref[at, :]
            both[at, :WIDTH] = v
            both[at, WIDTH:] = (v.astype(F32) * inverse).astype(BF16)

    out[...] = tn(p_ref[0], both[...]).reshape(GLOSSES // 2, TEXTS_DEV, 2 * WIDTH)
    part = nn(p_ref[0], g_ref[...])

    @pl.when(step == 0)
    def _():
        av_out[...] = part

    @pl.when(step > 0)
    def _():
        av_out[...] = av_out[...] + part


def gloss_send_kernel(c_got, by_clip, out, c_out, held, scr, sems):
    many = GLOSSES // QUADS
    copies = started(
        [
            pltpu.make_async_copy(by_clip.at[pl.ds(q * many, many)], held.at[pl.ds(q * many, many)], sems.at[q])
            for q in range(QUADS)
        ]
    )
    c_out[...] = added(c_got)
    col = inverse_texts(c_out[...])
    for q, copy in enumerate(copies):
        copy.wait()
        for k in range(many):
            g = q * many + k
            block = held[g, :, :WIDTH] * col + held[g, :, WIDTH:]
            row = g * OWN
            for x in range(NX):
                for c in range(OWN):
                    first = (x * OWN + c) * NY
                    put(scr, pl.ds(x * NY * GOWN + row + c, NY, stride=GOWN), block[first : first + NY])
    out[...] = get(scr, pl.ds(0, NXY * GOWN)).astype(BF16).reshape(NXY, GOWN, WIDTH)


def clip_send_kernel(c_got, r_ref, p_hbm, g_hbm, av_ref, mine, twin, p, g, g_by_text, sems):
    g_copy = pltpu.make_async_copy(g_hbm, g, sems.at[4])
    copies = []
    for (r, h, theirs), (_, _, here) in zip(halves_of(p_hbm), halves_of(p), strict=True):
        copies.append(pltpu.make_async_copy(theirs, here, sems.at[2 * r + h]))
    started([g_copy, *copies])
    c_row = added(c_got)
    col = inverse_texts(c_row)
    core = lax.rem(lax.axis_index("inner"), NCORE)
    inverse = jnp.broadcast_to(1.0 / column_of(r_ref[...], CLIPS_DEV), (CLIPS_DEV, WIDTH))
    half = CLIPS_DEV // 2
    g_copy.wait()
    for i in range(GLOSSES):
        at = pl.ds(i * TEXTS_DEV, TEXTS_DEV)
        g_by_text[at, :] = (g[at, :].astype(F32) * col).astype(BF16)
    for r in range(2):
        copies[2 * r].wait()
        copies[2 * r + 1].wait()
        at = pl.ds(r * VROWS // 2, VROWS // 2)
        part = nn(p[0, at, :], g_by_text[pl.ds(0, HALF), :]) + nn(p[1, at, :], g_by_text[pl.ds(HALF, HALF), :])
        for pair in range(FRAMES // 4):
            others = []
            for f in (2 * pair, 2 * pair + 1):
                full = r * FRAMES // 2 + f
                new = part[f * CLIPS_DEV : (f + 1) * CLIPS_DEV]
                block = av_ref[pl.ds(full * CLIPS_DEV, CLIPS_DEV), :] * inverse + new
                low, high = block[:half], block[half:]
                mine[pl.ds(full * half, half), :] = jnp.where(core == 0, low, high)
                others.append(jnp.where(core == 0, high, low))
            at = pl.ds((r * FRAMES // 4 + pair) * CLIPS_DEV, CLIPS_DEV)
            twin[at, :] = jnp.concatenate(others, axis=0).astype(BF16)
    real = iota((1, LANES), 1) < TEXTS_DEV
    logs = jnp.where(real, jnp.log(jnp.where(real, c_row, 1.0)), 0.0)
    extra = pieces(jnp.sum(logs, axis=1, keepdims=True))
    mine[pl.ds(FRAMES * half, EXTRA), :] = extra
    twin[pl.ds(FRAMES * half, EXTRA), :] = extra.astype(BF16)


def own_z():
    return lax.rem(lax.axis_index("outer"), NZ)


def clip_rows_kernel(mine, got, keep, send, scr):
    step = 2 * NZ
    for i in range(VOWN // 2):
        at = pl.ds(i * step, step)
        two = mine[at, :] + got[at, :].astype(F32)
        for k in range(2):
            put(scr, pl.ds(2 * i + k, NZ, stride=VOWN), two[k * NZ : (k + 1) * NZ])
    bit = lax.rem(own_z(), 2)
    owners = NZ // 2
    for i in range(owners):
        at = pl.ds(i * VOWN, VOWN)
        keep[at, :] = get(scr, pl.ds(pl.multiple_of((owners * bit + i) * VOWN, VOWN), VOWN))
        send[at, :] = get(scr, pl.ds(pl.multiple_of((owners * (1 - bit) + i) * VOWN, VOWN), VOWN)).astype(BF16)
    extra = loss_rows(mine, got, NZ)
    keep[pl.ds(owners * VOWN, EXTRA), :] = extra
    send[pl.ds(owners * VOWN, EXTRA), :] = extra.astype(BF16)


def loss_rows(mine, got, owners):
    tail = pl.ds(owners * VOWN, EXTRA)
    return pieces(unpiece(mine[tail, :]) + unpiece(got[tail, :].astype(F32)))


def quarter_kernel(mine, got, keep, *sends):
    own = lax.div(own_z(), 2)
    extra = loss_rows(mine, got, NZ // 2)
    for out, owner in zip((keep, *sends), (own, own ^ 1, own ^ 2, own ^ 3), strict=True):
        at = pl.ds(pl.multiple_of(owner * VOWN, VOWN), VOWN)
        out[pl.ds(0, VOWN), :] = (mine[at, :] + got[at, :].astype(F32)).astype(out.dtype)
        out[pl.ds(VOWN, EXTRA), :] = extra.astype(out.dtype)


def token_grads(total, scr, raw, out, tokens):
    put(scr, pl.ds(0, OWN * tokens), total)
    for c in range(OWN):
        x = raw[c].astype(F32)
        d = get(scr, pl.ds(c, tokens, stride=OWN))
        mean_sq = jnp.mean(x * x, axis=-1, keepdims=True) + EPSILON
        factor = lax.rsqrt(mean_sq) / math.sqrt(WIDTH)
        inner = jnp.sum(d * x, axis=-1, keepdims=True)
        out[c] = factor * d - factor * x * (inner / (WIDTH * mean_sq))


def video_grad_kernel(clips, mine, got1, got2, got3, c_row, diag, video, out, loss, scr):
    at = pl.ds(0, VOWN)
    total = mine[at, :]
    for got in (got1, got2, got3):
        total = total + got[at, :].astype(F32)
    token_grads(total + diag[...], scr, video, out, FRAMES)
    row_part = c_row[:, TEXTS_DEV : TEXTS_DEV + 1]
    tail = pl.ds(VOWN, EXTRA)
    near = unpiece(mine[tail, :]) + unpiece(got1[tail, :].astype(F32))
    far = unpiece(got2[tail, :].astype(F32)) + unpiece(got3[tail, :].astype(F32))
    loss[...] = (near + far + row_part) * (0.5 / clips)


def gloss_grad_kernel(got, diag, gloss, out, scr):
    total = got[0].astype(F32)
    for i in range(1, NXY):
        total = total + got[i].astype(F32)
    token_grads(total + diag[...], scr, gloss, out, GLOSSES)


def shape(*dims, dtype=F32):
    return jax.ShapeDtypeStruct(dims, dtype)


def on_device(clips, video, gloss, frame_count, gloss_count):
    vmem, hbm = pl.BlockSpec(memory_space=pltpu.VMEM), pl.BlockSpec(memory_space=pltpu.HBM)
    over_all = ("outer", "inner")

    def to_core(a):
        return lax.ppermute(a, "inner", [(i, i ^ 1) for i in range(lax.axis_size("inner"))])

    def to_z(a, mask):
        return lax.ppermute(a, "outer", [(i, i ^ mask) for i in range(lax.axis_size("outer"))])

    def exchanged(a, groups):
        return lax.all_to_all(a, over_all, 0, 0, axis_index_groups=groups, tiled=True)

    def gathered(a, groups):
        return lax.all_gather(a, over_all, axis=0, axis_index_groups=groups, tiled=True)

    def in_hbm(*arrays):
        return [pltpu.with_memory_space_constraint(a, pltpu.HBM) for a in arrays]

    with jax.named_scope("unit_tokens"):
        v_own, g_send, g_own, counts = pl.pallas_call(
            units_kernel,
            in_specs=[hbm] * 4,
            out_shape=(
                shape(VOWN, WIDTH, dtype=BF16),
                shape(NXY, GOWN, WIDTH, dtype=BF16),
                shape(GOWN, WIDTH, dtype=BF16),
                shape(8, LANES, dtype=jnp.int32),
            ),
            scratch_shapes=[
                pltpu.SMEM((OWN,), jnp.int32),
                pltpu.SMEM((OWN,), jnp.int32),
                pltpu.VMEM((OWN, FRAMES, WIDTH), BF16),
                pltpu.VMEM((OWN, GLOSSES, WIDTH), BF16),
                two_halves(VOWN),
                two_halves(GOWN),
                pltpu.SemaphoreType.DMA((4,)),
            ],
            compiler_params=params(),
            cost_estimate=cost(2e5, 7e5),
        )(*in_hbm(frame_count, gloss_count, video, gloss))

    with jax.named_scope("gather"):
        g_got = exchanged(g_send, XY_GROUPS)
        v_got = gathered(gathered(v_own, Z_QUADS), Z_PAIRS)
        v_got = gathered(v_got, CORE_GROUPS)

    def whole(*dims):
        return pl.BlockSpec(dims, lambda i: (0,) * len(dims))

    with jax.named_scope("forward"):
        v_all, g_all, row_inv, col_inv, e_pair, r_part, c_part = pl.pallas_call(
            forward_kernel,
            in_specs=[vmem] * 2,
            out_specs=[hbm] * 2 + [vmem] * 5,
            out_shape=(
                pltpu.HBM((VROWS, WIDTH), BF16),
                pltpu.HBM((GROWS, WIDTH), BF16),
                shape(VROWS, LANES),
                shape(TILES, CLIPS_DEV, LANES),
                shape(CLIPS_DEV, LANES),
                shape(NZC, 1, LANES),
                shape(1, LANES),
            ),
            scratch_shapes=[
                pltpu.VMEM((VROWS, WIDTH), BF16),
                pltpu.VMEM((GROWS, WIDTH), BF16),
                two_halves(VROWS),
                two_halves(NXY * GOWN),
                pltpu.VMEM((VROWS, LANES), F32),
                pltpu.VMEM((TILES, 1, LANES), F32),
                pltpu.VMEM((VROWS, 3 * LANES), F32),
                pltpu.VMEM((TILES, CLIPS_DEV, LANES), F32),
                pltpu.SemaphoreType.DMA((2,)),
            ],
            compiler_params=params(),
            cost_estimate=cost(2 * VROWS * GROWS * WIDTH, 8e6, VROWS * GROWS),
        )(v_got, g_got)

    with jax.named_scope("row_sums"):
        c_send, r_row = pl.pallas_call(
            row_sums_kernel,
            in_specs=[vmem] * 2,
            out_shape=(shape(NXY, 1, LANES), shape(1, LANES)),
            compiler_params=params(),
            cost_estimate=cost(1e5, 3e5),
        )(exchanged(r_part, ZC_GROUPS), c_part)
    with jax.named_scope("column_sums"):
        c_got = exchanged(c_send, XY_GROUPS)

    with jax.named_scope("weights"):
        weights = pl.pallas_call(
            weights_kernel,
            in_specs=[hbm, hbm, vmem, vmem, vmem],
            out_specs=hbm,
            out_shape=pltpu.HBM((2, VROWS, HALF), BF16),
            scratch_shapes=[
                pltpu.VMEM((VROWS, WIDTH), BF16),
                pltpu.VMEM((GROWS, WIDTH), BF16),
                pltpu.VMEM((2, VROWS, HALF), BF16),
                pltpu.SemaphoreType.DMA((6,)),
            ],
            compiler_params=params(),
            cost_estimate=cost(2 * VROWS * GROWS * WIDTH, 12e6, VROWS * GROWS),
        )(*in_hbm(v_all, g_all), row_inv, col_inv, e_pair)

    with jax.named_scope("by_clip"):
        by_clip, av = pl.pallas_call(
            by_clip_kernel,
            grid=(2,),
            in_specs=[
                whole(1, LANES),
                pl.BlockSpec((1, VROWS, HALF), lambda i: (i, 0, 0)),
                whole(VROWS, WIDTH),
                pl.BlockSpec((HALF, WIDTH), lambda i: (i, 0)),
            ],
            out_specs=(
                pl.BlockSpec((GLOSSES // 2, TEXTS_DEV, 2 * WIDTH), lambda i: (i, 0, 0)),
                whole(VROWS, WIDTH),
            ),
            out_shape=(pltpu.HBM((GLOSSES, TEXTS_DEV, 2 * WIDTH), F32), shape(VROWS, WIDTH)),
            scratch_shapes=[pltpu.VMEM((VROWS, 2 * WIDTH), BF16)],
            compiler_params=params(),
            cost_estimate=cost(6 * VROWS * GROWS * WIDTH, 14e6),
        )(r_row, *in_hbm(weights, v_all, g_all))

    with jax.named_scope("clip_send"):
        v_rows = FRAMES * CLIPS_DEV // 2 + EXTRA
        mine, twin = pl.pallas_call(
            clip_send_kernel,
            in_specs=[vmem, vmem, hbm, hbm, vmem],
            out_shape=(shape(v_rows, WIDTH), shape(v_rows, WIDTH, dtype=BF16)),
            scratch_shapes=[
                pltpu.VMEM((2, VROWS, HALF), BF16),
                pltpu.VMEM((GROWS, WIDTH), BF16),
                pltpu.VMEM((GROWS, WIDTH), BF16),
                pltpu.SemaphoreType.DMA((5,)),
            ],
            compiler_params=params(),
            cost_estimate=cost(2 * VROWS * GROWS * WIDTH, 1e7),
        )(c_got, r_row, *in_hbm(weights, g_all), av)

    with jax.named_scope("gloss_send"):
        twin, c_ready = lax.optimization_barrier((twin, c_got))
        dg_send, c_row = pl.pallas_call(
            gloss_send_kernel,
            in_specs=[vmem, hbm],
            out_shape=(shape(NXY, GOWN, WIDTH, dtype=BF16), shape(1, LANES)),
            scratch_shapes=[
                pltpu.VMEM((GLOSSES, TEXTS_DEV, 2 * WIDTH), F32),
                two_halves(NXY * GOWN),
                pltpu.SemaphoreType.DMA((QUADS,)),
            ],
            compiler_params=params(),
            cost_estimate=cost(2e6, 5e6),
        )(c_ready, *in_hbm(by_clip))
        dg_got = exchanged(dg_send, XY_GROUPS)

    def kept_and_sent(owners):
        rows = owners * VOWN + EXTRA
        return (shape(rows, WIDTH), shape(rows, WIDTH, dtype=BF16))

    with jax.named_scope("clips_by_core"):
        mine, sent = pl.pallas_call(
            clip_rows_kernel,
            in_specs=[vmem] * 2,
            out_shape=kept_and_sent(NZ // 2),
            scratch_shapes=[two_halves(NZ * VOWN)],
            compiler_params=params(),
            cost_estimate=cost(1e6, 2e6),
        )(mine, to_core(twin))
    with jax.named_scope("clips_by_z"):
        mine, *sent = pl.pallas_call(
            quarter_kernel,
            in_specs=[vmem] * 2,
            out_shape=kept_and_sent(1) + kept_and_sent(1)[1:] * 2,
            compiler_params=params(),
            cost_estimate=cost(1e10, 1e6),
        )(mine, to_z(sent, 1))

    with jax.named_scope("diagonal"):
        mine, v_own, g_own, counts = lax.optimization_barrier((mine, v_own, g_own, counts))
        dv_diag, dg_diag = pl.pallas_call(
            diagonal_kernel,
            in_specs=[vmem] * 3,
            out_shape=(shape(VOWN, WIDTH), shape(GOWN, WIDTH)),
            compiler_params=params(),
            cost_estimate=cost(2e7, 3e5),
        )(counts, v_own, g_own)

    with jax.named_scope("video_grad"):
        grad_video, loss = pl.pallas_call(
            functools.partial(video_grad_kernel, clips),
            in_specs=[vmem] * 7,
            out_shape=(shape(OWN, FRAMES, WIDTH), shape(1, 1)),
            scratch_shapes=[two_halves(VOWN)],
            compiler_params=params(),
            cost_estimate=cost(1e6, 1e6),
        )(mine, *[to_z(a, 2 * m) for m, a in enumerate(sent, start=1)], c_row, dv_diag, video)
    with jax.named_scope("gloss_grad"):
        grad_gloss = pl.pallas_call(
            gloss_grad_kernel,
            in_specs=[vmem] * 3,
            out_shape=shape(OWN, GLOSSES, WIDTH),
            scratch_shapes=[two_halves(GOWN)],
            compiler_params=params(),
            cost_estimate=cost(1e6, 1e6),
        )(dg_got, dg_diag, gloss)
    return loss.reshape(()), grad_video, grad_gloss


def solution(mesh):
    clips = OWN * mesh.shape["outer"] * mesh.shape["inner"]
    over_all = ("outer", "inner")
    tokens, counts = P(over_all, None, None), P(over_all)
    return jax.shard_map(
        functools.partial(on_device, clips),
        mesh=mesh,
        in_specs=(tokens, tokens, counts, counts),
        out_specs=(P(), tokens, tokens),
        check_vma=False,
    )
```

```python
import functools
import math

import jax
import jax.numpy as jnp
from jax import lax
from jax.experimental import pallas as pl
from jax.experimental.pallas import tpu as pltpu
from jax.sharding import PartitionSpec as P

F32 = jnp.float32
BF16 = jnp.bfloat16
EPSILON = 1e-06
EXP_SCALE = 10.0 * math.log2(math.e)
MARK = 2.0
MARK_LIMIT = 1.5
FAR = -1e30

NZ, NY, NX, NCORE = 8, 8, 4, 2
OWN = 3
FRAMES, GLOSSES, WIDTH = 32, 16, 256
CLIPS_DEV = NZ * NCORE * OWN
TEXTS_DEV = NY * NX * OWN
LANES = 128
VROWS = FRAMES * CLIPS_DEV
GROWS = GLOSSES * TEXTS_DEV
VOWN = FRAMES * OWN
GOWN = GLOSSES * OWN
EXTRA = 16
V_PITCH, G_PITCH = VOWN + 8, GOWN + 8
QUADS = GLOSSES // 4
TILES = GROWS // LANES
HALF = GROWS // 2
NXY, NZC = NX * NY, NZ * NCORE

def flat(x, z, y, core):
    return ((x % 2) * NZ + z) * 32 + (x // 2) * 16 + 2 * y + core


def z_groups(masks):
    return [
        [flat(x, z ^ mask, y, c) for mask in masks]
        for x in range(NX)
        for y in range(NY)
        for c in range(NCORE)
        for z in range(NZ)
        if not z & masks[-1] and not z & masks[len(masks) // 2]
    ]


Z_QUADS, Z_PAIRS = z_groups((0, 2, 4, 6)), z_groups((0, 1))
CORE_GROUPS = [[flat(x, z, y, c) for c in range(NCORE)] for x in range(NX) for y in range(NY) for z in range(NZ)]
XY_GROUPS = [[flat(x, z, y, c) for x in range(NX) for y in range(NY)] for z in range(NZ) for c in range(NCORE)]
ZC_GROUPS = [[flat(x, z, y, c) for c in range(NCORE) for z in range(NZ)] for x in range(NX) for y in range(NY)]


def params(limit_mb=32):
    return pltpu.CompilerParams(vmem_limit_bytes=limit_mb * 1024 * 1024)


def cost(flops, nbytes, trans=0):
    return pl.CostEstimate(flops=int(flops), bytes_accessed=int(nbytes), transcendentals=int(trans))


def iota(shape, dim):
    return lax.broadcasted_iota(jnp.int32, shape, dim)


def nt(a, b, **kw):
    return lax.dot_general(a, b, (((1,), (1,)), ((), ())), preferred_element_type=F32, **kw)


def nn(a, b, **kw):
    return lax.dot_general(a, b, (((1,), (0,)), ((), ())), preferred_element_type=F32, **kw)


def tn(a, b, **kw):
    return lax.dot_general(a, b, (((0,), (0,)), ((), ())), preferred_element_type=F32, **kw)


def column_of(row, n):
    eye = iota((n, LANES), 0) == iota((n, LANES), 1)
    return jnp.sum(jnp.where(eye, jnp.broadcast_to(row, (n, LANES)), 0.0), axis=1, keepdims=True)


def packed(x):
    lane = iota(x.shape, 1)
    a, b, c = (pltpu.roll(x, shift, 1) for shift in (96, 64, 32))
    return jnp.where(lane < 96, x, a), jnp.where(lane < 64, a, b), jnp.where(lane < 32, b, c)


def unpacked_sum(t0, t1, t2):
    lane = iota(t0.shape, 1)
    second = pltpu.roll(jnp.where(lane >= 96, t0, t1), 32, 1)
    third = pltpu.roll(jnp.where(lane >= 64, t1, t2), 64, 1)
    return (t0 + second) + (third + pltpu.roll(t2, 96, 1))


def pieces(value):
    lane = iota((EXTRA, WIDTH), 1)
    full = jnp.broadcast_to(value, (EXTRA, WIDTH))
    hi = full.astype(BF16).astype(F32)
    mid = (full - hi).astype(BF16).astype(F32)
    low = (full - hi - mid).astype(BF16).astype(F32)
    return jnp.where(lane == 0, hi, jnp.where(lane == 1, mid, jnp.where(lane == 2, low, 0.0)))


def unpiece(block):
    mine = (iota((EXTRA, WIDTH), 0) == 0) & (iota((EXTRA, WIDTH), 1) < 3)
    return jnp.sum(jnp.where(mine, block, 0.0), keepdims=True).reshape(1, 1)


def put(ref, at, value):
    ref[0, at, :] = value[:, :LANES]
    ref[1, at, :] = value[:, LANES:]


def get(ref, at):
    return jnp.concatenate([ref[0, at, :], ref[1, at, :]], axis=1)


def two_halves(rows):
    return pltpu.VMEM((2, rows, LANES), F32)


def units_kernel(fc_in, gc_in, video_in, gloss_in, v_out, g_out, g_one, count_out, fc, gc, video, gloss, v_scr, g_scr, sems):
    pairs = ((fc_in, fc), (gc_in, gc), (video_in, video), (gloss_in, gloss))
    copies = [pltpu.make_async_copy(a, b, sems.at[i]) for i, (a, b) in enumerate(pairs)]
    for copy in copies:
        copy.start()
    for copy in copies:
        copy.wait()
    row = iota((8, LANES), 0)
    counts = jnp.zeros((8, LANES), jnp.int32)
    for c in range(OWN):
        counts = jnp.where(row == c, fc[c], jnp.where(row == OWN + c, gc[c], counts))
    count_out[...] = counts
    for count, raw, scr, tokens in ((fc, video, v_scr, FRAMES), (gc, gloss, g_scr, GLOSSES)):
        row, lane = iota((tokens, WIDTH), 0), iota((tokens, WIDTH), 1)
        for c in range(OWN):
            x = raw[c].astype(F32)
            mean_sq = jnp.mean(x * x, axis=-1, keepdims=True) + EPSILON
            unit = x * (lax.rsqrt(mean_sq) / math.sqrt(WIDTH))
            mark = jnp.where(lane == 0, MARK, 0.0)
            put(scr, pl.ds(c, tokens, stride=OWN), jnp.where(row < count[c], unit, mark))
    v = get(v_scr, pl.ds(0, VOWN)).astype(BF16)
    g = get(g_scr, pl.ds(0, GOWN)).astype(BF16)
    v_out[...] = v
    g_one[...] = g
    for i in range(NXY):
        g_out[i] = g


def diagonal_kernel(count_ref, v_ref, g_ref, dv, dg):
    def pick(count, which):
        return jnp.where(which == 0, count[0], jnp.where(which == 1, count[1], count[2]))

    fc = [count_ref[c : c + 1, 0:1] for c in range(OWN)]
    gc = [count_ref[OWN + c : OWN + c + 1, 0:1] for c in range(OWN)]
    v, g = v_ref[...], g_ref[...]
    shape = (VOWN, GOWN)
    r, q = iota(shape, 0), iota(shape, 1)
    rc, qc = lax.rem(r, OWN), lax.rem(q, OWN)
    valid = (rc == qc) & (lax.div(r, OWN) < pick(fc, rc)) & (lax.div(q, OWN) < pick(gc, qc))
    e = jnp.where(valid, jnp.exp2(nt(v, g) * EXP_SCALE), 0.0)
    r1, q1 = iota((VOWN, 1), 0), iota((1, GOWN), 1)
    rc1, qc1 = lax.rem(r1, OWN), lax.rem(q1, OWN)
    frames_r, glosses_q = pick(fc, rc1), pick(gc, qc1)
    row_ok = lax.div(r1, OWN) < frames_r
    col_ok = lax.div(q1, OWN) < glosses_q
    frames_r, glosses_q = frames_r.astype(F32), glosses_q.astype(F32)
    rows = jnp.where(row_ok, jnp.sum(e, axis=1, keepdims=True), 1.0)
    cols = jnp.where(col_ok, jnp.sum(e, axis=0, keepdims=True), 1.0)
    weight = -5.0 * e * (1.0 / (rows * frames_r) + 1.0 / (cols * glosses_q))
    dv[...] = nn(weight, g.astype(F32), precision=lax.Precision.HIGHEST)
    dg[...] = tn(weight, v.astype(F32), precision=lax.Precision.HIGHEST)


def exp_scores(v, g):
    return jnp.exp2(nt(v, g) * EXP_SCALE)


def forward_kernel(
    v_got, g_got,
    v_hbm, g_hbm, row_out, col_out, e_out, r_out, c_out,
    v_out, g_out, v_scr, g_scr, frame_mask, gloss_mask, rows, cols, sems,
):
    results = ((v_out, v_hbm), (g_out, g_hbm))
    copies = [pltpu.make_async_copy(a, b, sems.at[i]) for i, (a, b) in enumerate(results)]
    for i in range(NZC):
        put(v_scr, pl.ds(i * V_PITCH, VOWN), v_got[pl.ds(i * VOWN, VOWN), :].astype(F32))
    for f in range(FRAMES):
        parts = [
            get(v_scr, pl.ds(k * NZ * V_PITCH + f * OWN + c, NZ, stride=V_PITCH)) for k in range(NCORE) for c in range(OWN)
        ]
        v_out[pl.ds(f * CLIPS_DEV, CLIPS_DEV), :] = jnp.concatenate(parts, axis=0).astype(BF16)
    copies[0].start()
    for i in range(NXY):
        put(g_scr, pl.ds(i * G_PITCH, GOWN), g_got[i].astype(F32))
    for g in range(GLOSSES):
        parts = [
            get(g_scr, pl.ds(x * NY * G_PITCH + g * OWN + c, NY, stride=G_PITCH)) for x in range(NX) for c in range(OWN)
        ]
        g_out[pl.ds(g * TEXTS_DEV, TEXTS_DEV), :] = jnp.concatenate(parts, axis=0).astype(BF16)
    copies[1].start()

    first = jnp.where(iota((WIDTH, LANES), 0) == 0, 1.0, 0.0).astype(BF16)
    frame_mask[...] = jnp.where(nn(v_out[...], first) < MARK_LIMIT, 1.0, 0.0)
    first_row = jnp.where(iota((16, WIDTH), 1) == 0, 1.0, 0.0).astype(BF16)
    for t in range(TILES):
        found = nt(first_row, g_out[pl.ds(t * LANES, LANES), :])[0:1]
        gloss_mask[t] = jnp.where(found < MARK_LIMIT, 1.0, 0.0)
    frames = jnp.zeros((CLIPS_DEV, LANES), F32)
    for f in range(FRAMES):
        frames = frames + frame_mask[pl.ds(f * CLIPS_DEV, CLIPS_DEV), :]
    by_tile = []
    for t in range(3):
        by_tile.append(gloss_mask[t] + gloss_mask[t + 3] + gloss_mask[t + 6] + gloss_mask[t + 9])
    lane = iota((CLIPS_DEV, LANES), 1)
    real = lane < TEXTS_DEV
    counts = unpacked_sum(*[jnp.broadcast_to(t, (8, LANES)) for t in by_tile])
    glosses = jnp.where(real[0:8], counts, 1.0)
    packed_glosses = [t[0:1] for t in packed(glosses)]
    glosses = glosses[0:1]

    for half in range(2):
        e = exp_scores(v_out[...], g_out[pl.ds(half * HALF, HALF), :])
        tiles = range(half * TILES // 2, (half + 1) * TILES // 2)
        masks = [gloss_mask[t] for t in tiles]
        sums = [jnp.zeros((CLIPS_DEV, LANES), F32) for _ in tiles]
        for f in range(FRAMES):
            at = pl.ds(f * CLIPS_DEV, CLIPS_DEV)
            mask = frame_mask[at, :]
            block = e[f * CLIPS_DEV : (f + 1) * CLIPS_DEV]
            parts = [block[:, k * LANES : (k + 1) * LANES] for k in range(TILES // 2)]
            sums = [total + part * mask for total, part in zip(sums, parts, strict=True)]
            for k in range(3):
                part = parts[k] * masks[k] + parts[k + 3] * masks[k + 3]
                rows[at, pl.ds(k * LANES, LANES)] = part if half == 0 else rows[at, pl.ds(k * LANES, LANES)] + part
        for k, t in enumerate(tiles):
            cols[t] = sums[k]

    video_part = jnp.zeros((CLIPS_DEV, LANES), F32)
    for f in range(FRAMES):
        at = pl.ds(f * CLIPS_DEV, CLIPS_DEV)
        mask = frame_mask[at, :]
        total = unpacked_sum(*[rows[at, pl.ds(k * LANES, LANES)] for k in range(3)])
        total = jnp.where(real, total, 1.0)
        video_part = video_part + mask * jnp.log(total)
        row_out[at, :] = jnp.where(mask > 0.0, 1.0 / (total * frames), FAR)
    video_part = video_part / frames - jnp.log(glosses)
    gloss_parts = [jnp.zeros((CLIPS_DEV, LANES), F32)] * 3
    for t in range(TILES):
        mask = gloss_mask[t]
        total = cols[t]
        gloss_parts[t % 3] = gloss_parts[t % 3] + mask * jnp.log(total)
        col_out[t] = jnp.where(mask > 0.0, 1.0 / (total * packed_glosses[t % 3]), FAR)
    gloss_part = unpacked_sum(*gloss_parts) / glosses - jnp.log(frames)
    logits = 0.5 * (video_part + gloss_part)
    e_pair = jnp.where(real, jnp.exp(logits), 0.0)
    e_out[...] = e_pair

    sums = jnp.sum(e_pair, axis=1, keepdims=True)
    across = lane == iota((CLIPS_DEV, LANES), 0)
    r_row = jnp.sum(jnp.where(across, jnp.broadcast_to(sums, (CLIPS_DEV, LANES)), 0.0), axis=0, keepdims=True)
    inner, outer = lax.axis_index("inner"), lax.axis_index("outer")
    z, core = lax.rem(outer, NZ), lax.rem(inner, NCORE)
    x, y = 2 * lax.div(inner, 16) + lax.div(outer, NZ), lax.rem(lax.div(inner, NCORE), NY)
    clip0 = core * OWN * NZ + lax.rem(z, 2) * (NZ // 2) + lax.div(z, 2)
    text0 = x * OWN * NY + y
    own = jnp.zeros((CLIPS_DEV, LANES), jnp.bool_)
    for c in range(OWN):
        own = own | ((iota((CLIPS_DEV, LANES), 0) == clip0 + c * NZ) & (lane == text0 + c * NY))
    diag = jnp.sum(jnp.where(own, logits, 0.0), keepdims=True).reshape(1, 1)
    r_row = jnp.where(iota((1, LANES), 1) == CLIPS_DEV, diag, r_row)
    for i in range(NZC):
        r_out[i] = r_row
    c_out[...] = jnp.sum(e_pair, axis=0, keepdims=True)
    for copy in copies:
        copy.wait()


def started(copies):
    for copy in copies:
        copy.start()
    return copies


def halves_of(p):
    return [(r, h, p.at[h, pl.ds(r * VROWS // 2, VROWS // 2)]) for r in range(2) for h in range(2)]


def weights_kernel(v_hbm, g_hbm, row_ref, col_ref, e_ref, p_hbm, v, g, p, sems):
    loads = started([pltpu.make_async_copy(a, b, sems.at[i]) for i, (a, b) in enumerate(((v_hbm, v), (g_hbm, g)))])
    scales = packed(2.5 * e_ref[...])
    for load in loads:
        load.wait()
    stores = []
    for (r, h, out), (_, _, here) in zip(halves_of(p_hbm), halves_of(p), strict=True):
        e = exp_scores(v[pl.ds(r * VROWS // 2, VROWS // 2), :], g[pl.ds(h * HALF, HALF), :])
        for f in range(FRAMES // 2):
            row = packed(row_ref[pl.ds((r * FRAMES // 2 + f) * CLIPS_DEV, CLIPS_DEV), :])
            block = e[f * CLIPS_DEV : (f + 1) * CLIPS_DEV]
            parts = []
            for k in range(TILES // 2):
                share = jnp.maximum(row[k % 3] + col_ref[h * TILES // 2 + k], 0.0)
                parts.append(scales[k % 3] * block[:, k * LANES : (k + 1) * LANES] * share)
            here[pl.ds(f * CLIPS_DEV, CLIPS_DEV), :] = jnp.concatenate(parts, axis=1).astype(BF16)
        stores += started([pltpu.make_async_copy(here, out, sems.at[2 + 2 * r + h])])
    for store in stores:
        store.wait()


def added(got):
    total = got[0]
    for i in range(1, got.shape[0]):
        total = total + got[i]
    return total


def row_sums_kernel(r_got, c_part, c_out, r_out):
    r_row = added(r_got)
    r_out[...] = r_row
    lane = iota((1, LANES), 1)
    logs = jnp.where(lane < CLIPS_DEV, jnp.log(jnp.where(lane < CLIPS_DEV, r_row, 1.0)), 0.0)
    logs = logs - jnp.where(lane == CLIPS_DEV, 2.0 * r_row, 0.0)
    total = jnp.sum(logs, axis=1, keepdims=True)
    message = jnp.where(lane == TEXTS_DEV, total, c_part[...])
    for i in range(NXY):
        c_out[i] = message


def inverse_texts(c_row):
    return jnp.broadcast_to(1.0 / column_of(c_row, TEXTS_DEV), (TEXTS_DEV, WIDTH))


def by_clip_kernel(r_ref, p_ref, v_ref, g_ref, out, av_out, both):
    step = pl.program_id(0)

    @pl.when(step == 0)
    def _():
        inverse = jnp.broadcast_to(1.0 / column_of(r_ref[...], CLIPS_DEV), (CLIPS_DEV, WIDTH))
        for f in range(FRAMES):
            at = pl.ds(f * CLIPS_DEV, CLIPS_DEV)
            v = v_ref[at, :]
            both[at, :WIDTH] = v
            both[at, WIDTH:] = (v.astype(F32) * inverse).astype(BF16)

    out[...] = tn(p_ref[0], both[...]).reshape(GLOSSES // 2, TEXTS_DEV, 2 * WIDTH)
    part = nn(p_ref[0], g_ref[...])

    @pl.when(step == 0)
    def _():
        av_out[...] = part

    @pl.when(step > 0)
    def _():
        av_out[...] = av_out[...] + part


def gloss_send_kernel(c_got, by_clip, out, c_out, held, scr, sems):
    many = GLOSSES // QUADS
    copies = started(
        [
            pltpu.make_async_copy(by_clip.at[pl.ds(q * many, many)], held.at[pl.ds(q * many, many)], sems.at[q])
            for q in range(QUADS)
        ]
    )
    c_out[...] = added(c_got)
    col = inverse_texts(c_out[...])
    for q, copy in enumerate(copies):
        copy.wait()
        for k in range(many):
            g = q * many + k
            block = held[g, :, :WIDTH] * col + held[g, :, WIDTH:]
            row = g * OWN
            for x in range(NX):
                for c in range(OWN):
                    first = (x * OWN + c) * NY
                    put(scr, pl.ds(x * NY * G_PITCH + row + c, NY, stride=G_PITCH), block[first : first + NY])
    for i in range(NXY):
        out[i] = get(scr, pl.ds(i * G_PITCH, GOWN)).astype(BF16)


def clip_send_kernel(c_got, r_ref, p_hbm, g, av_ref, mine, twin, p, g_by_text, sems):
    copies = []
    for (r, h, theirs), (_, _, here) in zip(halves_of(p_hbm), halves_of(p), strict=True):
        copies.append(pltpu.make_async_copy(theirs, here, sems.at[2 * r + h]))
    started(copies)
    c_row = added(c_got)
    col = inverse_texts(c_row)
    core = lax.rem(lax.axis_index("inner"), NCORE)
    inverse = jnp.broadcast_to(1.0 / column_of(r_ref[...], CLIPS_DEV), (CLIPS_DEV, WIDTH))
    half = CLIPS_DEV // 2
    for i in range(GLOSSES):
        at = pl.ds(i * TEXTS_DEV, TEXTS_DEV)
        g_by_text[at, :] = (g[at, :].astype(F32) * col).astype(BF16)
    for r in range(2):
        copies[2 * r].wait()
        copies[2 * r + 1].wait()
        at = pl.ds(r * VROWS // 2, VROWS // 2)
        part = nn(p[0, at, :], g_by_text[pl.ds(0, HALF), :]) + nn(p[1, at, :], g_by_text[pl.ds(HALF, HALF), :])
        for pair in range(FRAMES // 4):
            others = []
            for f in (2 * pair, 2 * pair + 1):
                full = r * FRAMES // 2 + f
                new = part[f * CLIPS_DEV : (f + 1) * CLIPS_DEV]
                block = av_ref[pl.ds(full * CLIPS_DEV, CLIPS_DEV), :] * inverse + new
                low, high = block[:half], block[half:]
                mine[pl.ds(full * half, half), :] = jnp.where(core == 0, low, high)
                others.append(jnp.where(core == 0, high, low))
            at = pl.ds((r * FRAMES // 4 + pair) * CLIPS_DEV, CLIPS_DEV)
            twin[at, :] = jnp.concatenate(others, axis=0).astype(BF16)
    real = iota((1, LANES), 1) < TEXTS_DEV
    logs = jnp.where(real, jnp.log(jnp.where(real, c_row, 1.0)), 0.0)
    extra = pieces(jnp.sum(logs, axis=1, keepdims=True))
    mine[pl.ds(FRAMES * half, EXTRA), :] = extra
    twin[pl.ds(FRAMES * half, EXTRA), :] = extra.astype(BF16)


def own_z():
    return lax.rem(lax.axis_index("outer"), NZ)


def clip_rows_kernel(mine, got, keep, send, scr):
    step = 2 * NZ
    for i in range(VOWN // 2):
        at = pl.ds(i * step, step)
        two = mine[at, :] + got[at, :].astype(F32)
        for k in range(2):
            put(scr, pl.ds(2 * i + k, NZ, stride=V_PITCH), two[k * NZ : (k + 1) * NZ])
    bit = lax.rem(own_z(), 2)
    owners = NZ // 2
    for i in range(owners):
        at = pl.ds(i * VOWN, VOWN)
        keep[at, :] = get(scr, pl.ds(pl.multiple_of((owners * bit + i) * V_PITCH, 8), VOWN))
        send[at, :] = get(scr, pl.ds(pl.multiple_of((owners * (1 - bit) + i) * V_PITCH, 8), VOWN)).astype(BF16)
    extra = loss_rows(mine, got, NZ)
    keep[pl.ds(owners * VOWN, EXTRA), :] = extra
    send[pl.ds(owners * VOWN, EXTRA), :] = extra.astype(BF16)


def loss_rows(mine, got, owners):
    tail = pl.ds(owners * VOWN, EXTRA)
    return pieces(unpiece(mine[tail, :]) + unpiece(got[tail, :].astype(F32)))


def quarter_kernel(mine, got, keep, *sends):
    own = lax.div(own_z(), 2)
    extra = loss_rows(mine, got, NZ // 2)
    for out, owner in zip((keep, *sends), (own, own ^ 1, own ^ 2, own ^ 3), strict=True):
        at = pl.ds(pl.multiple_of(owner * VOWN, VOWN), VOWN)
        out[pl.ds(0, VOWN), :] = (mine[at, :] + got[at, :].astype(F32)).astype(out.dtype)
        out[pl.ds(VOWN, EXTRA), :] = extra.astype(out.dtype)


def token_grads(total, scr, raw, out, tokens):
    put(scr, pl.ds(0, OWN * tokens), total)
    for c in range(OWN):
        x = raw[c].astype(F32)
        d = get(scr, pl.ds(c, tokens, stride=OWN))
        mean_sq = jnp.mean(x * x, axis=-1, keepdims=True) + EPSILON
        factor = lax.rsqrt(mean_sq) / math.sqrt(WIDTH)
        inner = jnp.sum(d * x, axis=-1, keepdims=True)
        out[c] = factor * d - factor * x * (inner / (WIDTH * mean_sq))


def video_grad_kernel(clips, mine, got1, got2, got3, c_row, diag, video, out, loss, scr):
    at = pl.ds(0, VOWN)
    total = mine[at, :]
    for got in (got1, got2, got3):
        total = total + got[at, :].astype(F32)
    token_grads(total + diag[...], scr, video, out, FRAMES)
    row_part = c_row[:, TEXTS_DEV : TEXTS_DEV + 1]
    tail = pl.ds(VOWN, EXTRA)
    near = unpiece(mine[tail, :]) + unpiece(got1[tail, :].astype(F32))
    far = unpiece(got2[tail, :].astype(F32)) + unpiece(got3[tail, :].astype(F32))
    loss[...] = (near + far + row_part) * (0.5 / clips)


def gloss_grad_kernel(got, diag, gloss, out, scr):
    total = got[0].astype(F32)
    for i in range(1, NXY):
        total = total + got[i].astype(F32)
    token_grads(total + diag[...], scr, gloss, out, GLOSSES)


def shape(*dims, dtype=F32):
    return jax.ShapeDtypeStruct(dims, dtype)


def on_device(clips, video, gloss, frame_count, gloss_count):
    vmem, hbm = pl.BlockSpec(memory_space=pltpu.VMEM), pl.BlockSpec(memory_space=pltpu.HBM)
    over_all = ("outer", "inner")

    def to_core(a):
        return lax.ppermute(a, "inner", [(i, i ^ 1) for i in range(lax.axis_size("inner"))])

    def to_z(a, mask):
        return lax.ppermute(a, "outer", [(i, i ^ mask) for i in range(lax.axis_size("outer"))])

    def exchanged(a, groups):
        return lax.all_to_all(a, over_all, 0, 0, axis_index_groups=groups, tiled=True)

    def gathered(a, groups):
        return lax.all_gather(a, over_all, axis=0, axis_index_groups=groups, tiled=True)

    def in_hbm(*arrays):
        return [pltpu.with_memory_space_constraint(a, pltpu.HBM) for a in arrays]

    with jax.named_scope("unit_tokens"):
        v_own, g_send, g_own, counts = pl.pallas_call(
            units_kernel,
            in_specs=[hbm] * 4,
            out_shape=(
                shape(VOWN, WIDTH, dtype=BF16),
                shape(NXY, GOWN, WIDTH, dtype=BF16),
                shape(GOWN, WIDTH, dtype=BF16),
                shape(8, LANES, dtype=jnp.int32),
            ),
            scratch_shapes=[
                pltpu.SMEM((OWN,), jnp.int32),
                pltpu.SMEM((OWN,), jnp.int32),
                pltpu.VMEM((OWN, FRAMES, WIDTH), BF16),
                pltpu.VMEM((OWN, GLOSSES, WIDTH), BF16),
                two_halves(VOWN),
                two_halves(GOWN),
                pltpu.SemaphoreType.DMA((4,)),
            ],
            compiler_params=params(),
            cost_estimate=cost(2e5, 7e5),
        )(*in_hbm(frame_count, gloss_count, video, gloss))

    with jax.named_scope("gather"):
        g_got = exchanged(g_send, XY_GROUPS)
        v_got = gathered(gathered(v_own, Z_QUADS), Z_PAIRS)
        v_got = gathered(v_got, CORE_GROUPS)

    def whole(*dims):
        return pl.BlockSpec(dims, lambda i: (0,) * len(dims))

    with jax.named_scope("forward"):
        v_all, g_all, row_inv, col_inv, e_pair, r_part, c_part = pl.pallas_call(
            forward_kernel,
            in_specs=[vmem] * 2,
            out_specs=[hbm] * 2 + [vmem] * 5,
            out_shape=(
                pltpu.HBM((VROWS, WIDTH), BF16),
                pltpu.HBM((GROWS, WIDTH), BF16),
                shape(VROWS, LANES),
                shape(TILES, CLIPS_DEV, LANES),
                shape(CLIPS_DEV, LANES),
                shape(NZC, 1, LANES),
                shape(1, LANES),
            ),
            scratch_shapes=[
                pltpu.VMEM((VROWS, WIDTH), BF16),
                pltpu.VMEM((GROWS, WIDTH), BF16),
                two_halves(NZC * V_PITCH),
                two_halves(NXY * G_PITCH),
                pltpu.VMEM((VROWS, LANES), F32),
                pltpu.VMEM((TILES, 1, LANES), F32),
                pltpu.VMEM((VROWS, 3 * LANES), F32),
                pltpu.VMEM((TILES, CLIPS_DEV, LANES), F32),
                pltpu.SemaphoreType.DMA((2,)),
            ],
            compiler_params=params(),
            cost_estimate=cost(2 * VROWS * GROWS * WIDTH, 8e6, VROWS * GROWS),
        )(v_got, g_got)

    with jax.named_scope("row_sums"):
        c_send, r_row = pl.pallas_call(
            row_sums_kernel,
            in_specs=[vmem] * 2,
            out_shape=(shape(NXY, 1, LANES), shape(1, LANES)),
            compiler_params=params(),
            cost_estimate=cost(1e5, 3e5),
        )(exchanged(r_part, ZC_GROUPS), c_part)
    with jax.named_scope("column_sums"):
        c_got = exchanged(c_send, XY_GROUPS)

    with jax.named_scope("weights"):
        weights = pl.pallas_call(
            weights_kernel,
            in_specs=[hbm, hbm, vmem, vmem, vmem],
            out_specs=hbm,
            out_shape=pltpu.HBM((2, VROWS, HALF), BF16),
            scratch_shapes=[
                pltpu.VMEM((VROWS, WIDTH), BF16),
                pltpu.VMEM((GROWS, WIDTH), BF16),
                pltpu.VMEM((2, VROWS, HALF), BF16),
                pltpu.SemaphoreType.DMA((6,)),
            ],
            compiler_params=params(),
            cost_estimate=cost(2 * VROWS * GROWS * WIDTH, 12e6, VROWS * GROWS),
        )(*in_hbm(v_all, g_all), row_inv, col_inv, e_pair)

    with jax.named_scope("by_clip"):
        by_clip, av = pl.pallas_call(
            by_clip_kernel,
            grid=(2,),
            in_specs=[
                whole(1, LANES),
                pl.BlockSpec((1, VROWS, HALF), lambda i: (i, 0, 0)),
                whole(VROWS, WIDTH),
                pl.BlockSpec((HALF, WIDTH), lambda i: (i, 0)),
            ],
            out_specs=(
                pl.BlockSpec((GLOSSES // 2, TEXTS_DEV, 2 * WIDTH), lambda i: (i, 0, 0)),
                whole(VROWS, WIDTH),
            ),
            out_shape=(pltpu.HBM((GLOSSES, TEXTS_DEV, 2 * WIDTH), F32), shape(VROWS, WIDTH)),
            scratch_shapes=[pltpu.VMEM((VROWS, 2 * WIDTH), BF16)],
            compiler_params=params(),
            cost_estimate=cost(6 * VROWS * GROWS * WIDTH, 14e6),
        )(r_row, *in_hbm(weights, v_all, g_all))

    with jax.named_scope("clip_send"):
        v_rows = FRAMES * CLIPS_DEV // 2 + EXTRA
        mine, twin = pl.pallas_call(
            clip_send_kernel,
            in_specs=[vmem, vmem, hbm, vmem, vmem],
            out_shape=(shape(v_rows, WIDTH), shape(v_rows, WIDTH, dtype=BF16)),
            scratch_shapes=[
                pltpu.VMEM((2, VROWS, HALF), BF16),
                pltpu.VMEM((GROWS, WIDTH), BF16),
                pltpu.SemaphoreType.DMA((4,)),
            ],
            compiler_params=params(),
            cost_estimate=cost(2 * VROWS * GROWS * WIDTH, 1e7),
        )(c_got, r_row, *in_hbm(weights), g_all, av)

    with jax.named_scope("gloss_send"):
        twin, c_ready = lax.optimization_barrier((twin, c_got))
        dg_send, c_row = pl.pallas_call(
            gloss_send_kernel,
            in_specs=[vmem, hbm],
            out_shape=(shape(NXY, GOWN, WIDTH, dtype=BF16), shape(1, LANES)),
            scratch_shapes=[
                pltpu.VMEM((GLOSSES, TEXTS_DEV, 2 * WIDTH), F32),
                two_halves(NXY * G_PITCH),
                pltpu.SemaphoreType.DMA((QUADS,)),
            ],
            compiler_params=params(),
            cost_estimate=cost(2e6, 5e6),
        )(c_ready, *in_hbm(by_clip))
        dg_got = exchanged(dg_send, XY_GROUPS)

    def kept_and_sent(owners):
        rows = owners * VOWN + EXTRA
        return (shape(rows, WIDTH), shape(rows, WIDTH, dtype=BF16))

    with jax.named_scope("clips_by_core"):
        mine, sent = pl.pallas_call(
            clip_rows_kernel,
            in_specs=[vmem] * 2,
            out_shape=kept_and_sent(NZ // 2),
            scratch_shapes=[two_halves(NZ * V_PITCH)],
            compiler_params=params(),
            cost_estimate=cost(1e6, 2e6),
        )(mine, to_core(twin))
    with jax.named_scope("clips_by_z"):
        mine, *sent = pl.pallas_call(
            quarter_kernel,
            in_specs=[vmem] * 2,
            out_shape=kept_and_sent(1) + kept_and_sent(1)[1:] * 2,
            compiler_params=params(),
            cost_estimate=cost(1e10, 1e6),
        )(mine, to_z(sent, 1))

    with jax.named_scope("diagonal"):
        mine, v_own, g_own, counts = lax.optimization_barrier((mine, v_own, g_own, counts))
        dv_diag, dg_diag = pl.pallas_call(
            diagonal_kernel,
            in_specs=[vmem] * 3,
            out_shape=(shape(VOWN, WIDTH), shape(GOWN, WIDTH)),
            compiler_params=params(),
            cost_estimate=cost(2e7, 3e5),
        )(counts, v_own, g_own)

    with jax.named_scope("gloss_grad"):
        grad_gloss = pl.pallas_call(
            gloss_grad_kernel,
            in_specs=[vmem] * 3,
            out_shape=shape(OWN, GLOSSES, WIDTH),
            scratch_shapes=[two_halves(GOWN)],
            compiler_params=params(),
            cost_estimate=cost(1e6, 1e6),
        )(dg_got, dg_diag, gloss)
    mine, grad_gloss = lax.optimization_barrier((mine, grad_gloss))

    with jax.named_scope("video_grad"):
        grad_video, loss = pl.pallas_call(
            functools.partial(video_grad_kernel, clips),
            in_specs=[vmem] * 7,
            out_shape=(shape(OWN, FRAMES, WIDTH), shape(1, 1)),
            scratch_shapes=[two_halves(VOWN)],
            compiler_params=params(),
            cost_estimate=cost(1e6, 1e6),
        )(mine, *[to_z(a, 2 * m) for m, a in enumerate(sent, start=1)], c_row, dv_diag, video)
    return loss.reshape(()), grad_video, grad_gloss


def solution(mesh):
    clips = OWN * mesh.shape["outer"] * mesh.shape["inner"]
    over_all = ("outer", "inner")
    tokens, counts = P(over_all, None, None), P(over_all)
    return jax.shard_map(
        functools.partial(on_device, clips),
        mesh=mesh,
        in_specs=(tokens, tokens, counts, counts),
        out_specs=(P(), tokens, tokens),
        check_vma=False,
    )
```

```python
import functools
import math

import jax
import jax.numpy as jnp
from jax import lax
from jax.experimental import pallas as pl
from jax.experimental.pallas import tpu as pltpu
from jax.sharding import PartitionSpec as P

F32 = jnp.float32
BF16 = jnp.bfloat16
EPSILON = 1e-06
EXP_SCALE = 10.0 * math.log2(math.e)
MARK = 2.0
MARK_LIMIT = 1.5
FAR = -1e30

NZ, NY, NX, NCORE = 8, 8, 4, 2
OWN = 3
FRAMES, GLOSSES, WIDTH = 32, 16, 256
CLIPS_DEV = NZ * NCORE * OWN
TEXTS_DEV = NY * NX * OWN
LANES = 128
VROWS = FRAMES * CLIPS_DEV
GROWS = GLOSSES * TEXTS_DEV
VOWN = FRAMES * OWN
GOWN = GLOSSES * OWN
EXTRA = 16
V_PITCH, G_PITCH = VOWN + 8, GOWN + 8
QUADS = GLOSSES // 4
TILES = GROWS // LANES
HALF = GROWS // 2
NXY, NZC = NX * NY, NZ * NCORE

def flat(x, z, y, core):
    return ((x % 2) * NZ + z) * 32 + (x // 2) * 16 + 2 * y + core


def z_groups(masks):
    return [
        [flat(x, z ^ mask, y, c) for mask in masks]
        for x in range(NX)
        for y in range(NY)
        for c in range(NCORE)
        for z in range(NZ)
        if not z & masks[-1] and not z & masks[len(masks) // 2]
    ]


Z_QUADS, Z_PAIRS = z_groups((0, 2, 4, 6)), z_groups((0, 1))
CORE_GROUPS = [[flat(x, z, y, c) for c in range(NCORE)] for x in range(NX) for y in range(NY) for z in range(NZ)]
XY_GROUPS = [[flat(x, z, y, c) for x in range(NX) for y in range(NY)] for z in range(NZ) for c in range(NCORE)]
HALF_GROUPS = [
    [flat(2 * hi + lo, z, y, c) for hi in range(NX // 2) for y in range(NY)]
    for lo in range(2)
    for z in range(NZ)
    for c in range(NCORE)
]
ZC_GROUPS = [[flat(x, z, y, c) for c in range(NCORE) for z in range(NZ)] for x in range(NX) for y in range(NY)]


def params(limit_mb=32):
    return pltpu.CompilerParams(vmem_limit_bytes=limit_mb * 1024 * 1024)


def cost(flops, nbytes, trans=0):
    return pl.CostEstimate(flops=int(flops), bytes_accessed=int(nbytes), transcendentals=int(trans))


def iota(shape, dim):
    return lax.broadcasted_iota(jnp.int32, shape, dim)


def nt(a, b, **kw):
    return lax.dot_general(a, b, (((1,), (1,)), ((), ())), preferred_element_type=F32, **kw)


def nn(a, b, **kw):
    return lax.dot_general(a, b, (((1,), (0,)), ((), ())), preferred_element_type=F32, **kw)


def tn(a, b, **kw):
    return lax.dot_general(a, b, (((0,), (0,)), ((), ())), preferred_element_type=F32, **kw)


def column_of(row, n):
    eye = iota((n, LANES), 0) == iota((n, LANES), 1)
    return jnp.sum(jnp.where(eye, jnp.broadcast_to(row, (n, LANES)), 0.0), axis=1, keepdims=True)


def packed(x):
    lane = iota(x.shape, 1)
    a, b, c = (pltpu.roll(x, shift, 1) for shift in (96, 64, 32))
    return jnp.where(lane < 96, x, a), jnp.where(lane < 64, a, b), jnp.where(lane < 32, b, c)


def unpacked_sum(t0, t1, t2):
    lane = iota(t0.shape, 1)
    second = pltpu.roll(jnp.where(lane >= 96, t0, t1), 32, 1)
    third = pltpu.roll(jnp.where(lane >= 64, t1, t2), 64, 1)
    return (t0 + second) + (third + pltpu.roll(t2, 96, 1))


def pieces(value):
    lane = iota((EXTRA, WIDTH), 1)
    full = jnp.broadcast_to(value, (EXTRA, WIDTH))
    hi = full.astype(BF16).astype(F32)
    mid = (full - hi).astype(BF16).astype(F32)
    low = (full - hi - mid).astype(BF16).astype(F32)
    return jnp.where(lane == 0, hi, jnp.where(lane == 1, mid, jnp.where(lane == 2, low, 0.0)))


def unpiece(block):
    mine = (iota((EXTRA, WIDTH), 0) == 0) & (iota((EXTRA, WIDTH), 1) < 3)
    return jnp.sum(jnp.where(mine, block, 0.0), keepdims=True).reshape(1, 1)


def put(ref, at, value):
    ref[0, at, :] = value[:, :LANES]
    ref[1, at, :] = value[:, LANES:]


def get(ref, at):
    return jnp.concatenate([ref[0, at, :], ref[1, at, :]], axis=1)


def two_halves(rows):
    return pltpu.VMEM((2, rows, LANES), F32)


def units_kernel(fc_in, gc_in, video_in, gloss_in, v_out, g_out, g_one, count_out, fc, gc, video, gloss, v_scr, g_scr, sems):
    pairs = ((fc_in, fc), (gc_in, gc), (video_in, video), (gloss_in, gloss))
    copies = [pltpu.make_async_copy(a, b, sems.at[i]) for i, (a, b) in enumerate(pairs)]
    for copy in copies:
        copy.start()
    for copy in copies:
        copy.wait()
    row = iota((8, LANES), 0)
    counts = jnp.zeros((8, LANES), jnp.int32)
    for c in range(OWN):
        counts = jnp.where(row == c, fc[c], jnp.where(row == OWN + c, gc[c], counts))
    count_out[...] = counts
    for count, raw, scr, tokens in ((fc, video, v_scr, FRAMES), (gc, gloss, g_scr, GLOSSES)):
        row, lane = iota((tokens, WIDTH), 0), iota((tokens, WIDTH), 1)
        for c in range(OWN):
            x = raw[c].astype(F32)
            mean_sq = jnp.mean(x * x, axis=-1, keepdims=True) + EPSILON
            unit = x * (lax.rsqrt(mean_sq) / math.sqrt(WIDTH))
            mark = jnp.where(lane == 0, MARK, 0.0)
            put(scr, pl.ds(c, tokens, stride=OWN), jnp.where(row < count[c], unit, mark))
    v = get(v_scr, pl.ds(0, VOWN)).astype(BF16)
    g = get(g_scr, pl.ds(0, GOWN)).astype(BF16)
    v_out[...] = v
    g_one[...] = g
    for i in range(NXY):
        g_out[i] = g


def diagonal_kernel(count_ref, v_ref, g_ref, dv, dg):
    def pick(count, which):
        return jnp.where(which == 0, count[0], jnp.where(which == 1, count[1], count[2]))

    fc = [count_ref[c : c + 1, 0:1] for c in range(OWN)]
    gc = [count_ref[OWN + c : OWN + c + 1, 0:1] for c in range(OWN)]
    v, g = v_ref[...], g_ref[...]
    shape = (VOWN, GOWN)
    r, q = iota(shape, 0), iota(shape, 1)
    rc, qc = lax.rem(r, OWN), lax.rem(q, OWN)
    valid = (rc == qc) & (lax.div(r, OWN) < pick(fc, rc)) & (lax.div(q, OWN) < pick(gc, qc))
    e = jnp.where(valid, jnp.exp2(nt(v, g) * EXP_SCALE), 0.0)
    r1, q1 = iota((VOWN, 1), 0), iota((1, GOWN), 1)
    rc1, qc1 = lax.rem(r1, OWN), lax.rem(q1, OWN)
    frames_r, glosses_q = pick(fc, rc1), pick(gc, qc1)
    row_ok = lax.div(r1, OWN) < frames_r
    col_ok = lax.div(q1, OWN) < glosses_q
    frames_r, glosses_q = frames_r.astype(F32), glosses_q.astype(F32)
    rows = jnp.where(row_ok, jnp.sum(e, axis=1, keepdims=True), 1.0)
    cols = jnp.where(col_ok, jnp.sum(e, axis=0, keepdims=True), 1.0)
    weight = -5.0 * e * (1.0 / (rows * frames_r) + 1.0 / (cols * glosses_q))
    dv[...] = nn(weight, g.astype(F32), precision=lax.Precision.HIGHEST)
    dg[...] = tn(weight, v.astype(F32), precision=lax.Precision.HIGHEST)


def exp_scores(v, g):
    return jnp.exp2(nt(v, g) * EXP_SCALE)


def forward_kernel(
    v_got, g_got,
    v_hbm, g_hbm, row_out, col_out, e_out, r_out, c_out,
    v_out, g_out, v_scr, g_scr, frame_mask, gloss_mask, rows, cols, sems,
):
    results = ((v_out, v_hbm), (g_out, g_hbm))
    copies = [pltpu.make_async_copy(a, b, sems.at[i]) for i, (a, b) in enumerate(results)]
    for i in range(NZC):
        put(v_scr, pl.ds(i * V_PITCH, VOWN), v_got[pl.ds(i * VOWN, VOWN), :].astype(F32))
    for f in range(FRAMES):
        parts = [
            get(v_scr, pl.ds(k * NZ * V_PITCH + f * OWN + c, NZ, stride=V_PITCH)) for k in range(NCORE) for c in range(OWN)
        ]
        v_out[pl.ds(f * CLIPS_DEV, CLIPS_DEV), :] = jnp.concatenate(parts, axis=0).astype(BF16)
    copies[0].start()
    for i in range(NXY):
        put(g_scr, pl.ds(i * G_PITCH, GOWN), g_got[i].astype(F32))
    for g in range(GLOSSES):
        parts = [
            get(g_scr, pl.ds(x * NY * G_PITCH + g * OWN + c, NY, stride=G_PITCH)) for x in range(NX) for c in range(OWN)
        ]
        g_out[pl.ds(g * TEXTS_DEV, TEXTS_DEV), :] = jnp.concatenate(parts, axis=0).astype(BF16)
    copies[1].start()

    first = jnp.where(iota((WIDTH, LANES), 0) == 0, 1.0, 0.0).astype(BF16)
    frame_mask[...] = jnp.where(nn(v_out[...], first) < MARK_LIMIT, 1.0, 0.0)
    first_row = jnp.where(iota((16, WIDTH), 1) == 0, 1.0, 0.0).astype(BF16)
    for t in range(TILES):
        found = nt(first_row, g_out[pl.ds(t * LANES, LANES), :])[0:1]
        gloss_mask[t] = jnp.where(found < MARK_LIMIT, 1.0, 0.0)
    frames = jnp.zeros((CLIPS_DEV, LANES), F32)
    for f in range(FRAMES):
        frames = frames + frame_mask[pl.ds(f * CLIPS_DEV, CLIPS_DEV), :]
    by_tile = []
    for t in range(3):
        by_tile.append(gloss_mask[t] + gloss_mask[t + 3] + gloss_mask[t + 6] + gloss_mask[t + 9])
    lane = iota((CLIPS_DEV, LANES), 1)
    real = lane < TEXTS_DEV
    counts = unpacked_sum(*[jnp.broadcast_to(t, (8, LANES)) for t in by_tile])
    glosses = jnp.where(real[0:8], counts, 1.0)
    packed_glosses = [t[0:1] for t in packed(glosses)]
    glosses = glosses[0:1]

    for half in range(2):
        e = exp_scores(v_out[...], g_out[pl.ds(half * HALF, HALF), :])
        tiles = range(half * TILES // 2, (half + 1) * TILES // 2)
        masks = [gloss_mask[t] for t in tiles]
        sums = [jnp.zeros((CLIPS_DEV, LANES), F32) for _ in tiles]
        for f in range(FRAMES):
            at = pl.ds(f * CLIPS_DEV, CLIPS_DEV)
            mask = frame_mask[at, :]
            block = e[f * CLIPS_DEV : (f + 1) * CLIPS_DEV]
            parts = [block[:, k * LANES : (k + 1) * LANES] for k in range(TILES // 2)]
            sums = [total + part * mask for total, part in zip(sums, parts, strict=True)]
            for k in range(3):
                part = parts[k] * masks[k] + parts[k + 3] * masks[k + 3]
                rows[at, pl.ds(k * LANES, LANES)] = part if half == 0 else rows[at, pl.ds(k * LANES, LANES)] + part
        for k, t in enumerate(tiles):
            cols[t] = sums[k]

    video_part = jnp.zeros((CLIPS_DEV, LANES), F32)
    for f in range(FRAMES):
        at = pl.ds(f * CLIPS_DEV, CLIPS_DEV)
        mask = frame_mask[at, :]
        total = unpacked_sum(*[rows[at, pl.ds(k * LANES, LANES)] for k in range(3)])
        total = jnp.where(real, total, 1.0)
        video_part = video_part + mask * jnp.log(total)
        row_out[at, :] = jnp.where(mask > 0.0, 1.0 / (total * frames), FAR)
    video_part = video_part / frames - jnp.log(glosses)
    gloss_parts = [jnp.zeros((CLIPS_DEV, LANES), F32)] * 3
    for t in range(TILES):
        mask = gloss_mask[t]
        total = cols[t]
        gloss_parts[t % 3] = gloss_parts[t % 3] + mask * jnp.log(total)
        col_out[t] = jnp.where(mask > 0.0, 1.0 / (total * packed_glosses[t % 3]), FAR)
    gloss_part = unpacked_sum(*gloss_parts) / glosses - jnp.log(frames)
    logits = 0.5 * (video_part + gloss_part)
    e_pair = jnp.where(real, jnp.exp(logits), 0.0)
    e_out[...] = e_pair

    sums = jnp.sum(e_pair, axis=1, keepdims=True)
    across = lane == iota((CLIPS_DEV, LANES), 0)
    r_row = jnp.sum(jnp.where(across, jnp.broadcast_to(sums, (CLIPS_DEV, LANES)), 0.0), axis=0, keepdims=True)
    inner, outer = lax.axis_index("inner"), lax.axis_index("outer")
    z, core = lax.rem(outer, NZ), lax.rem(inner, NCORE)
    x, y = 2 * lax.div(inner, 16) + lax.div(outer, NZ), lax.rem(lax.div(inner, NCORE), NY)
    clip0 = core * OWN * NZ + lax.rem(z, 2) * (NZ // 2) + lax.div(z, 2)
    text0 = x * OWN * NY + y
    own = jnp.zeros((CLIPS_DEV, LANES), jnp.bool_)
    for c in range(OWN):
        own = own | ((iota((CLIPS_DEV, LANES), 0) == clip0 + c * NZ) & (lane == text0 + c * NY))
    diag = jnp.sum(jnp.where(own, logits, 0.0), keepdims=True).reshape(1, 1)
    r_row = jnp.where(iota((1, LANES), 1) == CLIPS_DEV, diag, r_row)
    for i in range(NZC):
        r_out[i] = r_row
    c_out[...] = jnp.sum(e_pair, axis=0, keepdims=True)
    for copy in copies:
        copy.wait()


def started(copies):
    for copy in copies:
        copy.start()
    return copies


def halves_of(p):
    return [(r, h, p.at[h, pl.ds(r * VROWS // 2, VROWS // 2)]) for r in range(2) for h in range(2)]


def weights_kernel(v_hbm, g_hbm, row_ref, col_ref, e_ref, p_hbm, v, g, p, sems):
    loads = started([pltpu.make_async_copy(a, b, sems.at[i]) for i, (a, b) in enumerate(((v_hbm, v), (g_hbm, g)))])
    scales = packed(2.5 * e_ref[...])
    for load in loads:
        load.wait()
    stores = []
    for (r, h, out), (_, _, here) in zip(halves_of(p_hbm), halves_of(p), strict=True):
        e = exp_scores(v[pl.ds(r * VROWS // 2, VROWS // 2), :], g[pl.ds(h * HALF, HALF), :])
        for f in range(FRAMES // 2):
            row = packed(row_ref[pl.ds((r * FRAMES // 2 + f) * CLIPS_DEV, CLIPS_DEV), :])
            block = e[f * CLIPS_DEV : (f + 1) * CLIPS_DEV]
            parts = []
            for k in range(TILES // 2):
                share = jnp.maximum(row[k % 3] + col_ref[h * TILES // 2 + k], 0.0)
                parts.append(scales[k % 3] * block[:, k * LANES : (k + 1) * LANES] * share)
            here[pl.ds(f * CLIPS_DEV, CLIPS_DEV), :] = jnp.concatenate(parts, axis=1).astype(BF16)
        stores += started([pltpu.make_async_copy(here, out, sems.at[2 + 2 * r + h])])
    for store in stores:
        store.wait()


def added(got):
    total = got[0]
    for i in range(1, got.shape[0]):
        total = total + got[i]
    return total


def row_sums_kernel(r_got, c_part, c_near, c_out, r_out):
    r_row = added(r_got)
    r_out[...] = r_row
    lane = iota((1, LANES), 1)
    logs = jnp.where(lane < CLIPS_DEV, jnp.log(jnp.where(lane < CLIPS_DEV, r_row, 1.0)), 0.0)
    logs = logs - jnp.where(lane == CLIPS_DEV, 2.0 * r_row, 0.0)
    total = jnp.sum(logs, axis=1, keepdims=True)
    message = jnp.where(lane == TEXTS_DEV, total, c_part[...] + c_near[...])
    for i in range(NXY // 2):
        c_out[i] = message


def inverse_texts(c_row):
    return jnp.broadcast_to(1.0 / column_of(c_row, TEXTS_DEV), (TEXTS_DEV, WIDTH))


def by_clip_kernel(r_ref, p_ref, v_ref, g_ref, out, av_out, both):
    step = pl.program_id(0)

    @pl.when(step == 0)
    def _():
        inverse = jnp.broadcast_to(1.0 / column_of(r_ref[...], CLIPS_DEV), (CLIPS_DEV, WIDTH))
        for f in range(FRAMES):
            at = pl.ds(f * CLIPS_DEV, CLIPS_DEV)
            v = v_ref[at, :]
            both[at, :WIDTH] = v
            both[at, WIDTH:] = (v.astype(F32) * inverse).astype(BF16)

    out[...] = tn(p_ref[0], both[...]).reshape(GLOSSES // 2, TEXTS_DEV, 2 * WIDTH)
    part = nn(p_ref[0], g_ref[...])

    @pl.when(step == 0)
    def _():
        av_out[...] = part

    @pl.when(step > 0)
    def _():
        av_out[...] = av_out[...] + part


def gloss_send_kernel(c_got, by_clip, out, c_out, held, scr, sems):
    many = GLOSSES // QUADS
    copies = started(
        [
            pltpu.make_async_copy(by_clip.at[pl.ds(q * many, many)], held.at[pl.ds(q * many, many)], sems.at[q])
            for q in range(QUADS)
        ]
    )
    c_out[...] = added(c_got)
    col = inverse_texts(c_out[...])
    for q, copy in enumerate(copies):
        copy.wait()
        for k in range(many):
            g = q * many + k
            block = held[g, :, :WIDTH] * col + held[g, :, WIDTH:]
            row = g * OWN
            for x in range(NX):
                for c in range(OWN):
                    first = (x * OWN + c) * NY
                    put(scr, pl.ds(x * NY * G_PITCH + row + c, NY, stride=G_PITCH), block[first : first + NY])
    for i in range(NXY):
        out[i] = get(scr, pl.ds(i * G_PITCH, GOWN)).astype(BF16)


def clip_send_kernel(c_got, r_ref, p_hbm, g_hbm, av_ref, mine, twin, p, g, g_by_text, sems):
    g_copy = pltpu.make_async_copy(g_hbm, g, sems.at[4])
    copies = []
    for (r, h, theirs), (_, _, here) in zip(halves_of(p_hbm), halves_of(p), strict=True):
        copies.append(pltpu.make_async_copy(theirs, here, sems.at[2 * r + h]))
    started([g_copy, *copies])
    c_row = added(c_got)
    col = inverse_texts(c_row)
    core = lax.rem(lax.axis_index("inner"), NCORE)
    inverse = jnp.broadcast_to(1.0 / column_of(r_ref[...], CLIPS_DEV), (CLIPS_DEV, WIDTH))
    half = CLIPS_DEV // 2
    g_copy.wait()
    for i in range(GLOSSES):
        at = pl.ds(i * TEXTS_DEV, TEXTS_DEV)
        g_by_text[at, :] = (g[at, :].astype(F32) * col).astype(BF16)
    for r in range(2):
        copies[2 * r].wait()
        copies[2 * r + 1].wait()
        at = pl.ds(r * VROWS // 2, VROWS // 2)
        part = nn(p[0, at, :], g_by_text[pl.ds(0, HALF), :]) + nn(p[1, at, :], g_by_text[pl.ds(HALF, HALF), :])
        for pair in range(FRAMES // 4):
            others = []
            for f in (2 * pair, 2 * pair + 1):
                full = r * FRAMES // 2 + f
                new = part[f * CLIPS_DEV : (f + 1) * CLIPS_DEV]
                block = av_ref[pl.ds(full * CLIPS_DEV, CLIPS_DEV), :] * inverse + new
                low, high = block[:half], block[half:]
                mine[pl.ds(full * half, half), :] = jnp.where(core == 0, low, high)
                others.append(jnp.where(core == 0, high, low))
            at = pl.ds((r * FRAMES // 4 + pair) * CLIPS_DEV, CLIPS_DEV)
            twin[at, :] = jnp.concatenate(others, axis=0).astype(BF16)
    real = iota((1, LANES), 1) < TEXTS_DEV
    logs = jnp.where(real, jnp.log(jnp.where(real, c_row, 1.0)), 0.0)
    extra = pieces(jnp.sum(logs, axis=1, keepdims=True))
    mine[pl.ds(FRAMES * half, EXTRA), :] = extra
    twin[pl.ds(FRAMES * half, EXTRA), :] = extra.astype(BF16)


def own_z():
    return lax.rem(lax.axis_index("outer"), NZ)


def clip_rows_kernel(mine, got, keep, send, scr):
    step = 2 * NZ
    for i in range(VOWN // 2):
        at = pl.ds(i * step, step)
        two = mine[at, :] + got[at, :].astype(F32)
        for k in range(2):
            put(scr, pl.ds(2 * i + k, NZ, stride=V_PITCH), two[k * NZ : (k + 1) * NZ])
    bit = lax.rem(own_z(), 2)
    owners = NZ // 2
    for i in range(owners):
        at = pl.ds(i * VOWN, VOWN)
        keep[at, :] = get(scr, pl.ds(pl.multiple_of((owners * bit + i) * V_PITCH, 8), VOWN))
        send[at, :] = get(scr, pl.ds(pl.multiple_of((owners * (1 - bit) + i) * V_PITCH, 8), VOWN)).astype(BF16)
    extra = loss_rows(mine, got, NZ)
    keep[pl.ds(owners * VOWN, EXTRA), :] = extra
    send[pl.ds(owners * VOWN, EXTRA), :] = extra.astype(BF16)


def loss_rows(mine, got, owners):
    tail = pl.ds(owners * VOWN, EXTRA)
    return pieces(unpiece(mine[tail, :]) + unpiece(got[tail, :].astype(F32)))


def quarter_kernel(mine, got, keep, *sends):
    own = lax.div(own_z(), 2)
    extra = loss_rows(mine, got, NZ // 2)
    for out, owner in zip((keep, *sends), (own, own ^ 1, own ^ 2, own ^ 3), strict=True):
        at = pl.ds(pl.multiple_of(owner * VOWN, VOWN), VOWN)
        out[pl.ds(0, VOWN), :] = (mine[at, :] + got[at, :].astype(F32)).astype(out.dtype)
        out[pl.ds(VOWN, EXTRA), :] = extra.astype(out.dtype)


def token_grads(total, scr, raw, out, tokens):
    put(scr, pl.ds(0, OWN * tokens), total)
    for c in range(OWN):
        x = raw[c].astype(F32)
        d = get(scr, pl.ds(c, tokens, stride=OWN))
        mean_sq = jnp.mean(x * x, axis=-1, keepdims=True) + EPSILON
        factor = lax.rsqrt(mean_sq) / math.sqrt(WIDTH)
        inner = jnp.sum(d * x, axis=-1, keepdims=True)
        out[c] = factor * d - factor * x * (inner / (WIDTH * mean_sq))


def video_grad_kernel(clips, mine, got1, got2, got3, c_row, c_near, diag, video, out, loss, scr):
    at = pl.ds(0, VOWN)
    total = mine[at, :]
    for got in (got1, got2, got3):
        total = total + got[at, :].astype(F32)
    token_grads(total + diag[...], scr, video, out, FRAMES)
    at_sum = pl.ds(TEXTS_DEV, 1)
    row_part = c_row[:, at_sum] + c_near[:, at_sum]
    tail = pl.ds(VOWN, EXTRA)
    near = unpiece(mine[tail, :]) + unpiece(got1[tail, :].astype(F32))
    far = unpiece(got2[tail, :].astype(F32)) + unpiece(got3[tail, :].astype(F32))
    loss[...] = (near + far + row_part) * (0.5 / clips)


def gloss_grad_kernel(got, diag, gloss, out, scr):
    total = got[0].astype(F32)
    for i in range(1, NXY):
        total = total + got[i].astype(F32)
    token_grads(total + diag[...], scr, gloss, out, GLOSSES)


def shape(*dims, dtype=F32):
    return jax.ShapeDtypeStruct(dims, dtype)


def on_device(clips, video, gloss, frame_count, gloss_count):
    vmem, hbm = pl.BlockSpec(memory_space=pltpu.VMEM), pl.BlockSpec(memory_space=pltpu.HBM)
    over_all = ("outer", "inner")

    def to_core(a):
        return lax.ppermute(a, "inner", [(i, i ^ 1) for i in range(lax.axis_size("inner"))])

    def to_z(a, mask):
        return lax.ppermute(a, "outer", [(i, i ^ mask) for i in range(lax.axis_size("outer"))])

    def to_near_x(a):
        return lax.ppermute(a, "outer", [(i, i ^ NZ) for i in range(lax.axis_size("outer"))])

    def exchanged(a, groups):
        return lax.all_to_all(a, over_all, 0, 0, axis_index_groups=groups, tiled=True)

    def gathered(a, groups):
        return lax.all_gather(a, over_all, axis=0, axis_index_groups=groups, tiled=True)

    def in_hbm(*arrays):
        return [pltpu.with_memory_space_constraint(a, pltpu.HBM) for a in arrays]

    with jax.named_scope("unit_tokens"):
        v_own, g_send, g_own, counts = pl.pallas_call(
            units_kernel,
            in_specs=[hbm] * 4,
            out_shape=(
                shape(VOWN, WIDTH, dtype=BF16),
                shape(NXY, GOWN, WIDTH, dtype=BF16),
                shape(GOWN, WIDTH, dtype=BF16),
                shape(8, LANES, dtype=jnp.int32),
            ),
            scratch_shapes=[
                pltpu.SMEM((OWN,), jnp.int32),
                pltpu.SMEM((OWN,), jnp.int32),
                pltpu.VMEM((OWN, FRAMES, WIDTH), BF16),
                pltpu.VMEM((OWN, GLOSSES, WIDTH), BF16),
                two_halves(VOWN),
                two_halves(GOWN),
                pltpu.SemaphoreType.DMA((4,)),
            ],
            compiler_params=params(),
            cost_estimate=cost(2e5, 7e5),
        )(*in_hbm(frame_count, gloss_count, video, gloss))

    with jax.named_scope("gather"):
        g_got = exchanged(g_send, XY_GROUPS)
        v_got = gathered(gathered(v_own, Z_QUADS), Z_PAIRS)
        v_got = gathered(v_got, CORE_GROUPS)

    def whole(*dims):
        return pl.BlockSpec(dims, lambda i: (0,) * len(dims))

    with jax.named_scope("forward"):
        v_all, g_all, row_inv, col_inv, e_pair, r_part, c_part = pl.pallas_call(
            forward_kernel,
            in_specs=[vmem] * 2,
            out_specs=[hbm] * 2 + [vmem] * 5,
            out_shape=(
                pltpu.HBM((VROWS, WIDTH), BF16),
                pltpu.HBM((GROWS, WIDTH), BF16),
                shape(VROWS, LANES),
                shape(TILES, CLIPS_DEV, LANES),
                shape(CLIPS_DEV, LANES),
                shape(NZC, 1, LANES),
                shape(1, LANES),
            ),
            scratch_shapes=[
                pltpu.VMEM((VROWS, WIDTH), BF16),
                pltpu.VMEM((GROWS, WIDTH), BF16),
                two_halves(NZC * V_PITCH),
                two_halves(NXY * G_PITCH),
                pltpu.VMEM((VROWS, LANES), F32),
                pltpu.VMEM((TILES, 1, LANES), F32),
                pltpu.VMEM((VROWS, 3 * LANES), F32),
                pltpu.VMEM((TILES, CLIPS_DEV, LANES), F32),
                pltpu.SemaphoreType.DMA((2,)),
            ],
            compiler_params=params(),
            cost_estimate=cost(2 * VROWS * GROWS * WIDTH, 8e6, VROWS * GROWS),
        )(v_got, g_got)

    with jax.named_scope("row_sums"):
        c_send, r_row = pl.pallas_call(
            row_sums_kernel,
            in_specs=[vmem] * 3,
            out_shape=(shape(NXY // 2, 1, LANES), shape(1, LANES)),
            compiler_params=params(),
            cost_estimate=cost(1e5, 3e5),
        )(exchanged(r_part, ZC_GROUPS), c_part, to_near_x(c_part))
    with jax.named_scope("column_sums"):
        c_got = exchanged(c_send, HALF_GROUPS)

    with jax.named_scope("weights"):
        weights = pl.pallas_call(
            weights_kernel,
            in_specs=[hbm, hbm, vmem, vmem, vmem],
            out_specs=hbm,
            out_shape=pltpu.HBM((2, VROWS, HALF), BF16),
            scratch_shapes=[
                pltpu.VMEM((VROWS, WIDTH), BF16),
                pltpu.VMEM((GROWS, WIDTH), BF16),
                pltpu.VMEM((2, VROWS, HALF), BF16),
                pltpu.SemaphoreType.DMA((6,)),
            ],
            compiler_params=params(),
            cost_estimate=cost(2 * VROWS * GROWS * WIDTH, 12e6, VROWS * GROWS),
        )(*in_hbm(v_all, g_all), row_inv, col_inv, e_pair)

    with jax.named_scope("by_clip"):
        by_clip, av = pl.pallas_call(
            by_clip_kernel,
            grid=(2,),
            in_specs=[
                whole(1, LANES),
                pl.BlockSpec((1, VROWS, HALF), lambda i: (i, 0, 0)),
                whole(VROWS, WIDTH),
                pl.BlockSpec((HALF, WIDTH), lambda i: (i, 0)),
            ],
            out_specs=(
                pl.BlockSpec((GLOSSES // 2, TEXTS_DEV, 2 * WIDTH), lambda i: (i, 0, 0)),
                whole(VROWS, WIDTH),
            ),
            out_shape=(pltpu.HBM((GLOSSES, TEXTS_DEV, 2 * WIDTH), F32), shape(VROWS, WIDTH)),
            scratch_shapes=[pltpu.VMEM((VROWS, 2 * WIDTH), BF16)],
            compiler_params=params(),
            cost_estimate=cost(6 * VROWS * GROWS * WIDTH, 14e6),
        )(r_row, *in_hbm(weights, v_all, g_all))

    with jax.named_scope("clip_send"):
        v_rows = FRAMES * CLIPS_DEV // 2 + EXTRA
        mine, twin = pl.pallas_call(
            clip_send_kernel,
            in_specs=[vmem, vmem, hbm, hbm, vmem],
            out_shape=(shape(v_rows, WIDTH), shape(v_rows, WIDTH, dtype=BF16)),
            scratch_shapes=[
                pltpu.VMEM((2, VROWS, HALF), BF16),
                pltpu.VMEM((GROWS, WIDTH), BF16),
                pltpu.VMEM((GROWS, WIDTH), BF16),
                pltpu.SemaphoreType.DMA((5,)),
            ],
            compiler_params=params(),
            cost_estimate=cost(2 * VROWS * GROWS * WIDTH, 1e7),
        )(c_got, r_row, *in_hbm(weights, g_all), av)

    with jax.named_scope("gloss_send"):
        twin, c_ready = lax.optimization_barrier((twin, c_got))
        dg_send, c_row = pl.pallas_call(
            gloss_send_kernel,
            in_specs=[vmem, hbm],
            out_shape=(shape(NXY, GOWN, WIDTH, dtype=BF16), shape(1, LANES)),
            scratch_shapes=[
                pltpu.VMEM((GLOSSES, TEXTS_DEV, 2 * WIDTH), F32),
                two_halves(NXY * G_PITCH),
                pltpu.SemaphoreType.DMA((QUADS,)),
            ],
            compiler_params=params(),
            cost_estimate=cost(2e6, 5e6),
        )(c_ready, *in_hbm(by_clip))
        dg_got = exchanged(dg_send, XY_GROUPS)

    def kept_and_sent(owners):
        rows = owners * VOWN + EXTRA
        return (shape(rows, WIDTH), shape(rows, WIDTH, dtype=BF16))

    with jax.named_scope("clips_by_core"):
        mine, sent = pl.pallas_call(
            clip_rows_kernel,
            in_specs=[vmem] * 2,
            out_shape=kept_and_sent(NZ // 2),
            scratch_shapes=[two_halves(NZ * V_PITCH)],
            compiler_params=params(),
            cost_estimate=cost(1e6, 2e6),
        )(mine, to_core(twin))
    with jax.named_scope("clips_by_z"):
        mine, *sent = pl.pallas_call(
            quarter_kernel,
            in_specs=[vmem] * 2,
            out_shape=kept_and_sent(1) + kept_and_sent(1)[1:] * 2,
            compiler_params=params(),
            cost_estimate=cost(1e10, 1e6),
        )(mine, to_z(sent, 1))

    with jax.named_scope("diagonal"):
        mine, v_own, g_own, counts = lax.optimization_barrier((mine, v_own, g_own, counts))
        dv_diag, dg_diag = pl.pallas_call(
            diagonal_kernel,
            in_specs=[vmem] * 3,
            out_shape=(shape(VOWN, WIDTH), shape(GOWN, WIDTH)),
            compiler_params=params(),
            cost_estimate=cost(2e7, 3e5),
        )(counts, v_own, g_own)

    with jax.named_scope("gloss_grad"):
        grad_gloss = pl.pallas_call(
            gloss_grad_kernel,
            in_specs=[vmem] * 3,
            out_shape=shape(OWN, GLOSSES, WIDTH),
            scratch_shapes=[two_halves(GOWN)],
            compiler_params=params(),
            cost_estimate=cost(1e6, 1e6),
        )(dg_got, dg_diag, gloss)
    mine, grad_gloss = lax.optimization_barrier((mine, grad_gloss))

    with jax.named_scope("video_grad"):
        grad_video, loss = pl.pallas_call(
            functools.partial(video_grad_kernel, clips),
            in_specs=[vmem] * 8,
            out_shape=(shape(OWN, FRAMES, WIDTH), shape(1, 1)),
            scratch_shapes=[two_halves(VOWN)],
            compiler_params=params(),
            cost_estimate=cost(1e6, 1e6),
        )(mine, *[to_z(a, 2 * m) for m, a in enumerate(sent, start=1)], c_row, to_near_x(c_row), dv_diag, video)
    return loss.reshape(()), grad_video, grad_gloss


def solution(mesh):
    clips = OWN * mesh.shape["outer"] * mesh.shape["inner"]
    over_all = ("outer", "inner")
    tokens, counts = P(over_all, None, None), P(over_all)
    return jax.shard_map(
        functools.partial(on_device, clips),
        mesh=mesh,
        in_specs=(tokens, tokens, counts, counts),
        out_specs=(P(), tokens, tokens),
        check_vma=False,
    )
```

```python
import functools
import math

import jax
import jax.numpy as jnp
from jax import lax
from jax.experimental import pallas as pl
from jax.experimental.pallas import tpu as pltpu
from jax.sharding import PartitionSpec as P

F32 = jnp.float32
BF16 = jnp.bfloat16
EPSILON = 1e-06
EXP_SCALE = 10.0 * math.log2(math.e)
MARK = 2.0
MARK_LIMIT = 1.5
FAR = -1e30

NZ, NY, NX, NCORE = 8, 8, 4, 2
OWN = 3
FRAMES, GLOSSES, WIDTH = 32, 16, 256
CLIPS_DEV = NZ * NCORE * OWN
TEXTS_DEV = NY * NX * OWN
LANES = 128
VROWS = FRAMES * CLIPS_DEV
GROWS = GLOSSES * TEXTS_DEV
VOWN = FRAMES * OWN
GOWN = GLOSSES * OWN
EXTRA = 16
V_PITCH, G_PITCH = VOWN + 8, GOWN + 8
QUADS = GLOSSES // 4
TILES = GROWS // LANES
HALF = GROWS // 2
NXY, NZC = NX * NY, NZ * NCORE

def flat(x, z, y, core):
    return ((x % 2) * NZ + z) * 32 + (x // 2) * 16 + 2 * y + core


def z_groups(masks):
    return [
        [flat(x, z ^ mask, y, c) for mask in masks]
        for x in range(NX)
        for y in range(NY)
        for c in range(NCORE)
        for z in range(NZ)
        if not z & masks[-1] and not z & masks[len(masks) // 2]
    ]


Z_QUADS, Z_PAIRS = z_groups((0, 2, 4, 6)), z_groups((0, 1))
CORE_GROUPS = [[flat(x, z, y, c) for c in range(NCORE)] for x in range(NX) for y in range(NY) for z in range(NZ)]
XY_GROUPS = [[flat(x, z, y, c) for x in range(NX) for y in range(NY)] for z in range(NZ) for c in range(NCORE)]
ZC_GROUPS = [[flat(x, z, y, c) for c in range(NCORE) for z in range(NZ)] for x in range(NX) for y in range(NY)]


def params(limit_mb=32):
    return pltpu.CompilerParams(vmem_limit_bytes=limit_mb * 1024 * 1024)


def cost(flops, nbytes, trans=0):
    return pl.CostEstimate(flops=int(flops), bytes_accessed=int(nbytes), transcendentals=int(trans))


def iota(shape, dim):
    return lax.broadcasted_iota(jnp.int32, shape, dim)


def nt(a, b, **kw):
    return lax.dot_general(a, b, (((1,), (1,)), ((), ())), preferred_element_type=F32, **kw)


def nn(a, b, **kw):
    return lax.dot_general(a, b, (((1,), (0,)), ((), ())), preferred_element_type=F32, **kw)


def tn(a, b, **kw):
    return lax.dot_general(a, b, (((0,), (0,)), ((), ())), preferred_element_type=F32, **kw)


def column_of(row, n):
    eye = iota((n, LANES), 0) == iota((n, LANES), 1)
    return jnp.sum(jnp.where(eye, jnp.broadcast_to(row, (n, LANES)), 0.0), axis=1, keepdims=True)


def packed(x):
    lane = iota(x.shape, 1)
    a, b, c = (pltpu.roll(x, shift, 1) for shift in (96, 64, 32))
    return jnp.where(lane < 96, x, a), jnp.where(lane < 64, a, b), jnp.where(lane < 32, b, c)


def unpacked_sum(t0, t1, t2):
    lane = iota(t0.shape, 1)
    second = pltpu.roll(jnp.where(lane >= 96, t0, t1), 32, 1)
    third = pltpu.roll(jnp.where(lane >= 64, t1, t2), 64, 1)
    return (t0 + second) + (third + pltpu.roll(t2, 96, 1))


def pieces(value):
    lane = iota((EXTRA, WIDTH), 1)
    full = jnp.broadcast_to(value, (EXTRA, WIDTH))
    hi = full.astype(BF16).astype(F32)
    mid = (full - hi).astype(BF16).astype(F32)
    low = (full - hi - mid).astype(BF16).astype(F32)
    return jnp.where(lane == 0, hi, jnp.where(lane == 1, mid, jnp.where(lane == 2, low, 0.0)))


def unpiece(block):
    mine = (iota((EXTRA, WIDTH), 0) == 0) & (iota((EXTRA, WIDTH), 1) < 3)
    return jnp.sum(jnp.where(mine, block, 0.0), keepdims=True).reshape(1, 1)


def put(ref, at, value):
    ref[0, at, :] = value[:, :LANES]
    ref[1, at, :] = value[:, LANES:]


def get(ref, at):
    return jnp.concatenate([ref[0, at, :], ref[1, at, :]], axis=1)


def two_halves(rows):
    return pltpu.VMEM((2, rows, LANES), F32)


def units_kernel(fc_in, gc_in, video_in, gloss_in, v_out, g_out, g_one, count_out, fc, gc, video, gloss, v_scr, g_scr, sems):
    pairs = ((fc_in, fc), (gc_in, gc), (video_in, video), (gloss_in, gloss))
    copies = [pltpu.make_async_copy(a, b, sems.at[i]) for i, (a, b) in enumerate(pairs)]
    for copy in copies:
        copy.start()
    for copy in copies:
        copy.wait()
    row = iota((8, LANES), 0)
    counts = jnp.zeros((8, LANES), jnp.int32)
    for c in range(OWN):
        counts = jnp.where(row == c, fc[c], jnp.where(row == OWN + c, gc[c], counts))
    count_out[...] = counts
    for count, raw, scr, tokens in ((fc, video, v_scr, FRAMES), (gc, gloss, g_scr, GLOSSES)):
        row, lane = iota((tokens, WIDTH), 0), iota((tokens, WIDTH), 1)
        for c in range(OWN):
            x = raw[c].astype(F32)
            mean_sq = jnp.mean(x * x, axis=-1, keepdims=True) + EPSILON
            unit = x * (lax.rsqrt(mean_sq) / math.sqrt(WIDTH))
            mark = jnp.where(lane == 0, MARK, 0.0)
            put(scr, pl.ds(c, tokens, stride=OWN), jnp.where(row < count[c], unit, mark))
    v = get(v_scr, pl.ds(0, VOWN)).astype(BF16)
    g = get(g_scr, pl.ds(0, GOWN)).astype(BF16)
    v_out[...] = v
    g_one[...] = g
    for i in range(NXY):
        g_out[i] = g


def diagonal_kernel(count_ref, v_ref, g_ref, dv, dg):
    def pick(count, which):
        return jnp.where(which == 0, count[0], jnp.where(which == 1, count[1], count[2]))

    fc = [count_ref[c : c + 1, 0:1] for c in range(OWN)]
    gc = [count_ref[OWN + c : OWN + c + 1, 0:1] for c in range(OWN)]
    v, g = v_ref[...], g_ref[...]
    shape = (VOWN, GOWN)
    r, q = iota(shape, 0), iota(shape, 1)
    rc, qc = lax.rem(r, OWN), lax.rem(q, OWN)
    valid = (rc == qc) & (lax.div(r, OWN) < pick(fc, rc)) & (lax.div(q, OWN) < pick(gc, qc))
    e = jnp.where(valid, jnp.exp2(nt(v, g) * EXP_SCALE), 0.0)
    r1, q1 = iota((VOWN, 1), 0), iota((1, GOWN), 1)
    rc1, qc1 = lax.rem(r1, OWN), lax.rem(q1, OWN)
    frames_r, glosses_q = pick(fc, rc1), pick(gc, qc1)
    row_ok = lax.div(r1, OWN) < frames_r
    col_ok = lax.div(q1, OWN) < glosses_q
    frames_r, glosses_q = frames_r.astype(F32), glosses_q.astype(F32)
    rows = jnp.where(row_ok, jnp.sum(e, axis=1, keepdims=True), 1.0)
    cols = jnp.where(col_ok, jnp.sum(e, axis=0, keepdims=True), 1.0)
    weight = -5.0 * e * (1.0 / (rows * frames_r) + 1.0 / (cols * glosses_q))
    dv[...] = nn(weight, g.astype(F32), precision=lax.Precision.HIGHEST)
    dg[...] = tn(weight, v.astype(F32), precision=lax.Precision.HIGHEST)


def exp_scores(v, g):
    return jnp.exp2(nt(v, g) * EXP_SCALE)


def forward_kernel(
    v_got, g_got,
    v_hbm, g_hbm, row_out, col_out, e_out, r_out, c_out,
    v_out, g_out, v_scr, g_scr, frame_mask, gloss_mask, rows, cols, sems,
):
    results = ((v_out, v_hbm), (g_out, g_hbm))
    copies = [pltpu.make_async_copy(a, b, sems.at[i]) for i, (a, b) in enumerate(results)]
    for i in range(NZC):
        put(v_scr, pl.ds(i * V_PITCH, VOWN), v_got[pl.ds(i * VOWN, VOWN), :].astype(F32))
    for f in range(FRAMES):
        parts = [
            get(v_scr, pl.ds(k * NZ * V_PITCH + f * OWN + c, NZ, stride=V_PITCH)) for k in range(NCORE) for c in range(OWN)
        ]
        v_out[pl.ds(f * CLIPS_DEV, CLIPS_DEV), :] = jnp.concatenate(parts, axis=0).astype(BF16)
    copies[0].start()
    for i in range(NXY):
        put(g_scr, pl.ds(i * G_PITCH, GOWN), g_got[i].astype(F32))
    for g in range(GLOSSES):
        parts = [
            get(g_scr, pl.ds(x * NY * G_PITCH + g * OWN + c, NY, stride=G_PITCH)) for x in range(NX) for c in range(OWN)
        ]
        g_out[pl.ds(g * TEXTS_DEV, TEXTS_DEV), :] = jnp.concatenate(parts, axis=0).astype(BF16)
    copies[1].start()

    first = jnp.where(iota((WIDTH, LANES), 0) == 0, 1.0, 0.0).astype(BF16)
    frame_mask[...] = jnp.where(nn(v_out[...], first) < MARK_LIMIT, 1.0, 0.0)
    first_row = jnp.where(iota((16, WIDTH), 1) == 0, 1.0, 0.0).astype(BF16)
    for t in range(TILES):
        found = nt(first_row, g_out[pl.ds(t * LANES, LANES), :])[0:1]
        gloss_mask[t] = jnp.where(found < MARK_LIMIT, 1.0, 0.0)
    frames = jnp.zeros((CLIPS_DEV, LANES), F32)
    for f in range(FRAMES):
        frames = frames + frame_mask[pl.ds(f * CLIPS_DEV, CLIPS_DEV), :]
    by_tile = []
    for t in range(3):
        by_tile.append(gloss_mask[t] + gloss_mask[t + 3] + gloss_mask[t + 6] + gloss_mask[t + 9])
    lane = iota((CLIPS_DEV, LANES), 1)
    real = lane < TEXTS_DEV
    counts = unpacked_sum(*[jnp.broadcast_to(t, (8, LANES)) for t in by_tile])
    glosses = jnp.where(real[0:8], counts, 1.0)
    packed_glosses = [t[0:1] for t in packed(glosses)]
    glosses = glosses[0:1]

    for half in range(2):
        e = exp_scores(v_out[...], g_out[pl.ds(half * HALF, HALF), :])
        tiles = range(half * TILES // 2, (half + 1) * TILES // 2)
        masks = [gloss_mask[t] for t in tiles]
        sums = [jnp.zeros((CLIPS_DEV, LANES), F32) for _ in tiles]
        for f in range(FRAMES):
            at = pl.ds(f * CLIPS_DEV, CLIPS_DEV)
            mask = frame_mask[at, :]
            block = e[f * CLIPS_DEV : (f + 1) * CLIPS_DEV]
            parts = [block[:, k * LANES : (k + 1) * LANES] for k in range(TILES // 2)]
            sums = [total + part * mask for total, part in zip(sums, parts, strict=True)]
            for k in range(3):
                part = parts[k] * masks[k] + parts[k + 3] * masks[k + 3]
                rows[at, pl.ds(k * LANES, LANES)] = part if half == 0 else rows[at, pl.ds(k * LANES, LANES)] + part
        for k, t in enumerate(tiles):
            cols[t] = sums[k]

    video_part = jnp.zeros((CLIPS_DEV, LANES), F32)
    for f in range(FRAMES):
        at = pl.ds(f * CLIPS_DEV, CLIPS_DEV)
        mask = frame_mask[at, :]
        total = unpacked_sum(*[rows[at, pl.ds(k * LANES, LANES)] for k in range(3)])
        total = jnp.where(real, total, 1.0)
        product = jnp.where(mask > 0.0, total, 1.0) * (1.0 if f % 4 == 0 else product)
        if f % 4 == 3:
            video_part = video_part + jnp.log(product)
        row_out[at, :] = jnp.where(mask > 0.0, 1.0 / (total * frames), FAR)
    video_part = video_part / frames - jnp.log(glosses)
    gloss_parts = [jnp.zeros((CLIPS_DEV, LANES), F32)] * 3
    for t in range(TILES):
        mask = gloss_mask[t]
        total = cols[t]
        gloss_parts[t % 3] = gloss_parts[t % 3] + mask * jnp.log(total)
        col_out[t] = jnp.where(mask > 0.0, 1.0 / (total * packed_glosses[t % 3]), FAR)
    gloss_part = unpacked_sum(*gloss_parts) / glosses - jnp.log(frames)
    logits = 0.5 * (video_part + gloss_part)
    e_pair = jnp.where(real, jnp.exp(logits), 0.0)
    e_out[...] = e_pair

    sums = jnp.sum(e_pair, axis=1, keepdims=True)
    across = lane == iota((CLIPS_DEV, LANES), 0)
    r_row = jnp.sum(jnp.where(across, jnp.broadcast_to(sums, (CLIPS_DEV, LANES)), 0.0), axis=0, keepdims=True)
    inner, outer = lax.axis_index("inner"), lax.axis_index("outer")
    z, core = lax.rem(outer, NZ), lax.rem(inner, NCORE)
    x, y = 2 * lax.div(inner, 16) + lax.div(outer, NZ), lax.rem(lax.div(inner, NCORE), NY)
    clip0 = core * OWN * NZ + lax.rem(z, 2) * (NZ // 2) + lax.div(z, 2)
    text0 = x * OWN * NY + y
    own = jnp.zeros((CLIPS_DEV, LANES), jnp.bool_)
    for c in range(OWN):
        own = own | ((iota((CLIPS_DEV, LANES), 0) == clip0 + c * NZ) & (lane == text0 + c * NY))
    diag = jnp.sum(jnp.where(own, logits, 0.0), keepdims=True).reshape(1, 1)
    r_row = jnp.where(iota((1, LANES), 1) == CLIPS_DEV, diag, r_row)
    for i in range(NZC):
        r_out[i] = r_row
    c_out[...] = jnp.sum(e_pair, axis=0, keepdims=True)
    for copy in copies:
        copy.wait()


def started(copies):
    for copy in copies:
        copy.start()
    return copies


def halves_of(p):
    return [(r, h, p.at[h, pl.ds(r * VROWS // 2, VROWS // 2)]) for r in range(2) for h in range(2)]


def weights_kernel(v_hbm, g_hbm, row_ref, col_ref, e_ref, p_hbm, v, g, p, sems):
    firsts = [pl.ds(0, VROWS // 2), pl.ds(VROWS // 2, VROWS // 2)]
    order = ((v_hbm, v, 0), (g_hbm, g, 0), (g_hbm, g, 1), (v_hbm, v, 1))
    loads = started([pltpu.make_async_copy(a.at[firsts[i]], b.at[firsts[i]], sems.at[k]) for k, (a, b, i) in enumerate(order)])
    scales = packed(2.5 * e_ref[...])
    stores = []
    for (r, h, out), (_, _, here) in zip(halves_of(p_hbm), halves_of(p), strict=True):
        for load in loads[: 2 if r + h == 0 else 1]:
            load.wait()
        loads = loads[2 if r + h == 0 else 1 :]
        e = exp_scores(v[pl.ds(r * VROWS // 2, VROWS // 2), :], g[pl.ds(h * HALF, HALF), :])
        for f in range(FRAMES // 2):
            row = packed(row_ref[pl.ds((r * FRAMES // 2 + f) * CLIPS_DEV, CLIPS_DEV), :])
            block = e[f * CLIPS_DEV : (f + 1) * CLIPS_DEV]
            parts = []
            for k in range(TILES // 2):
                share = jnp.maximum(row[k % 3] + col_ref[h * TILES // 2 + k], 0.0)
                parts.append(scales[k % 3] * block[:, k * LANES : (k + 1) * LANES] * share)
            here[pl.ds(f * CLIPS_DEV, CLIPS_DEV), :] = jnp.concatenate(parts, axis=1).astype(BF16)
            if f % 8 == 7:
                at = pl.ds((f - 7) * CLIPS_DEV, 8 * CLIPS_DEV)
                stores += started([pltpu.make_async_copy(here.at[at], out.at[at], sems.at[4 + 4 * r + 2 * h + f // 8])])
    for store in stores:
        store.wait()


def added(got):
    total = got[0]
    for i in range(1, got.shape[0]):
        total = total + got[i]
    return total


def row_sums_kernel(r_got, c_part, c_out, r_out):
    r_row = added(r_got)
    r_out[...] = r_row
    lane = iota((1, LANES), 1)
    logs = jnp.where(lane < CLIPS_DEV, jnp.log(jnp.where(lane < CLIPS_DEV, r_row, 1.0)), 0.0)
    logs = logs - jnp.where(lane == CLIPS_DEV, 2.0 * r_row, 0.0)
    total = jnp.sum(logs, axis=1, keepdims=True)
    message = jnp.where(lane == TEXTS_DEV, total, c_part[...])
    for i in range(NXY):
        c_out[i] = message


def inverse_texts(c_row):
    return jnp.broadcast_to(1.0 / column_of(c_row, TEXTS_DEV), (TEXTS_DEV, WIDTH))


def by_clip_kernel(r_ref, p_ref, v_ref, g_ref, out, av_out, both):
    step = pl.program_id(0)

    @pl.when(step == 0)
    def _():
        inverse = jnp.broadcast_to(1.0 / column_of(r_ref[...], CLIPS_DEV), (CLIPS_DEV, WIDTH))
        for f in range(FRAMES):
            at = pl.ds(f * CLIPS_DEV, CLIPS_DEV)
            v = v_ref[at, :]
            both[at, :WIDTH] = v
            both[at, WIDTH:] = (v.astype(F32) * inverse).astype(BF16)

    out[...] = tn(p_ref[0], both[...]).reshape(GLOSSES // 2, TEXTS_DEV, 2 * WIDTH)
    part = nn(p_ref[0], g_ref[...])

    @pl.when(step == 0)
    def _():
        av_out[...] = part

    @pl.when(step > 0)
    def _():
        av_out[...] = av_out[...] + part


def gloss_send_kernel(c_got, by_clip, out, c_out, held, scr, sems):
    many = GLOSSES // QUADS
    copies = started(
        [
            pltpu.make_async_copy(by_clip.at[pl.ds(q * many, many)], held.at[pl.ds(q * many, many)], sems.at[q])
            for q in range(QUADS)
        ]
    )
    c_out[...] = added(c_got)
    col = inverse_texts(c_out[...])
    for q, copy in enumerate(copies):
        copy.wait()
        for k in range(many):
            g = q * many + k
            block = held[g, :, :WIDTH] * col + held[g, :, WIDTH:]
            row = g * OWN
            for x in range(NX):
                for c in range(OWN):
                    first = (x * OWN + c) * NY
                    put(scr, pl.ds(x * NY * G_PITCH + row + c, NY, stride=G_PITCH), block[first : first + NY])
    for i in range(NXY):
        out[i] = get(scr, pl.ds(i * G_PITCH, GOWN)).astype(BF16)


def clip_send_kernel(c_got, r_ref, p_hbm, g_hbm, av_ref, mine, twin, p, g, g_by_text, sems):
    g_copy = pltpu.make_async_copy(g_hbm, g, sems.at[4])
    copies = []
    for (r, h, theirs), (_, _, here) in zip(halves_of(p_hbm), halves_of(p), strict=True):
        copies.append(pltpu.make_async_copy(theirs, here, sems.at[2 * r + h]))
    started([g_copy, *copies])
    c_row = added(c_got)
    col = inverse_texts(c_row)
    core = lax.rem(lax.axis_index("inner"), NCORE)
    inverse = jnp.broadcast_to(1.0 / column_of(r_ref[...], CLIPS_DEV), (CLIPS_DEV, WIDTH))
    half = CLIPS_DEV // 2
    g_copy.wait()
    for i in range(GLOSSES):
        at = pl.ds(i * TEXTS_DEV, TEXTS_DEV)
        g_by_text[at, :] = (g[at, :].astype(F32) * col).astype(BF16)
    for r in range(2):
        copies[2 * r].wait()
        copies[2 * r + 1].wait()
        at = pl.ds(r * VROWS // 2, VROWS // 2)
        part = nn(p[0, at, :], g_by_text[pl.ds(0, HALF), :]) + nn(p[1, at, :], g_by_text[pl.ds(HALF, HALF), :])
        for pair in range(FRAMES // 4):
            others = []
            for f in (2 * pair, 2 * pair + 1):
                full = r * FRAMES // 2 + f
                new = part[f * CLIPS_DEV : (f + 1) * CLIPS_DEV]
                block = av_ref[pl.ds(full * CLIPS_DEV, CLIPS_DEV), :] * inverse + new
                low, high = block[:half], block[half:]
                mine[pl.ds(full * half, half), :] = jnp.where(core == 0, low, high)
                others.append(jnp.where(core == 0, high, low))
            at = pl.ds((r * FRAMES // 4 + pair) * CLIPS_DEV, CLIPS_DEV)
            twin[at, :] = jnp.concatenate(others, axis=0).astype(BF16)
    real = iota((1, LANES), 1) < TEXTS_DEV
    logs = jnp.where(real, jnp.log(jnp.where(real, c_row, 1.0)), 0.0)
    extra = pieces(jnp.sum(logs, axis=1, keepdims=True))
    mine[pl.ds(FRAMES * half, EXTRA), :] = extra
    twin[pl.ds(FRAMES * half, EXTRA), :] = extra.astype(BF16)


def own_z():
    return lax.rem(lax.axis_index("outer"), NZ)


def clip_rows_kernel(mine, got, keep, send, scr):
    step = 2 * NZ
    for i in range(VOWN // 2):
        at = pl.ds(i * step, step)
        two = mine[at, :] + got[at, :].astype(F32)
        for k in range(2):
            put(scr, pl.ds(2 * i + k, NZ, stride=V_PITCH), two[k * NZ : (k + 1) * NZ])
    bit = lax.rem(own_z(), 2)
    owners = NZ // 2
    for i in range(owners):
        at = pl.ds(i * VOWN, VOWN)
        keep[at, :] = get(scr, pl.ds(pl.multiple_of((owners * bit + i) * V_PITCH, 8), VOWN))
        send[at, :] = get(scr, pl.ds(pl.multiple_of((owners * (1 - bit) + i) * V_PITCH, 8), VOWN)).astype(BF16)
    extra = loss_rows(mine, got, NZ)
    keep[pl.ds(owners * VOWN, EXTRA), :] = extra
    send[pl.ds(owners * VOWN, EXTRA), :] = extra.astype(BF16)


def loss_rows(mine, got, owners):
    tail = pl.ds(owners * VOWN, EXTRA)
    return pieces(unpiece(mine[tail, :]) + unpiece(got[tail, :].astype(F32)))


def quarter_kernel(mine, got, keep, *sends):
    own = lax.div(own_z(), 2)
    extra = loss_rows(mine, got, NZ // 2)
    for out, owner in zip((keep, *sends), (own, own ^ 1, own ^ 2, own ^ 3), strict=True):
        at = pl.ds(pl.multiple_of(owner * VOWN, VOWN), VOWN)
        out[pl.ds(0, VOWN), :] = (mine[at, :] + got[at, :].astype(F32)).astype(out.dtype)
        out[pl.ds(VOWN, EXTRA), :] = extra.astype(out.dtype)


def token_grads(total, scr, raw, out, tokens):
    put(scr, pl.ds(0, OWN * tokens), total)
    for c in range(OWN):
        x = raw[c].astype(F32)
        d = get(scr, pl.ds(c, tokens, stride=OWN))
        mean_sq = jnp.mean(x * x, axis=-1, keepdims=True) + EPSILON
        factor = lax.rsqrt(mean_sq) / math.sqrt(WIDTH)
        inner = jnp.sum(d * x, axis=-1, keepdims=True)
        out[c] = factor * d - factor * x * (inner / (WIDTH * mean_sq))


def video_grad_kernel(clips, mine, got1, got2, got3, c_row, diag, video, out, loss, scr):
    at = pl.ds(0, VOWN)
    total = mine[at, :]
    for got in (got1, got2, got3):
        total = total + got[at, :].astype(F32)
    token_grads(total + diag[...], scr, video, out, FRAMES)
    row_part = c_row[:, TEXTS_DEV : TEXTS_DEV + 1]
    tail = pl.ds(VOWN, EXTRA)
    near = unpiece(mine[tail, :]) + unpiece(got1[tail, :].astype(F32))
    far = unpiece(got2[tail, :].astype(F32)) + unpiece(got3[tail, :].astype(F32))
    loss[...] = (near + far + row_part) * (0.5 / clips)


def gloss_grad_kernel(got, diag, gloss, out, scr):
    total = got[0].astype(F32)
    for i in range(1, NXY):
        total = total + got[i].astype(F32)
    token_grads(total + diag[...], scr, gloss, out, GLOSSES)


def shape(*dims, dtype=F32):
    return jax.ShapeDtypeStruct(dims, dtype)


def on_device(clips, video, gloss, frame_count, gloss_count):
    vmem, hbm = pl.BlockSpec(memory_space=pltpu.VMEM), pl.BlockSpec(memory_space=pltpu.HBM)
    over_all = ("outer", "inner")

    def to_core(a):
        return lax.ppermute(a, "inner", [(i, i ^ 1) for i in range(lax.axis_size("inner"))])

    def to_z(a, mask):
        return lax.ppermute(a, "outer", [(i, i ^ mask) for i in range(lax.axis_size("outer"))])

    def exchanged(a, groups):
        return lax.all_to_all(a, over_all, 0, 0, axis_index_groups=groups, tiled=True)

    def gathered(a, groups):
        return lax.all_gather(a, over_all, axis=0, axis_index_groups=groups, tiled=True)

    def in_hbm(*arrays):
        return [pltpu.with_memory_space_constraint(a, pltpu.HBM) for a in arrays]

    with jax.named_scope("unit_tokens"):
        v_own, g_send, g_own, counts = pl.pallas_call(
            units_kernel,
            in_specs=[hbm] * 4,
            out_shape=(
                shape(VOWN, WIDTH, dtype=BF16),
                shape(NXY, GOWN, WIDTH, dtype=BF16),
                shape(GOWN, WIDTH, dtype=BF16),
                shape(8, LANES, dtype=jnp.int32),
            ),
            scratch_shapes=[
                pltpu.SMEM((OWN,), jnp.int32),
                pltpu.SMEM((OWN,), jnp.int32),
                pltpu.VMEM((OWN, FRAMES, WIDTH), BF16),
                pltpu.VMEM((OWN, GLOSSES, WIDTH), BF16),
                two_halves(VOWN),
                two_halves(GOWN),
                pltpu.SemaphoreType.DMA((4,)),
            ],
            compiler_params=params(),
            cost_estimate=cost(2e5, 7e5),
        )(*in_hbm(frame_count, gloss_count, video, gloss))

    with jax.named_scope("gather"):
        g_got = exchanged(g_send, XY_GROUPS)
        v_got = gathered(gathered(v_own, Z_QUADS), Z_PAIRS)
        v_got = gathered(v_got, CORE_GROUPS)

    def whole(*dims):
        return pl.BlockSpec(dims, lambda i: (0,) * len(dims))

    with jax.named_scope("forward"):
        v_all, g_all, row_inv, col_inv, e_pair, r_part, c_part = pl.pallas_call(
            forward_kernel,
            in_specs=[vmem] * 2,
            out_specs=[hbm] * 2 + [vmem] * 5,
            out_shape=(
                pltpu.HBM((VROWS, WIDTH), BF16),
                pltpu.HBM((GROWS, WIDTH), BF16),
                shape(VROWS, LANES),
                shape(TILES, CLIPS_DEV, LANES),
                shape(CLIPS_DEV, LANES),
                shape(NZC, 1, LANES),
                shape(1, LANES),
            ),
            scratch_shapes=[
                pltpu.VMEM((VROWS, WIDTH), BF16),
                pltpu.VMEM((GROWS, WIDTH), BF16),
                two_halves(NZC * V_PITCH),
                two_halves(NXY * G_PITCH),
                pltpu.VMEM((VROWS, LANES), F32),
                pltpu.VMEM((TILES, 1, LANES), F32),
                pltpu.VMEM((VROWS, 3 * LANES), F32),
                pltpu.VMEM((TILES, CLIPS_DEV, LANES), F32),
                pltpu.SemaphoreType.DMA((2,)),
            ],
            compiler_params=params(),
            cost_estimate=cost(2 * VROWS * GROWS * WIDTH, 8e6, VROWS * GROWS),
        )(v_got, g_got)

    with jax.named_scope("row_sums"):
        c_send, r_row = pl.pallas_call(
            row_sums_kernel,
            in_specs=[vmem] * 2,
            out_shape=(shape(NXY, 1, LANES), shape(1, LANES)),
            compiler_params=params(),
            cost_estimate=cost(1e5, 3e5),
        )(exchanged(r_part, ZC_GROUPS), c_part)
    with jax.named_scope("column_sums"):
        c_got = exchanged(c_send, XY_GROUPS)

    with jax.named_scope("weights"):
        weights = pl.pallas_call(
            weights_kernel,
            in_specs=[hbm, hbm, vmem, vmem, vmem],
            out_specs=hbm,
            out_shape=pltpu.HBM((2, VROWS, HALF), BF16),
            scratch_shapes=[
                pltpu.VMEM((VROWS, WIDTH), BF16),
                pltpu.VMEM((GROWS, WIDTH), BF16),
                pltpu.VMEM((2, VROWS, HALF), BF16),
                pltpu.SemaphoreType.DMA((12,)),
            ],
            compiler_params=params(),
            cost_estimate=cost(2 * VROWS * GROWS * WIDTH, 12e6, VROWS * GROWS),
        )(*in_hbm(v_all, g_all), row_inv, col_inv, e_pair)

    with jax.named_scope("by_clip"):
        by_clip, av = pl.pallas_call(
            by_clip_kernel,
            grid=(2,),
            in_specs=[
                whole(1, LANES),
                pl.BlockSpec((1, VROWS, HALF), lambda i: (i, 0, 0)),
                whole(VROWS, WIDTH),
                pl.BlockSpec((HALF, WIDTH), lambda i: (i, 0)),
            ],
            out_specs=(
                pl.BlockSpec((GLOSSES // 2, TEXTS_DEV, 2 * WIDTH), lambda i: (i, 0, 0)),
                whole(VROWS, WIDTH),
            ),
            out_shape=(pltpu.HBM((GLOSSES, TEXTS_DEV, 2 * WIDTH), F32), shape(VROWS, WIDTH)),
            scratch_shapes=[pltpu.VMEM((VROWS, 2 * WIDTH), BF16)],
            compiler_params=params(),
            cost_estimate=cost(6 * VROWS * GROWS * WIDTH, 14e6),
        )(r_row, *in_hbm(weights, v_all, g_all))

    with jax.named_scope("clip_send"):
        v_rows = FRAMES * CLIPS_DEV // 2 + EXTRA
        mine, twin = pl.pallas_call(
            clip_send_kernel,
            in_specs=[vmem, vmem, hbm, hbm, vmem],
            out_shape=(shape(v_rows, WIDTH), shape(v_rows, WIDTH, dtype=BF16)),
            scratch_shapes=[
                pltpu.VMEM((2, VROWS, HALF), BF16),
                pltpu.VMEM((GROWS, WIDTH), BF16),
                pltpu.VMEM((GROWS, WIDTH), BF16),
                pltpu.SemaphoreType.DMA((5,)),
            ],
            compiler_params=params(),
            cost_estimate=cost(2 * VROWS * GROWS * WIDTH, 1e7),
        )(c_got, r_row, *in_hbm(weights, g_all), av)

    with jax.named_scope("gloss_send"):
        twin, c_ready = lax.optimization_barrier((twin, c_got))
        dg_send, c_row = pl.pallas_call(
            gloss_send_kernel,
            in_specs=[vmem, hbm],
            out_shape=(shape(NXY, GOWN, WIDTH, dtype=BF16), shape(1, LANES)),
            scratch_shapes=[
                pltpu.VMEM((GLOSSES, TEXTS_DEV, 2 * WIDTH), F32),
                two_halves(NXY * G_PITCH),
                pltpu.SemaphoreType.DMA((QUADS,)),
            ],
            compiler_params=params(),
            cost_estimate=cost(2e6, 5e6),
        )(c_ready, *in_hbm(by_clip))
        dg_got = exchanged(dg_send, XY_GROUPS)

    def kept_and_sent(owners):
        rows = owners * VOWN + EXTRA
        return (shape(rows, WIDTH), shape(rows, WIDTH, dtype=BF16))

    with jax.named_scope("clips_by_core"):
        mine, sent = pl.pallas_call(
            clip_rows_kernel,
            in_specs=[vmem] * 2,
            out_shape=kept_and_sent(NZ // 2),
            scratch_shapes=[two_halves(NZ * V_PITCH)],
            compiler_params=params(),
            cost_estimate=cost(1e6, 2e6),
        )(mine, to_core(twin))
    with jax.named_scope("clips_by_z"):
        mine, *sent = pl.pallas_call(
            quarter_kernel,
            in_specs=[vmem] * 2,
            out_shape=kept_and_sent(1) + kept_and_sent(1)[1:] * 2,
            compiler_params=params(),
            cost_estimate=cost(1e10, 1e6),
        )(mine, to_z(sent, 1))

    with jax.named_scope("diagonal"):
        mine, v_own, g_own, counts = lax.optimization_barrier((mine, v_own, g_own, counts))
        dv_diag, dg_diag = pl.pallas_call(
            diagonal_kernel,
            in_specs=[vmem] * 3,
            out_shape=(shape(VOWN, WIDTH), shape(GOWN, WIDTH)),
            compiler_params=params(),
            cost_estimate=cost(2e7, 3e5),
        )(counts, v_own, g_own)

    with jax.named_scope("gloss_grad"):
        grad_gloss = pl.pallas_call(
            gloss_grad_kernel,
            in_specs=[vmem] * 3,
            out_shape=shape(OWN, GLOSSES, WIDTH),
            scratch_shapes=[two_halves(GOWN)],
            compiler_params=params(),
            cost_estimate=cost(1e6, 1e6),
        )(dg_got, dg_diag, gloss)
    mine, grad_gloss = lax.optimization_barrier((mine, grad_gloss))

    with jax.named_scope("video_grad"):
        grad_video, loss = pl.pallas_call(
            functools.partial(video_grad_kernel, clips),
            in_specs=[vmem] * 7,
            out_shape=(shape(OWN, FRAMES, WIDTH), shape(1, 1)),
            scratch_shapes=[two_halves(VOWN)],
            compiler_params=params(),
            cost_estimate=cost(1e6, 1e6),
        )(mine, *[to_z(a, 2 * m) for m, a in enumerate(sent, start=1)], c_row, dv_diag, video)
    return loss.reshape(()), grad_video, grad_gloss


def solution(mesh):
    clips = OWN * mesh.shape["outer"] * mesh.shape["inner"]
    over_all = ("outer", "inner")
    tokens, counts = P(over_all, None, None), P(over_all)
    return jax.shard_map(
        functools.partial(on_device, clips),
        mesh=mesh,
        in_specs=(tokens, tokens, counts, counts),
        out_specs=(P(), tokens, tokens),
        check_vma=False,
    )
```

```python
import functools
import math

import jax
import jax.numpy as jnp
from jax import lax
from jax.experimental import pallas as pl
from jax.experimental.pallas import tpu as pltpu
from jax.sharding import PartitionSpec as P

F32 = jnp.float32
BF16 = jnp.bfloat16
EPSILON = 1e-06
EXP_SCALE = 10.0 * math.log2(math.e)
MARK = 2.0
MARK_LIMIT = 1.5
FAR = -1e30

NZ, NY, NX, NCORE = 8, 8, 4, 2
OWN = 3
FRAMES, GLOSSES, WIDTH = 32, 16, 256
CLIPS_DEV = NZ * NCORE * OWN
TEXTS_DEV = NY * NX * OWN
LANES = 128
VROWS = FRAMES * CLIPS_DEV
GROWS = GLOSSES * TEXTS_DEV
VOWN = FRAMES * OWN
GOWN = GLOSSES * OWN
EXTRA = 16
V_PITCH, G_PITCH = VOWN + 8, GOWN + 8
QUADS = GLOSSES // 4
TILES = GROWS // LANES
HALF = GROWS // 2
NXY, NZC = NX * NY, NZ * NCORE

def flat(x, z, y, core):
    return ((x % 2) * NZ + z) * 32 + (x // 2) * 16 + 2 * y + core


def z_groups(masks):
    return [
        [flat(x, z ^ mask, y, c) for mask in masks]
        for x in range(NX)
        for y in range(NY)
        for c in range(NCORE)
        for z in range(NZ)
        if not z & masks[-1] and not z & masks[len(masks) // 2]
    ]


Z_QUADS, Z_PAIRS = z_groups((0, 2, 4, 6)), z_groups((0, 1))
CORE_GROUPS = [[flat(x, z, y, c) for c in range(NCORE)] for x in range(NX) for y in range(NY) for z in range(NZ)]
XY_GROUPS = [[flat(x, z, y, c) for x in range(NX) for y in range(NY)] for z in range(NZ) for c in range(NCORE)]
ZC_GROUPS = [[flat(x, z, y, c) for c in range(NCORE) for z in range(NZ)] for x in range(NX) for y in range(NY)]


def params(limit_mb=32):
    return pltpu.CompilerParams(vmem_limit_bytes=limit_mb * 1024 * 1024)


def cost(flops, nbytes, trans=0):
    return pl.CostEstimate(flops=int(flops), bytes_accessed=int(nbytes), transcendentals=int(trans))


def iota(shape, dim):
    return lax.broadcasted_iota(jnp.int32, shape, dim)


def nt(a, b, **kw):
    return lax.dot_general(a, b, (((1,), (1,)), ((), ())), preferred_element_type=F32, **kw)


def nn(a, b, **kw):
    return lax.dot_general(a, b, (((1,), (0,)), ((), ())), preferred_element_type=F32, **kw)


def tn(a, b, **kw):
    return lax.dot_general(a, b, (((0,), (0,)), ((), ())), preferred_element_type=F32, **kw)


def column_of(row, n):
    eye = iota((n, LANES), 0) == iota((n, LANES), 1)
    return jnp.sum(jnp.where(eye, jnp.broadcast_to(row, (n, LANES)), 0.0), axis=1, keepdims=True)


def packed(x):
    lane = iota(x.shape, 1)
    a, b, c = (pltpu.roll(x, shift, 1) for shift in (96, 64, 32))
    return jnp.where(lane < 96, x, a), jnp.where(lane < 64, a, b), jnp.where(lane < 32, b, c)


def unpacked_sum(t0, t1, t2):
    lane = iota(t0.shape, 1)
    second = pltpu.roll(jnp.where(lane >= 96, t0, t1), 32, 1)
    third = pltpu.roll(jnp.where(lane >= 64, t1, t2), 64, 1)
    return (t0 + second) + (third + pltpu.roll(t2, 96, 1))


def pieces(value):
    lane = iota((EXTRA, WIDTH), 1)
    full = jnp.broadcast_to(value, (EXTRA, WIDTH))
    hi = full.astype(BF16).astype(F32)
    mid = (full - hi).astype(BF16).astype(F32)
    low = (full - hi - mid).astype(BF16).astype(F32)
    return jnp.where(lane == 0, hi, jnp.where(lane == 1, mid, jnp.where(lane == 2, low, 0.0)))


def unpiece(block):
    mine = (iota((EXTRA, WIDTH), 0) == 0) & (iota((EXTRA, WIDTH), 1) < 3)
    return jnp.sum(jnp.where(mine, block, 0.0), keepdims=True).reshape(1, 1)


def put(ref, at, value):
    ref[0, at, :] = value[:, :LANES]
    ref[1, at, :] = value[:, LANES:]


def get(ref, at):
    return jnp.concatenate([ref[0, at, :], ref[1, at, :]], axis=1)


def two_halves(rows, stride):
    return pltpu.VMEM((2, rows + -(-stride // 8) * 8, LANES), F32)


def units_kernel(fc_in, gc_in, video_in, gloss_in, v_out, g_out, g_one, count_out, fc, gc, video, gloss, v_scr, g_scr, sems):
    pairs = ((fc_in, fc), (gc_in, gc), (video_in, video), (gloss_in, gloss))
    copies = [pltpu.make_async_copy(a, b, sems.at[i]) for i, (a, b) in enumerate(pairs)]
    for copy in copies:
        copy.start()
    for copy in copies:
        copy.wait()
    row = iota((8, LANES), 0)
    counts = jnp.zeros((8, LANES), jnp.int32)
    for c in range(OWN):
        counts = jnp.where(row == c, fc[c], jnp.where(row == OWN + c, gc[c], counts))
    count_out[...] = counts
    for count, raw, scr, tokens in ((fc, video, v_scr, FRAMES), (gc, gloss, g_scr, GLOSSES)):
        row, lane = iota((tokens, WIDTH), 0), iota((tokens, WIDTH), 1)
        for c in range(OWN):
            x = raw[c].astype(F32)
            mean_sq = jnp.mean(x * x, axis=-1, keepdims=True) + EPSILON
            unit = x * (lax.rsqrt(mean_sq) / math.sqrt(WIDTH))
            mark = jnp.where(lane == 0, MARK, 0.0)
            put(scr, pl.ds(c, tokens, stride=OWN), jnp.where(row < count[c], unit, mark))
    v = get(v_scr, pl.ds(0, VOWN)).astype(BF16)
    g = get(g_scr, pl.ds(0, GOWN)).astype(BF16)
    v_out[...] = v
    g_one[...] = g
    for i in range(NXY):
        g_out[i] = g


def diagonal_kernel(count_ref, v_ref, g_ref, dv, dg):
    def pick(count, which):
        return jnp.where(which == 0, count[0], jnp.where(which == 1, count[1], count[2]))

    fc = [count_ref[c : c + 1, 0:1] for c in range(OWN)]
    gc = [count_ref[OWN + c : OWN + c + 1, 0:1] for c in range(OWN)]
    v, g = v_ref[...], g_ref[...]
    shape = (VOWN, GOWN)
    r, q = iota(shape, 0), iota(shape, 1)
    rc, qc = lax.rem(r, OWN), lax.rem(q, OWN)
    valid = (rc == qc) & (lax.div(r, OWN) < pick(fc, rc)) & (lax.div(q, OWN) < pick(gc, qc))
    e = jnp.where(valid, jnp.exp2(nt(v, g) * EXP_SCALE), 0.0)
    r1, q1 = iota((VOWN, 1), 0), iota((1, GOWN), 1)
    rc1, qc1 = lax.rem(r1, OWN), lax.rem(q1, OWN)
    frames_r, glosses_q = pick(fc, rc1), pick(gc, qc1)
    row_ok = lax.div(r1, OWN) < frames_r
    col_ok = lax.div(q1, OWN) < glosses_q
    frames_r, glosses_q = frames_r.astype(F32), glosses_q.astype(F32)
    rows = jnp.where(row_ok, jnp.sum(e, axis=1, keepdims=True), 1.0)
    cols = jnp.where(col_ok, jnp.sum(e, axis=0, keepdims=True), 1.0)
    weight = -5.0 * e * (1.0 / (rows * frames_r) + 1.0 / (cols * glosses_q))
    dv[...] = nn(weight, g.astype(F32), precision=lax.Precision.HIGHEST)
    dg[...] = tn(weight, v.astype(F32), precision=lax.Precision.HIGHEST)


def exp_scores(v, g):
    return jnp.exp2(nt(v, g) * EXP_SCALE)


def forward_kernel(
    v_got, g_got,
    v_hbm, g_hbm, row_out, col_out, e_out, r_out, c_out,
    v_out, g_out, v_scr, g_scr, frame_mask, gloss_mask, rows, cols, sems,
):
    results = ((v_out, v_hbm), (g_out, g_hbm))
    copies = [pltpu.make_async_copy(a, b, sems.at[i]) for i, (a, b) in enumerate(results)]
    for i in range(NZC):
        put(v_scr, pl.ds(i * V_PITCH, VOWN), v_got[pl.ds(i * VOWN, VOWN), :].astype(F32))
    for f in range(FRAMES):
        parts = [
            get(v_scr, pl.ds(k * NZ * V_PITCH + f * OWN + c, NZ, stride=V_PITCH)) for k in range(NCORE) for c in range(OWN)
        ]
        v_out[pl.ds(f * CLIPS_DEV, CLIPS_DEV), :] = jnp.concatenate(parts, axis=0).astype(BF16)
    copies[0].start()
    for i in range(NXY):
        put(g_scr, pl.ds(i * G_PITCH, GOWN), g_got[i].astype(F32))
    for g in range(GLOSSES):
        parts = [
            get(g_scr, pl.ds(x * NY * G_PITCH + g * OWN + c, NY, stride=G_PITCH)) for x in range(NX) for c in range(OWN)
        ]
        g_out[pl.ds(g * TEXTS_DEV, TEXTS_DEV), :] = jnp.concatenate(parts, axis=0).astype(BF16)
    copies[1].start()

    first = jnp.where(iota((WIDTH, LANES), 0) == 0, 1.0, 0.0).astype(BF16)
    frame_mask[...] = jnp.where(nn(v_out[...], first) < MARK_LIMIT, 1.0, 0.0)
    first_row = jnp.where(iota((16, WIDTH), 1) == 0, 1.0, 0.0).astype(BF16)
    for t in range(TILES):
        found = nt(first_row, g_out[pl.ds(t * LANES, LANES), :])[0:1]
        gloss_mask[t] = jnp.where(found < MARK_LIMIT, 1.0, 0.0)
    frames = jnp.zeros((CLIPS_DEV, LANES), F32)
    for f in range(FRAMES):
        frames = frames + frame_mask[pl.ds(f * CLIPS_DEV, CLIPS_DEV), :]
    by_tile = []
    for t in range(3):
        by_tile.append(gloss_mask[t] + gloss_mask[t + 3] + gloss_mask[t + 6] + gloss_mask[t + 9])
    lane = iota((CLIPS_DEV, LANES), 1)
    real = lane < TEXTS_DEV
    counts = unpacked_sum(*[jnp.broadcast_to(t, (8, LANES)) for t in by_tile])
    glosses = jnp.where(real[0:8], counts, 1.0)
    packed_glosses = [t[0:1] for t in packed(glosses)]
    glosses = glosses[0:1]

    for half in range(2):
        e = exp_scores(v_out[...], g_out[pl.ds(half * HALF, HALF), :])
        tiles = range(half * TILES // 2, (half + 1) * TILES // 2)
        masks = [gloss_mask[t] for t in tiles]
        sums = [jnp.zeros((CLIPS_DEV, LANES), F32) for _ in tiles]
        for f in range(FRAMES):
            at = pl.ds(f * CLIPS_DEV, CLIPS_DEV)
            mask = frame_mask[at, :]
            block = e[f * CLIPS_DEV : (f + 1) * CLIPS_DEV]
            parts = [block[:, k * LANES : (k + 1) * LANES] for k in range(TILES // 2)]
            sums = [total + part * mask for total, part in zip(sums, parts, strict=True)]
            for k in range(3):
                part = parts[k] * masks[k] + parts[k + 3] * masks[k + 3]
                rows[at, pl.ds(k * LANES, LANES)] = part if half == 0 else rows[at, pl.ds(k * LANES, LANES)] + part
        for k, t in enumerate(tiles):
            cols[t] = sums[k]

    video_part = jnp.zeros((CLIPS_DEV, LANES), F32)
    for f in range(FRAMES):
        at = pl.ds(f * CLIPS_DEV, CLIPS_DEV)
        mask = frame_mask[at, :]
        total = unpacked_sum(*[rows[at, pl.ds(k * LANES, LANES)] for k in range(3)])
        total = jnp.where(real, total, 1.0)
        product = jnp.where(mask > 0.0, total, 1.0) * (1.0 if f % 4 == 0 else product)
        if f % 4 == 3:
            video_part = video_part + jnp.log(product)
        row_out[at, :] = jnp.where(mask > 0.0, 1.0 / (total * frames), FAR)
    video_part = video_part / frames - jnp.log(glosses)
    gloss_parts = [jnp.zeros((CLIPS_DEV, LANES), F32)] * 3
    for t in range(TILES):
        mask = gloss_mask[t]
        total = cols[t]
        gloss_parts[t % 3] = gloss_parts[t % 3] + mask * jnp.log(total)
        col_out[t] = jnp.where(mask > 0.0, 1.0 / (total * packed_glosses[t % 3]), FAR)
    gloss_part = unpacked_sum(*gloss_parts) / glosses - jnp.log(frames)
    logits = 0.5 * (video_part + gloss_part)
    e_pair = jnp.where(real, jnp.exp(logits), 0.0)
    e_out[...] = e_pair

    sums = jnp.sum(e_pair, axis=1, keepdims=True)
    across = lane == iota((CLIPS_DEV, LANES), 0)
    r_row = jnp.sum(jnp.where(across, jnp.broadcast_to(sums, (CLIPS_DEV, LANES)), 0.0), axis=0, keepdims=True)
    inner, outer = lax.axis_index("inner"), lax.axis_index("outer")
    z, core = lax.rem(outer, NZ), lax.rem(inner, NCORE)
    x, y = 2 * lax.div(inner, 16) + lax.div(outer, NZ), lax.rem(lax.div(inner, NCORE), NY)
    clip0 = core * OWN * NZ + lax.rem(z, 2) * (NZ // 2) + lax.div(z, 2)
    text0 = x * OWN * NY + y
    own = jnp.zeros((CLIPS_DEV, LANES), jnp.bool_)
    for c in range(OWN):
        own = own | ((iota((CLIPS_DEV, LANES), 0) == clip0 + c * NZ) & (lane == text0 + c * NY))
    diag = jnp.sum(jnp.where(own, logits, 0.0), keepdims=True).reshape(1, 1)
    r_row = jnp.where(iota((1, LANES), 1) == CLIPS_DEV, diag, r_row)
    for i in range(NZC):
        r_out[i] = r_row
    c_out[...] = jnp.sum(e_pair, axis=0, keepdims=True)
    for copy in copies:
        copy.wait()


def started(copies):
    for copy in copies:
        copy.start()
    return copies


def halves_of(p):
    return [(r, h, p.at[h, pl.ds(r * VROWS // 2, VROWS // 2)]) for r in range(2) for h in range(2)]


def weights_kernel(v_hbm, g_hbm, row_ref, col_ref, e_ref, p_hbm, v, g, p, sems):
    firsts = [pl.ds(0, VROWS // 2), pl.ds(VROWS // 2, VROWS // 2)]
    order = ((v_hbm, v, 0), (g_hbm, g, 0), (g_hbm, g, 1), (v_hbm, v, 1))
    loads = started([pltpu.make_async_copy(a.at[firsts[i]], b.at[firsts[i]], sems.at[k]) for k, (a, b, i) in enumerate(order)])
    scales = packed(2.5 * e_ref[...])
    stores = []
    for (r, h, out), (_, _, here) in zip(halves_of(p_hbm), halves_of(p), strict=True):
        for load in loads[: 2 if r + h == 0 else 1]:
            load.wait()
        loads = loads[2 if r + h == 0 else 1 :]
        e = exp_scores(v[pl.ds(r * VROWS // 2, VROWS // 2), :], g[pl.ds(h * HALF, HALF), :])
        for f in range(FRAMES // 2):
            row = packed(row_ref[pl.ds((r * FRAMES // 2 + f) * CLIPS_DEV, CLIPS_DEV), :])
            block = e[f * CLIPS_DEV : (f + 1) * CLIPS_DEV]
            parts = []
            for k in range(TILES // 2):
                share = jnp.maximum(row[k % 3] + col_ref[h * TILES // 2 + k], 0.0)
                parts.append(scales[k % 3] * block[:, k * LANES : (k + 1) * LANES] * share)
            here[pl.ds(f * CLIPS_DEV, CLIPS_DEV), :] = jnp.concatenate(parts, axis=1).astype(BF16)
            if f % 8 == 7:
                at = pl.ds((f - 7) * CLIPS_DEV, 8 * CLIPS_DEV)
                stores += started([pltpu.make_async_copy(here.at[at], out.at[at], sems.at[4 + 4 * r + 2 * h + f // 8])])
    for store in stores:
        store.wait()


def added(got):
    total = got[0]
    for i in range(1, got.shape[0]):
        total = total + got[i]
    return total


def row_sums_kernel(r_got, c_part, c_out, r_out):
    r_row = added(r_got)
    r_out[...] = r_row
    lane = iota((1, LANES), 1)
    logs = jnp.where(lane < CLIPS_DEV, jnp.log(jnp.where(lane < CLIPS_DEV, r_row, 1.0)), 0.0)
    logs = logs - jnp.where(lane == CLIPS_DEV, 2.0 * r_row, 0.0)
    total = jnp.sum(logs, axis=1, keepdims=True)
    message = jnp.where(lane == TEXTS_DEV, total, c_part[...])
    for i in range(NXY):
        c_out[i] = message


def inverse_texts(c_row):
    return jnp.broadcast_to(1.0 / column_of(c_row, TEXTS_DEV), (TEXTS_DEV, WIDTH))


def by_clip_kernel(r_ref, p_ref, v_ref, g_ref, out, av_out, both):
    step = pl.program_id(0)

    @pl.when(step == 0)
    def _():
        inverse = jnp.broadcast_to(1.0 / column_of(r_ref[...], CLIPS_DEV), (CLIPS_DEV, WIDTH))
        for f in range(FRAMES):
            at = pl.ds(f * CLIPS_DEV, CLIPS_DEV)
            v = v_ref[at, :]
            both[at, :WIDTH] = v
            both[at, WIDTH:] = (v.astype(F32) * inverse).astype(BF16)

    out[...] = tn(p_ref[0], both[...]).reshape(GLOSSES // 2, TEXTS_DEV, 2 * WIDTH)
    part = nn(p_ref[0], g_ref[...])

    @pl.when(step == 0)
    def _():
        av_out[...] = part

    @pl.when(step > 0)
    def _():
        av_out[...] = av_out[...] + part


def gloss_send_kernel(c_got, by_clip, out, c_out, held, scr, sems):
    many = GLOSSES // QUADS
    copies = started(
        [
            pltpu.make_async_copy(by_clip.at[pl.ds(q * many, many)], held.at[pl.ds(q * many, many)], sems.at[q])
            for q in range(QUADS)
        ]
    )
    c_out[...] = added(c_got)
    col = inverse_texts(c_out[...])
    for q, copy in enumerate(copies):
        copy.wait()
        for k in range(many):
            g = q * many + k
            block = held[g, :, :WIDTH] * col + held[g, :, WIDTH:]
            row = g * OWN
            for x in range(NX):
                for c in range(OWN):
                    first = (x * OWN + c) * NY
                    put(scr, pl.ds(x * NY * G_PITCH + row + c, NY, stride=G_PITCH), block[first : first + NY])
    for i in range(NXY):
        out[i] = get(scr, pl.ds(i * G_PITCH, GOWN)).astype(BF16)


def clip_send_kernel(c_got, r_ref, p_hbm, g_hbm, av_ref, mine, twin, p, g, g_by_text, sems):
    g_copy = pltpu.make_async_copy(g_hbm, g, sems.at[4])
    copies = []
    for (r, h, theirs), (_, _, here) in zip(halves_of(p_hbm), halves_of(p), strict=True):
        copies.append(pltpu.make_async_copy(theirs, here, sems.at[2 * r + h]))
    started([g_copy, *copies])
    c_row = added(c_got)
    col = inverse_texts(c_row)
    core = lax.rem(lax.axis_index("inner"), NCORE)
    inverse = jnp.broadcast_to(1.0 / column_of(r_ref[...], CLIPS_DEV), (CLIPS_DEV, WIDTH))
    half = CLIPS_DEV // 2
    g_copy.wait()
    for i in range(GLOSSES):
        at = pl.ds(i * TEXTS_DEV, TEXTS_DEV)
        g_by_text[at, :] = (g[at, :].astype(F32) * col).astype(BF16)
    for r in range(2):
        copies[2 * r].wait()
        copies[2 * r + 1].wait()
        at = pl.ds(r * VROWS // 2, VROWS // 2)
        part = nn(p[0, at, :], g_by_text[pl.ds(0, HALF), :]) + nn(p[1, at, :], g_by_text[pl.ds(HALF, HALF), :])
        for pair in range(FRAMES // 4):
            others = []
            for f in (2 * pair, 2 * pair + 1):
                full = r * FRAMES // 2 + f
                new = part[f * CLIPS_DEV : (f + 1) * CLIPS_DEV]
                block = av_ref[pl.ds(full * CLIPS_DEV, CLIPS_DEV), :] * inverse + new
                low, high = block[:half], block[half:]
                mine[pl.ds(full * half, half), :] = jnp.where(core == 0, low, high)
                others.append(jnp.where(core == 0, high, low))
            at = pl.ds((r * FRAMES // 4 + pair) * CLIPS_DEV, CLIPS_DEV)
            twin[at, :] = jnp.concatenate(others, axis=0).astype(BF16)
    real = iota((1, LANES), 1) < TEXTS_DEV
    logs = jnp.where(real, jnp.log(jnp.where(real, c_row, 1.0)), 0.0)
    extra = pieces(jnp.sum(logs, axis=1, keepdims=True))
    mine[pl.ds(FRAMES * half, EXTRA), :] = extra
    twin[pl.ds(FRAMES * half, EXTRA), :] = extra.astype(BF16)


def own_z():
    return lax.rem(lax.axis_index("outer"), NZ)


def clip_rows_kernel(mine, got, keep, send, scr):
    step = 2 * NZ
    for i in range(VOWN // 2):
        at = pl.ds(i * step, step)
        two = mine[at, :] + got[at, :].astype(F32)
        for k in range(2):
            put(scr, pl.ds(2 * i + k, NZ, stride=V_PITCH), two[k * NZ : (k + 1) * NZ])
    bit = lax.rem(own_z(), 2)
    owners = NZ // 2
    for i in range(owners):
        at = pl.ds(i * VOWN, VOWN)
        keep[at, :] = get(scr, pl.ds(pl.multiple_of((owners * bit + i) * V_PITCH, 8), VOWN))
        send[at, :] = get(scr, pl.ds(pl.multiple_of((owners * (1 - bit) + i) * V_PITCH, 8), VOWN)).astype(BF16)
    extra = loss_rows(mine, got, NZ)
    keep[pl.ds(owners * VOWN, EXTRA), :] = extra
    send[pl.ds(owners * VOWN, EXTRA), :] = extra.astype(BF16)


def loss_rows(mine, got, owners):
    tail = pl.ds(owners * VOWN, EXTRA)
    return pieces(unpiece(mine[tail, :]) + unpiece(got[tail, :].astype(F32)))


def quarter_kernel(mine, got, keep, *sends):
    own = lax.div(own_z(), 2)
    extra = loss_rows(mine, got, NZ // 2)
    for out, owner in zip((keep, *sends), (own, own ^ 1, own ^ 2, own ^ 3), strict=True):
        at = pl.ds(pl.multiple_of(owner * VOWN, VOWN), VOWN)
        out[pl.ds(0, VOWN), :] = (mine[at, :] + got[at, :].astype(F32)).astype(out.dtype)
        out[pl.ds(VOWN, EXTRA), :] = extra.astype(out.dtype)


def token_grads(total, scr, raw, out, tokens):
    put(scr, pl.ds(0, OWN * tokens), total)
    for c in range(OWN):
        x = raw[c].astype(F32)
        d = get(scr, pl.ds(c, tokens, stride=OWN))
        mean_sq = jnp.mean(x * x, axis=-1, keepdims=True) + EPSILON
        factor = lax.rsqrt(mean_sq) / math.sqrt(WIDTH)
        inner = jnp.sum(d * x, axis=-1, keepdims=True)
        out[c] = factor * d - factor * x * (inner / (WIDTH * mean_sq))


def video_grad_kernel(clips, mine, got1, got2, got3, c_row, diag, video, out, loss, scr):
    at = pl.ds(0, VOWN)
    total = mine[at, :]
    for got in (got1, got2, got3):
        total = total + got[at, :].astype(F32)
    token_grads(total + diag[...], scr, video, out, FRAMES)
    row_part = c_row[:, TEXTS_DEV : TEXTS_DEV + 1]
    tail = pl.ds(VOWN, EXTRA)
    near = unpiece(mine[tail, :]) + unpiece(got1[tail, :].astype(F32))
    far = unpiece(got2[tail, :].astype(F32)) + unpiece(got3[tail, :].astype(F32))
    loss[...] = (near + far + row_part) * (0.5 / clips)


def gloss_grad_kernel(got, diag, gloss, out, scr):
    total = got[0].astype(F32)
    for i in range(1, NXY):
        total = total + got[i].astype(F32)
    token_grads(total + diag[...], scr, gloss, out, GLOSSES)


def shape(*dims, dtype=F32):
    return jax.ShapeDtypeStruct(dims, dtype)


def on_device(clips, video, gloss, frame_count, gloss_count):
    vmem, hbm = pl.BlockSpec(memory_space=pltpu.VMEM), pl.BlockSpec(memory_space=pltpu.HBM)
    over_all = ("outer", "inner")

    def to_core(a):
        return lax.ppermute(a, "inner", [(i, i ^ 1) for i in range(lax.axis_size("inner"))])

    def to_z(a, mask):
        return lax.ppermute(a, "outer", [(i, i ^ mask) for i in range(lax.axis_size("outer"))])

    def exchanged(a, groups):
        return lax.all_to_all(a, over_all, 0, 0, axis_index_groups=groups, tiled=True)

    def gathered(a, groups):
        return lax.all_gather(a, over_all, axis=0, axis_index_groups=groups, tiled=True)

    def in_hbm(*arrays):
        return [pltpu.with_memory_space_constraint(a, pltpu.HBM) for a in arrays]

    with jax.named_scope("unit_tokens"):
        v_own, g_send, g_own, counts = pl.pallas_call(
            units_kernel,
            in_specs=[hbm] * 4,
            out_shape=(
                shape(VOWN, WIDTH, dtype=BF16),
                shape(NXY, GOWN, WIDTH, dtype=BF16),
                shape(GOWN, WIDTH, dtype=BF16),
                shape(8, LANES, dtype=jnp.int32),
            ),
            scratch_shapes=[
                pltpu.SMEM((OWN,), jnp.int32),
                pltpu.SMEM((OWN,), jnp.int32),
                pltpu.VMEM((OWN, FRAMES, WIDTH), BF16),
                pltpu.VMEM((OWN, GLOSSES, WIDTH), BF16),
                two_halves(VOWN, OWN),
                two_halves(GOWN, OWN),
                pltpu.SemaphoreType.DMA((4,)),
            ],
            compiler_params=params(),
            cost_estimate=cost(2e5, 7e5),
        )(*in_hbm(frame_count, gloss_count, video, gloss))

    with jax.named_scope("gather"):
        g_got = exchanged(g_send, XY_GROUPS)
        v_got = gathered(gathered(v_own, Z_QUADS), Z_PAIRS)
        v_got = gathered(v_got, CORE_GROUPS)

    def whole(*dims):
        return pl.BlockSpec(dims, lambda i: (0,) * len(dims))

    with jax.named_scope("forward"):
        v_all, g_all, row_inv, col_inv, e_pair, r_part, c_part = pl.pallas_call(
            forward_kernel,
            in_specs=[vmem] * 2,
            out_specs=[hbm] * 2 + [vmem] * 5,
            out_shape=(
                pltpu.HBM((VROWS, WIDTH), BF16),
                pltpu.HBM((GROWS, WIDTH), BF16),
                shape(VROWS, LANES),
                shape(TILES, CLIPS_DEV, LANES),
                shape(CLIPS_DEV, LANES),
                shape(NZC, 1, LANES),
                shape(1, LANES),
            ),
            scratch_shapes=[
                pltpu.VMEM((VROWS, WIDTH), BF16),
                pltpu.VMEM((GROWS, WIDTH), BF16),
                two_halves(NZC * V_PITCH, V_PITCH),
                two_halves(NXY * G_PITCH, G_PITCH),
                pltpu.VMEM((VROWS, LANES), F32),
                pltpu.VMEM((TILES, 1, LANES), F32),
                pltpu.VMEM((VROWS, 3 * LANES), F32),
                pltpu.VMEM((TILES, CLIPS_DEV, LANES), F32),
                pltpu.SemaphoreType.DMA((2,)),
            ],
            compiler_params=params(),
            cost_estimate=cost(2 * VROWS * GROWS * WIDTH, 8e6, VROWS * GROWS),
        )(v_got, g_got)

    with jax.named_scope("row_sums"):
        c_send, r_row = pl.pallas_call(
            row_sums_kernel,
            in_specs=[vmem] * 2,
            out_shape=(shape(NXY, 1, LANES), shape(1, LANES)),
            compiler_params=params(),
            cost_estimate=cost(1e5, 3e5),
        )(exchanged(r_part, ZC_GROUPS), c_part)
    with jax.named_scope("column_sums"):
        c_got = exchanged(c_send, XY_GROUPS)

    with jax.named_scope("weights"):
        weights = pl.pallas_call(
            weights_kernel,
            in_specs=[hbm, hbm, vmem, vmem, vmem],
            out_specs=hbm,
            out_shape=pltpu.HBM((2, VROWS, HALF), BF16),
            scratch_shapes=[
                pltpu.VMEM((VROWS, WIDTH), BF16),
                pltpu.VMEM((GROWS, WIDTH), BF16),
                pltpu.VMEM((2, VROWS, HALF), BF16),
                pltpu.SemaphoreType.DMA((12,)),
            ],
            compiler_params=params(),
            cost_estimate=cost(2 * VROWS * GROWS * WIDTH, 12e6, VROWS * GROWS),
        )(*in_hbm(v_all, g_all), row_inv, col_inv, e_pair)

    with jax.named_scope("by_clip"):
        by_clip, av = pl.pallas_call(
            by_clip_kernel,
            grid=(2,),
            in_specs=[
                whole(1, LANES),
                pl.BlockSpec((1, VROWS, HALF), lambda i: (i, 0, 0)),
                whole(VROWS, WIDTH),
                pl.BlockSpec((HALF, WIDTH), lambda i: (i, 0)),
            ],
            out_specs=(
                pl.BlockSpec((GLOSSES // 2, TEXTS_DEV, 2 * WIDTH), lambda i: (i, 0, 0)),
                whole(VROWS, WIDTH),
            ),
            out_shape=(pltpu.HBM((GLOSSES, TEXTS_DEV, 2 * WIDTH), F32), shape(VROWS, WIDTH)),
            scratch_shapes=[pltpu.VMEM((VROWS, 2 * WIDTH), BF16)],
            compiler_params=params(),
            cost_estimate=cost(6 * VROWS * GROWS * WIDTH, 14e6),
        )(r_row, *in_hbm(weights, v_all, g_all))

    with jax.named_scope("clip_send"):
        v_rows = FRAMES * CLIPS_DEV // 2 + EXTRA
        mine, twin = pl.pallas_call(
            clip_send_kernel,
            in_specs=[vmem, vmem, hbm, hbm, vmem],
            out_shape=(shape(v_rows, WIDTH), shape(v_rows, WIDTH, dtype=BF16)),
            scratch_shapes=[
                pltpu.VMEM((2, VROWS, HALF), BF16),
                pltpu.VMEM((GROWS, WIDTH), BF16),
                pltpu.VMEM((GROWS, WIDTH), BF16),
                pltpu.SemaphoreType.DMA((5,)),
            ],
            compiler_params=params(),
            cost_estimate=cost(2 * VROWS * GROWS * WIDTH, 1e7),
        )(c_got, r_row, *in_hbm(weights, g_all), av)

    with jax.named_scope("gloss_send"):
        twin, c_ready = lax.optimization_barrier((twin, c_got))
        dg_send, c_row = pl.pallas_call(
            gloss_send_kernel,
            in_specs=[vmem, hbm],
            out_shape=(shape(NXY, GOWN, WIDTH, dtype=BF16), shape(1, LANES)),
            scratch_shapes=[
                pltpu.VMEM((GLOSSES, TEXTS_DEV, 2 * WIDTH), F32),
                two_halves(NXY * G_PITCH, G_PITCH),
                pltpu.SemaphoreType.DMA((QUADS,)),
            ],
            compiler_params=params(),
            cost_estimate=cost(2e6, 5e6),
        )(c_ready, *in_hbm(by_clip))
        dg_got = exchanged(dg_send, XY_GROUPS)

    def kept_and_sent(owners):
        rows = owners * VOWN + EXTRA
        return (shape(rows, WIDTH), shape(rows, WIDTH, dtype=BF16))

    with jax.named_scope("clips_by_core"):
        mine, sent = pl.pallas_call(
            clip_rows_kernel,
            in_specs=[vmem] * 2,
            out_shape=kept_and_sent(NZ // 2),
            scratch_shapes=[two_halves(NZ * V_PITCH, V_PITCH)],
            compiler_params=params(),
            cost_estimate=cost(1e6, 2e6),
        )(mine, to_core(twin))
    with jax.named_scope("clips_by_z"):
        mine, *sent = pl.pallas_call(
            quarter_kernel,
            in_specs=[vmem] * 2,
            out_shape=kept_and_sent(1) + kept_and_sent(1)[1:] * 2,
            compiler_params=params(),
            cost_estimate=cost(1e10, 1e6),
        )(mine, to_z(sent, 1))

    with jax.named_scope("diagonal"):
        mine, v_own, g_own, counts = lax.optimization_barrier((mine, v_own, g_own, counts))
        dv_diag, dg_diag = pl.pallas_call(
            diagonal_kernel,
            in_specs=[vmem] * 3,
            out_shape=(shape(VOWN, WIDTH), shape(GOWN, WIDTH)),
            compiler_params=params(),
            cost_estimate=cost(2e7, 3e5),
        )(counts, v_own, g_own)

    with jax.named_scope("gloss_grad"):
        grad_gloss = pl.pallas_call(
            gloss_grad_kernel,
            in_specs=[vmem] * 3,
            out_shape=shape(OWN, GLOSSES, WIDTH),
            scratch_shapes=[two_halves(GOWN, OWN)],
            compiler_params=params(),
            cost_estimate=cost(1e6, 1e6),
        )(dg_got, dg_diag, gloss)
    mine, grad_gloss = lax.optimization_barrier((mine, grad_gloss))

    with jax.named_scope("video_grad"):
        grad_video, loss = pl.pallas_call(
            functools.partial(video_grad_kernel, clips),
            in_specs=[vmem] * 7,
            out_shape=(shape(OWN, FRAMES, WIDTH), shape(1, 1)),
            scratch_shapes=[two_halves(VOWN, OWN)],
            compiler_params=params(),
            cost_estimate=cost(1e6, 1e6),
        )(mine, *[to_z(a, 2 * m) for m, a in enumerate(sent, start=1)], c_row, dv_diag, video)
    return loss.reshape(()), grad_video, grad_gloss


def solution(mesh):
    clips = OWN * mesh.shape["outer"] * mesh.shape["inner"]
    over_all = ("outer", "inner")
    tokens, counts = P(over_all, None, None), P(over_all)
    return jax.shard_map(
        functools.partial(on_device, clips),
        mesh=mesh,
        in_specs=(tokens, tokens, counts, counts),
        out_specs=(P(), tokens, tokens),
        check_vma=False,
    )
```

```python
import functools
import math

import jax
import jax.numpy as jnp
from jax import lax
from jax.experimental import pallas as pl
from jax.experimental.pallas import tpu as pltpu
from jax.sharding import PartitionSpec as P

F32 = jnp.float32
BF16 = jnp.bfloat16
EPSILON = 1e-06
EXP_SCALE = 10.0 * math.log2(math.e)
MARK = 2.0
MARK_LIMIT = 1.5
FAR = -1e30

NZ, NY, NX, NCORE = 8, 8, 4, 2
OWN = 3
FRAMES, GLOSSES, WIDTH = 32, 16, 256
CLIPS_DEV = NZ * NCORE * OWN
TEXTS_DEV = NY * NX * OWN
LANES = 128
VROWS = FRAMES * CLIPS_DEV
GROWS = GLOSSES * TEXTS_DEV
VOWN = FRAMES * OWN
GOWN = GLOSSES * OWN
EXTRA = 16
V_PITCH, G_PITCH = VOWN + 8, GOWN + 8
QUADS = GLOSSES // 4
TILES = GROWS // LANES
HALF = GROWS // 2
NXY, NZC = NX * NY, NZ * NCORE

def flat(x, z, y, core):
    return ((x % 2) * NZ + z) * 32 + (x // 2) * 16 + 2 * y + core


def z_groups(masks):
    return [
        [flat(x, z ^ mask, y, c) for mask in masks]
        for x in range(NX)
        for y in range(NY)
        for c in range(NCORE)
        for z in range(NZ)
        if not z & masks[-1] and not z & masks[len(masks) // 2]
    ]


Z_QUADS, Z_PAIRS = z_groups((0, 2, 4, 6)), z_groups((0, 1))
CORE_GROUPS = [[flat(x, z, y, c) for c in range(NCORE)] for x in range(NX) for y in range(NY) for z in range(NZ)]
XY_GROUPS = [[flat(x, z, y, c) for x in range(NX) for y in range(NY)] for z in range(NZ) for c in range(NCORE)]
ZC_GROUPS = [[flat(x, z, y, c) for c in range(NCORE) for z in range(NZ)] for x in range(NX) for y in range(NY)]


def params(limit_mb=32):
    return pltpu.CompilerParams(vmem_limit_bytes=limit_mb * 1024 * 1024)


def cost(flops, nbytes, trans=0):
    return pl.CostEstimate(flops=int(flops), bytes_accessed=int(nbytes), transcendentals=int(trans))


def iota(shape, dim):
    return lax.broadcasted_iota(jnp.int32, shape, dim)


def nt(a, b, **kw):
    return lax.dot_general(a, b, (((1,), (1,)), ((), ())), preferred_element_type=F32, **kw)


def nn(a, b, **kw):
    return lax.dot_general(a, b, (((1,), (0,)), ((), ())), preferred_element_type=F32, **kw)


def tn(a, b, **kw):
    return lax.dot_general(a, b, (((0,), (0,)), ((), ())), preferred_element_type=F32, **kw)


def column_of(row, n):
    eye = iota((n, LANES), 0) == iota((n, LANES), 1)
    return jnp.sum(jnp.where(eye, jnp.broadcast_to(row, (n, LANES)), 0.0), axis=1, keepdims=True)


def packed(x):
    lane = iota(x.shape, 1)
    a, b, c = (pltpu.roll(x, shift, 1) for shift in (96, 64, 32))
    return jnp.where(lane < 96, x, a), jnp.where(lane < 64, a, b), jnp.where(lane < 32, b, c)


def unpacked_sum(t0, t1, t2):
    lane = iota(t0.shape, 1)
    second = pltpu.roll(jnp.where(lane >= 96, t0, t1), 32, 1)
    third = pltpu.roll(jnp.where(lane >= 64, t1, t2), 64, 1)
    return (t0 + second) + (third + pltpu.roll(t2, 96, 1))


def pieces(value):
    lane = iota((EXTRA, WIDTH), 1)
    full = jnp.broadcast_to(value, (EXTRA, WIDTH))
    hi = full.astype(BF16).astype(F32)
    mid = (full - hi).astype(BF16).astype(F32)
    low = (full - hi - mid).astype(BF16).astype(F32)
    return jnp.where(lane == 0, hi, jnp.where(lane == 1, mid, jnp.where(lane == 2, low, 0.0)))


def unpiece(block):
    mine = (iota((EXTRA, WIDTH), 0) == 0) & (iota((EXTRA, WIDTH), 1) < 3)
    return jnp.sum(jnp.where(mine, block, 0.0), keepdims=True).reshape(1, 1)


def put(ref, at, value):
    ref[0, at, :] = value[:, :LANES]
    ref[1, at, :] = value[:, LANES:]


def get(ref, at):
    return jnp.concatenate([ref[0, at, :], ref[1, at, :]], axis=1)


def two_halves(rows, stride):
    return pltpu.VMEM((2, rows + -(-stride // 8) * 8, LANES), F32)


def units_kernel(fc_in, gc_in, video_in, gloss_in, v_out, g_out, g_one, count_out, fc, gc, video, gloss, v_scr, g_scr, sems):
    pairs = ((fc_in, fc), (gc_in, gc), (video_in, video), (gloss_in, gloss))
    copies = [pltpu.make_async_copy(a, b, sems.at[i]) for i, (a, b) in enumerate(pairs)]
    for copy in copies:
        copy.start()
    for copy in copies:
        copy.wait()
    row = iota((8, LANES), 0)
    counts = jnp.zeros((8, LANES), jnp.int32)
    for c in range(OWN):
        counts = jnp.where(row == c, fc[c], jnp.where(row == OWN + c, gc[c], counts))
    count_out[...] = counts
    for count, raw, scr, tokens in ((fc, video, v_scr, FRAMES), (gc, gloss, g_scr, GLOSSES)):
        row, lane = iota((tokens, WIDTH), 0), iota((tokens, WIDTH), 1)
        for c in range(OWN):
            x = raw[c].astype(F32)
            mean_sq = jnp.mean(x * x, axis=-1, keepdims=True) + EPSILON
            unit = x * (lax.rsqrt(mean_sq) / math.sqrt(WIDTH))
            mark = jnp.where(lane == 0, MARK, 0.0)
            put(scr, pl.ds(c, tokens, stride=OWN), jnp.where(row < count[c], unit, mark))
    v = get(v_scr, pl.ds(0, VOWN)).astype(BF16)
    g = get(g_scr, pl.ds(0, GOWN)).astype(BF16)
    v_out[...] = v
    g_one[...] = g
    for i in range(NXY):
        g_out[i] = g


def diagonal_kernel(count_ref, v_ref, g_ref, dv, dg):
    def pick(count, which):
        return jnp.where(which == 0, count[0], jnp.where(which == 1, count[1], count[2]))

    fc = [count_ref[c : c + 1, 0:1] for c in range(OWN)]
    gc = [count_ref[OWN + c : OWN + c + 1, 0:1] for c in range(OWN)]
    v, g = v_ref[...], g_ref[...]
    shape = (VOWN, GOWN)
    r, q = iota(shape, 0), iota(shape, 1)
    rc, qc = lax.rem(r, OWN), lax.rem(q, OWN)
    valid = (rc == qc) & (lax.div(r, OWN) < pick(fc, rc)) & (lax.div(q, OWN) < pick(gc, qc))
    e = jnp.where(valid, jnp.exp2(nt(v, g) * EXP_SCALE), 0.0)
    r1, q1 = iota((VOWN, 1), 0), iota((1, GOWN), 1)
    rc1, qc1 = lax.rem(r1, OWN), lax.rem(q1, OWN)
    frames_r, glosses_q = pick(fc, rc1), pick(gc, qc1)
    row_ok = lax.div(r1, OWN) < frames_r
    col_ok = lax.div(q1, OWN) < glosses_q
    frames_r, glosses_q = frames_r.astype(F32), glosses_q.astype(F32)
    rows = jnp.where(row_ok, jnp.sum(e, axis=1, keepdims=True), 1.0)
    cols = jnp.where(col_ok, jnp.sum(e, axis=0, keepdims=True), 1.0)
    weight = -5.0 * e * (1.0 / (rows * frames_r) + 1.0 / (cols * glosses_q))
    dv[...] = nn(weight, g.astype(F32), precision=lax.Precision.HIGHEST)
    dg[...] = tn(weight, v.astype(F32), precision=lax.Precision.HIGHEST)


def exp_scores(v, g):
    return jnp.exp2(nt(v, g) * EXP_SCALE)


def forward_kernel(
    v_got, g_got,
    v_hbm, g_hbm, row_out, col_out, e_out, r_out, c_out,
    v_out, g_out, v_scr, g_scr, frame_mask, gloss_mask, rows, cols, sems,
):
    results = ((v_out, v_hbm), (g_out, g_hbm))
    copies = [pltpu.make_async_copy(a, b, sems.at[i]) for i, (a, b) in enumerate(results)]
    for i in range(NZC):
        put(v_scr, pl.ds(i * V_PITCH, VOWN), v_got[pl.ds(i * VOWN, VOWN), :].astype(F32))
    for f in range(FRAMES):
        parts = [
            get(v_scr, pl.ds(k * NZ * V_PITCH + f * OWN + c, NZ, stride=V_PITCH)) for k in range(NCORE) for c in range(OWN)
        ]
        v_out[pl.ds(f * CLIPS_DEV, CLIPS_DEV), :] = jnp.concatenate(parts, axis=0).astype(BF16)
    copies[0].start()
    for i in range(NXY):
        put(g_scr, pl.ds(i * G_PITCH, GOWN), g_got[i].astype(F32))
    for g in range(GLOSSES):
        parts = [
            get(g_scr, pl.ds(x * NY * G_PITCH + g * OWN + c, NY, stride=G_PITCH)) for x in range(NX) for c in range(OWN)
        ]
        g_out[pl.ds(g * TEXTS_DEV, TEXTS_DEV), :] = jnp.concatenate(parts, axis=0).astype(BF16)
    copies[1].start()

    first = jnp.where(iota((WIDTH, LANES), 0) == 0, 1.0, 0.0).astype(BF16)
    frame_mask[...] = jnp.where(nn(v_out[...], first) < MARK_LIMIT, 1.0, 0.0)
    first_row = jnp.where(iota((16, WIDTH), 1) == 0, 1.0, 0.0).astype(BF16)
    for t in range(TILES):
        found = nt(first_row, g_out[pl.ds(t * LANES, LANES), :])[0:1]
        gloss_mask[t] = jnp.where(found < MARK_LIMIT, 1.0, 0.0)
    frames = jnp.zeros((CLIPS_DEV, LANES), F32)
    for f in range(FRAMES):
        frames = frames + frame_mask[pl.ds(f * CLIPS_DEV, CLIPS_DEV), :]
    by_tile = []
    for t in range(3):
        by_tile.append(gloss_mask[t] + gloss_mask[t + 3] + gloss_mask[t + 6] + gloss_mask[t + 9])
    lane = iota((CLIPS_DEV, LANES), 1)
    real = lane < TEXTS_DEV
    counts = unpacked_sum(*[jnp.broadcast_to(t, (8, LANES)) for t in by_tile])
    glosses = jnp.where(real[0:8], counts, 1.0)
    packed_glosses = [t[0:1] for t in packed(glosses)]
    glosses = glosses[0:1]

    for half in range(2):
        e = exp_scores(v_out[...], g_out[pl.ds(half * HALF, HALF), :])
        tiles = range(half * TILES // 2, (half + 1) * TILES // 2)
        masks = [gloss_mask[t] for t in tiles]
        sums = [jnp.zeros((CLIPS_DEV, LANES), F32) for _ in tiles]
        for f in range(FRAMES):
            at = pl.ds(f * CLIPS_DEV, CLIPS_DEV)
            mask = frame_mask[at, :]
            block = e[f * CLIPS_DEV : (f + 1) * CLIPS_DEV]
            parts = [block[:, k * LANES : (k + 1) * LANES] for k in range(TILES // 2)]
            sums = [total + part * mask for total, part in zip(sums, parts, strict=True)]
            for k in range(3):
                part = parts[k] * masks[k] + parts[k + 3] * masks[k + 3]
                rows[at, pl.ds(k * LANES, LANES)] = part if half == 0 else rows[at, pl.ds(k * LANES, LANES)] + part
        for k, t in enumerate(tiles):
            cols[t] = sums[k]

    video_part = jnp.zeros((CLIPS_DEV, LANES), F32)
    for f in range(FRAMES):
        at = pl.ds(f * CLIPS_DEV, CLIPS_DEV)
        mask = frame_mask[at, :]
        total = unpacked_sum(*[rows[at, pl.ds(k * LANES, LANES)] for k in range(3)])
        total = jnp.where(real, total, 1.0)
        product = jnp.where(mask > 0.0, total, 1.0) * (1.0 if f % 4 == 0 else product)
        if f % 4 == 3:
            video_part = video_part + jnp.log(product)
        row_out[at, :] = jnp.where(mask > 0.0, 1.0 / (total * frames), FAR)
    video_part = video_part / frames - jnp.log(glosses)
    gloss_parts = [jnp.zeros((CLIPS_DEV, LANES), F32)] * 3
    for t in range(TILES):
        mask = gloss_mask[t]
        total = cols[t]
        gloss_parts[t % 3] = gloss_parts[t % 3] + mask * jnp.log(total)
        col_out[t] = jnp.where(mask > 0.0, 1.0 / (total * packed_glosses[t % 3]), FAR)
    gloss_part = unpacked_sum(*gloss_parts) / glosses - jnp.log(frames)
    logits = 0.5 * (video_part + gloss_part)
    e_pair = jnp.where(real, jnp.exp(logits), 0.0)
    e_out[...] = e_pair

    sums = jnp.sum(e_pair, axis=1, keepdims=True)
    across = lane == iota((CLIPS_DEV, LANES), 0)
    r_row = jnp.sum(jnp.where(across, jnp.broadcast_to(sums, (CLIPS_DEV, LANES)), 0.0), axis=0, keepdims=True)
    inner, outer = lax.axis_index("inner"), lax.axis_index("outer")
    z, core = lax.rem(outer, NZ), lax.rem(inner, NCORE)
    x, y = 2 * lax.div(inner, 16) + lax.div(outer, NZ), lax.rem(lax.div(inner, NCORE), NY)
    clip0 = core * OWN * NZ + lax.rem(z, 2) * (NZ // 2) + lax.div(z, 2)
    text0 = x * OWN * NY + y
    own = jnp.zeros((CLIPS_DEV, LANES), jnp.bool_)
    for c in range(OWN):
        own = own | ((iota((CLIPS_DEV, LANES), 0) == clip0 + c * NZ) & (lane == text0 + c * NY))
    diag = jnp.sum(jnp.where(own, logits, 0.0), keepdims=True).reshape(1, 1)
    r_row = jnp.where(iota((1, LANES), 1) == CLIPS_DEV, diag, r_row)
    for i in range(NZC):
        r_out[i] = r_row
    c_out[...] = jnp.sum(e_pair, axis=0, keepdims=True)
    for copy in copies:
        copy.wait()


def started(copies):
    for copy in copies:
        copy.start()
    return copies


def halves_of(p):
    return [(r, h, p.at[h, pl.ds(r * VROWS // 2, VROWS // 2)]) for r in range(2) for h in range(2)]


def weights_kernel(v_hbm, g_hbm, row_ref, col_ref, e_ref, p_hbm, v, g, p, sems):
    firsts = [pl.ds(0, VROWS // 2), pl.ds(VROWS // 2, VROWS // 2)]
    order = ((v_hbm, v, 0), (g_hbm, g, 0), (g_hbm, g, 1), (v_hbm, v, 1))
    loads = started([pltpu.make_async_copy(a.at[firsts[i]], b.at[firsts[i]], sems.at[k]) for k, (a, b, i) in enumerate(order)])
    scales = packed(2.5 * e_ref[...])
    stores = []
    for (r, h, out), (_, _, here) in zip(halves_of(p_hbm), halves_of(p), strict=True):
        for load in loads[: 2 if r + h == 0 else 1]:
            load.wait()
        loads = loads[2 if r + h == 0 else 1 :]
        e = exp_scores(v[pl.ds(r * VROWS // 2, VROWS // 2), :], g[pl.ds(h * HALF, HALF), :])
        for f in range(FRAMES // 2):
            row = packed(row_ref[pl.ds((r * FRAMES // 2 + f) * CLIPS_DEV, CLIPS_DEV), :])
            block = e[f * CLIPS_DEV : (f + 1) * CLIPS_DEV]
            parts = []
            for k in range(TILES // 2):
                share = jnp.maximum(row[k % 3] + col_ref[h * TILES // 2 + k], 0.0)
                parts.append(scales[k % 3] * block[:, k * LANES : (k + 1) * LANES] * share)
            here[pl.ds(f * CLIPS_DEV, CLIPS_DEV), :] = jnp.concatenate(parts, axis=1).astype(BF16)
            if f % 8 == 7:
                at = pl.ds((f - 7) * CLIPS_DEV, 8 * CLIPS_DEV)
                stores += started([pltpu.make_async_copy(here.at[at], out.at[at], sems.at[4 + 4 * r + 2 * h + f // 8])])
    for store in stores:
        store.wait()


def added(got):
    total = got[0]
    for i in range(1, got.shape[0]):
        total = total + got[i]
    return total


def row_sums_kernel(r_got, c_part, c_out, r_out):
    r_row = added(r_got)
    r_out[...] = r_row
    lane = iota((1, LANES), 1)
    logs = jnp.where(lane < CLIPS_DEV, jnp.log(jnp.where(lane < CLIPS_DEV, r_row, 1.0)), 0.0)
    logs = logs - jnp.where(lane == CLIPS_DEV, 2.0 * r_row, 0.0)
    total = jnp.sum(logs, axis=1, keepdims=True)
    message = jnp.where(lane == TEXTS_DEV, total, c_part[...])
    for i in range(NXY):
        c_out[i] = message


def inverse_texts(c_row):
    return jnp.broadcast_to(1.0 / column_of(c_row, TEXTS_DEV), (TEXTS_DEV, WIDTH))


def by_clip_kernel(r_ref, p_ref, v_ref, g_ref, out, av_out, both):
    step = pl.program_id(0)

    @pl.when(step == 0)
    def _():
        inverse = jnp.broadcast_to(1.0 / column_of(r_ref[...], CLIPS_DEV), (CLIPS_DEV, WIDTH))
        for f in range(FRAMES):
            at = pl.ds(f * CLIPS_DEV, CLIPS_DEV)
            v = v_ref[at, :]
            both[at, :WIDTH] = v
            both[at, WIDTH:] = (v.astype(F32) * inverse).astype(BF16)

    out[...] = tn(p_ref[0], both[...]).astype(BF16).reshape(GLOSSES // 2, TEXTS_DEV, 2 * WIDTH)
    part = nn(p_ref[0], g_ref[...])

    @pl.when(step == 0)
    def _():
        av_out[...] = part

    @pl.when(step > 0)
    def _():
        av_out[...] = av_out[...] + part


def gloss_send_kernel(c_got, by_clip, out, c_out, held, scr, sems):
    many = GLOSSES // QUADS
    copies = started(
        [
            pltpu.make_async_copy(by_clip.at[pl.ds(q * many, many)], held.at[pl.ds(q * many, many)], sems.at[q])
            for q in range(QUADS)
        ]
    )
    c_out[...] = added(c_got)
    col = inverse_texts(c_out[...])
    for q, copy in enumerate(copies):
        copy.wait()
        for k in range(many):
            g = q * many + k
            both = held[g].astype(F32)
            block = both[:, :WIDTH] * col + both[:, WIDTH:]
            row = g * OWN
            for x in range(NX):
                for c in range(OWN):
                    first = (x * OWN + c) * NY
                    put(scr, pl.ds(x * NY * G_PITCH + row + c, NY, stride=G_PITCH), block[first : first + NY])
    for i in range(NXY):
        out[i] = get(scr, pl.ds(i * G_PITCH, GOWN)).astype(BF16)


def clip_send_kernel(c_got, r_ref, p_hbm, g_hbm, av_ref, mine, twin, p, g, g_by_text, sems):
    g_copy = pltpu.make_async_copy(g_hbm, g, sems.at[4])
    copies = []
    for (r, h, theirs), (_, _, here) in zip(halves_of(p_hbm), halves_of(p), strict=True):
        copies.append(pltpu.make_async_copy(theirs, here, sems.at[2 * r + h]))
    started([g_copy, *copies])
    c_row = added(c_got)
    col = inverse_texts(c_row)
    core = lax.rem(lax.axis_index("inner"), NCORE)
    inverse = jnp.broadcast_to(1.0 / column_of(r_ref[...], CLIPS_DEV), (CLIPS_DEV, WIDTH))
    half = CLIPS_DEV // 2
    g_copy.wait()
    for i in range(GLOSSES):
        at = pl.ds(i * TEXTS_DEV, TEXTS_DEV)
        g_by_text[at, :] = (g[at, :].astype(F32) * col).astype(BF16)
    for r in range(2):
        copies[2 * r].wait()
        copies[2 * r + 1].wait()
        at = pl.ds(r * VROWS // 2, VROWS // 2)
        part = nn(p[0, at, :], g_by_text[pl.ds(0, HALF), :]) + nn(p[1, at, :], g_by_text[pl.ds(HALF, HALF), :])
        for pair in range(FRAMES // 4):
            others = []
            for f in (2 * pair, 2 * pair + 1):
                full = r * FRAMES // 2 + f
                new = part[f * CLIPS_DEV : (f + 1) * CLIPS_DEV]
                block = av_ref[pl.ds(full * CLIPS_DEV, CLIPS_DEV), :] * inverse + new
                low, high = block[:half], block[half:]
                mine[pl.ds(full * half, half), :] = jnp.where(core == 0, low, high)
                others.append(jnp.where(core == 0, high, low))
            at = pl.ds((r * FRAMES // 4 + pair) * CLIPS_DEV, CLIPS_DEV)
            twin[at, :] = jnp.concatenate(others, axis=0).astype(BF16)
    real = iota((1, LANES), 1) < TEXTS_DEV
    logs = jnp.where(real, jnp.log(jnp.where(real, c_row, 1.0)), 0.0)
    extra = pieces(jnp.sum(logs, axis=1, keepdims=True))
    mine[pl.ds(FRAMES * half, EXTRA), :] = extra
    twin[pl.ds(FRAMES * half, EXTRA), :] = extra.astype(BF16)


def own_z():
    return lax.rem(lax.axis_index("outer"), NZ)


def clip_rows_kernel(mine, got, keep, send, scr):
    step = 2 * NZ
    for i in range(VOWN // 2):
        at = pl.ds(i * step, step)
        two = mine[at, :] + got[at, :].astype(F32)
        for k in range(2):
            put(scr, pl.ds(2 * i + k, NZ, stride=V_PITCH), two[k * NZ : (k + 1) * NZ])
    bit = lax.rem(own_z(), 2)
    owners = NZ // 2
    for i in range(owners):
        at = pl.ds(i * VOWN, VOWN)
        keep[at, :] = get(scr, pl.ds(pl.multiple_of((owners * bit + i) * V_PITCH, 8), VOWN))
        send[at, :] = get(scr, pl.ds(pl.multiple_of((owners * (1 - bit) + i) * V_PITCH, 8), VOWN)).astype(BF16)
    extra = loss_rows(mine, got, NZ)
    keep[pl.ds(owners * VOWN, EXTRA), :] = extra
    send[pl.ds(owners * VOWN, EXTRA), :] = extra.astype(BF16)


def loss_rows(mine, got, owners):
    tail = pl.ds(owners * VOWN, EXTRA)
    return pieces(unpiece(mine[tail, :]) + unpiece(got[tail, :].astype(F32)))


def quarter_kernel(mine, got, keep, *sends):
    own = lax.div(own_z(), 2)
    extra = loss_rows(mine, got, NZ // 2)
    for out, owner in zip((keep, *sends), (own, own ^ 1, own ^ 2, own ^ 3), strict=True):
        at = pl.ds(pl.multiple_of(owner * VOWN, VOWN), VOWN)
        out[pl.ds(0, VOWN), :] = (mine[at, :] + got[at, :].astype(F32)).astype(out.dtype)
        out[pl.ds(VOWN, EXTRA), :] = extra.astype(out.dtype)


def token_grads(total, scr, raw, out, tokens):
    put(scr, pl.ds(0, OWN * tokens), total)
    for c in range(OWN):
        x = raw[c].astype(F32)
        d = get(scr, pl.ds(c, tokens, stride=OWN))
        mean_sq = jnp.mean(x * x, axis=-1, keepdims=True) + EPSILON
        factor = lax.rsqrt(mean_sq) / math.sqrt(WIDTH)
        inner = jnp.sum(d * x, axis=-1, keepdims=True)
        out[c] = factor * d - factor * x * (inner / (WIDTH * mean_sq))


def video_grad_kernel(clips, mine, got1, got2, got3, c_row, diag, video, out, loss, scr):
    at = pl.ds(0, VOWN)
    total = mine[at, :]
    for got in (got1, got2, got3):
        total = total + got[at, :].astype(F32)
    token_grads(total + diag[...], scr, video, out, FRAMES)
    row_part = c_row[:, TEXTS_DEV : TEXTS_DEV + 1]
    tail = pl.ds(VOWN, EXTRA)
    near = unpiece(mine[tail, :]) + unpiece(got1[tail, :].astype(F32))
    far = unpiece(got2[tail, :].astype(F32)) + unpiece(got3[tail, :].astype(F32))
    loss[...] = (near + far + row_part) * (0.5 / clips)


def gloss_grad_kernel(got, diag, gloss, out, scr):
    total = got[0].astype(F32)
    for i in range(1, NXY):
        total = total + got[i].astype(F32)
    token_grads(total + diag[...], scr, gloss, out, GLOSSES)


def shape(*dims, dtype=F32):
    return jax.ShapeDtypeStruct(dims, dtype)


def on_device(clips, video, gloss, frame_count, gloss_count):
    vmem, hbm = pl.BlockSpec(memory_space=pltpu.VMEM), pl.BlockSpec(memory_space=pltpu.HBM)
    over_all = ("outer", "inner")

    def to_core(a):
        return lax.ppermute(a, "inner", [(i, i ^ 1) for i in range(lax.axis_size("inner"))])

    def to_z(a, mask):
        return lax.ppermute(a, "outer", [(i, i ^ mask) for i in range(lax.axis_size("outer"))])

    def exchanged(a, groups):
        return lax.all_to_all(a, over_all, 0, 0, axis_index_groups=groups, tiled=True)

    def gathered(a, groups):
        return lax.all_gather(a, over_all, axis=0, axis_index_groups=groups, tiled=True)

    def in_hbm(*arrays):
        return [pltpu.with_memory_space_constraint(a, pltpu.HBM) for a in arrays]

    with jax.named_scope("unit_tokens"):
        v_own, g_send, g_own, counts = pl.pallas_call(
            units_kernel,
            in_specs=[hbm] * 4,
            out_shape=(
                shape(VOWN, WIDTH, dtype=BF16),
                shape(NXY, GOWN, WIDTH, dtype=BF16),
                shape(GOWN, WIDTH, dtype=BF16),
                shape(8, LANES, dtype=jnp.int32),
            ),
            scratch_shapes=[
                pltpu.SMEM((OWN,), jnp.int32),
                pltpu.SMEM((OWN,), jnp.int32),
                pltpu.VMEM((OWN, FRAMES, WIDTH), BF16),
                pltpu.VMEM((OWN, GLOSSES, WIDTH), BF16),
                two_halves(VOWN, OWN),
                two_halves(GOWN, OWN),
                pltpu.SemaphoreType.DMA((4,)),
            ],
            compiler_params=params(),
            cost_estimate=cost(2e5, 7e5),
        )(*in_hbm(frame_count, gloss_count, video, gloss))

    with jax.named_scope("gather"):
        g_got = exchanged(g_send, XY_GROUPS)
        v_got = gathered(gathered(v_own, Z_QUADS), Z_PAIRS)
        v_got = gathered(v_got, CORE_GROUPS)

    def whole(*dims):
        return pl.BlockSpec(dims, lambda i: (0,) * len(dims))

    with jax.named_scope("forward"):
        v_all, g_all, row_inv, col_inv, e_pair, r_part, c_part = pl.pallas_call(
            forward_kernel,
            in_specs=[vmem] * 2,
            out_specs=[hbm] * 2 + [vmem] * 5,
            out_shape=(
                pltpu.HBM((VROWS, WIDTH), BF16),
                pltpu.HBM((GROWS, WIDTH), BF16),
                shape(VROWS, LANES),
                shape(TILES, CLIPS_DEV, LANES),
                shape(CLIPS_DEV, LANES),
                shape(NZC, 1, LANES),
                shape(1, LANES),
            ),
            scratch_shapes=[
                pltpu.VMEM((VROWS, WIDTH), BF16),
                pltpu.VMEM((GROWS, WIDTH), BF16),
                two_halves(NZC * V_PITCH, V_PITCH),
                two_halves(NXY * G_PITCH, G_PITCH),
                pltpu.VMEM((VROWS, LANES), F32),
                pltpu.VMEM((TILES, 1, LANES), F32),
                pltpu.VMEM((VROWS, 3 * LANES), F32),
                pltpu.VMEM((TILES, CLIPS_DEV, LANES), F32),
                pltpu.SemaphoreType.DMA((2,)),
            ],
            compiler_params=params(),
            cost_estimate=cost(2 * VROWS * GROWS * WIDTH, 8e6, VROWS * GROWS),
        )(v_got, g_got)

    with jax.named_scope("row_sums"):
        c_send, r_row = pl.pallas_call(
            row_sums_kernel,
            in_specs=[vmem] * 2,
            out_shape=(shape(NXY, 1, LANES), shape(1, LANES)),
            compiler_params=params(),
            cost_estimate=cost(1e5, 3e5),
        )(exchanged(r_part, ZC_GROUPS), c_part)
    with jax.named_scope("column_sums"):
        c_got = exchanged(c_send, XY_GROUPS)

    with jax.named_scope("weights"):
        weights = pl.pallas_call(
            weights_kernel,
            in_specs=[hbm, hbm, vmem, vmem, vmem],
            out_specs=hbm,
            out_shape=pltpu.HBM((2, VROWS, HALF), BF16),
            scratch_shapes=[
                pltpu.VMEM((VROWS, WIDTH), BF16),
                pltpu.VMEM((GROWS, WIDTH), BF16),
                pltpu.VMEM((2, VROWS, HALF), BF16),
                pltpu.SemaphoreType.DMA((12,)),
            ],
            compiler_params=params(),
            cost_estimate=cost(2 * VROWS * GROWS * WIDTH, 12e6, VROWS * GROWS),
        )(*in_hbm(v_all, g_all), row_inv, col_inv, e_pair)

    with jax.named_scope("by_clip"):
        by_clip, av = pl.pallas_call(
            by_clip_kernel,
            grid=(2,),
            in_specs=[
                whole(1, LANES),
                pl.BlockSpec((1, VROWS, HALF), lambda i: (i, 0, 0)),
                whole(VROWS, WIDTH),
                pl.BlockSpec((HALF, WIDTH), lambda i: (i, 0)),
            ],
            out_specs=(
                pl.BlockSpec((GLOSSES // 2, TEXTS_DEV, 2 * WIDTH), lambda i: (i, 0, 0)),
                whole(VROWS, WIDTH),
            ),
            out_shape=(pltpu.HBM((GLOSSES, TEXTS_DEV, 2 * WIDTH), BF16), shape(VROWS, WIDTH)),
            scratch_shapes=[pltpu.VMEM((VROWS, 2 * WIDTH), BF16)],
            compiler_params=params(),
            cost_estimate=cost(6 * VROWS * GROWS * WIDTH, 14e6),
        )(r_row, *in_hbm(weights, v_all, g_all))

    with jax.named_scope("clip_send"):
        v_rows = FRAMES * CLIPS_DEV // 2 + EXTRA
        mine, twin = pl.pallas_call(
            clip_send_kernel,
            in_specs=[vmem, vmem, hbm, hbm, vmem],
            out_shape=(shape(v_rows, WIDTH), shape(v_rows, WIDTH, dtype=BF16)),
            scratch_shapes=[
                pltpu.VMEM((2, VROWS, HALF), BF16),
                pltpu.VMEM((GROWS, WIDTH), BF16),
                pltpu.VMEM((GROWS, WIDTH), BF16),
                pltpu.SemaphoreType.DMA((5,)),
            ],
            compiler_params=params(),
            cost_estimate=cost(2 * VROWS * GROWS * WIDTH, 1e7),
        )(c_got, r_row, *in_hbm(weights, g_all), av)

    with jax.named_scope("gloss_send"):
        twin, c_ready = lax.optimization_barrier((twin, c_got))
        dg_send, c_row = pl.pallas_call(
            gloss_send_kernel,
            in_specs=[vmem, hbm],
            out_shape=(shape(NXY, GOWN, WIDTH, dtype=BF16), shape(1, LANES)),
            scratch_shapes=[
                pltpu.VMEM((GLOSSES, TEXTS_DEV, 2 * WIDTH), BF16),
                two_halves(NXY * G_PITCH, G_PITCH),
                pltpu.SemaphoreType.DMA((QUADS,)),
            ],
            compiler_params=params(),
            cost_estimate=cost(2e6, 5e6),
        )(c_ready, *in_hbm(by_clip))
        dg_got = exchanged(dg_send, XY_GROUPS)

    def kept_and_sent(owners):
        rows = owners * VOWN + EXTRA
        return (shape(rows, WIDTH), shape(rows, WIDTH, dtype=BF16))

    with jax.named_scope("clips_by_core"):
        mine, sent = pl.pallas_call(
            clip_rows_kernel,
            in_specs=[vmem] * 2,
            out_shape=kept_and_sent(NZ // 2),
            scratch_shapes=[two_halves(NZ * V_PITCH, V_PITCH)],
            compiler_params=params(),
            cost_estimate=cost(1e6, 2e6),
        )(mine, to_core(twin))
    with jax.named_scope("clips_by_z"):
        mine, *sent = pl.pallas_call(
            quarter_kernel,
            in_specs=[vmem] * 2,
            out_shape=kept_and_sent(1) + kept_and_sent(1)[1:] * 2,
            compiler_params=params(),
            cost_estimate=cost(1e10, 1e6),
        )(mine, to_z(sent, 1))

    with jax.named_scope("diagonal"):
        mine, v_own, g_own, counts = lax.optimization_barrier((mine, v_own, g_own, counts))
        dv_diag, dg_diag = pl.pallas_call(
            diagonal_kernel,
            in_specs=[vmem] * 3,
            out_shape=(shape(VOWN, WIDTH), shape(GOWN, WIDTH)),
            compiler_params=params(),
            cost_estimate=cost(2e7, 3e5),
        )(counts, v_own, g_own)

    with jax.named_scope("gloss_grad"):
        grad_gloss = pl.pallas_call(
            gloss_grad_kernel,
            in_specs=[vmem] * 3,
            out_shape=shape(OWN, GLOSSES, WIDTH),
            scratch_shapes=[two_halves(GOWN, OWN)],
            compiler_params=params(),
            cost_estimate=cost(1e6, 1e6),
        )(dg_got, dg_diag, gloss)
    mine, grad_gloss = lax.optimization_barrier((mine, grad_gloss))

    with jax.named_scope("video_grad"):
        grad_video, loss = pl.pallas_call(
            functools.partial(video_grad_kernel, clips),
            in_specs=[vmem] * 7,
            out_shape=(shape(OWN, FRAMES, WIDTH), shape(1, 1)),
            scratch_shapes=[two_halves(VOWN, OWN)],
            compiler_params=params(),
            cost_estimate=cost(1e6, 1e6),
        )(mine, *[to_z(a, 2 * m) for m, a in enumerate(sent, start=1)], c_row, dv_diag, video)
    return loss.reshape(()), grad_video, grad_gloss


def solution(mesh):
    clips = OWN * mesh.shape["outer"] * mesh.shape["inner"]
    over_all = ("outer", "inner")
    tokens, counts = P(over_all, None, None), P(over_all)
    return jax.shard_map(
        functools.partial(on_device, clips),
        mesh=mesh,
        in_specs=(tokens, tokens, counts, counts),
        out_specs=(P(), tokens, tokens),
        check_vma=False,
    )
```
